32 devices in a mesh: groups: 2 (over y), blk: 4 (over z), ops: 2 (over x), sub: 2 (over core).
Axes of the slice: x: 2, y: 2, z: 4, core: 2. Of those that a mesh axis runs over, the one named last changes fastest.
Arguments:
- theta: bfloat16 [4, 2048, 2048], P('groups', ('blk', 'sub')), parts along dimension 0, may hold values from -6 to 6
- hdiag: bfloat16 [4096, 2048], P(('groups', 'blk', 'sub')), parts along dimension 0, may hold values from -1 to 7
- pattern: int32 [32, 16], P('groups'), parts along dimension 0, may hold values 0 or 1
- left_blocks: bfloat16 [4, 16, 3, 128, 128], P(('groups', 'ops')), parts along dimension 0, may hold values from -0.21875 to 0.21875
- left_cols: int32 [4, 16, 3], P(('groups', 'ops')), parts along dimension 0, may hold values from 0 to 15, as said below
- right_blocks: bfloat16 [4, 16, 3, 128, 128], P(('groups', 'ops')), parts along dimension 0, may hold values from -0.3125 to 0.3125
- right_cols: int32 [4, 16, 3], P(('groups', 'ops')), parts along dimension 0, may hold values from 0 to 15, as said below
Outputs:
- correction: bfloat16 [4, 2048, 2048], P('groups', ('blk', 'sub')), parts along dimension 0
- sigma_two: bfloat16 [4, 2048, 2048], P('groups', ('blk', 'sub')), parts along dimension 0
- subspace: float32 [4, 4], P('groups'), parts along dimension 0
The draws below stay inside these ranges and needn't reach their ends.
There are 2 independent parts, one for each index of `groups`. The reference program is written for one: setup_inputs(seed, part) draws one part's arguments, and reference() takes and returns one part's arrays. A program takes and returns all parts, laid end to end along the dimension named above; each array names one. Nothing has to cross between parts.
Inputs may be any that keep to these rules, and one draw needn't show every extreme that they name: pattern is 1 where a block of the wavefunction is allowed by the symmetry. `left_cols`: the 3 block columns of each block row of a term are distinct. `right_cols`: the 3 block columns of each block row of a term are distinct.
All inputs are finite; a program needn't handle non-finite values.
Results may differ from the reference program's by a relative error of at most 0.0048.
The reference program's roundings to bfloat16 on the way count: a program that leaves them out, or rounds other values in their place, can miss the bound.
Values may be sent and summed in bfloat16 or wider, within the bound.
No kernel may reach another device: no remote copies, remote signals or barrier semaphores. Data moves between devices by JAX's collectives and lax.ppermute only.
A program may use at most 128 MiB of HBM per device.

```python
import jax
import jax.numpy as jnp
from jax import lax

BOND = 2048
BLOCK = 128
SECTORS = 16
LINKS = 3
TERMS = 2
ROOTS = 2


def choose_columns(key):
    scores = jax.random.randint(key, (TERMS, SECTORS, SECTORS), 0, 65536) * SECTORS
    scores = scores + jnp.arange(SECTORS, dtype=jnp.int32)
    ordering = jnp.argsort(scores, axis=-1)
    return ordering[:, :, :LINKS].astype(jnp.int32)


def draw_left_cols(key, part):
    key = jax.random.fold_in(key, 21)
    return choose_columns(key)


def draw_right_cols(key, part):
    key = jax.random.fold_in(key, 22)
    return choose_columns(key)


def touch_ends(entries, own_key, least, largest):
    spot = [jax.random.randint(jax.random.fold_in(own_key, axis), (), 0, length) for axis, length in enumerate(entries.shape)]
    longest = entries.shape.index(max(entries.shape))
    neighbour = spot[:longest] + [(spot[longest] + 1) % entries.shape[longest]] + spot[longest + 1:]
    return entries.at[tuple(spot)].set(least).at[tuple(neighbour)].set(largest)


def steps_of(key, extent, shards, low, largest):
    gain, own = 1.0, jax.random.fold_in(key, 6)
    for dim, blocks in shards:
        draws = jnp.exp(jax.random.uniform(jax.random.fold_in(own, dim), (blocks,), jnp.float32, low / len(shards), largest / len(shards)))
        gain = gain * jnp.repeat(draws, extent[dim] // blocks).reshape([-1 if axis == dim else 1 for axis in range(len(extent))])
    return gain


def centred(own_key, extent, deviation, limit, cuts=(), kind=jnp.bfloat16):
    loudness = steps_of(own_key, extent, cuts, -0.22, 0.18) if cuts else 1.0
    array = jax.random.normal(own_key, extent, jnp.float32) * deviation * loudness
    return jnp.minimum(jnp.maximum(array, -limit), limit).astype(kind)


def setup_inputs(seed: int = 0, part: int = 0) -> dict:
    seeds = jax.random.split(jax.random.key(seed), 8)
    part_splits = jax.random.split(jax.random.fold_in(seeds[7], part), 8)
    return {
        "theta": centred(part_splits[0], (ROOTS, BOND, BOND), 1.0, 6.0, ((1, 8),)),
        "hdiag": jnp.clip(-1.0 + 8.0 * jax.random.uniform(part_splits[1], (BOND, BOND), jnp.float32) ** steps_of(part_splits[1], (BOND, BOND), ((0, 8),), -0.2, 0.2), -1.0, 7.0).astype(jnp.bfloat16),
        "pattern": touch_ends((jax.random.randint(part_splits[2], (SECTORS, SECTORS), 0, 3) < 2).astype(jnp.int32), jax.random.fold_in(part_splits[2], 1), 0, 1),
        "left_blocks": centred(part_splits[3], (TERMS, SECTORS, LINKS, BLOCK, BLOCK), (LINKS * BLOCK * TERMS) ** -0.5, 0.21875, ((0, 2),)),
        "left_cols": draw_left_cols(jax.random.fold_in(jax.random.fold_in(seeds[7], part), 71), part),
        "right_blocks": centred(part_splits[5], (TERMS, SECTORS, LINKS, BLOCK, BLOCK), (LINKS * BLOCK) ** -0.5, 0.3125, ((0, 2),)),
        "right_cols": draw_right_cols(jax.random.fold_in(jax.random.fold_in(seeds[7], part), 71), part),
    }


def right_apply(field_in, blocks, columns):
    grouped = field_in.astype(jnp.float32).reshape(ROOTS, BOND, SECTORS, BLOCK)
    picked = jnp.take(grouped, columns.reshape(-1).astype(jnp.int32), axis=2)
    picked = picked.reshape(ROOTS, BOND, SECTORS, LINKS, BLOCK)
    product = jnp.einsum('nrbjq,bjpq->nrbp', picked, blocks.astype(jnp.float32))
    return product.reshape(ROOTS, BOND, BOND).astype(jnp.bfloat16)

def left_apply(images, blocks, columns):
    grouped = images.astype(jnp.float32).reshape(ROOTS, SECTORS, BLOCK, BOND)
    picked = jnp.take(grouped, columns.reshape(-1).astype(jnp.int32), axis=1)
    picked = picked.reshape(ROOTS, SECTORS, LINKS, BLOCK, BOND)
    product = jnp.einsum('ajpq,najqc->napc', blocks.astype(jnp.float32), picked)
    return product.reshape(ROOTS, BOND, BOND)

def reference(theta, hdiag, pattern, left_blocks, left_cols, right_blocks, right_cols):
    allowed = jnp.repeat(jnp.repeat(pattern, BLOCK, axis=0), BLOCK, axis=1).astype(jnp.bfloat16)
    diagonal = hdiag.astype(jnp.float32)

    def operate(field_in):
        summed = jnp.zeros((ROOTS, BOND, BOND), jnp.float32)
        for term in range(TERMS):
            images = right_apply(field_in, right_blocks[term], right_cols[term])
            summed = summed + left_apply(images, left_blocks[term], left_cols[term])
        offdiag = summed.astype(jnp.bfloat16) * allowed[None]
        return diagonal[None] * field_in.astype(jnp.float32) + offdiag.astype(jnp.float32)
    projected = theta * allowed[None]
    wave = projected.astype(jnp.float32)
    sigma_one = operate(projected)
    norm_sq = lax.optimization_barrier(jnp.sum(wave * wave, axis=(1, 2)))
    energy_sum = lax.optimization_barrier(jnp.sum(wave * sigma_one, axis=(1, 2)))
    denominator = norm_sq + 1e-06
    energy = energy_sum / denominator
    shifted = diagonal[None] - energy[:, None, None]
    update = (sigma_one - energy[:, None, None] * wave) * shifted / (shifted * shifted + 1.0)
    correlation = lax.optimization_barrier(jnp.sum(wave * update, axis=(1, 2)))
    orthogonal = update - (correlation / denominator)[:, None, None] * wave
    length_sq = lax.optimization_barrier(jnp.sum(orthogonal * orthogonal, axis=(1, 2)))
    correction = (orthogonal * jnp.sqrt(norm_sq / (length_sq + 1e-06))[:, None, None]).astype(jnp.bfloat16)
    sigma_two = operate(correction).astype(jnp.bfloat16)
    second = sigma_two.astype(jnp.float32)
    fixed = correction.astype(jnp.float32)
    cross_one = lax.optimization_barrier(jnp.sum(wave * second, axis=(1, 2)))
    cross_two = lax.optimization_barrier(jnp.sum(fixed * sigma_one, axis=(1, 2)))
    cross_three = lax.optimization_barrier(jnp.sum(fixed * second, axis=(1, 2)))
    subspace = jnp.stack([energy_sum, cross_one, cross_two, cross_three], axis=1) / denominator[:, None]
    return (correction, sigma_two, subspace)
```

```python
import functools

import jax
import jax.numpy as jnp
from jax import lax
from jax.experimental import pallas as pl
from jax.experimental.pallas import tpu as pltpu
from jax.sharding import PartitionSpec as P

ANY = pl.BlockSpec(memory_space=pl.ANY)
SMEM = pl.BlockSpec(memory_space=pltpu.SMEM)
VMEM = pl.BlockSpec(memory_space=pltpu.VMEM)
VMEM_LIMIT = 56 * 1024 * 1024
LANES = 128


def apply_right(field_in, blocks, columns):
    roots_here, row_count, full_width = field_in.shape
    term_count, sectors, link_count = columns.shape
    block_size = full_width // sectors
    grouped = field_in.reshape(roots_here, row_count, sectors, block_size)
    picked = jnp.take(grouped, columns.reshape(-1), axis=2)
    picked = picked.reshape(roots_here, row_count, term_count, sectors, link_count, block_size)
    product = jnp.einsum("nrkbjq,kbjpq->knrbp", picked, blocks, preferred_element_type=jnp.float32)
    return product.reshape(term_count, roots_here, row_count, full_width).astype(jnp.bfloat16)


def take_rows(stacked, indices):
    return jnp.take(stacked, indices, axis=1)


def apply_left(arrived, blocks, columns):
    term_count, roots_here, full_width, col_count = arrived.shape
    sectors = columns.shape[1]
    link_count = columns.shape[2]
    block_size = full_width // sectors
    grouped = arrived.reshape(term_count, roots_here, sectors, block_size, col_count)
    picked = jax.vmap(take_rows)(grouped, columns.reshape(term_count, sectors * link_count))
    picked = picked.reshape(term_count, roots_here, sectors, link_count, block_size, col_count)
    product = jnp.einsum("kajpq,knajqc->napc", blocks, picked, preferred_element_type=jnp.float32)
    return product.reshape(roots_here, full_width, col_count)


def general_shards(theta, hdiag, pattern, left_blocks, left_cols, right_blocks, right_cols):
    roots_here, row_count, full_width = theta.shape
    sectors = pattern.shape[0]
    block_size = full_width // sectors
    first_row = lax.axis_index(("blk", "sub")) * row_count
    block_row = (first_row + jnp.arange(row_count, dtype=jnp.int32)) // block_size
    onehot = (block_row[:, None] == jnp.arange(sectors, dtype=jnp.int32)[None, :]).astype(
        jnp.float32
    )
    row_pattern = jnp.dot(onehot, pattern.astype(jnp.float32), preferred_element_type=jnp.float32)
    allowed = jnp.broadcast_to(row_pattern[:, :, None], (row_count, sectors, block_size))
    allowed = allowed.reshape(row_count, full_width).astype(jnp.bfloat16)
    diagonal = hdiag.astype(jnp.float32)
    peers = lax.axis_size("blk") * lax.axis_size("sub")

    def left_part(arrived):
        return apply_left(arrived, left_blocks, left_cols)

    def operate(field_in):
        images = apply_right(field_in, right_blocks, right_cols)
        partial_sum = left_part(
            lax.all_to_all(images, ("blk", "sub"), split_axis=3, concat_axis=2, tiled=True)
        )
        shares = lax.psum_scatter(partial_sum, "ops", scatter_dimension=2, tiled=True)
        returned = lax.all_to_all(
            shares.astype(jnp.bfloat16), ("blk", "sub"), split_axis=1, concat_axis=2, tiled=True
        )
        gathered = lax.all_gather(returned, "ops", axis=2, tiled=True)
        narrow = returned.shape[2] // peers
        gathered = gathered.reshape(roots_here, row_count, lax.axis_size("ops"), peers, narrow)
        offdiag = gathered.transpose(0, 1, 3, 2, 4).reshape(roots_here, row_count, full_width)
        offdiag = offdiag * allowed[None]
        return diagonal[None] * field_in.astype(jnp.float32) + offdiag.astype(jnp.float32)

    projected = theta * allowed[None]
    wave = projected.astype(jnp.float32)
    sigma_one = operate(projected)
    norm_sq, energy_sum = lax.psum(
        (jnp.sum(wave * wave, axis=(1, 2)), jnp.sum(wave * sigma_one, axis=(1, 2))), ("blk", "sub")
    )
    denominator = norm_sq + 1e-06
    energy = energy_sum / denominator
    shifted = diagonal[None] - energy[:, None, None]
    update = (sigma_one - energy[:, None, None] * wave) * shifted / (shifted * shifted + 1.0)
    correlation = lax.psum(jnp.sum(wave * update, axis=(1, 2)), ("blk", "sub"))
    factor = correlation / denominator
    orthogonal = update - factor[:, None, None] * wave
    length_sq = lax.psum(jnp.sum(orthogonal * orthogonal, axis=(1, 2)), ("blk", "sub"))
    correction = (orthogonal * jnp.sqrt(norm_sq / (length_sq + 1e-06))[:, None, None]).astype(
        jnp.bfloat16
    )
    sigma_two = operate(correction).astype(jnp.bfloat16)
    second = sigma_two.astype(jnp.float32)
    fixed = correction.astype(jnp.float32)
    cross_one, cross_two, cross_three = lax.psum(
        (
            jnp.sum(wave * second, axis=(1, 2)),
            jnp.sum(fixed * sigma_one, axis=(1, 2)),
            jnp.sum(fixed * second, axis=(1, 2)),
        ),
        ("blk", "sub"),
    )
    subspace = (
        jnp.stack([energy_sum, cross_one, cross_two, cross_three], axis=1) / denominator[:, None]
    )
    return (correction, sigma_two, subspace)


def halves_fit(mesh):
    sizes = dict(mesh.shape)
    return sizes["blk"] == 4 and sizes["ops"] == 2 and sizes["sub"] == 2


def across(value, axis, distance):
    size = lax.axis_size(axis)
    return lax.ppermute(value, axis, [(i, i ^ distance) for i in range(size)])


def share(stats):
    axes = ("blk", "ops", "sub")
    count = lax.axis_size("blk") * lax.axis_size("ops") * lax.axis_size("sub")
    found = [stats]
    for distance in range(1, 8):
        found.append(lax.ppermute(stats, axes, [(i, i ^ distance) for i in range(count)]))
    return found


def place():
    return lax.axis_index("blk"), lax.axis_index("ops"), lax.axis_index("sub")


def fold(value):
    rows, width = value.shape
    value = jnp.sum(value.reshape(rows // 8, 8, width), axis=0)
    return sum(value[:, at : at + LANES] for at in range(0, width, LANES))


def operate_kernel(
    first, plan, cols, pattern, right_own, right_near, right_far, left_own, left_other, hd_own, hd_far, *refs
):
    count = len(plan)
    pieces, refs = refs[:count], refs[count:]
    if first:
        psi_out, sigma_out, stats_out = refs[:3]
        refs = refs[3:]
    else:
        psi_in, sigma_in, near_out, far_out, stats_out = refs[:5]
        refs = refs[5:]
    field, picked, images, right, left, diag, sems = refs
    z, x, c = place()
    sectors, block, width = field.shape
    links = right.shape[2]
    mine = 4 * z + 2 * c + x
    rows = (mine, mine ^ 8)

    copies = []

    def begin(source, target):
        copy = pltpu.make_async_copy(source, target, sems.at[len(copies)])
        copy.start()
        copies.append(copy)

    for piece, offsets in zip(pieces, plan):
        for at, (dz, dx, dc) in enumerate(offsets):
            row = 4 * (z ^ dz) + 2 * (c ^ dc) + (x ^ dx if dx < 2 else dx - 2)
            begin(piece.at[at], field.at[row])
    part = right_near.shape[0]
    begin(right_own.at[0], right.at[0])
    begin(right_near, right.at[1, pl.ds(c * part, part)])
    begin(right_far, right.at[1, pl.ds((1 - c) * part, part)])
    for at in range(2):
        begin(left_own.at[0, rows[at]], left.at[0, at])
    begin(left_other, left.at[1])
    begin(hd_own.at[x], diag.at[0])
    begin(hd_far, diag.at[1])
    for copy in copies:
        copy.wait()

    table = sectors * links

    def right_col(term, b, j):
        return cols[(2 * term) * table + b * links + j]

    def left_col(term, a, j):
        return cols[(2 * term + 1) * table + a * links + j]

    def allowed(a, q, value):
        return jnp.where(pattern[a * sectors + q] != 0, value, jnp.zeros_like(value))

    for term in range(2):
        for at in range(2):
            for j in range(links):
                source = left_col(term, rows[at], j)
                spot = (at * links + j) * block
                for q in range(sectors):
                    span = slice(q * block, (q + 1) * block)
                    value = field[source, :, span]
                    if first:
                        value = allowed(source, q, value)
                    picked[term, spot : spot + block, span] = value

    def image(b, carry):
        for term in range(2):
            lhs = []
            for j in range(links):
                start = pl.multiple_of(right_col(term, b, j) * block, block)
                lhs.append(picked[term, :, pl.ds(start, block)])
            rhs = [right[term, b, j] for j in range(links)]
            product = lax.dot_general(
                jnp.concatenate(lhs, axis=1),
                jnp.concatenate(rhs, axis=1),
                (((1,), (1,)), ((), ())),
                preferred_element_type=jnp.float32,
            )
            images[term, :, pl.ds(pl.multiple_of(b * block, block), block)] = product.astype(jnp.bfloat16)
        return carry

    lax.fori_loop(0, sectors, image, 0)

    step = 2
    deep = links * block
    zero = jnp.zeros((8, LANES), jnp.float32)

    def column(n, sums):
        start = pl.multiple_of(n * step * block, step * block)
        span = pl.ds(start, step * block)
        sums = list(sums)
        for at in range(2):
            total = None
            for term in range(2):
                weights = jnp.concatenate([left[term, at, j] for j in range(links)], axis=1)
                product = jnp.dot(
                    weights,
                    images[term, at * deep : (at + 1) * deep, span],
                    preferred_element_type=jnp.float32,
                )
                total = product if total is None else total + product
            total = total.astype(jnp.bfloat16).astype(jnp.float32)
            offdiag = jnp.concatenate(
                [allowed(rows[at], n * step + i, total[:, i * block : (i + 1) * block]) for i in range(step)],
                axis=1,
            )
            own = field[rows[at], :, span].astype(jnp.float32)
            if first:
                own = jnp.concatenate(
                    [allowed(rows[at], n * step + i, own[:, i * block : (i + 1) * block]) for i in range(step)],
                    axis=1,
                )
            result = diag[at, :, span].astype(jnp.float32) * own + offdiag
            if first:
                psi_out[at, :, span] = own.astype(jnp.bfloat16)
                sigma_out[at, :, span] = result
                sums[0] += fold(own * own)
                sums[1] += fold(own * result)
            else:
                narrow = result.astype(jnp.bfloat16)
                (near_out, far_out)[at][:, span] = narrow
                second = narrow.astype(jnp.float32)
                sums[0] += fold(psi_in[at, :, span].astype(jnp.float32) * second)
                sums[1] += fold(own * sigma_in[at, :, span])
                sums[2] += fold(own * second)
        return tuple(sums)

    sums = lax.fori_loop(0, sectors // step, column, (zero,) * (2 if first else 3))
    stats_out[...] = jnp.zeros_like(stats_out)
    for at, value in enumerate(sums):
        stats_out[at : at + 1, :] = jnp.sum(value, axis=0, keepdims=True)


def operate(first, plan, pieces, cols, pattern, right, left, diag, extra=()):
    _, block, width = pieces[0].shape
    right_own, right_near, right_far = right
    _, sectors, links = right_own.shape[:3]
    rows = jax.ShapeDtypeStruct((2, block, width), jnp.bfloat16)
    one = jax.ShapeDtypeStruct((block, width), jnp.bfloat16)
    stats = jax.ShapeDtypeStruct((8, LANES), jnp.float32)
    if first:
        out_shape = (rows, jax.ShapeDtypeStruct((2, block, width), jnp.float32), stats)
    else:
        out_shape = (one, one, stats)
    copies = sum(len(offsets) for offsets in plan) + 8
    inner = 2 * 2 * sectors * 2 * links * links * block * block * block
    outer = 2 * 2 * 2 * links * block * block * width
    return pl.pallas_call(
        functools.partial(operate_kernel, first, plan),
        out_shape=out_shape,
        in_specs=[SMEM, SMEM] + [ANY] * (7 + len(pieces)) + [VMEM] * len(extra),
        out_specs=(VMEM,) * len(out_shape),
        scratch_shapes=[
            pltpu.VMEM((sectors, block, width), jnp.bfloat16),
            pltpu.VMEM((2, 2 * links * block, width), jnp.bfloat16),
            pltpu.VMEM((2, 2 * links * block, width), jnp.bfloat16),
            pltpu.VMEM((2, sectors, links, block, block), jnp.bfloat16),
            pltpu.VMEM((2, 2, links, block, block), jnp.bfloat16),
            pltpu.VMEM((2, block, width), jnp.bfloat16),
            pltpu.SemaphoreType.DMA((copies,)),
        ],
        compiler_params=pltpu.CompilerParams(vmem_limit_bytes=VMEM_LIMIT),
        cost_estimate=pl.CostEstimate(
            flops=inner + outer, bytes_accessed=16 * 1024 * 1024, transcendentals=0
        ),
        name="operate_first" if first else "operate_second",
    )(cols, pattern, right_own, right_near, right_far, *left, *diag, *pieces, *extra)


def total_of(rows):
    return jnp.sum(rows, axis=1, keepdims=True)


def update_kernel(psi, sigma, hd_own, hd_far, *refs):
    stats, (t_out, stats_out, diag, sems) = refs[:8], refs[8:]
    z, x, c = place()
    copies = [
        pltpu.make_async_copy(hd_own.at[x], diag.at[0], sems.at[0]),
        pltpu.make_async_copy(hd_far, diag.at[1], sems.at[1]),
    ]
    for copy in copies:
        copy.start()
    whole = sum(ref[0:2, :] for ref in stats)
    norm_sq, energy_sum = total_of(whole[0:1, :]), total_of(whole[1:2, :])
    energy = energy_sum / (norm_sq + 1e-06)
    mine = total_of(stats[0][0:1, :])
    for copy in copies:
        copy.wait()
    _, block, width = psi.shape
    step = 16
    zero = jnp.zeros((8, LANES), jnp.float32)

    def chunk(n, total):
        span = pl.ds(pl.multiple_of(n * step, step), step)
        for at in range(2):
            wave = psi[at, span, :].astype(jnp.float32)
            shifted = diag[at, span, :].astype(jnp.float32) - energy
            t = (sigma[at, span, :] - energy * wave) * shifted / (shifted * shifted + 1.0)
            t_out[at, span, :] = t
            total = total + fold(wave * t)
        return total

    lanes = jnp.sum(lax.fori_loop(0, block // step, chunk, zero), axis=0, keepdims=True)
    correlation = total_of(lanes)
    local = jnp.where(mine > 0.0, correlation / jnp.where(mine > 0.0, mine, 1.0), 0.0)

    def within(n, total):
        span = pl.ds(pl.multiple_of(n * step, step), step)
        for at in range(2):
            rest = t_out[at, span, :] - local * psi[at, span, :].astype(jnp.float32)
            total = total + fold(rest * rest)
        return total

    spread = jnp.sum(lax.fori_loop(0, block // step, within, zero), axis=0, keepdims=True)
    stats_out[...] = jnp.zeros_like(stats_out)
    stats_out[0:1, :] = jnp.broadcast_to(correlation, (1, LANES))
    stats_out[1:2, :] = jnp.broadcast_to(total_of(spread), (1, LANES))
    stats_out[2:3, :] = jnp.broadcast_to(mine, (1, LANES))
    stats_out[3:4, :] = jnp.broadcast_to(local, (1, LANES))
    stats_out[4:5, :] = jnp.broadcast_to(norm_sq, (1, LANES))


def correct_kernel(psi, t, *refs):
    stats, (out,) = refs[:8], refs[8:]
    norm_sq = stats[0][4:5, 0:1]
    factor = sum(ref[0:1, 0:1] for ref in stats) / (norm_sq + 1e-06)
    length_sq = jnp.zeros((1, 1), jnp.float32)
    for ref in stats:
        gap = factor - ref[3:4, 0:1]
        length_sq = length_sq + (ref[1:2, 0:1] + gap * gap * ref[2:3, 0:1])
    scale = jnp.sqrt(norm_sq / (length_sq + 1e-06))
    _, block, width = psi.shape
    step = 16

    def chunk(n, carry):
        span = pl.ds(pl.multiple_of(n * step, step), step)
        for at in range(2):
            wave = psi[at, span, :].astype(jnp.float32)
            out[at, span, :] = ((t[at, span, :] - factor * wave) * scale).astype(jnp.bfloat16)
        return carry

    lax.fori_loop(0, block // step, chunk, 0)


def assemble_kernel(near, near_x, far, far_x, out, sems):
    z, x, c = place()
    half = z // 2
    copies = [
        pltpu.make_async_copy(near, out.at[half, x], sems.at[0]),
        pltpu.make_async_copy(near_x, out.at[half, 1 - x], sems.at[1]),
        pltpu.make_async_copy(far, out.at[1 - half, x], sems.at[2]),
        pltpu.make_async_copy(far_x, out.at[1 - half, 1 - x], sems.at[3]),
    ]
    for copy in copies:
        copy.start()
    for copy in copies:
        copy.wait()


def assemble(near, near_x, far, far_x):
    block, width = near.shape
    return pl.pallas_call(
        assemble_kernel,
        out_shape=jax.ShapeDtypeStruct((2, 2, block, width), near.dtype),
        in_specs=[ANY] * 4,
        out_specs=ANY,
        scratch_shapes=[pltpu.SemaphoreType.DMA((4,))],
        name="assemble",
    )(near, near_x, far, far_x).reshape(2, 2 * block, width)


def shards(theta, hdiag, pattern, left_blocks, left_cols, right_blocks, right_cols):
    roots, row_count, width = theta.shape
    sectors = pattern.shape[0]
    block = width // sectors
    links = left_cols.shape[2]
    z, x, c = place()
    half = z // 2
    mine = 4 * z + 2 * c + x

    halves = theta.reshape(roots, 2, block, width)
    diag = hdiag.reshape(2, block, width)

    own = lax.dynamic_index_in_dim(halves, half, 0, keepdims=False)
    given = lax.dynamic_slice(halves, (1 - half, x, 0, 0), (1, 1, block, width))[0]
    far = across(given, "blk", 2)
    near_z = across(own, "blk", 1)
    cols_own = jnp.stack([right_cols[0], left_cols[0]])
    cols_other = across(cols_own, "ops", 1)
    part = sectors // 2
    right_near = across(lax.dynamic_slice_in_dim(right_blocks[0], c * part, part, 0), "ops", 1)
    wanted = jnp.stack(
        [
            lax.dynamic_index_in_dim(left_blocks[0], mine ^ 1, 0, keepdims=False),
            lax.dynamic_index_in_dim(left_blocks[0], mine ^ 9, 0, keepdims=False),
        ]
    )
    left_other = across(wanted, "ops", 1)
    own_core = across(own, "sub", 1)
    right_far = across(right_near, "sub", 1)
    near_z_core = across(near_z, "sub", 1)
    far_z = across(far, "blk", 1)
    far_x = across(far, "ops", 1)
    far_core = across(far, "sub", 1)
    far_zx = across(far_z, "ops", 1)
    far_x_core = across(far_x, "sub", 1)
    far_z_core = across(far_z, "sub", 1)
    far_zx_core = across(far_zx, "sub", 1)
    hd_far = across(lax.dynamic_index_in_dim(diag, x, 0, keepdims=False), "blk", 2)

    cols = jnp.concatenate([cols_own.reshape(-1), cols_other.reshape(-1)])
    allowed = pattern.reshape(-1)
    right = (right_blocks, right_near, right_far)
    left = (left_blocks, left_other)
    pieces = [own, own_core, near_z, near_z_core]
    plan = [
        ((0, 2, 0), (0, 3, 0)),
        ((0, 2, 1), (0, 3, 1)),
        ((1, 2, 0), (1, 3, 0)),
        ((1, 2, 1), (1, 3, 1)),
    ]
    for piece, offset in (
        (far, (2, 0, 0)),
        (far_x, (2, 1, 0)),
        (far_z, (3, 0, 0)),
        (far_zx, (3, 1, 0)),
        (far_core, (2, 0, 1)),
        (far_x_core, (2, 1, 1)),
        (far_z_core, (3, 0, 1)),
        (far_zx_core, (3, 1, 1)),
    ):
        pieces.append(piece)
        plan.append((offset,))
    pieces = [piece.reshape(-1, block, width) for piece in pieces]
    psi, sigma_one, stats_one = operate(
        True, tuple(plan), pieces, cols, allowed, right, left, (diag, hd_far)
    )

    found = share(stats_one)
    t, stats_two = pl.pallas_call(
        update_kernel,
        out_shape=(
            jax.ShapeDtypeStruct((2, block, width), jnp.float32),
            jax.ShapeDtypeStruct((8, LANES), jnp.float32),
        ),
        in_specs=[VMEM, VMEM, ANY, ANY] + [VMEM] * 8,
        out_specs=(VMEM, VMEM),
        scratch_shapes=[
            pltpu.VMEM((2, block, width), jnp.bfloat16),
            pltpu.SemaphoreType.DMA((2,)),
        ],
        compiler_params=pltpu.CompilerParams(vmem_limit_bytes=VMEM_LIMIT),
        name="update",
    )(psi, sigma_one, diag, hd_far, *found)
    found = share(stats_two)
    changed = pl.pallas_call(
        correct_kernel,
        out_shape=jax.ShapeDtypeStruct((2, block, width), jnp.bfloat16),
        in_specs=[VMEM, VMEM] + [VMEM] * 8,
        out_specs=VMEM,
        compiler_params=pltpu.CompilerParams(vmem_limit_bytes=VMEM_LIMIT),
        name="correct",
    )(psi, t, *found)

    by_z = across(changed, "blk", 1)
    by_x = across(changed, "ops", 1)
    by_core = across(changed, "sub", 1)
    by_zx_near = across(by_z[0], "ops", 1)
    by_zx_far = across(by_x[1], "blk", 1)
    by_z_core = across(by_z, "sub", 1)
    by_x_core = across(by_x, "sub", 1)
    by_zx_near_core = across(by_zx_near, "sub", 1)
    by_zx_far_core = across(by_zx_far, "sub", 1)
    pieces, plan = [], []
    for piece, offset in (
        (changed, (0, 0, 0)),
        (by_z, (1, 0, 0)),
        (by_x, (0, 1, 0)),
        (by_core, (0, 0, 1)),
        (by_z_core, (1, 0, 1)),
        (by_x_core, (0, 1, 1)),
    ):
        pieces.append(piece)
        plan.append((offset, (offset[0] ^ 2, offset[1], offset[2])))
    for piece, offset in (
        (by_zx_near, (1, 1, 0)),
        (by_zx_far, (3, 1, 0)),
        (by_zx_near_core, (1, 1, 1)),
        (by_zx_far_core, (3, 1, 1)),
    ):
        pieces.append(piece[None])
        plan.append((offset,))
    two_near, two_far, stats_three = operate(
        False, tuple(plan), pieces, cols, allowed, right, left, (diag, hd_far), (psi, sigma_one)
    )

    other = across(changed[1], "blk", 2)
    correction = assemble(changed[0], by_x[0], other, across(other, "ops", 1))
    other = across(two_far, "blk", 2)
    sigma_two = assemble(two_near, across(two_near, "ops", 1), other, across(other, "ops", 1))

    sums = jnp.concatenate([jnp.sum(stats_one[:2], axis=1), jnp.sum(stats_three[:3], axis=1)])
    here = (jnp.arange(roots) == half)[:, None]
    sums = lax.psum(jnp.where(here, sums[None, :], 0.0), ("blk", "ops", "sub"))
    subspace = sums[:, 1:5] / (sums[:, 0:1] + 1e-06)
    return correction, sigma_two, subspace


def solution(mesh):
    in_specs = (
        P("groups", ("blk", "sub"), None),
        P(("groups", "blk", "sub"), None),
        P("groups", None),
        P(("groups", "ops"), None, None, None, None),
        P(("groups", "ops"), None, None),
        P(("groups", "ops"), None, None, None, None),
        P(("groups", "ops"), None, None),
    )
    out_specs = (
        P("groups", ("blk", "sub"), None),
        P("groups", ("blk", "sub"), None),
        P("groups", None),
    )
    body = shards if halves_fit(mesh) else general_shards
    return jax.shard_map(body, mesh=mesh, in_specs=in_specs, out_specs=out_specs, check_vma=False)
```

```python
import functools

import jax
import jax.numpy as jnp
from jax import lax
from jax.experimental import pallas as pl
from jax.experimental.pallas import tpu as pltpu
from jax.sharding import PartitionSpec as P

ANY = pl.BlockSpec(memory_space=pl.ANY)
SMEM = pl.BlockSpec(memory_space=pltpu.SMEM)
VMEM = pl.BlockSpec(memory_space=pltpu.VMEM)
VMEM_LIMIT = 56 * 1024 * 1024
LANES = 128


def apply_right(field_in, blocks, columns):
    roots_here, row_count, full_width = field_in.shape
    term_count, sectors, link_count = columns.shape
    block_size = full_width // sectors
    grouped = field_in.reshape(roots_here, row_count, sectors, block_size)
    picked = jnp.take(grouped, columns.reshape(-1), axis=2)
    picked = picked.reshape(roots_here, row_count, term_count, sectors, link_count, block_size)
    product = jnp.einsum("nrkbjq,kbjpq->knrbp", picked, blocks, preferred_element_type=jnp.float32)
    return product.reshape(term_count, roots_here, row_count, full_width).astype(jnp.bfloat16)


def take_rows(stacked, indices):
    return jnp.take(stacked, indices, axis=1)


def apply_left(arrived, blocks, columns):
    term_count, roots_here, full_width, col_count = arrived.shape
    sectors = columns.shape[1]
    link_count = columns.shape[2]
    block_size = full_width // sectors
    grouped = arrived.reshape(term_count, roots_here, sectors, block_size, col_count)
    picked = jax.vmap(take_rows)(grouped, columns.reshape(term_count, sectors * link_count))
    picked = picked.reshape(term_count, roots_here, sectors, link_count, block_size, col_count)
    product = jnp.einsum("kajpq,knajqc->napc", blocks, picked, preferred_element_type=jnp.float32)
    return product.reshape(roots_here, full_width, col_count)


def general_shards(theta, hdiag, pattern, left_blocks, left_cols, right_blocks, right_cols):
    roots_here, row_count, full_width = theta.shape
    sectors = pattern.shape[0]
    block_size = full_width // sectors
    first_row = lax.axis_index(("blk", "sub")) * row_count
    block_row = (first_row + jnp.arange(row_count, dtype=jnp.int32)) // block_size
    onehot = (block_row[:, None] == jnp.arange(sectors, dtype=jnp.int32)[None, :]).astype(
        jnp.float32
    )
    row_pattern = jnp.dot(onehot, pattern.astype(jnp.float32), preferred_element_type=jnp.float32)
    allowed = jnp.broadcast_to(row_pattern[:, :, None], (row_count, sectors, block_size))
    allowed = allowed.reshape(row_count, full_width).astype(jnp.bfloat16)
    diagonal = hdiag.astype(jnp.float32)
    peers = lax.axis_size("blk") * lax.axis_size("sub")

    def left_part(arrived):
        return apply_left(arrived, left_blocks, left_cols)

    def operate(field_in):
        images = apply_right(field_in, right_blocks, right_cols)
        partial_sum = left_part(
            lax.all_to_all(images, ("blk", "sub"), split_axis=3, concat_axis=2, tiled=True)
        )
        shares = lax.psum_scatter(partial_sum, "ops", scatter_dimension=2, tiled=True)
        returned = lax.all_to_all(
            shares.astype(jnp.bfloat16), ("blk", "sub"), split_axis=1, concat_axis=2, tiled=True
        )
        gathered = lax.all_gather(returned, "ops", axis=2, tiled=True)
        narrow = returned.shape[2] // peers
        gathered = gathered.reshape(roots_here, row_count, lax.axis_size("ops"), peers, narrow)
        offdiag = gathered.transpose(0, 1, 3, 2, 4).reshape(roots_here, row_count, full_width)
        offdiag = offdiag * allowed[None]
        return diagonal[None] * field_in.astype(jnp.float32) + offdiag.astype(jnp.float32)

    projected = theta * allowed[None]
    wave = projected.astype(jnp.float32)
    sigma_one = operate(projected)
    norm_sq, energy_sum = lax.psum(
        (jnp.sum(wave * wave, axis=(1, 2)), jnp.sum(wave * sigma_one, axis=(1, 2))), ("blk", "sub")
    )
    denominator = norm_sq + 1e-06
    energy = energy_sum / denominator
    shifted = diagonal[None] - energy[:, None, None]
    update = (sigma_one - energy[:, None, None] * wave) * shifted / (shifted * shifted + 1.0)
    correlation = lax.psum(jnp.sum(wave * update, axis=(1, 2)), ("blk", "sub"))
    factor = correlation / denominator
    orthogonal = update - factor[:, None, None] * wave
    length_sq = lax.psum(jnp.sum(orthogonal * orthogonal, axis=(1, 2)), ("blk", "sub"))
    correction = (orthogonal * jnp.sqrt(norm_sq / (length_sq + 1e-06))[:, None, None]).astype(
        jnp.bfloat16
    )
    sigma_two = operate(correction).astype(jnp.bfloat16)
    second = sigma_two.astype(jnp.float32)
    fixed = correction.astype(jnp.float32)
    cross_one, cross_two, cross_three = lax.psum(
        (
            jnp.sum(wave * second, axis=(1, 2)),
            jnp.sum(fixed * sigma_one, axis=(1, 2)),
            jnp.sum(fixed * second, axis=(1, 2)),
        ),
        ("blk", "sub"),
    )
    subspace = (
        jnp.stack([energy_sum, cross_one, cross_two, cross_three], axis=1) / denominator[:, None]
    )
    return (correction, sigma_two, subspace)


def halves_fit(mesh):
    sizes = dict(mesh.shape)
    return sizes["blk"] == 4 and sizes["ops"] == 2 and sizes["sub"] == 2


def across(value, axis, distance):
    size = lax.axis_size(axis)
    return lax.ppermute(value, axis, [(i, i ^ distance) for i in range(size)])


def share(stats):
    axes = ("blk", "ops", "sub")
    count = lax.axis_size("blk") * lax.axis_size("ops") * lax.axis_size("sub")
    found = [stats]
    for distance in range(1, 8):
        found.append(lax.ppermute(stats, axes, [(i, i ^ distance) for i in range(count)]))
    return found


def place():
    return lax.axis_index("blk"), lax.axis_index("ops"), lax.axis_index("sub")


def fold(value):
    rows, width = value.shape
    value = jnp.sum(value.reshape(rows // 8, 8, width), axis=0)
    return sum(value[:, at : at + LANES] for at in range(0, width, LANES))


def row_of(dz, dx, dc):
    z, x, c = place()
    return 4 * (z ^ dz) + 2 * (c ^ dc) + (x ^ dx if dx < 2 else dx - 2)


def operate_kernel(first, plan, cols, pattern, right_own, right_near, right_far, left_own, *refs):
    count = len(plan)
    pieces, refs = refs[:count], refs[count:]
    if first:
        weight_own, weight_far, psi_out, off_out, stats_out = refs[:5]
        refs = refs[5:]
    else:
        hd_own, hd_far, psi_in, off_in, near_out, far_out, late_out, stats_out = refs[:8]
        refs = refs[8:]
    field, images, right, left, diag, sems = refs
    z, x, c = place()
    sectors, block, width = field.shape
    links = right.shape[2]
    mine = 4 * z + 2 * c + x
    rows = (mine, mine ^ 8)

    copies = []

    def begin(source, target):
        copy = pltpu.make_async_copy(source, target, sems.at[len(copies)])
        copy.start()
        copies.append(copy)

    part = sectors // 2
    near, far = pl.ds(c * part, part), pl.ds((1 - c) * part, part)
    begin(right_own.at[0], right.at[x])
    for piece, offsets in zip(pieces, plan):
        tall = piece.shape[1]
        for at, (dz, dx, dc, chunk) in enumerate(offsets):
            begin(piece.at[at], field.at[row_of(dz, dx, dc), pl.ds(chunk * tall, tall)])
    begin(right_near.at[pl.ds(0, part)], right.at[1 - x, near])
    begin(right_far, right.at[1 - x, far])
    early = len(copies)
    for at in range(2):
        begin(left_own.at[0, rows[at]], left.at[x, at])
    begin(right_near.at[pl.ds(part, 2)], left.at[1 - x])
    if not first:
        begin(hd_own.at[x], diag.at[0])
        begin(hd_far, diag.at[1])
    for copy in copies[:early]:
        copy.wait()

    table = sectors * links

    def right_col(term, b, j):
        return cols[(2 * term) * table + b * links + j]

    def left_col(term, a, j):
        return cols[(2 * term + 1) * table + a * links + j]

    def allowed(a, q, value):
        return jnp.where(pattern[a * sectors + q] != 0, value, jnp.zeros_like(value))

    sources = [[left_col(term, rows[at], j) for at in range(2) for j in range(links)] for term in range(2)]

    def image(b, carry):
        for term in range(2):
            found = [right_col(term, b, j) for j in range(links)]
            lhs = []
            for source in sources[term]:
                line = []
                for col in found:
                    value = field[source, :, pl.ds(pl.multiple_of(col * block, block), block)]
                    line.append(allowed(source, col, value) if first else value)
                lhs.append(jnp.concatenate(line, axis=1))
            rhs = [right[term, b, j] for j in range(links)]
            product = lax.dot_general(
                jnp.concatenate(lhs, axis=0),
                jnp.concatenate(rhs, axis=1),
                (((1,), (1,)), ((), ())),
                preferred_element_type=jnp.float32,
            )
            images[term, :, pl.ds(pl.multiple_of(b * block, block), block)] = product.astype(jnp.bfloat16)
        return carry

    lax.fori_loop(0, sectors, image, 0)
    for copy in copies[early:]:
        copy.wait()

    step = 2
    deep = links * block
    half = block // 2
    zero = jnp.zeros((8, LANES), jnp.float32)

    def column(n, sums):
        start = pl.multiple_of(n * step * block, step * block)
        span = pl.ds(start, step * block)
        sums = list(sums)

        def masked(a, value):
            parts = [
                allowed(a, n * step + i, value[:, i * block : (i + 1) * block]) for i in range(step)
            ]
            return jnp.concatenate(parts, axis=1)

        for at in range(2):
            total = None
            for term in range(2):
                weights = jnp.concatenate([left[term, at, j] for j in range(links)], axis=1)
                product = jnp.dot(
                    weights,
                    images[term, at * deep : (at + 1) * deep, span],
                    preferred_element_type=jnp.float32,
                )
                total = product if total is None else total + product
            offdiag = masked(rows[at], total.astype(jnp.bfloat16).astype(jnp.float32))
            own = field[rows[at], :, span].astype(jnp.float32)
            if first:
                own = masked(rows[at], own)
                psi_out[at, :, span] = own.astype(jnp.bfloat16)
                off_out[at, :, span] = offdiag.astype(jnp.bfloat16)
                sums[0] += fold(own * own)
                sums[1] += fold(own * offdiag)
            else:
                weight = diag[at, :, span].astype(jnp.float32)
                narrow = (weight * own + offdiag).astype(jnp.bfloat16)
                if at == 0:
                    near_out[:, span] = narrow
                else:
                    far_out[:, span] = narrow[:half]
                    late_out[:, span] = narrow[half:]
                second = narrow.astype(jnp.float32)
                wave = psi_in[at, :, span].astype(jnp.float32)
                sigma_one = weight * wave + off_in[at, :, span].astype(jnp.float32)
                sums[0] += fold(wave * second)
                sums[1] += fold(own * sigma_one)
                sums[2] += fold(own * second)
        return tuple(sums)

    sums = list(lax.fori_loop(0, sectors // step, column, (zero,) * (2 if first else 3)))
    if first:
        sums[1] += weight_own[...] + weight_far[...]
    stats_out[...] = jnp.zeros_like(stats_out)
    for at, value in enumerate(sums):
        stats_out[at : at + 1, :] = jnp.sum(value, axis=0, keepdims=True)


def operate(first, plan, pieces, cols, pattern, right, left, extra):
    right_own, right_near, right_far = right
    _, sectors, links, block = right_own.shape[:4]
    width = sectors * block
    rows = jax.ShapeDtypeStruct((2, block, width), jnp.bfloat16)
    one = jax.ShapeDtypeStruct((block, width), jnp.bfloat16)
    some = jax.ShapeDtypeStruct((block // 2, width), jnp.bfloat16)
    stats = jax.ShapeDtypeStruct((8, LANES), jnp.float32)
    out_shape = (rows, rows, stats) if first else (one, some, some, stats)
    extra_specs = [VMEM, VMEM] if first else [ANY, ANY, VMEM, VMEM]
    copies = sum(len(offsets) for offsets in plan) + 8
    inner = 2 * 2 * sectors * 2 * links * links * block * block * block
    outer = 2 * 2 * 2 * links * block * block * width
    return pl.pallas_call(
        functools.partial(operate_kernel, first, plan),
        out_shape=out_shape,
        in_specs=[SMEM, SMEM] + [ANY] * (4 + len(pieces)) + extra_specs,
        out_specs=(VMEM,) * len(out_shape),
        scratch_shapes=[
            pltpu.VMEM((sectors, block, width), jnp.bfloat16),
            pltpu.VMEM((2, 2 * links * block, width), jnp.bfloat16),
            pltpu.VMEM((2, sectors, links, block, block), jnp.bfloat16),
            pltpu.VMEM((2, 2, links, block, block), jnp.bfloat16),
            pltpu.VMEM((2, block, width), jnp.bfloat16),
            pltpu.SemaphoreType.DMA((copies,)),
        ],
        compiler_params=pltpu.CompilerParams(vmem_limit_bytes=VMEM_LIMIT),
        cost_estimate=pl.CostEstimate(
            flops=inner + outer, bytes_accessed=16 * 1024 * 1024, transcendentals=0
        ),
        name="operate_first" if first else "operate_second",
    )(cols, pattern, right_own, right_near, right_far, left, *pieces, *extra)


def weigh_kernel(pattern, theta, hd, own_out, other_out, waves, diag, sems):
    z, x, c = place()
    copies = [
        pltpu.make_async_copy(theta.at[0, x], waves.at[0], sems.at[0]),
        pltpu.make_async_copy(theta.at[1, x], waves.at[1], sems.at[1]),
        pltpu.make_async_copy(hd.at[x], diag, sems.at[2]),
    ]
    for copy in copies:
        copy.start()
    for copy in copies:
        copy.wait()
    block, width = diag.shape
    sectors = width // block
    mine = 4 * z + 2 * c + x
    zero = jnp.zeros((8, LANES), jnp.float32)

    def column(q, sums):
        span = pl.ds(pl.multiple_of(q * block, block), block)
        weight = diag[:, span].astype(jnp.float32)
        weight = jnp.where(pattern[mine * sectors + q] != 0, weight, jnp.zeros_like(weight))
        found = []
        for root in range(2):
            wave = waves[root, :, span].astype(jnp.float32)
            found.append(sums[root] + fold(weight * wave * wave))
        return tuple(found)

    sums = lax.fori_loop(0, sectors, column, (zero, zero))
    upper = z // 2 == 1
    own_out[...] = jnp.where(upper, sums[1], sums[0])
    other_out[...] = jnp.where(upper, sums[0], sums[1])


def weigh(pattern, theta, hd):
    _, _, block, width = theta.shape
    stats = jax.ShapeDtypeStruct((8, LANES), jnp.float32)
    return pl.pallas_call(
        weigh_kernel,
        out_shape=(stats, stats),
        in_specs=[SMEM, ANY, ANY],
        out_specs=(VMEM, VMEM),
        scratch_shapes=[
            pltpu.VMEM((2, block, width), theta.dtype),
            pltpu.VMEM((block, width), hd.dtype),
            pltpu.SemaphoreType.DMA((3,)),
        ],
        name="weigh",
    )(pattern, theta, hd)


def total_of(rows):
    return jnp.sum(rows, axis=1, keepdims=True)


def update_kernel(psi, off, hd_own, hd_far, *refs):
    stats, (t_out, stats_out, diag, sems) = refs[:8], refs[8:]
    z, x, c = place()
    copies = [
        pltpu.make_async_copy(hd_own.at[x], diag.at[0], sems.at[0]),
        pltpu.make_async_copy(hd_far, diag.at[1], sems.at[1]),
    ]
    for copy in copies:
        copy.start()
    whole = sum(ref[0:2, :] for ref in stats)
    norm_sq, energy_sum = total_of(whole[0:1, :]), total_of(whole[1:2, :])
    energy = energy_sum / (norm_sq + 1e-06)
    mine = total_of(stats[0][0:1, :])
    for copy in copies:
        copy.wait()
    _, block, width = psi.shape
    step = 16
    zero = jnp.zeros((8, LANES), jnp.float32)

    def chunk(n, total):
        span = pl.ds(pl.multiple_of(n * step, step), step)
        for at in range(2):
            wave = psi[at, span, :].astype(jnp.float32)
            weight = diag[at, span, :].astype(jnp.float32)
            sigma = weight * wave + off[at, span, :].astype(jnp.float32)
            shifted = weight - energy
            t = (sigma - energy * wave) * shifted / (shifted * shifted + 1.0)
            t_out[at, span, :] = t
            total = total + fold(wave * t)
        return total

    lanes = jnp.sum(lax.fori_loop(0, block // step, chunk, zero), axis=0, keepdims=True)
    correlation = total_of(lanes)
    local = jnp.where(mine > 0.0, correlation / jnp.where(mine > 0.0, mine, 1.0), 0.0)

    def within(n, total):
        span = pl.ds(pl.multiple_of(n * step, step), step)
        for at in range(2):
            rest = t_out[at, span, :] - local * psi[at, span, :].astype(jnp.float32)
            total = total + fold(rest * rest)
        return total

    spread = jnp.sum(lax.fori_loop(0, block // step, within, zero), axis=0, keepdims=True)
    stats_out[...] = jnp.zeros_like(stats_out)
    stats_out[0:1, :] = jnp.broadcast_to(correlation, (1, LANES))
    stats_out[1:2, :] = jnp.broadcast_to(total_of(spread), (1, LANES))
    stats_out[2:3, :] = jnp.broadcast_to(mine, (1, LANES))
    stats_out[3:4, :] = jnp.broadcast_to(local, (1, LANES))
    stats_out[4:5, :] = jnp.broadcast_to(norm_sq, (1, LANES))


def correct_kernel(psi, t, *refs):
    stats, outs = refs[:8], refs[8:]
    norm_sq = stats[0][4:5, 0:1]
    factor = sum(ref[0:1, 0:1] for ref in stats) / (norm_sq + 1e-06)
    length_sq = jnp.zeros((1, 1), jnp.float32)
    for ref in stats:
        gap = factor - ref[3:4, 0:1]
        length_sq = length_sq + (ref[1:2, 0:1] + gap * gap * ref[2:3, 0:1])
    scale = jnp.sqrt(norm_sq / (length_sq + 1e-06))
    _, block, width = psi.shape
    step = 16

    def chunk(n, carry):
        span = pl.ds(pl.multiple_of(n * step, step), step)
        for at in range(2):
            wave = psi[at, span, :].astype(jnp.float32)
            outs[at][span, :] = ((t[at, span, :] - factor * wave) * scale).astype(jnp.bfloat16)
        return carry

    lax.fori_loop(0, block // step, chunk, 0)


def assemble_kernel(tall, *refs):
    count = len(tall)
    pieces, (out, sems) = refs[:count], refs[count:]
    z, x, c = place()
    half = z // 2
    copies = []
    for at, (root, flip, chunk) in enumerate(tall):
        size = pieces[at].shape[0]
        target = out.at[half ^ root, x ^ flip, pl.ds(chunk * size, size)]
        copies.append(pltpu.make_async_copy(pieces[at], target, sems.at[at]))
    for copy in copies:
        copy.start()
    for copy in copies:
        copy.wait()


def assemble(block, pieces, tall):
    width = pieces[0].shape[1]
    return pl.pallas_call(
        functools.partial(assemble_kernel, tall),
        out_shape=jax.ShapeDtypeStruct((2, 2, block, width), pieces[0].dtype),
        in_specs=[VMEM] * len(pieces),
        out_specs=ANY,
        scratch_shapes=[pltpu.SemaphoreType.DMA((len(pieces),))],
        compiler_params=pltpu.CompilerParams(vmem_limit_bytes=VMEM_LIMIT),
        name="assemble",
    )(*pieces).reshape(2, 2 * block, width)


def after(value, *others):
    return lax.optimization_barrier((value, *others))[0]


def shards(theta, hdiag, pattern, left_blocks, left_cols, right_blocks, right_cols):
    roots, row_count, width = theta.shape
    sectors = pattern.shape[0]
    block = width // sectors
    z, x, c = place()
    half = z // 2
    mine = 4 * z + 2 * c + x

    halves = theta.reshape(roots, 2, block, width)
    diag = hdiag.reshape(2, block, width)
    allowed = pattern.reshape(-1)
    chunk = block // 2

    def given(at):
        return lax.dynamic_slice(halves, (1 - half, x, at * chunk, 0), (1, 1, chunk, width))[0, 0]

    far_a = across(given(0), "blk", 2)
    own = [
        lax.dynamic_slice(halves, (half, at, 0, 0), (1, 1, block, width))[0, 0] for at in range(2)
    ]
    near_a = across(own[0], "blk", 1)
    part = sectors // 2
    packed = jnp.concatenate(
        [
            lax.dynamic_slice_in_dim(right_blocks[0], c * part, part, 0),
            lax.dynamic_slice_in_dim(left_blocks[0], mine ^ 1, 1, 0),
            lax.dynamic_slice_in_dim(left_blocks[0], mine ^ 9, 1, 0),
        ]
    )
    operators = across(packed, "ops", 1)
    cols = jnp.concatenate([right_cols.reshape(-1), left_cols.reshape(-1)])
    cols = lax.all_gather(cols, "ops").reshape(-1)
    own_core = [across(value, "sub", 1) for value in own]
    weight_own, weight_far = weigh(allowed, halves, diag)

    far_b = across(after(given(1), far_a, *own_core), "blk", 2)
    far_za = across(far_a, "blk", 1)
    far_xa = across(far_a, "ops", 1)
    operators_core = across(operators[:part], "sub", 1)
    near_a_core = across(near_a, "sub", 1)

    far_zb = across(far_b, "blk", 1)
    far_xb = across(far_b, "ops", 1)
    far_zxa = across(after(far_za, far_b), "ops", 1)
    near_b = across(after(own[1], far_b), "blk", 1)
    core_a = across(jnp.stack([far_a, far_b, far_xa, far_za]), "sub", 1)
    far_zxb = across(after(far_zb, far_xb), "ops", 1)
    weight_far = across(after(weight_far, far_zb), "blk", 2)
    core_b = across(jnp.stack([far_xb, far_zxa, far_zb]), "sub", 1)
    near_b_core = across(near_b, "sub", 1)
    far_zxb_core = across(far_zxb, "sub", 1)
    hd_far = lax.dynamic_index_in_dim(diag, x, 0, keepdims=False)
    hd_far = across(after(hd_far, far_zb), "blk", 2)

    right = (right_blocks, operators, operators_core)
    pieces = []
    plan = []
    for piece, offsets in (
        (own[0], ((0, 2, 0, 0),)),
        (own[1], ((0, 3, 0, 0),)),
        (own_core[0], ((0, 2, 1, 0),)),
        (own_core[1], ((0, 3, 1, 0),)),
        (near_a, ((1, 2, 0, 0),)),
        (near_b, ((1, 3, 0, 0),)),
        (near_a_core, ((1, 2, 1, 0),)),
        (near_b_core, ((1, 3, 1, 0),)),
        (far_a, ((2, 0, 0, 0),)),
        (far_b, ((2, 0, 0, 1),)),
        (far_xa, ((2, 1, 0, 0),)),
        (far_xb, ((2, 1, 0, 1),)),
        (far_za, ((3, 0, 0, 0),)),
        (far_zb, ((3, 0, 0, 1),)),
        (far_zxa, ((3, 1, 0, 0),)),
        (far_zxb, ((3, 1, 0, 1),)),
        (far_zxb_core, ((3, 1, 1, 1),)),
        (core_a, ((2, 0, 1, 0), (2, 0, 1, 1), (2, 1, 1, 0), (3, 0, 1, 0))),
        (core_b, ((2, 1, 1, 1), (3, 1, 1, 0), (3, 0, 1, 1))),
    ):
        pieces.append(piece if piece.ndim == 3 else piece[None])
        plan.append(offsets)
    psi, off_one, stats_one = operate(
        True, tuple(plan), pieces, cols, allowed, right, left_blocks, (weight_own, weight_far)
    )

    found = share(stats_one)
    t, stats_two = pl.pallas_call(
        update_kernel,
        out_shape=(
            jax.ShapeDtypeStruct((2, block, width), jnp.float32),
            jax.ShapeDtypeStruct((8, LANES), jnp.float32),
        ),
        in_specs=[VMEM, VMEM, ANY, ANY] + [VMEM] * 8,
        out_specs=(VMEM, VMEM),
        scratch_shapes=[
            pltpu.VMEM((2, block, width), jnp.bfloat16),
            pltpu.SemaphoreType.DMA((2,)),
        ],
        compiler_params=pltpu.CompilerParams(vmem_limit_bytes=VMEM_LIMIT),
        name="update",
    )(psi, off_one, diag, hd_far, *found)
    found = share(stats_two)
    one = jax.ShapeDtypeStruct((block, width), jnp.bfloat16)
    near, far = pl.pallas_call(
        correct_kernel,
        out_shape=(one, one),
        in_specs=[VMEM, VMEM] + [VMEM] * 8,
        out_specs=(VMEM, VMEM),
        compiler_params=pltpu.CompilerParams(vmem_limit_bytes=VMEM_LIMIT),
        name="correct",
    )(psi, t, *found)

    near_z = across(near, "blk", 1)
    far_x = across(far, "ops", 1)
    near_core = across(near, "sub", 1)
    far_core = across(far, "sub", 1)
    near_zx = across(after(near_z, far_x), "ops", 1)
    far_xz = across(after(far_x, near_z), "blk", 1)
    near_x = across(after(near, near_z, far_x), "ops", 1)
    far_z = across(after(far, near_z, far_x), "blk", 1)
    near_z_core = across(near_z, "sub", 1)
    far_x_core = across(far_x, "sub", 1)
    near_x_core = across(near_x, "sub", 1)
    far_z_core = across(far_z, "sub", 1)
    near_zx_core = across(near_zx, "sub", 1)
    far_xz_core = across(far_xz, "sub", 1)
    other = across(after(far, near_x, far_z), "blk", 2)
    pieces, plan = [], []
    for piece, offset in (
        (near, (0, 0, 0, 0)),
        (far, (2, 0, 0, 0)),
        (near_core, (0, 0, 1, 0)),
        (far_core, (2, 0, 1, 0)),
        (near_z, (1, 0, 0, 0)),
        (far_z, (3, 0, 0, 0)),
        (near_z_core, (1, 0, 1, 0)),
        (far_z_core, (3, 0, 1, 0)),
        (near_x, (0, 1, 0, 0)),
        (far_x, (2, 1, 0, 0)),
        (near_x_core, (0, 1, 1, 0)),
        (far_x_core, (2, 1, 1, 0)),
        (near_zx, (1, 1, 0, 0)),
        (far_xz, (3, 1, 0, 0)),
        (near_zx_core, (1, 1, 1, 0)),
        (far_xz_core, (3, 1, 1, 0)),
    ):
        pieces.append(piece[None])
        plan.append((offset,))
    two_near, two_far, two_late, stats_three = operate(
        False, tuple(plan), pieces, cols, allowed, right, left_blocks, (diag, hd_far, psi, off_one)
    )

    far_in = across(two_far, "blk", 2)
    near_in = across(two_near, "ops", 1)
    late_in = across(after(two_late, far_in), "blk", 2)
    far_in_x = across(far_in, "ops", 1)
    other_x = across(after(other, two_near), "ops", 1)
    sums = jnp.concatenate([jnp.sum(stats_one[:2], axis=1), jnp.sum(stats_three[:3], axis=1)])
    here = (jnp.arange(roots) == half)[:, None]
    sums = lax.psum(jnp.where(here, sums[None, :], 0.0), ("blk", "ops", "sub"))
    subspace = sums[:, 1:5] / (sums[:, 0:1] + 1e-06)
    late_in_x = across(after(late_in, sums), "ops", 1)
    places = ((0, 0, 0), (0, 1, 0), (1, 0, 0), (1, 1, 0))
    correction = assemble(block, (near, near_x, other, other_x), places)
    places = ((0, 0, 0), (0, 1, 0), (1, 0, 0), (1, 0, 1), (1, 1, 0), (1, 1, 1))
    sigma_two = assemble(block, (two_near, near_in, far_in, late_in, far_in_x, late_in_x), places)
    return correction, sigma_two, subspace


def solution(mesh):
    in_specs = (
        P("groups", ("blk", "sub"), None),
        P(("groups", "blk", "sub"), None),
        P("groups", None),
        P(("groups", "ops"), None, None, None, None),
        P(("groups", "ops"), None, None),
        P(("groups", "ops"), None, None, None, None),
        P(("groups", "ops"), None, None),
    )
    out_specs = (
        P("groups", ("blk", "sub"), None),
        P("groups", ("blk", "sub"), None),
        P("groups", None),
    )
    body = shards if halves_fit(mesh) else general_shards
    return jax.shard_map(body, mesh=mesh, in_specs=in_specs, out_specs=out_specs, check_vma=False)
```

```python
import functools

import jax
import jax.numpy as jnp
from jax import lax
from jax.experimental import pallas as pl
from jax.experimental.pallas import tpu as pltpu
from jax.sharding import PartitionSpec as P

ANY = pl.BlockSpec(memory_space=pl.ANY)
SMEM = pl.BlockSpec(memory_space=pltpu.SMEM)
VMEM = pl.BlockSpec(memory_space=pltpu.VMEM)
VMEM_LIMIT = 56 * 1024 * 1024
LANES = 128


def apply_right(field_in, blocks, columns):
    roots_here, row_count, full_width = field_in.shape
    term_count, sectors, link_count = columns.shape
    block_size = full_width // sectors
    grouped = field_in.reshape(roots_here, row_count, sectors, block_size)
    picked = jnp.take(grouped, columns.reshape(-1), axis=2)
    picked = picked.reshape(roots_here, row_count, term_count, sectors, link_count, block_size)
    product = jnp.einsum("nrkbjq,kbjpq->knrbp", picked, blocks, preferred_element_type=jnp.float32)
    return product.reshape(term_count, roots_here, row_count, full_width).astype(jnp.bfloat16)


def take_rows(stacked, indices):
    return jnp.take(stacked, indices, axis=1)


def apply_left(arrived, blocks, columns):
    term_count, roots_here, full_width, col_count = arrived.shape
    sectors = columns.shape[1]
    link_count = columns.shape[2]
    block_size = full_width // sectors
    grouped = arrived.reshape(term_count, roots_here, sectors, block_size, col_count)
    picked = jax.vmap(take_rows)(grouped, columns.reshape(term_count, sectors * link_count))
    picked = picked.reshape(term_count, roots_here, sectors, link_count, block_size, col_count)
    product = jnp.einsum("kajpq,knajqc->napc", blocks, picked, preferred_element_type=jnp.float32)
    return product.reshape(roots_here, full_width, col_count)


def general_shards(theta, hdiag, pattern, left_blocks, left_cols, right_blocks, right_cols):
    roots_here, row_count, full_width = theta.shape
    sectors = pattern.shape[0]
    block_size = full_width // sectors
    first_row = lax.axis_index(("blk", "sub")) * row_count
    block_row = (first_row + jnp.arange(row_count, dtype=jnp.int32)) // block_size
    onehot = (block_row[:, None] == jnp.arange(sectors, dtype=jnp.int32)[None, :]).astype(
        jnp.float32
    )
    row_pattern = jnp.dot(onehot, pattern.astype(jnp.float32), preferred_element_type=jnp.float32)
    allowed = jnp.broadcast_to(row_pattern[:, :, None], (row_count, sectors, block_size))
    allowed = allowed.reshape(row_count, full_width).astype(jnp.bfloat16)
    diagonal = hdiag.astype(jnp.float32)
    peers = lax.axis_size("blk") * lax.axis_size("sub")

    def left_part(arrived):
        return apply_left(arrived, left_blocks, left_cols)

    def operate(field_in):
        images = apply_right(field_in, right_blocks, right_cols)
        partial_sum = left_part(
            lax.all_to_all(images, ("blk", "sub"), split_axis=3, concat_axis=2, tiled=True)
        )
        shares = lax.psum_scatter(partial_sum, "ops", scatter_dimension=2, tiled=True)
        returned = lax.all_to_all(
            shares.astype(jnp.bfloat16), ("blk", "sub"), split_axis=1, concat_axis=2, tiled=True
        )
        gathered = lax.all_gather(returned, "ops", axis=2, tiled=True)
        narrow = returned.shape[2] // peers
        gathered = gathered.reshape(roots_here, row_count, lax.axis_size("ops"), peers, narrow)
        offdiag = gathered.transpose(0, 1, 3, 2, 4).reshape(roots_here, row_count, full_width)
        offdiag = offdiag * allowed[None]
        return diagonal[None] * field_in.astype(jnp.float32) + offdiag.astype(jnp.float32)

    projected = theta * allowed[None]
    wave = projected.astype(jnp.float32)
    sigma_one = operate(projected)
    norm_sq, energy_sum = lax.psum(
        (jnp.sum(wave * wave, axis=(1, 2)), jnp.sum(wave * sigma_one, axis=(1, 2))), ("blk", "sub")
    )
    denominator = norm_sq + 1e-06
    energy = energy_sum / denominator
    shifted = diagonal[None] - energy[:, None, None]
    update = (sigma_one - energy[:, None, None] * wave) * shifted / (shifted * shifted + 1.0)
    correlation = lax.psum(jnp.sum(wave * update, axis=(1, 2)), ("blk", "sub"))
    factor = correlation / denominator
    orthogonal = update - factor[:, None, None] * wave
    length_sq = lax.psum(jnp.sum(orthogonal * orthogonal, axis=(1, 2)), ("blk", "sub"))
    correction = (orthogonal * jnp.sqrt(norm_sq / (length_sq + 1e-06))[:, None, None]).astype(
        jnp.bfloat16
    )
    sigma_two = operate(correction).astype(jnp.bfloat16)
    second = sigma_two.astype(jnp.float32)
    fixed = correction.astype(jnp.float32)
    cross_one, cross_two, cross_three = lax.psum(
        (
            jnp.sum(wave * second, axis=(1, 2)),
            jnp.sum(fixed * sigma_one, axis=(1, 2)),
            jnp.sum(fixed * second, axis=(1, 2)),
        ),
        ("blk", "sub"),
    )
    subspace = (
        jnp.stack([energy_sum, cross_one, cross_two, cross_three], axis=1) / denominator[:, None]
    )
    return (correction, sigma_two, subspace)


def halves_fit(mesh):
    sizes = dict(mesh.shape)
    return sizes["blk"] == 4 and sizes["ops"] == 2 and sizes["sub"] == 2


def across(value, axis, distance):
    size = lax.axis_size(axis)
    return lax.ppermute(value, axis, [(i, i ^ distance) for i in range(size)])


def share(stats):
    axes = ("blk", "ops")
    count = lax.axis_size("blk") * lax.axis_size("ops")
    pair = jnp.stack([stats, across(stats, "sub", 1)])
    found = [pair]
    for distance in (1, 2, 3):
        found.append(lax.ppermute(pair, axes, [(i, i ^ distance) for i in range(count)]))
    return found


def place():
    return lax.axis_index("blk"), lax.axis_index("ops"), lax.axis_index("sub")


def fold(value):
    rows, width = value.shape
    value = jnp.sum(value.reshape(rows // 8, 8, width), axis=0)
    return sum(value[:, at : at + LANES] for at in range(0, width, LANES))


def row_of(dz, dx, dc):
    z, x, c = place()
    return 4 * (z ^ dz) + 2 * (c ^ dc) + (x ^ dx if dx < 2 else dx - 2)


def operate_kernel(first, plan, cols, pattern, right_own, right_near, right_far, left_own, *refs):
    count = len(plan)
    pieces, refs = refs[:count], refs[count:]
    if first:
        weight_own, weight_far, psi_out, off_out, stats_out = refs[:5]
        refs = refs[5:]
    else:
        hd_own, hd_far, psi_in, off_in, stats_in, near_out, far_out, late_out, stats_out = refs[:9]
        refs = refs[9:]
    field, images, right, left, diag, sems = refs
    z, x, c = place()
    sectors, block, width = field.shape
    links = right.shape[2]
    mine = 4 * z + 2 * c + x
    rows = (mine, mine ^ 8)

    copies = []

    def begin(source, target):
        copy = pltpu.make_async_copy(source, target, sems.at[len(copies)])
        copy.start()
        copies.append(copy)

    part = sectors // 2
    near, far = pl.ds(c * part, part), pl.ds((1 - c) * part, part)
    begin(right_own.at[0], right.at[0])
    for piece, offsets in zip(pieces, plan):
        tall = piece.shape[1]
        for at, (dz, dx, dc, chunk) in enumerate(offsets):
            begin(piece.at[at], field.at[row_of(dz, dx, dc), pl.ds(chunk * tall, tall)])
    begin(right_near.at[pl.ds(0, part)], right.at[1, near])
    begin(right_far, right.at[1, far])
    early = len(copies)
    for at in range(2):
        begin(left_own.at[0, rows[at]], left.at[0, at])
    begin(right_near.at[pl.ds(part, 2)], left.at[1])
    if not first:
        begin(hd_own.at[x], diag.at[0])
        begin(hd_far, diag.at[1])
    for copy in copies[:early]:
        copy.wait()

    table = sectors * links

    def right_col(term, b, j):
        return cols[(2 * term) * table + b * links + j]

    def left_col(term, a, j):
        return cols[(2 * term + 1) * table + a * links + j]

    def allowed(a, q, value):
        return jnp.where(pattern[a * sectors + q] != 0, value, jnp.zeros_like(value))

    sources = [[left_col(term, rows[at], j) for at in range(2) for j in range(links)] for term in range(2)]

    deep = links * block

    def image(b, carry):
        for term in range(2):
            found = [right_col(term, b, j) for j in range(links)]
            lhs = []
            for source in sources[term]:
                line = []
                for col in found:
                    value = field[source, :, pl.ds(pl.multiple_of(col * block, block), block)]
                    line.append(allowed(source, col, value) if first else value)
                lhs.append(jnp.concatenate(line, axis=1))
            rhs = [right[term, b, j] for j in range(links)]
            product = lax.dot_general(
                jnp.concatenate(lhs, axis=0),
                jnp.concatenate(rhs, axis=1),
                (((1,), (1,)), ((), ())),
                preferred_element_type=jnp.float32,
            )
            product = product.astype(jnp.bfloat16)
            span = pl.ds(pl.multiple_of(b * block, block), block)
            for at in range(2):
                images[at, term * deep : (term + 1) * deep, span] = product[at * deep : (at + 1) * deep]
        return carry

    lax.fori_loop(0, sectors, image, 0, unroll=2)
    for copy in copies[early:]:
        copy.wait()

    step = 2
    half = block // 2
    zero = jnp.zeros((8, LANES), jnp.float32)

    def column(n, sums):
        start = pl.multiple_of(n * step * block, step * block)
        span = pl.ds(start, step * block)
        sums = list(sums)

        def masked(a, value):
            parts = [
                allowed(a, n * step + i, value[:, i * block : (i + 1) * block]) for i in range(step)
            ]
            return jnp.concatenate(parts, axis=1)

        for at in range(2):
            weights = [left[term, at, j] for term in range(2) for j in range(links)]
            total = jnp.dot(
                jnp.concatenate(weights, axis=1),
                images[at, :, span],
                preferred_element_type=jnp.float32,
            )
            offdiag = masked(rows[at], total.astype(jnp.bfloat16).astype(jnp.float32))
            own = field[rows[at], :, span].astype(jnp.float32)
            if first:
                own = masked(rows[at], own)
                psi_out[at, :, span] = own.astype(jnp.bfloat16)
                off_out[at, :, span] = offdiag.astype(jnp.bfloat16)
                sums[0] += fold(own * own)
                sums[1] += fold(own * offdiag)
            else:
                weight = diag[at, :, span].astype(jnp.float32)
                narrow = (weight * own + offdiag).astype(jnp.bfloat16)
                if at == 0:
                    near_out[:, span] = narrow
                else:
                    far_out[:, span] = narrow[:half]
                    late_out[:, span] = narrow[half:]
                second = narrow.astype(jnp.float32)
                wave = psi_in[at, :, span].astype(jnp.float32)
                sigma_one = weight * wave + off_in[at, :, span].astype(jnp.float32)
                sums[0] += fold(wave * second)
                sums[1] += fold(own * sigma_one)
                sums[2] += fold(own * second)
        return tuple(sums)

    sums = list(lax.fori_loop(0, sectors // step, column, (zero,) * (2 if first else 3)))
    if first:
        sums[1] += weight_own[...] + weight_far[...]
    stats_out[...] = jnp.zeros_like(stats_out)
    for at, value in enumerate(sums):
        stats_out[at : at + 1, :] = jnp.sum(value, axis=0, keepdims=True)
    if not first:
        stats_out[3:5, :] = stats_in[0:2, :]


def operate(first, plan, pieces, cols, pattern, right, left, extra):
    right_own, right_near, right_far = right
    _, sectors, links, block = right_own.shape[:4]
    width = sectors * block
    rows = jax.ShapeDtypeStruct((2, block, width), jnp.bfloat16)
    one = jax.ShapeDtypeStruct((block, width), jnp.bfloat16)
    some = jax.ShapeDtypeStruct((block // 2, width), jnp.bfloat16)
    stats = jax.ShapeDtypeStruct((8, LANES), jnp.float32)
    out_shape = (rows, rows, stats) if first else (one, some, some, stats)
    extra_specs = [VMEM, VMEM] if first else [ANY, ANY, VMEM, VMEM, VMEM]
    copies = sum(len(offsets) for offsets in plan) + 8
    inner = 2 * 2 * sectors * 2 * links * links * block * block * block
    outer = 2 * 2 * 2 * links * block * block * width
    return pl.pallas_call(
        functools.partial(operate_kernel, first, plan),
        out_shape=out_shape,
        in_specs=[SMEM, SMEM] + [ANY] * (4 + len(pieces)) + extra_specs,
        out_specs=(VMEM,) * len(out_shape),
        scratch_shapes=[
            pltpu.VMEM((sectors, block, width), jnp.bfloat16),
            pltpu.VMEM((2, 2 * links * block, width), jnp.bfloat16),
            pltpu.VMEM((2, sectors, links, block, block), jnp.bfloat16),
            pltpu.VMEM((2, 2, links, block, block), jnp.bfloat16),
            pltpu.VMEM((2, block, width), jnp.bfloat16),
            pltpu.SemaphoreType.DMA((copies,)),
        ],
        compiler_params=pltpu.CompilerParams(vmem_limit_bytes=VMEM_LIMIT),
        cost_estimate=pl.CostEstimate(
            flops=inner + outer, bytes_accessed=16 * 1024 * 1024, transcendentals=0
        ),
        name="operate_first" if first else "operate_second",
    )(cols, pattern, right_own, right_near, right_far, left, *pieces, *extra)


def weigh_kernel(pattern, theta, hd, own_out, other_out, waves, diag, sems):
    z, x, c = place()
    copies = [
        pltpu.make_async_copy(theta.at[0, x], waves.at[0], sems.at[0]),
        pltpu.make_async_copy(theta.at[1, x], waves.at[1], sems.at[1]),
        pltpu.make_async_copy(hd.at[x], diag, sems.at[2]),
    ]
    for copy in copies:
        copy.start()
    for copy in copies:
        copy.wait()
    block, width = diag.shape
    sectors = width // block
    mine = 4 * z + 2 * c + x
    zero = jnp.zeros((8, LANES), jnp.float32)

    def column(q, sums):
        span = pl.ds(pl.multiple_of(q * block, block), block)
        weight = diag[:, span].astype(jnp.float32)
        weight = jnp.where(pattern[mine * sectors + q] != 0, weight, jnp.zeros_like(weight))
        found = []
        for root in range(2):
            wave = waves[root, :, span].astype(jnp.float32)
            found.append(sums[root] + fold(weight * wave * wave))
        return tuple(found)

    sums = lax.fori_loop(0, sectors, column, (zero, zero))
    upper = z // 2 == 1
    own_out[...] = jnp.where(upper, sums[1], sums[0])
    other_out[...] = jnp.where(upper, sums[0], sums[1])


def weigh(pattern, theta, hd):
    _, _, block, width = theta.shape
    stats = jax.ShapeDtypeStruct((8, LANES), jnp.float32)
    return pl.pallas_call(
        weigh_kernel,
        out_shape=(stats, stats),
        in_specs=[SMEM, ANY, ANY],
        out_specs=(VMEM, VMEM),
        scratch_shapes=[
            pltpu.VMEM((2, block, width), theta.dtype),
            pltpu.VMEM((block, width), hd.dtype),
            pltpu.SemaphoreType.DMA((3,)),
        ],
        name="weigh",
    )(pattern, theta, hd)


def total_of(rows):
    return jnp.sum(rows, axis=1, keepdims=True)


def update_kernel(psi, off, hd_own, hd_far, *refs):
    stats, (t_out, stats_out, diag, sems) = refs[:4], refs[4:]
    z, x, c = place()
    copies = [
        pltpu.make_async_copy(hd_own.at[x], diag.at[0], sems.at[0]),
        pltpu.make_async_copy(hd_far, diag.at[1], sems.at[1]),
    ]
    for copy in copies:
        copy.start()
    whole = sum(ref[at, 0:2, :] for ref in stats for at in range(2))
    norm_sq, energy_sum = total_of(whole[0:1, :]), total_of(whole[1:2, :])
    energy = energy_sum / (norm_sq + 1e-06)
    mine = total_of(stats[0][0, 0:1, :])
    for copy in copies:
        copy.wait()
    _, block, width = psi.shape
    step = 16
    zero = jnp.zeros((8, LANES), jnp.float32)

    def chunk(n, total):
        span = pl.ds(pl.multiple_of(n * step, step), step)
        for at in range(2):
            wave = psi[at, span, :].astype(jnp.float32)
            weight = diag[at, span, :].astype(jnp.float32)
            sigma = weight * wave + off[at, span, :].astype(jnp.float32)
            shifted = weight - energy
            t = (sigma - energy * wave) * shifted / (shifted * shifted + 1.0)
            t_out[at, span, :] = t
            total = total + fold(wave * t)
        return total

    lanes = jnp.sum(lax.fori_loop(0, block // step, chunk, zero), axis=0, keepdims=True)
    correlation = total_of(lanes)
    local = jnp.where(mine > 0.0, correlation / jnp.where(mine > 0.0, mine, 1.0), 0.0)

    def within(n, total):
        span = pl.ds(pl.multiple_of(n * step, step), step)
        for at in range(2):
            rest = t_out[at, span, :] - local * psi[at, span, :].astype(jnp.float32)
            total = total + fold(rest * rest)
        return total

    spread = jnp.sum(lax.fori_loop(0, block // step, within, zero), axis=0, keepdims=True)
    stats_out[...] = jnp.zeros_like(stats_out)
    stats_out[0:1, :] = jnp.broadcast_to(correlation, (1, LANES))
    stats_out[1:2, :] = jnp.broadcast_to(total_of(spread), (1, LANES))
    stats_out[2:3, :] = jnp.broadcast_to(mine, (1, LANES))
    stats_out[3:4, :] = jnp.broadcast_to(local, (1, LANES))
    stats_out[4:5, :] = jnp.broadcast_to(norm_sq, (1, LANES))


def correct_kernel(psi, t, *refs):
    stats, outs = refs[:4], refs[4:]
    stats = [ref.at[at] for ref in stats for at in range(2)]
    norm_sq = stats[0][4:5, 0:1]
    factor = sum(ref[0:1, 0:1] for ref in stats) / (norm_sq + 1e-06)
    length_sq = jnp.zeros((1, 1), jnp.float32)
    for ref in stats:
        gap = factor - ref[3:4, 0:1]
        length_sq = length_sq + (ref[1:2, 0:1] + gap * gap * ref[2:3, 0:1])
    scale = jnp.sqrt(norm_sq / (length_sq + 1e-06))
    _, block, width = psi.shape
    step = 16

    def chunk(n, carry):
        span = pl.ds(pl.multiple_of(n * step, step), step)
        for at in range(2):
            wave = psi[at, span, :].astype(jnp.float32)
            outs[at][span, :] = ((t[at, span, :] - factor * wave) * scale).astype(jnp.bfloat16)
        return carry

    lax.fori_loop(0, block // step, chunk, 0)


def assemble_kernel(tall, *refs):
    count = len(tall)
    pieces, (out, sems) = refs[:count], refs[count:]
    z, x, c = place()
    half = z // 2
    copies = []
    for at, (root, flip, chunk) in enumerate(tall):
        size = pieces[at].shape[0]
        target = out.at[half ^ root, x ^ flip, pl.ds(chunk * size, size)]
        copies.append(pltpu.make_async_copy(pieces[at], target, sems.at[at]))
    for copy in copies:
        copy.start()
    for copy in copies:
        copy.wait()


def assemble(block, pieces, tall):
    width = pieces[0].shape[1]
    return pl.pallas_call(
        functools.partial(assemble_kernel, tall),
        out_shape=jax.ShapeDtypeStruct((2, 2, block, width), pieces[0].dtype),
        in_specs=[VMEM] * len(pieces),
        out_specs=ANY,
        scratch_shapes=[pltpu.SemaphoreType.DMA((len(pieces),))],
        compiler_params=pltpu.CompilerParams(vmem_limit_bytes=VMEM_LIMIT),
        name="assemble",
    )(*pieces).reshape(2, 2 * block, width)


def after(value, *others):
    return lax.optimization_barrier((value, *others))[0]


def shards(theta, hdiag, pattern, left_blocks, left_cols, right_blocks, right_cols):
    roots, row_count, width = theta.shape
    sectors = pattern.shape[0]
    block = width // sectors
    z, x, c = place()
    half = z // 2
    mine = 4 * z + 2 * c + x

    halves = theta.reshape(roots, 2, block, width)
    diag = hdiag.reshape(2, block, width)
    allowed = pattern.reshape(-1)
    chunk = block // 2

    def given(at):
        return lax.dynamic_slice(halves, (1 - half, x, at * chunk, 0), (1, 1, chunk, width))[0, 0]

    first = given(0)
    far_a = across(first, "blk", 2)
    halves = after(halves, first)
    own = [
        lax.dynamic_slice(halves, (half, at, 0, 0), (1, 1, block, width))[0, 0] for at in range(2)
    ]
    near_a = across(own[0], "blk", 1)
    cols = jnp.concatenate([right_cols.reshape(-1), left_cols.reshape(-1)])
    cols_other = across(cols, "ops", 1)
    cols = jnp.concatenate([cols, cols_other])
    part = sectors // 2
    packed = jnp.concatenate(
        [
            lax.dynamic_slice_in_dim(right_blocks[0], c * part, part, 0),
            lax.dynamic_slice_in_dim(left_blocks[0], mine ^ 1, 1, 0),
            lax.dynamic_slice_in_dim(left_blocks[0], mine ^ 9, 1, 0),
        ]
    )
    operators = across(after(packed, cols_other), "ops", 1)
    own_core = [across(value, "sub", 1) for value in own]
    weight_own, weight_far = weigh(allowed, halves, diag)

    far_a, second = after((far_a, given(1)), weight_own, cols, *own_core)
    far_b = across(after(second, far_a), "blk", 2)
    far_za = across(far_a, "blk", 1)
    far_xa = across(far_a, "ops", 1)
    weight_far = across(weight_far, "blk", 2)

    far_zb = across(after(far_b, far_za), "blk", 1)
    near_b = across(after(own[1], far_b), "blk", 1)
    far_zxa = across(after(far_za, far_b), "ops", 1)
    far_xb = across(far_b, "ops", 1)
    operators_core = across(after(operators[:part], far_b), "sub", 1)
    near_a_core = across(after(near_a, far_b), "sub", 1)
    core_a = across(jnp.stack([far_a, far_b, far_xa, far_za]), "sub", 1)

    far_zxb = across(after(far_zb, far_xb, far_zxa), "ops", 1)
    core_b = across(jnp.stack([far_xb, far_zxa, far_zb]), "sub", 1)
    near_b_core = across(near_b, "sub", 1)
    hd_far = lax.dynamic_index_in_dim(diag, x, 0, keepdims=False)
    hd_far = across(after(hd_far, far_zb), "blk", 2)
    far_zxb_core = across(far_zxb, "sub", 1)

    right = (right_blocks, operators, operators_core)
    pieces = []
    plan = []
    for piece, offsets in (
        (own[0], ((0, 2, 0, 0),)),
        (own[1], ((0, 3, 0, 0),)),
        (own_core[0], ((0, 2, 1, 0),)),
        (own_core[1], ((0, 3, 1, 0),)),
        (near_a, ((1, 2, 0, 0),)),
        (near_b, ((1, 3, 0, 0),)),
        (near_a_core, ((1, 2, 1, 0),)),
        (near_b_core, ((1, 3, 1, 0),)),
        (far_a, ((2, 0, 0, 0),)),
        (far_b, ((2, 0, 0, 1),)),
        (far_xa, ((2, 1, 0, 0),)),
        (far_xb, ((2, 1, 0, 1),)),
        (far_za, ((3, 0, 0, 0),)),
        (far_zb, ((3, 0, 0, 1),)),
        (far_zxa, ((3, 1, 0, 0),)),
        (far_zxb, ((3, 1, 0, 1),)),
        (far_zxb_core, ((3, 1, 1, 1),)),
        (core_a, ((2, 0, 1, 0), (2, 0, 1, 1), (2, 1, 1, 0), (3, 0, 1, 0))),
        (core_b, ((2, 1, 1, 1), (3, 1, 1, 0), (3, 0, 1, 1))),
    ):
        pieces.append(piece if piece.ndim == 3 else piece[None])
        plan.append(offsets)
    psi, off_one, stats_one = operate(
        True, tuple(plan), pieces, cols, allowed, right, left_blocks, (weight_own, weight_far)
    )

    found = share(stats_one)
    t, stats_two = pl.pallas_call(
        update_kernel,
        out_shape=(
            jax.ShapeDtypeStruct((2, block, width), jnp.float32),
            jax.ShapeDtypeStruct((8, LANES), jnp.float32),
        ),
        in_specs=[VMEM, VMEM, ANY, ANY] + [VMEM] * 4,
        out_specs=(VMEM, VMEM),
        scratch_shapes=[
            pltpu.VMEM((2, block, width), jnp.bfloat16),
            pltpu.SemaphoreType.DMA((2,)),
        ],
        compiler_params=pltpu.CompilerParams(vmem_limit_bytes=VMEM_LIMIT),
        name="update",
    )(psi, off_one, diag, hd_far, *found)
    found = share(stats_two)
    one = jax.ShapeDtypeStruct((block, width), jnp.bfloat16)
    near, far = pl.pallas_call(
        correct_kernel,
        out_shape=(one, one),
        in_specs=[VMEM, VMEM] + [VMEM] * 4,
        out_specs=(VMEM, VMEM),
        compiler_params=pltpu.CompilerParams(vmem_limit_bytes=VMEM_LIMIT),
        name="correct",
    )(psi, t, *found)

    near_z = across(near, "blk", 1)
    far_x = across(far, "ops", 1)
    near_core = across(near, "sub", 1)
    far_core = across(far, "sub", 1)
    near_zx = across(after(near_z, far_x), "ops", 1)
    far_xz = across(after(far_x, near_z), "blk", 1)
    near_x = across(after(near, near_z, far_x), "ops", 1)
    far_z = across(after(far, near_z, far_x), "blk", 1)
    near_z_core = across(near_z, "sub", 1)
    far_x_core = across(far_x, "sub", 1)
    near_x_core = across(near_x, "sub", 1)
    far_z_core = across(far_z, "sub", 1)
    near_zx_core = across(near_zx, "sub", 1)
    far_xz_core = across(far_xz, "sub", 1)
    other = across(after(far, near_x, far_z), "blk", 2)
    pieces, plan = [], []
    for piece, offset in (
        (near, (0, 0, 0, 0)),
        (far, (2, 0, 0, 0)),
        (near_core, (0, 0, 1, 0)),
        (far_core, (2, 0, 1, 0)),
        (near_z, (1, 0, 0, 0)),
        (far_z, (3, 0, 0, 0)),
        (near_z_core, (1, 0, 1, 0)),
        (far_z_core, (3, 0, 1, 0)),
        (near_x, (0, 1, 0, 0)),
        (far_x, (2, 1, 0, 0)),
        (near_x_core, (0, 1, 1, 0)),
        (far_x_core, (2, 1, 1, 0)),
        (near_zx, (1, 1, 0, 0)),
        (far_xz, (3, 1, 0, 0)),
        (near_zx_core, (1, 1, 1, 0)),
        (far_xz_core, (3, 1, 1, 0)),
    ):
        pieces.append(piece[None])
        plan.append((offset,))
    two_near, two_far, two_late, stats_three = operate(
        False, tuple(plan), pieces, cols, allowed, right, left_blocks, (diag, hd_far, psi, off_one, stats_one)
    )

    far_in = across(two_far, "blk", 2)
    near_in = across(two_near, "ops", 1)
    late_in = across(after(two_late, far_in), "blk", 2)
    far_in_x = across(far_in, "ops", 1)
    other_x = across(after(other, two_near), "ops", 1)
    late_in_x = across(late_in, "ops", 1)
    sums = stats_three + across(stats_three, "sub", 1)
    sums = sums + across(sums, "ops", 1)
    sums = sums + across(sums, "blk", 1)
    both = jnp.stack([sums, across(sums, "blk", 2)])
    both = jnp.sum(jnp.where(half == 0, both, both[::-1])[:, :5], axis=2)
    scale = both[:, 3:4] + 1e-06
    subspace = jnp.concatenate([both[:, 4:5], both[:, 0:3]], axis=1) / scale
    places = ((0, 0, 0), (0, 1, 0), (1, 0, 0), (1, 1, 0))
    correction = assemble(block, (near, near_x, other, other_x), places)
    places = ((0, 0, 0), (0, 1, 0), (1, 0, 0), (1, 0, 1), (1, 1, 0), (1, 1, 1))
    sigma_two = assemble(block, (two_near, near_in, far_in, late_in, far_in_x, late_in_x), places)
    return correction, sigma_two, subspace


def solution(mesh):
    in_specs = (
        P("groups", ("blk", "sub"), None),
        P(("groups", "blk", "sub"), None),
        P("groups", None),
        P(("groups", "ops"), None, None, None, None),
        P(("groups", "ops"), None, None),
        P(("groups", "ops"), None, None, None, None),
        P(("groups", "ops"), None, None),
    )
    out_specs = (
        P("groups", ("blk", "sub"), None),
        P("groups", ("blk", "sub"), None),
        P("groups", None),
    )
    body = shards if halves_fit(mesh) else general_shards
    return jax.shard_map(body, mesh=mesh, in_specs=in_specs, out_specs=out_specs, check_vma=False)
```

```python
import functools

import jax
import jax.numpy as jnp
from jax import lax
from jax.experimental import pallas as pl
from jax.experimental.pallas import tpu as pltpu
from jax.sharding import PartitionSpec as P

ANY = pl.BlockSpec(memory_space=pl.ANY)
SMEM = pl.BlockSpec(memory_space=pltpu.SMEM)
VMEM = pl.BlockSpec(memory_space=pltpu.VMEM)
VMEM_LIMIT = 56 * 1024 * 1024
LANES = 128


def apply_right(field_in, blocks, columns):
    roots_here, row_count, full_width = field_in.shape
    term_count, sectors, link_count = columns.shape
    block_size = full_width // sectors
    grouped = field_in.reshape(roots_here, row_count, sectors, block_size)
    picked = jnp.take(grouped, columns.reshape(-1), axis=2)
    picked = picked.reshape(roots_here, row_count, term_count, sectors, link_count, block_size)
    product = jnp.einsum("nrkbjq,kbjpq->knrbp", picked, blocks, preferred_element_type=jnp.float32)
    return product.reshape(term_count, roots_here, row_count, full_width).astype(jnp.bfloat16)


def take_rows(stacked, indices):
    return jnp.take(stacked, indices, axis=1)


def apply_left(arrived, blocks, columns):
    term_count, roots_here, full_width, col_count = arrived.shape
    sectors = columns.shape[1]
    link_count = columns.shape[2]
    block_size = full_width // sectors
    grouped = arrived.reshape(term_count, roots_here, sectors, block_size, col_count)
    picked = jax.vmap(take_rows)(grouped, columns.reshape(term_count, sectors * link_count))
    picked = picked.reshape(term_count, roots_here, sectors, link_count, block_size, col_count)
    product = jnp.einsum("kajpq,knajqc->napc", blocks, picked, preferred_element_type=jnp.float32)
    return product.reshape(roots_here, full_width, col_count)


def general_shards(theta, hdiag, pattern, left_blocks, left_cols, right_blocks, right_cols):
    roots_here, row_count, full_width = theta.shape
    sectors = pattern.shape[0]
    block_size = full_width // sectors
    first_row = lax.axis_index(("blk", "sub")) * row_count
    block_row = (first_row + jnp.arange(row_count, dtype=jnp.int32)) // block_size
    onehot = (block_row[:, None] == jnp.arange(sectors, dtype=jnp.int32)[None, :]).astype(
        jnp.float32
    )
    row_pattern = jnp.dot(onehot, pattern.astype(jnp.float32), preferred_element_type=jnp.float32)
    allowed = jnp.broadcast_to(row_pattern[:, :, None], (row_count, sectors, block_size))
    allowed = allowed.reshape(row_count, full_width).astype(jnp.bfloat16)
    diagonal = hdiag.astype(jnp.float32)
    peers = lax.axis_size("blk") * lax.axis_size("sub")

    def left_part(arrived):
        return apply_left(arrived, left_blocks, left_cols)

    def operate(field_in):
        images = apply_right(field_in, right_blocks, right_cols)
        partial_sum = left_part(
            lax.all_to_all(images, ("blk", "sub"), split_axis=3, concat_axis=2, tiled=True)
        )
        shares = lax.psum_scatter(partial_sum, "ops", scatter_dimension=2, tiled=True)
        returned = lax.all_to_all(
            shares.astype(jnp.bfloat16), ("blk", "sub"), split_axis=1, concat_axis=2, tiled=True
        )
        gathered = lax.all_gather(returned, "ops", axis=2, tiled=True)
        narrow = returned.shape[2] // peers
        gathered = gathered.reshape(roots_here, row_count, lax.axis_size("ops"), peers, narrow)
        offdiag = gathered.transpose(0, 1, 3, 2, 4).reshape(roots_here, row_count, full_width)
        offdiag = offdiag * allowed[None]
        return diagonal[None] * field_in.astype(jnp.float32) + offdiag.astype(jnp.float32)

    projected = theta * allowed[None]
    wave = projected.astype(jnp.float32)
    sigma_one = operate(projected)
    norm_sq, energy_sum = lax.psum(
        (jnp.sum(wave * wave, axis=(1, 2)), jnp.sum(wave * sigma_one, axis=(1, 2))), ("blk", "sub")
    )
    denominator = norm_sq + 1e-06
    energy = energy_sum / denominator
    shifted = diagonal[None] - energy[:, None, None]
    update = (sigma_one - energy[:, None, None] * wave) * shifted / (shifted * shifted + 1.0)
    correlation = lax.psum(jnp.sum(wave * update, axis=(1, 2)), ("blk", "sub"))
    factor = correlation / denominator
    orthogonal = update - factor[:, None, None] * wave
    length_sq = lax.psum(jnp.sum(orthogonal * orthogonal, axis=(1, 2)), ("blk", "sub"))
    correction = (orthogonal * jnp.sqrt(norm_sq / (length_sq + 1e-06))[:, None, None]).astype(
        jnp.bfloat16
    )
    sigma_two = operate(correction).astype(jnp.bfloat16)
    second = sigma_two.astype(jnp.float32)
    fixed = correction.astype(jnp.float32)
    cross_one, cross_two, cross_three = lax.psum(
        (
            jnp.sum(wave * second, axis=(1, 2)),
            jnp.sum(fixed * sigma_one, axis=(1, 2)),
            jnp.sum(fixed * second, axis=(1, 2)),
        ),
        ("blk", "sub"),
    )
    subspace = (
        jnp.stack([energy_sum, cross_one, cross_two, cross_three], axis=1) / denominator[:, None]
    )
    return (correction, sigma_two, subspace)


def halves_fit(mesh):
    sizes = dict(mesh.shape)
    return sizes["blk"] == 4 and sizes["ops"] == 2 and sizes["sub"] == 2


def across(value, axis, distance):
    size = lax.axis_size(axis)
    return lax.ppermute(value, axis, [(i, i ^ distance) for i in range(size)])


def share(stats):
    axes = ("blk", "ops")
    count = lax.axis_size("blk") * lax.axis_size("ops")
    pair = jnp.stack([stats, across(stats, "sub", 1)])
    found = [pair]
    for distance in (1, 2, 3):
        found.append(lax.ppermute(pair, axes, [(i, i ^ distance) for i in range(count)]))
    return found


def place():
    return lax.axis_index("blk"), lax.axis_index("ops"), lax.axis_index("sub")


def fold(value):
    rows, width = value.shape
    value = jnp.sum(value.reshape(rows // 8, 8, width), axis=0)
    return sum(value[:, at : at + LANES] for at in range(0, width, LANES))


def row_of(dz, dx, dc):
    z, x, c = place()
    return 4 * (z ^ dz) + 2 * (c ^ dc) + (x ^ dx if dx < 2 else dx - 2)


def operate_kernel(first, plan, cols, pattern, right_own, right_near, right_far, left_own, *refs):
    count = len(plan)
    pieces, refs = refs[:count], refs[count:]
    if first:
        weight_own, psi_out, off_out, stats_out = refs[:4]
        refs = refs[4:]
    else:
        hd_own, hd_far, psi_in, off_in, stats_in, near_out, far_out, late_out, stats_out = refs[:9]
        refs = refs[9:]
    field, images, right, left, diag, parts, sems = refs
    z, x, c = place()
    sectors, block, width = field.shape
    links = right.shape[2]
    mine = 4 * z + 2 * c + x
    rows = (mine, mine ^ 8)

    copies = []

    def begin(source, target):
        copy = pltpu.make_async_copy(source, target, sems.at[len(copies)])
        copy.start()
        copies.append(copy)

    part = sectors // 2
    near, far = pl.ds(c * part, part), pl.ds((1 - c) * part, part)
    begin(right_own.at[0], right.at[0])
    for piece, offsets in zip(pieces, plan):
        for at, (dz, dx, dc, start, tall) in enumerate(offsets):
            target = field.at[row_of(dz, dx, dc), pl.ds(start, tall)]
            begin(piece.at[at, pl.ds(0, tall)], target)
            if first and (dz, dx, dc, start) == (2, 0, 0, block - tall):
                begin(piece.at[at, pl.ds(tall, parts.shape[0]), pl.ds(0, parts.shape[1])], parts)
    begin(right_near.at[pl.ds(0, part)], right.at[1, near])
    begin(right_far, right.at[1, far])
    early = len(copies)
    for at in range(2):
        begin(left_own.at[0, rows[at]], left.at[0, at])
    begin(right_near.at[pl.ds(part, 2)], left.at[1])
    if not first:
        begin(hd_own.at[x], diag.at[0])
        begin(hd_far, diag.at[1])
    for copy in copies[:early]:
        copy.wait()

    table = sectors * links

    def right_col(term, b, j):
        return cols[(2 * term) * table + b * links + j]

    def left_col(term, a, j):
        return cols[(2 * term + 1) * table + a * links + j]

    def allowed(a, q, value):
        return jnp.where(pattern[a * sectors + q] != 0, value, jnp.zeros_like(value))

    sources = [[left_col(term, rows[at], j) for at in range(2) for j in range(links)] for term in range(2)]

    deep = links * block

    def image(b, carry):
        for term in range(2):
            found = [right_col(term, b, j) for j in range(links)]
            lhs = []
            for source in sources[term]:
                line = []
                for col in found:
                    value = field[source, :, pl.ds(pl.multiple_of(col * block, block), block)]
                    line.append(allowed(source, col, value) if first else value)
                lhs.append(jnp.concatenate(line, axis=1))
            rhs = [right[term, b, j] for j in range(links)]
            product = lax.dot_general(
                jnp.concatenate(lhs, axis=0),
                jnp.concatenate(rhs, axis=1),
                (((1,), (1,)), ((), ())),
                preferred_element_type=jnp.float32,
            )
            product = product.astype(jnp.bfloat16)
            span = pl.ds(pl.multiple_of(b * block, block), block)
            for at in range(2):
                images[at, term * deep : (term + 1) * deep, span] = product[at * deep : (at + 1) * deep]
        return carry

    lax.fori_loop(0, sectors, image, 0, unroll=2)
    for copy in copies[early:]:
        copy.wait()

    step = 2
    half = block // 2
    zero = jnp.zeros((8, LANES), jnp.float32)

    def column(n, sums):
        start = pl.multiple_of(n * step * block, step * block)
        span = pl.ds(start, step * block)
        sums = list(sums)

        def masked(a, value):
            parts = [
                allowed(a, n * step + i, value[:, i * block : (i + 1) * block]) for i in range(step)
            ]
            return jnp.concatenate(parts, axis=1)

        for at in range(2):
            weights = [left[term, at, j] for term in range(2) for j in range(links)]
            total = jnp.dot(
                jnp.concatenate(weights, axis=1),
                images[at, :, span],
                preferred_element_type=jnp.float32,
            )
            offdiag = masked(rows[at], total.astype(jnp.bfloat16).astype(jnp.float32))
            own = field[rows[at], :, span].astype(jnp.float32)
            if first:
                own = masked(rows[at], own)
                psi_out[at, :, span] = own.astype(jnp.bfloat16)
                off_out[at, :, span] = offdiag.astype(jnp.bfloat16)
                sums[0] += fold(own * own)
                sums[1] += fold(own * offdiag)
            else:
                weight = diag[at, :, span].astype(jnp.float32)
                narrow = (weight * own + offdiag).astype(jnp.bfloat16)
                if at == 0:
                    near_out[:, span] = narrow
                else:
                    far_out[:, span] = narrow[:half]
                    late_out[:, span] = narrow[half:]
                second = narrow.astype(jnp.float32)
                wave = psi_in[at, :, span].astype(jnp.float32)
                sigma_one = weight * wave + off_in[at, :, span].astype(jnp.float32)
                sums[0] += fold(wave * second)
                sums[1] += fold(own * sigma_one)
                sums[2] += fold(own * second)
        return tuple(sums)

    sums = list(lax.fori_loop(0, sectors // step, column, (zero,) * (2 if first else 3)))
    if first:
        far_weight = parts[...].astype(jnp.float32)[:8]
        sums[1] += weight_own[...] + sum(far_weight[:, i * LANES : (i + 1) * LANES] for i in range(3))
    stats_out[...] = jnp.zeros_like(stats_out)
    for at, value in enumerate(sums):
        stats_out[at : at + 1, :] = jnp.sum(value, axis=0, keepdims=True)
    if not first:
        stats_out[3:5, :] = stats_in[0:2, :]


def operate(first, plan, pieces, cols, pattern, right, left, extra):
    right_own, right_near, right_far = right
    _, sectors, links, block = right_own.shape[:4]
    width = sectors * block
    rows = jax.ShapeDtypeStruct((2, block, width), jnp.bfloat16)
    one = jax.ShapeDtypeStruct((block, width), jnp.bfloat16)
    some = jax.ShapeDtypeStruct((block // 2, width), jnp.bfloat16)
    stats = jax.ShapeDtypeStruct((8, LANES), jnp.float32)
    out_shape = (rows, rows, stats) if first else (one, some, some, stats)
    extra_specs = [VMEM] if first else [ANY, ANY, VMEM, VMEM, VMEM]
    copies = sum(len(offsets) for offsets in plan) + 9
    inner = 2 * 2 * sectors * 2 * links * links * block * block * block
    outer = 2 * 2 * 2 * links * block * block * width
    return pl.pallas_call(
        functools.partial(operate_kernel, first, plan),
        out_shape=out_shape,
        in_specs=[SMEM, SMEM] + [ANY] * (4 + len(pieces)) + extra_specs,
        out_specs=(VMEM,) * len(out_shape),
        scratch_shapes=[
            pltpu.VMEM((sectors, block, width), jnp.bfloat16),
            pltpu.VMEM((2, 2 * links * block, width), jnp.bfloat16),
            pltpu.VMEM((2, sectors, links, block, block), jnp.bfloat16),
            pltpu.VMEM((2, 2, links, block, block), jnp.bfloat16),
            pltpu.VMEM((2, block, width), jnp.bfloat16),
            pltpu.VMEM((16, 3 * LANES), jnp.bfloat16),
            pltpu.SemaphoreType.DMA((copies,)),
        ],
        compiler_params=pltpu.CompilerParams(vmem_limit_bytes=VMEM_LIMIT),
        cost_estimate=pl.CostEstimate(
            flops=inner + outer, bytes_accessed=16 * 1024 * 1024, transcendentals=0
        ),
        name="operate_first" if first else "operate_second",
    )(cols, pattern, right_own, right_near, right_far, left, *pieces, *extra)


def prepare_kernel(theta, right, left, first, own, packed, sems):
    z, x, c = place()
    half = z // 2
    mine = 4 * z + 2 * c + x
    part = right.shape[1] // 2
    tall = first.shape[0]
    copies = [
        pltpu.make_async_copy(theta.at[1 - half, x, pl.ds(0, tall)], first, sems.at[0]),
        pltpu.make_async_copy(theta.at[half], own, sems.at[1]),
        pltpu.make_async_copy(right.at[0, pl.ds(c * part, part)], packed.at[pl.ds(0, part)], sems.at[2]),
        pltpu.make_async_copy(left.at[0, mine ^ 1], packed.at[part], sems.at[3]),
        pltpu.make_async_copy(left.at[0, mine ^ 9], packed.at[part + 1], sems.at[4]),
    ]
    for copy in copies:
        copy.start()
    for copy in copies:
        copy.wait()


def prepare(tall, theta, right, left):
    _, _, block, width = theta.shape
    _, sectors, links = right.shape[:3]
    kind = jnp.bfloat16
    return pl.pallas_call(
        prepare_kernel,
        out_shape=(
            jax.ShapeDtypeStruct((tall, width), kind),
            jax.ShapeDtypeStruct((2, block, width), kind),
            jax.ShapeDtypeStruct((sectors // 2 + 2, links, block, block), kind),
        ),
        in_specs=[ANY] * 3,
        out_specs=(VMEM,) * 3,
        scratch_shapes=[pltpu.SemaphoreType.DMA((5,))],
        compiler_params=pltpu.CompilerParams(vmem_limit_bytes=VMEM_LIMIT),
        name="prepare",
    )(theta, right, left)


def weigh_kernel(pattern, theta, hd, own_out, second, waves, diag, sems):
    z, x, c = place()
    half = z // 2
    block, width = diag.shape
    rest = second.shape[0] - 16
    copies = [
        pltpu.make_async_copy(theta.at[half, x], waves.at[0], sems.at[0]),
        pltpu.make_async_copy(theta.at[1 - half, x], waves.at[1], sems.at[1]),
        pltpu.make_async_copy(hd.at[x], diag, sems.at[2]),
        pltpu.make_async_copy(
            theta.at[1 - half, x, pl.ds(block - rest, rest)], second.at[pl.ds(0, rest)], sems.at[3]
        ),
    ]
    for copy in copies:
        copy.start()
    for copy in copies:
        copy.wait()
    sectors = width // block
    mine = 4 * z + 2 * c + x
    zero = jnp.zeros((8, LANES), jnp.float32)

    def column(q, sums):
        span = pl.ds(pl.multiple_of(q * block, block), block)
        weight = diag[:, span].astype(jnp.float32)
        weight = jnp.where(pattern[mine * sectors + q] != 0, weight, jnp.zeros_like(weight))
        found = []
        for root in range(2):
            wave = waves[root, :, span].astype(jnp.float32)
            found.append(sums[root] + fold(weight * wave * wave))
        return tuple(found)

    near, far = lax.fori_loop(0, sectors, column, (zero, zero))
    own_out[...] = near
    left = jnp.concatenate([far, zero], axis=0)
    parts = []
    for _ in range(3):
        part = left.astype(jnp.bfloat16)
        parts.append(part)
        left = left - part.astype(jnp.float32)
    parts.append(jnp.zeros((16, width - 3 * LANES), jnp.bfloat16))
    second[rest:, :] = jnp.concatenate(parts, axis=1)


def weigh(rest, pattern, theta, hd):
    _, _, block, width = theta.shape
    return pl.pallas_call(
        weigh_kernel,
        out_shape=(
            jax.ShapeDtypeStruct((8, LANES), jnp.float32),
            jax.ShapeDtypeStruct((rest + 16, width), theta.dtype),
        ),
        in_specs=[SMEM, ANY, ANY],
        out_specs=(VMEM, VMEM),
        scratch_shapes=[
            pltpu.VMEM((2, block, width), theta.dtype),
            pltpu.VMEM((block, width), hd.dtype),
            pltpu.SemaphoreType.DMA((4,)),
        ],
        cost_estimate=pl.CostEstimate(flops=0, bytes_accessed=64 * 1024 * 1024, transcendentals=0),
        compiler_params=pltpu.CompilerParams(vmem_limit_bytes=VMEM_LIMIT),
        name="weigh",
    )(pattern, theta, hd)


def total_of(rows):
    return jnp.sum(rows, axis=1, keepdims=True)


def update_kernel(psi, off, hd_own, hd_far, *refs):
    stats, (t_out, stats_out, diag, sems) = refs[:4], refs[4:]
    z, x, c = place()
    copies = [
        pltpu.make_async_copy(hd_own.at[x], diag.at[0], sems.at[0]),
        pltpu.make_async_copy(hd_far, diag.at[1], sems.at[1]),
    ]
    for copy in copies:
        copy.start()
    whole = sum(ref[at, 0:2, :] for ref in stats for at in range(2))
    norm_sq, energy_sum = total_of(whole[0:1, :]), total_of(whole[1:2, :])
    energy = energy_sum / (norm_sq + 1e-06)
    mine = total_of(stats[0][0, 0:1, :])
    for copy in copies:
        copy.wait()
    _, block, width = psi.shape
    step = 16
    zero = jnp.zeros((8, LANES), jnp.float32)

    def chunk(n, total):
        span = pl.ds(pl.multiple_of(n * step, step), step)
        for at in range(2):
            wave = psi[at, span, :].astype(jnp.float32)
            weight = diag[at, span, :].astype(jnp.float32)
            sigma = weight * wave + off[at, span, :].astype(jnp.float32)
            shifted = weight - energy
            t = (sigma - energy * wave) * shifted / (shifted * shifted + 1.0)
            t_out[at, span, :] = t
            total = total + fold(wave * t)
        return total

    lanes = jnp.sum(lax.fori_loop(0, block // step, chunk, zero), axis=0, keepdims=True)
    correlation = total_of(lanes)
    local = jnp.where(mine > 0.0, correlation / jnp.where(mine > 0.0, mine, 1.0), 0.0)

    def within(n, total):
        span = pl.ds(pl.multiple_of(n * step, step), step)
        for at in range(2):
            rest = t_out[at, span, :] - local * psi[at, span, :].astype(jnp.float32)
            total = total + fold(rest * rest)
        return total

    spread = jnp.sum(lax.fori_loop(0, block // step, within, zero), axis=0, keepdims=True)
    stats_out[...] = jnp.zeros_like(stats_out)
    stats_out[0:1, :] = jnp.broadcast_to(correlation, (1, LANES))
    stats_out[1:2, :] = jnp.broadcast_to(total_of(spread), (1, LANES))
    stats_out[2:3, :] = jnp.broadcast_to(mine, (1, LANES))
    stats_out[3:4, :] = jnp.broadcast_to(local, (1, LANES))
    stats_out[4:5, :] = jnp.broadcast_to(norm_sq, (1, LANES))


def correct_kernel(psi, t, *refs):
    stats, outs = refs[:4], refs[4:]
    stats = [ref.at[at] for ref in stats for at in range(2)]
    norm_sq = stats[0][4:5, 0:1]
    factor = sum(ref[0:1, 0:1] for ref in stats) / (norm_sq + 1e-06)
    length_sq = jnp.zeros((1, 1), jnp.float32)
    for ref in stats:
        gap = factor - ref[3:4, 0:1]
        length_sq = length_sq + (ref[1:2, 0:1] + gap * gap * ref[2:3, 0:1])
    scale = jnp.sqrt(norm_sq / (length_sq + 1e-06))
    _, block, width = psi.shape
    step = 16

    def chunk(n, carry):
        span = pl.ds(pl.multiple_of(n * step, step), step)
        for at in range(2):
            wave = psi[at, span, :].astype(jnp.float32)
            outs[at][span, :] = ((t[at, span, :] - factor * wave) * scale).astype(jnp.bfloat16)
        return carry

    lax.fori_loop(0, block // step, chunk, 0)


def assemble_kernel(places, based, *refs):
    count = len(places)
    pieces, (out, sems) = refs[:count], refs[count + based :]
    z, x, c = place()
    half = z // 2
    copies = []
    for at, (root, flip, start) in enumerate(places):
        size = pieces[at].shape[0]
        target = out.at[half ^ root, x ^ flip, pl.ds(start, size)]
        copies.append(pltpu.make_async_copy(pieces[at], target, sems.at[at]))
    for copy in copies:
        copy.start()
    for copy in copies:
        copy.wait()


def assemble(block, pieces, places, base=None):
    width = pieces[0].shape[1]
    based = [] if base is None else [base]
    return pl.pallas_call(
        functools.partial(assemble_kernel, places, len(based)),
        out_shape=jax.ShapeDtypeStruct((2, 2, block, width), pieces[0].dtype),
        in_specs=[VMEM] * len(pieces) + [ANY] * len(based),
        out_specs=ANY,
        scratch_shapes=[pltpu.SemaphoreType.DMA((len(pieces),))],
        input_output_aliases={len(pieces): 0} if based else {},
        compiler_params=pltpu.CompilerParams(vmem_limit_bytes=VMEM_LIMIT),
        name="assemble",
    )(*pieces, *based)


def after(value, *others):
    return lax.optimization_barrier((value, *others))[0]


def shards(theta, hdiag, pattern, left_blocks, left_cols, right_blocks, right_cols):
    roots, row_count, width = theta.shape
    sectors = pattern.shape[0]
    block = width // sectors
    z, x, c = place()
    half = z // 2
    mine = 4 * z + 2 * c + x

    halves = theta.reshape(roots, 2, block, width)
    diag = hdiag.reshape(2, block, width)
    allowed = pattern.reshape(-1)
    tall = block * 5 // 8
    rest = block - tall

    first, own, packed = prepare(tall, halves, right_blocks, left_blocks)
    far_a = across(first, "blk", 2)
    near = across(own, "blk", 1)
    cols = jnp.concatenate([right_cols.reshape(-1), left_cols.reshape(-1)])
    cols_other = across(cols, "ops", 1)
    cols = jnp.concatenate([cols, cols_other])
    operators = across(packed, "ops", 1)
    own_core = across(own, "sub", 1)
    weight_own, second = weigh(rest, allowed, halves, diag)

    far_a, second = after((far_a, second), cols, own_core)
    far_b = across(after(second, far_a), "blk", 2)
    far_za = across(far_a, "blk", 1)
    far_xa = across(far_a, "ops", 1)

    far_zb = across(after(far_b, far_za), "blk", 1)
    far_zxa = across(after(far_za, far_b), "ops", 1)
    far_xb = across(far_b, "ops", 1)
    operators_core = across(after(operators, far_b)[: sectors // 2], "sub", 1)
    near_core = across(after(near, far_b), "sub", 1)
    core_a = across(jnp.stack([far_a, far_xa, far_za]), "sub", 1)

    far_zxb = across(after(far_zb, far_xb, far_zxa), "ops", 1)
    core_b = across(jnp.stack([far_b, far_xb, far_zb]), "sub", 1)
    far_zxa_core = across(far_zxa, "sub", 1)
    far_zxb_core = across(far_zxb, "sub", 1)
    hd_far = lax.dynamic_index_in_dim(diag, x, 0, keepdims=False)
    hd_far = across(after(hd_far, far_zb), "blk", 2)

    right = (right_blocks, operators, operators_core)
    pieces = []
    plan = []
    for piece, offsets in (
        (own, ((0, 2, 0), (0, 3, 0))),
        (own_core, ((0, 2, 1), (0, 3, 1))),
        (near, ((1, 2, 0), (1, 3, 0))),
        (near_core, ((1, 2, 1), (1, 3, 1))),
    ):
        pieces.append(piece)
        plan.append(tuple(offset + (0, block) for offset in offsets))
    for start, count, group in (
        (
            0,
            tall,
            (
                (far_a, ((2, 0, 0),)),
                (far_xa, ((2, 1, 0),)),
                (far_za, ((3, 0, 0),)),
                (far_zxa, ((3, 1, 0),)),
                (core_a, ((2, 0, 1), (2, 1, 1), (3, 0, 1))),
                (far_zxa_core, ((3, 1, 1),)),
            ),
        ),
        (
            tall,
            rest,
            (
                (far_b, ((2, 0, 0),)),
                (far_xb, ((2, 1, 0),)),
                (far_zb, ((3, 0, 0),)),
                (far_zxb, ((3, 1, 0),)),
                (core_b, ((2, 0, 1), (2, 1, 1), (3, 0, 1))),
                (far_zxb_core, ((3, 1, 1),)),
            ),
        ),
    ):
        for piece, offsets in group:
            pieces.append(piece if piece.ndim == 3 else piece[None])
            plan.append(tuple(offset + (start, count) for offset in offsets))
    psi, off_one, stats_one = operate(
        True, tuple(plan), pieces, cols, allowed, right, left_blocks, (weight_own,)
    )

    found = share(stats_one)
    t, stats_two = pl.pallas_call(
        update_kernel,
        out_shape=(
            jax.ShapeDtypeStruct((2, block, width), jnp.float32),
            jax.ShapeDtypeStruct((8, LANES), jnp.float32),
        ),
        in_specs=[VMEM, VMEM, ANY, ANY] + [VMEM] * 4,
        out_specs=(VMEM, VMEM),
        scratch_shapes=[
            pltpu.VMEM((2, block, width), jnp.bfloat16),
            pltpu.SemaphoreType.DMA((2,)),
        ],
        compiler_params=pltpu.CompilerParams(vmem_limit_bytes=VMEM_LIMIT),
        name="update",
    )(psi, off_one, diag, hd_far, *found)
    found = share(stats_two)
    one = jax.ShapeDtypeStruct((block, width), jnp.bfloat16)
    changed_near, changed_far = pl.pallas_call(
        correct_kernel,
        out_shape=(one, one),
        in_specs=[VMEM, VMEM] + [VMEM] * 4,
        out_specs=(VMEM, VMEM),
        compiler_params=pltpu.CompilerParams(vmem_limit_bytes=VMEM_LIMIT),
        name="correct",
    )(psi, t, *found)

    near_z = across(changed_near, "blk", 1)
    far_x = across(changed_far, "ops", 1)
    near_core = across(changed_near, "sub", 1)
    far_core = across(changed_far, "sub", 1)
    near_zx = across(after(near_z, far_x), "ops", 1)
    far_xz = across(after(far_x, near_z), "blk", 1)
    near_x = across(after(changed_near, near_z, far_x), "ops", 1)
    far_z = across(after(changed_far, near_z, far_x), "blk", 1)
    near_z_core = across(near_z, "sub", 1)
    far_x_core = across(far_x, "sub", 1)
    near_x_core = across(near_x, "sub", 1)
    far_z_core = across(far_z, "sub", 1)
    near_zx_core = across(near_zx, "sub", 1)
    far_xz_core = across(far_xz, "sub", 1)
    other = across(after(changed_far, near_z, far_x), "blk", 2)
    pieces, plan = [], []
    for piece, offset in (
        (changed_near, (0, 0, 0)),
        (changed_far, (2, 0, 0)),
        (near_core, (0, 0, 1)),
        (far_core, (2, 0, 1)),
        (near_z, (1, 0, 0)),
        (far_z, (3, 0, 0)),
        (near_z_core, (1, 0, 1)),
        (far_z_core, (3, 0, 1)),
        (near_x, (0, 1, 0)),
        (far_x, (2, 1, 0)),
        (near_x_core, (0, 1, 1)),
        (far_x_core, (2, 1, 1)),
        (near_zx, (1, 1, 0)),
        (far_xz, (3, 1, 0)),
        (near_zx_core, (1, 1, 1)),
        (far_xz_core, (3, 1, 1)),
    ):
        pieces.append(piece[None])
        plan.append((offset + (0, block),))
    two_near, two_far, two_late, stats_three = operate(
        False, tuple(plan), pieces, cols, allowed, right, left_blocks, (diag, hd_far, psi, off_one, stats_one)
    )

    far_in = across(two_far, "blk", 2)
    near_in = across(two_near, "ops", 1)
    late_in = across(after(two_late, far_in, near_in), "blk", 2)
    far_in_x = across(after(far_in, near_in), "ops", 1)
    other_x = across(after(other, near_in), "ops", 1)
    late_in_x = across(after(late_in, other_x, far_in_x), "ops", 1)
    sums = stats_three + across(stats_three, "sub", 1)
    sums = sums + across(sums, "blk", 1)
    both = jnp.stack([sums, across(sums, "blk", 2)])
    both = both + across(after(both, near_in), "ops", 1)
    both = jnp.sum(jnp.where(half == 0, both, both[::-1])[:, :5], axis=2)
    scale = both[:, 3:4] + 1e-06
    subspace = jnp.concatenate([both[:, 4:5], both[:, 0:3]], axis=1) / scale
    places = ((0, 0, 0), (0, 1, 0), (1, 0, 0), (1, 1, 0))
    correction = assemble(block, (changed_near, near_x, other, other_x), places)
    places = ((0, 0, 0), (0, 1, 0), (1, 0, 0), (1, 0, block // 2), (1, 1, 0))
    sigma_two = assemble(block, (two_near, near_in, far_in, late_in, far_in_x), places)
    sigma_two = assemble(block, (late_in_x,), ((1, 1, block // 2),), sigma_two)
    return correction.reshape(theta.shape), sigma_two.reshape(theta.shape), subspace


def solution(mesh):
    in_specs = (
        P("groups", ("blk", "sub"), None),
        P(("groups", "blk", "sub"), None),
        P("groups", None),
        P(("groups", "ops"), None, None, None, None),
        P(("groups", "ops"), None, None),
        P(("groups", "ops"), None, None, None, None),
        P(("groups", "ops"), None, None),
    )
    out_specs = (
        P("groups", ("blk", "sub"), None),
        P("groups", ("blk", "sub"), None),
        P("groups", None),
    )
    body = shards if halves_fit(mesh) else general_shards
    return jax.shard_map(body, mesh=mesh, in_specs=in_specs, out_specs=out_specs, check_vma=False)
```

```python
import functools

import jax
import jax.numpy as jnp
from jax import lax
from jax.experimental import pallas as pl
from jax.experimental.pallas import tpu as pltpu
from jax.sharding import PartitionSpec as P

ANY = pl.BlockSpec(memory_space=pl.ANY)
SMEM = pl.BlockSpec(memory_space=pltpu.SMEM)
VMEM = pl.BlockSpec(memory_space=pltpu.VMEM)
VMEM_LIMIT = 56 * 1024 * 1024
LANES = 128


def apply_right(field_in, blocks, columns):
    roots_here, row_count, full_width = field_in.shape
    term_count, sectors, link_count = columns.shape
    block_size = full_width // sectors
    grouped = field_in.reshape(roots_here, row_count, sectors, block_size)
    picked = jnp.take(grouped, columns.reshape(-1), axis=2)
    picked = picked.reshape(roots_here, row_count, term_count, sectors, link_count, block_size)
    product = jnp.einsum("nrkbjq,kbjpq->knrbp", picked, blocks, preferred_element_type=jnp.float32)
    return product.reshape(term_count, roots_here, row_count, full_width).astype(jnp.bfloat16)


def take_rows(stacked, indices):
    return jnp.take(stacked, indices, axis=1)


def apply_left(arrived, blocks, columns):
    term_count, roots_here, full_width, col_count = arrived.shape
    sectors = columns.shape[1]
    link_count = columns.shape[2]
    block_size = full_width // sectors
    grouped = arrived.reshape(term_count, roots_here, sectors, block_size, col_count)
    picked = jax.vmap(take_rows)(grouped, columns.reshape(term_count, sectors * link_count))
    picked = picked.reshape(term_count, roots_here, sectors, link_count, block_size, col_count)
    product = jnp.einsum("kajpq,knajqc->napc", blocks, picked, preferred_element_type=jnp.float32)
    return product.reshape(roots_here, full_width, col_count)


def general_shards(theta, hdiag, pattern, left_blocks, left_cols, right_blocks, right_cols):
    roots_here, row_count, full_width = theta.shape
    sectors = pattern.shape[0]
    block_size = full_width // sectors
    first_row = lax.axis_index(("blk", "sub")) * row_count
    block_row = (first_row + jnp.arange(row_count, dtype=jnp.int32)) // block_size
    onehot = (block_row[:, None] == jnp.arange(sectors, dtype=jnp.int32)[None, :]).astype(
        jnp.float32
    )
    row_pattern = jnp.dot(onehot, pattern.astype(jnp.float32), preferred_element_type=jnp.float32)
    allowed = jnp.broadcast_to(row_pattern[:, :, None], (row_count, sectors, block_size))
    allowed = allowed.reshape(row_count, full_width).astype(jnp.bfloat16)
    diagonal = hdiag.astype(jnp.float32)
    peers = lax.axis_size("blk") * lax.axis_size("sub")

    def left_part(arrived):
        return apply_left(arrived, left_blocks, left_cols)

    def operate(field_in):
        images = apply_right(field_in, right_blocks, right_cols)
        partial_sum = left_part(
            lax.all_to_all(images, ("blk", "sub"), split_axis=3, concat_axis=2, tiled=True)
        )
        shares = lax.psum_scatter(partial_sum, "ops", scatter_dimension=2, tiled=True)
        returned = lax.all_to_all(
            shares.astype(jnp.bfloat16), ("blk", "sub"), split_axis=1, concat_axis=2, tiled=True
        )
        gathered = lax.all_gather(returned, "ops", axis=2, tiled=True)
        narrow = returned.shape[2] // peers
        gathered = gathered.reshape(roots_here, row_count, lax.axis_size("ops"), peers, narrow)
        offdiag = gathered.transpose(0, 1, 3, 2, 4).reshape(roots_here, row_count, full_width)
        offdiag = offdiag * allowed[None]
        return diagonal[None] * field_in.astype(jnp.float32) + offdiag.astype(jnp.float32)

    projected = theta * allowed[None]
    wave = projected.astype(jnp.float32)
    sigma_one = operate(projected)
    norm_sq, energy_sum = lax.psum(
        (jnp.sum(wave * wave, axis=(1, 2)), jnp.sum(wave * sigma_one, axis=(1, 2))), ("blk", "sub")
    )
    denominator = norm_sq + 1e-06
    energy = energy_sum / denominator
    shifted = diagonal[None] - energy[:, None, None]
    update = (sigma_one - energy[:, None, None] * wave) * shifted / (shifted * shifted + 1.0)
    correlation = lax.psum(jnp.sum(wave * update, axis=(1, 2)), ("blk", "sub"))
    factor = correlation / denominator
    orthogonal = update - factor[:, None, None] * wave
    length_sq = lax.psum(jnp.sum(orthogonal * orthogonal, axis=(1, 2)), ("blk", "sub"))
    correction = (orthogonal * jnp.sqrt(norm_sq / (length_sq + 1e-06))[:, None, None]).astype(
        jnp.bfloat16
    )
    sigma_two = operate(correction).astype(jnp.bfloat16)
    second = sigma_two.astype(jnp.float32)
    fixed = correction.astype(jnp.float32)
    cross_one, cross_two, cross_three = lax.psum(
        (
            jnp.sum(wave * second, axis=(1, 2)),
            jnp.sum(fixed * sigma_one, axis=(1, 2)),
            jnp.sum(fixed * second, axis=(1, 2)),
        ),
        ("blk", "sub"),
    )
    subspace = (
        jnp.stack([energy_sum, cross_one, cross_two, cross_three], axis=1) / denominator[:, None]
    )
    return (correction, sigma_two, subspace)


def halves_fit(mesh):
    sizes = dict(mesh.shape)
    return sizes["blk"] == 4 and sizes["ops"] == 2 and sizes["sub"] == 2


def across(value, axis, distance):
    size = lax.axis_size(axis)
    return lax.ppermute(value, axis, [(i, i ^ distance) for i in range(size)])


def share(stats):
    axes = ("blk", "ops")
    count = lax.axis_size("blk") * lax.axis_size("ops")
    pair = jnp.stack([stats, across(stats, "sub", 1)])
    found = [pair]
    for distance in (1, 2, 3):
        found.append(lax.ppermute(pair, axes, [(i, i ^ distance) for i in range(count)]))
    return found


def place():
    return lax.axis_index("blk"), lax.axis_index("ops"), lax.axis_index("sub")


def fold(value):
    rows, width = value.shape
    value = jnp.sum(value.reshape(rows // 8, 8, width), axis=0)
    return sum(value[:, at : at + LANES] for at in range(0, width, LANES))


def row_of(dz, dx, dc):
    z, x, c = place()
    return 4 * (z ^ dz) + 2 * (c ^ dc) + (x ^ dx if dx < 2 else dx - 2)


def operate_kernel(first, plan, cols, pattern, right_own, right_near, right_far, left_own, *refs):
    count = len(plan)
    pieces, refs = refs[:count], refs[count:]
    if first:
        weight_own, psi_out, off_out, stats_out = refs[:4]
        refs = refs[4:]
    else:
        hd_own, hd_far, psi_in, off_in, stats_in, near_out, far_out, late_out, stats_out = refs[:9]
        refs = refs[9:]
    field, images, right, left, diag, parts, sems = refs
    z, x, c = place()
    sectors, block, width = field.shape
    table = right.shape[1]
    links = table // sectors
    mine = 4 * z + 2 * c + x
    rows = (mine, mine ^ 8)

    copies = []

    def begin(source, target):
        copy = pltpu.make_async_copy(source, target, sems.at[len(copies)])
        copy.start()
        copies.append(copy)

    part = table // 2
    near, far = pl.ds(c * part, part), pl.ds((1 - c) * part, part)
    begin(right_own, right.at[0])
    for piece, offsets in zip(pieces, plan):
        for at, (dz, dx, dc, start, tall) in enumerate(offsets):
            target = field.at[row_of(dz, dx, dc), pl.ds(start, tall)]
            begin(piece.at[at, pl.ds(0, tall)], target)
            if first and (dz, dx, dc, start) == (2, 0, 0, block - tall):
                begin(piece.at[at, pl.ds(tall, parts.shape[0]), pl.ds(0, parts.shape[1])], parts)
    begin(right_near.at[pl.ds(0, part)], right.at[1, near])
    begin(right_far, right.at[1, far])
    early = len(copies)
    for at in range(2):
        begin(left_own.at[pl.ds(rows[at] * links, links)], left.at[0, pl.ds(at * links, links)])
    begin(right_near.at[pl.ds(part, 2 * links)], left.at[1])
    if not first:
        begin(hd_own.at[x], diag.at[0])
        begin(hd_far, diag.at[1])
    for copy in copies[:early]:
        copy.wait()

    def right_col(term, b, j):
        return cols[(2 * term) * table + b * links + j]

    def left_col(term, a, j):
        return cols[(2 * term + 1) * table + a * links + j]

    def allowed(a, q, value):
        return jnp.where(pattern[a * sectors + q] != 0, value, jnp.zeros_like(value))

    sources = [[left_col(term, rows[at], j) for at in range(2) for j in range(links)] for term in range(2)]

    deep = links * block

    def image(b, carry):
        for term in range(2):
            found = [right_col(term, b, j) for j in range(links)]
            lhs = []
            for source in sources[term]:
                line = []
                for col in found:
                    value = field[source, :, pl.ds(pl.multiple_of(col * block, block), block)]
                    line.append(allowed(source, col, value) if first else value)
                lhs.append(jnp.concatenate(line, axis=1))
            rhs = [right[term, b * links + j] for j in range(links)]
            product = lax.dot_general(
                jnp.concatenate(lhs, axis=0),
                jnp.concatenate(rhs, axis=1),
                (((1,), (1,)), ((), ())),
                preferred_element_type=jnp.float32,
            )
            product = product.astype(jnp.bfloat16)
            span = pl.ds(pl.multiple_of(b * block, block), block)
            for at in range(2):
                images[at, term * deep : (term + 1) * deep, span] = product[at * deep : (at + 1) * deep]
        return carry

    lax.fori_loop(0, sectors, image, 0, unroll=2)
    for copy in copies[early:]:
        copy.wait()

    step = 2
    half = block // 2
    zero = jnp.zeros((8, LANES), jnp.float32)

    def column(n, sums):
        start = pl.multiple_of(n * step * block, step * block)
        span = pl.ds(start, step * block)
        sums = list(sums)

        def masked(a, value):
            parts = [
                allowed(a, n * step + i, value[:, i * block : (i + 1) * block]) for i in range(step)
            ]
            return jnp.concatenate(parts, axis=1)

        for at in range(2):
            weights = [left[term, at * links + j] for term in range(2) for j in range(links)]
            total = jnp.dot(
                jnp.concatenate(weights, axis=1),
                images[at, :, span],
                preferred_element_type=jnp.float32,
            )
            offdiag = masked(rows[at], total.astype(jnp.bfloat16).astype(jnp.float32))
            own = field[rows[at], :, span].astype(jnp.float32)
            if first:
                own = masked(rows[at], own)
                psi_out[at, :, span] = own.astype(jnp.bfloat16)
                off_out[at, :, span] = offdiag.astype(jnp.bfloat16)
                sums[0] += fold(own * own)
                sums[1] += fold(own * offdiag)
            else:
                weight = diag[at, :, span].astype(jnp.float32)
                narrow = (weight * own + offdiag).astype(jnp.bfloat16)
                if at == 0:
                    near_out[:, span] = narrow
                else:
                    far_out[:, span] = narrow[:half]
                    late_out[:, span] = narrow[half:]
                second = narrow.astype(jnp.float32)
                wave = psi_in[at, :, span].astype(jnp.float32)
                sigma_one = weight * wave + off_in[at, :, span].astype(jnp.float32)
                sums[0] += fold(wave * second)
                sums[1] += fold(own * sigma_one)
                sums[2] += fold(own * second)
        return tuple(sums)

    sums = list(lax.fori_loop(0, sectors // step, column, (zero,) * (2 if first else 3)))
    if first:
        far_weight = parts[...].astype(jnp.float32)[:8]
        sums[1] += weight_own[...] + sum(far_weight[:, i * LANES : (i + 1) * LANES] for i in range(3))
    stats_out[...] = jnp.zeros_like(stats_out)
    for at, value in enumerate(sums):
        stats_out[at : at + 1, :] = jnp.sum(value, axis=0, keepdims=True)
    if not first:
        stats_out[3:5, :] = stats_in[0:2, :]


def operate(first, plan, pieces, cols, pattern, right, left, extra):
    right_own, right_near, right_far = right
    table, block, _ = right_own.shape
    width = pieces[0].shape[2]
    sectors = width // block
    links = table // sectors
    rows = jax.ShapeDtypeStruct((2, block, width), jnp.bfloat16)
    one = jax.ShapeDtypeStruct((block, width), jnp.bfloat16)
    some = jax.ShapeDtypeStruct((block // 2, width), jnp.bfloat16)
    stats = jax.ShapeDtypeStruct((8, LANES), jnp.float32)
    out_shape = (rows, rows, stats) if first else (one, some, some, stats)
    extra_specs = [VMEM] if first else [ANY, ANY, VMEM, VMEM, VMEM]
    copies = sum(len(offsets) for offsets in plan) + 9
    inner = 2 * 2 * sectors * 2 * links * links * block * block * block
    outer = 2 * 2 * 2 * links * block * block * width
    return pl.pallas_call(
        functools.partial(operate_kernel, first, plan),
        out_shape=out_shape,
        in_specs=[SMEM, SMEM] + [ANY] * (4 + len(pieces)) + extra_specs,
        out_specs=(VMEM,) * len(out_shape),
        scratch_shapes=[
            pltpu.VMEM((sectors, block, width), jnp.bfloat16),
            pltpu.VMEM((2, 2 * links * block, width), jnp.bfloat16),
            pltpu.VMEM((2, table, block, block), jnp.bfloat16),
            pltpu.VMEM((2, 2 * links, block, block), jnp.bfloat16),
            pltpu.VMEM((2, block, width), jnp.bfloat16),
            pltpu.VMEM((16, 3 * LANES), jnp.bfloat16),
            pltpu.SemaphoreType.DMA((copies,)),
        ],
        compiler_params=pltpu.CompilerParams(vmem_limit_bytes=VMEM_LIMIT),
        cost_estimate=pl.CostEstimate(
            flops=inner + outer if first else 0,
            bytes_accessed=16 * 1024 * 1024 if first else 1024,
            transcendentals=0,
        ),
        name="operate_first" if first else "operate_second",
    )(cols, pattern, right_own, right_near, right_far, left, *pieces, *extra)


def prepare_kernel(theta, right, left, cols, after_this, own_a, own_b, packed, sems):
    z, x, c = place()
    half = z // 2
    mine = 4 * z + 2 * c + x
    block, width = own_a.shape
    links = right.shape[0] * block // width
    part = right.shape[0] // 2
    sources = (
        (theta.at[half, 0], own_a),
        (theta.at[half, 1], own_b),
        (right.at[pl.ds(c * part, part)], packed.at[pl.ds(0, part)]),
        (left.at[pl.ds((mine ^ 1) * links, links)], packed.at[pl.ds(part, links)]),
        (left.at[pl.ds((mine ^ 9) * links, links)], packed.at[pl.ds(part + links, links)]),
    )
    copies = [
        pltpu.make_async_copy(source, target, sems.at[at])
        for at, (source, target) in enumerate(sources)
    ]
    for copy in copies:
        copy.start()
    last = part + 2 * links
    packed[last] = jnp.zeros_like(packed[last])
    packed[last, 0 : cols.shape[0], :] = cols[...]
    for copy in copies:
        copy.wait()


def prepare(theta, right, left, cols, after_this):
    _, _, block, width = theta.shape
    table = right.shape[0]
    links = table * block // width
    one = jax.ShapeDtypeStruct((block, width), jnp.bfloat16)
    packed = jax.ShapeDtypeStruct((table // 2 + 2 * links + 1, block, block), jnp.bfloat16)
    return pl.pallas_call(
        prepare_kernel,
        out_shape=(one, one, packed),
        in_specs=[ANY, ANY, ANY, VMEM, ANY],
        out_specs=(VMEM,) * 3,
        scratch_shapes=[pltpu.SemaphoreType.DMA((5,))],
        cost_estimate=pl.CostEstimate(flops=0, bytes_accessed=64 * 1024 * 1024, transcendentals=0),
        compiler_params=pltpu.CompilerParams(vmem_limit_bytes=VMEM_LIMIT),
        name="prepare",
    )(theta, right, left, cols, after_this)


def weigh_kernel(pattern, theta, hd, own_out, second, waves, diag, sems):
    z, x, c = place()
    half = z // 2
    block, width = diag.shape
    rest = second.shape[0] - 16
    copies = [
        pltpu.make_async_copy(theta.at[half, x], waves.at[0], sems.at[0]),
        pltpu.make_async_copy(theta.at[1 - half, x], waves.at[1], sems.at[1]),
        pltpu.make_async_copy(hd.at[x], diag, sems.at[2]),
        pltpu.make_async_copy(
            theta.at[1 - half, x, pl.ds(block - rest, rest)], second.at[pl.ds(0, rest)], sems.at[3]
        ),
    ]
    for copy in copies:
        copy.start()
    for copy in copies:
        copy.wait()
    sectors = width // block
    mine = 4 * z + 2 * c + x
    zero = jnp.zeros((8, LANES), jnp.float32)

    def column(q, sums):
        span = pl.ds(pl.multiple_of(q * block, block), block)
        weight = diag[:, span].astype(jnp.float32)
        weight = jnp.where(pattern[mine * sectors + q] != 0, weight, jnp.zeros_like(weight))
        found = []
        for root in range(2):
            wave = waves[root, :, span].astype(jnp.float32)
            found.append(sums[root] + fold(weight * wave * wave))
        return tuple(found)

    near, far = lax.fori_loop(0, sectors, column, (zero, zero))
    own_out[...] = near
    left = jnp.concatenate([far, zero], axis=0)
    parts = []
    for _ in range(3):
        part = left.astype(jnp.bfloat16)
        parts.append(part)
        left = left - part.astype(jnp.float32)
    parts.append(jnp.zeros((16, width - 3 * LANES), jnp.bfloat16))
    second[rest:, :] = jnp.concatenate(parts, axis=1)


def weigh(rest, pattern, theta, hd):
    _, _, block, width = theta.shape
    return pl.pallas_call(
        weigh_kernel,
        out_shape=(
            jax.ShapeDtypeStruct((8, LANES), jnp.float32),
            jax.ShapeDtypeStruct((rest + 16, width), theta.dtype),
        ),
        in_specs=[SMEM, ANY, ANY],
        out_specs=(VMEM, VMEM),
        scratch_shapes=[
            pltpu.VMEM((2, block, width), theta.dtype),
            pltpu.VMEM((block, width), hd.dtype),
            pltpu.SemaphoreType.DMA((4,)),
        ],
        compiler_params=pltpu.CompilerParams(vmem_limit_bytes=VMEM_LIMIT),
        name="weigh",
    )(pattern, theta, hd)


def total_of(rows):
    return jnp.sum(rows, axis=1, keepdims=True)


def update_kernel(psi, off, hd_own, hd_far, *refs):
    stats, (t_out, stats_out, diag, sems) = refs[:4], refs[4:]
    z, x, c = place()
    copies = [
        pltpu.make_async_copy(hd_own.at[x], diag.at[0], sems.at[0]),
        pltpu.make_async_copy(hd_far, diag.at[1], sems.at[1]),
    ]
    for copy in copies:
        copy.start()
    whole = sum(ref[at, 0:2, :] for ref in stats for at in range(2))
    norm_sq, energy_sum = total_of(whole[0:1, :]), total_of(whole[1:2, :])
    energy = energy_sum / (norm_sq + 1e-06)
    mine = total_of(stats[0][0, 0:1, :])
    for copy in copies:
        copy.wait()
    _, block, width = psi.shape
    step = 16
    zero = jnp.zeros((8, LANES), jnp.float32)

    def chunk(n, total):
        span = pl.ds(pl.multiple_of(n * step, step), step)
        for at in range(2):
            wave = psi[at, span, :].astype(jnp.float32)
            weight = diag[at, span, :].astype(jnp.float32)
            sigma = weight * wave + off[at, span, :].astype(jnp.float32)
            shifted = weight - energy
            t = (sigma - energy * wave) * shifted / (shifted * shifted + 1.0)
            t_out[at, span, :] = t
            total = total + fold(wave * t)
        return total

    lanes = jnp.sum(lax.fori_loop(0, block // step, chunk, zero), axis=0, keepdims=True)
    correlation = total_of(lanes)
    local = jnp.where(mine > 0.0, correlation / jnp.where(mine > 0.0, mine, 1.0), 0.0)

    def within(n, total):
        span = pl.ds(pl.multiple_of(n * step, step), step)
        for at in range(2):
            rest = t_out[at, span, :] - local * psi[at, span, :].astype(jnp.float32)
            total = total + fold(rest * rest)
        return total

    spread = jnp.sum(lax.fori_loop(0, block // step, within, zero), axis=0, keepdims=True)
    stats_out[...] = jnp.zeros_like(stats_out)
    stats_out[0:1, :] = jnp.broadcast_to(correlation, (1, LANES))
    stats_out[1:2, :] = jnp.broadcast_to(total_of(spread), (1, LANES))
    stats_out[2:3, :] = jnp.broadcast_to(mine, (1, LANES))
    stats_out[3:4, :] = jnp.broadcast_to(local, (1, LANES))
    stats_out[4:5, :] = jnp.broadcast_to(norm_sq, (1, LANES))


def correct_kernel(psi, t, found, *outs):
    z, x, c = place()
    stats = [found.at[8 * (z // 2) + at] for at in range(8)]
    norm_sq = stats[0][4:5, 0:1]
    factor = sum(ref[0:1, 0:1] for ref in stats) / (norm_sq + 1e-06)
    length_sq = jnp.zeros((1, 1), jnp.float32)
    for ref in stats:
        gap = factor - ref[3:4, 0:1]
        length_sq = length_sq + (ref[1:2, 0:1] + gap * gap * ref[2:3, 0:1])
    scale = jnp.sqrt(norm_sq / (length_sq + 1e-06))
    _, block, width = psi.shape
    step = 16

    def chunk(n, carry):
        span = pl.ds(pl.multiple_of(n * step, step), step)
        for at in range(2):
            wave = psi[at, span, :].astype(jnp.float32)
            outs[at][span, :] = ((t[at, span, :] - factor * wave) * scale).astype(jnp.bfloat16)
        return carry

    lax.fori_loop(0, block // step, chunk, 0)


def assemble_kernel(places, based, *refs):
    count = len(places)
    pieces, (out, sems) = refs[:count], refs[count + based :]
    z, x, c = place()
    half = z // 2
    copies = []
    for at, (root, flip, start) in enumerate(places):
        size = pieces[at].shape[0]
        target = out.at[half ^ root, x ^ flip, pl.ds(start, size)]
        copies.append(pltpu.make_async_copy(pieces[at], target, sems.at[at]))
    for copy in copies:
        copy.start()
    for copy in copies:
        copy.wait()


def assemble(block, pieces, places, base=None):
    width = pieces[0].shape[1]
    based = [] if base is None else [base]
    return pl.pallas_call(
        functools.partial(assemble_kernel, places, len(based)),
        out_shape=jax.ShapeDtypeStruct((2, 2, block, width), pieces[0].dtype),
        in_specs=[VMEM] * len(pieces) + [ANY] * len(based),
        out_specs=ANY,
        scratch_shapes=[pltpu.SemaphoreType.DMA((len(pieces),))],
        input_output_aliases={len(pieces): 0} if based else {},
        compiler_params=pltpu.CompilerParams(vmem_limit_bytes=VMEM_LIMIT),
        name="assemble",
    )(*pieces, *based)


def after(value, *others):
    return lax.optimization_barrier((value, *others))[0]


def shards(theta, hdiag, pattern, left_blocks, left_cols, right_blocks, right_cols):
    roots, row_count, width = theta.shape
    sectors = pattern.shape[0]
    block = width // sectors
    z, x, c = place()
    half = z // 2
    mine = 4 * z + 2 * c + x

    halves = theta.reshape(roots, 2, block, width)
    diag = hdiag.reshape(2, block, width)
    allowed = pattern.reshape(-1)
    tall = block * 5 // 8
    rest = block - tall

    right = right_blocks.reshape(-1, block, block)
    left = left_blocks.reshape(-1, block, block)
    table = right.shape[0]
    cols = jnp.concatenate([right_cols.reshape(-1), left_cols.reshape(-1)])

    first = lax.dynamic_slice(halves, (1 - half, x, 0, 0), (1, 1, tall, width))[0, 0]
    far_a = across(first, "blk", 2)
    weight_own, second = weigh(rest, allowed, halves, diag)
    far_b = across(second, "blk", 2)
    spots = jnp.pad(cols, (0, 16 * LANES - cols.shape[0])).reshape(16, LANES).astype(jnp.bfloat16)
    own_a, own_b, packed = prepare(halves, right, left, spots, weight_own)
    operators = across(packed, "ops", 1)
    own_core_a = across(own_a, "sub", 1)
    own_core_b = across(own_b, "sub", 1)

    far_a = after(far_a, own_core_a, own_core_b)
    far_za = across(far_a, "blk", 1)
    far_xa = across(far_a, "ops", 1)

    far_zb = across(far_b, "blk", 1)
    far_xb = across(far_b, "ops", 1)
    far_zxa = across(far_za, "ops", 1)
    near_a = across(after(own_a, far_za, far_b), "blk", 1)
    near_b = across(after(own_b, far_za, far_b), "blk", 1)
    operators_core = across(after(operators, far_b)[: table // 2], "sub", 1)
    found = operators[-1].reshape(-1)[: cols.shape[0]].astype(jnp.int32)
    cols = jnp.concatenate([cols, found])

    far_zxb = across(after(far_zb, far_za), "ops", 1)
    hd_far = lax.dynamic_index_in_dim(diag, x, 0, keepdims=False)
    hd_far = across(after(hd_far, far_zb), "blk", 2)
    core_a = across(jnp.stack([far_a, far_xa, far_za, far_zxa]), "sub", 1)
    near_a_core = across(near_a, "sub", 1)
    core_b = across(jnp.stack([far_b, far_xb, far_zb, far_zxb]), "sub", 1)
    near_b_core = across(near_b, "sub", 1)

    operators = (right, operators, operators_core)
    pieces = []
    plan = []
    for piece, offset in (
        (own_a, (0, 2, 0)),
        (own_b, (0, 3, 0)),
        (own_core_a, (0, 2, 1)),
        (own_core_b, (0, 3, 1)),
        (near_a, (1, 2, 0)),
        (near_b, (1, 3, 0)),
        (near_a_core, (1, 2, 1)),
        (near_b_core, (1, 3, 1)),
    ):
        pieces.append(piece[None])
        plan.append((offset + (0, block),))
    crossed = ((2, 0), (2, 1), (3, 0), (3, 1))
    for start, count, group, core in (
        (0, tall, (far_a, far_xa, far_za, far_zxa), core_a),
        (tall, rest, (far_b, far_xb, far_zb, far_zxb), core_b),
    ):
        for piece, offset in zip(group, crossed):
            pieces.append(piece[None])
            plan.append((offset + (0, start, count),))
        pieces.append(core)
        plan.append(tuple(offset + (1, start, count) for offset in crossed))
    psi, off_one, stats_one = operate(
        True, tuple(plan), pieces, cols, allowed, operators, left, (weight_own,)
    )

    found = share(stats_one)
    t, stats_two = pl.pallas_call(
        update_kernel,
        out_shape=(
            jax.ShapeDtypeStruct((2, block, width), jnp.float32),
            jax.ShapeDtypeStruct((8, LANES), jnp.float32),
        ),
        in_specs=[VMEM, VMEM, ANY, ANY] + [VMEM] * 4,
        out_specs=(VMEM, VMEM),
        scratch_shapes=[
            pltpu.VMEM((2, block, width), jnp.bfloat16),
            pltpu.SemaphoreType.DMA((2,)),
        ],
        compiler_params=pltpu.CompilerParams(vmem_limit_bytes=VMEM_LIMIT),
        name="update",
    )(psi, off_one, diag, hd_far, *found)
    found = lax.all_gather(stats_two, ("blk", "ops", "sub"))
    one = jax.ShapeDtypeStruct((block, width), jnp.bfloat16)
    changed_near, changed_far = pl.pallas_call(
        correct_kernel,
        out_shape=(one, one),
        in_specs=[VMEM, VMEM, VMEM],
        out_specs=(VMEM, VMEM),
        compiler_params=pltpu.CompilerParams(vmem_limit_bytes=VMEM_LIMIT),
        name="correct",
    )(psi, t, found)

    near_z = across(changed_near, "blk", 1)
    far_x = across(changed_far, "ops", 1)
    near_core = across(changed_near, "sub", 1)
    far_core = across(changed_far, "sub", 1)
    near_zx = across(after(near_z, far_x), "ops", 1)
    far_xz = across(after(far_x, near_z), "blk", 1)
    near_x = across(after(changed_near, near_z, far_x), "ops", 1)
    far_z = across(after(changed_far, near_z, far_x), "blk", 1)
    near_z_core = across(near_z, "sub", 1)
    far_x_core = across(far_x, "sub", 1)
    near_x_core = across(near_x, "sub", 1)
    far_z_core = across(far_z, "sub", 1)
    near_zx_core = across(near_zx, "sub", 1)
    far_xz_core = across(far_xz, "sub", 1)
    other = across(after(changed_far, near_z, far_x), "blk", 2)
    pieces, plan = [], []
    for piece, offset in (
        (changed_near, (0, 0, 0)),
        (changed_far, (2, 0, 0)),
        (near_core, (0, 0, 1)),
        (far_core, (2, 0, 1)),
        (near_z, (1, 0, 0)),
        (far_z, (3, 0, 0)),
        (near_z_core, (1, 0, 1)),
        (far_z_core, (3, 0, 1)),
        (near_x, (0, 1, 0)),
        (far_x, (2, 1, 0)),
        (near_x_core, (0, 1, 1)),
        (far_x_core, (2, 1, 1)),
        (near_zx, (1, 1, 0)),
        (far_xz, (3, 1, 0)),
        (near_zx_core, (1, 1, 1)),
        (far_xz_core, (3, 1, 1)),
    ):
        pieces.append(piece[None])
        plan.append((offset + (0, block),))
    two_near, two_far, two_late, stats_three = operate(
        False, tuple(plan), pieces, cols, allowed, operators, left, (diag, hd_far, psi, off_one, stats_one)
    )

    far_in = across(two_far, "blk", 2)
    near_in = across(two_near, "ops", 1)
    late_in = across(after(two_late, far_in, near_in), "blk", 2)
    far_in_x = across(after(far_in, near_in), "ops", 1)
    other_x = across(after(other, near_in), "ops", 1)
    late_in_x = across(after(late_in, other_x, far_in_x), "ops", 1)
    sums = stats_three + across(stats_three, "sub", 1)
    sums = sums + across(sums, "blk", 1)
    both = jnp.stack([sums, across(sums, "blk", 2)])
    both = both + across(after(both, near_in), "ops", 1)
    both = jnp.sum(jnp.where(half == 0, both, both[::-1])[:, :5], axis=2)
    scale = both[:, 3:4] + 1e-06
    subspace = jnp.concatenate([both[:, 4:5], both[:, 0:3]], axis=1) / scale
    places = ((0, 0, 0), (0, 1, 0), (1, 0, 0), (1, 1, 0))
    correction = assemble(block, (changed_near, near_x, other, other_x), places)
    places = ((0, 0, 0), (0, 1, 0), (1, 0, 0), (1, 0, block // 2), (1, 1, 0))
    sigma_two = assemble(block, (two_near, near_in, far_in, late_in, far_in_x), places)
    sigma_two = assemble(block, (late_in_x,), ((1, 1, block // 2),), sigma_two)
    return correction.reshape(theta.shape), sigma_two.reshape(theta.shape), subspace


def solution(mesh):
    in_specs = (
        P("groups", ("blk", "sub"), None),
        P(("groups", "blk", "sub"), None),
        P("groups", None),
        P(("groups", "ops"), None, None, None, None),
        P(("groups", "ops"), None, None),
        P(("groups", "ops"), None, None, None, None),
        P(("groups", "ops"), None, None),
    )
    out_specs = (
        P("groups", ("blk", "sub"), None),
        P("groups", ("blk", "sub"), None),
        P("groups", None),
    )
    body = shards if halves_fit(mesh) else general_shards
    return jax.shard_map(body, mesh=mesh, in_specs=in_specs, out_specs=out_specs, check_vma=False)
```

```python
import functools

import jax
import jax.numpy as jnp
from jax import lax
from jax.experimental import pallas as pl
from jax.experimental.pallas import tpu as pltpu
from jax.sharding import PartitionSpec as P

ANY = pl.BlockSpec(memory_space=pl.ANY)
SMEM = pl.BlockSpec(memory_space=pltpu.SMEM)
VMEM = pl.BlockSpec(memory_space=pltpu.VMEM)
VMEM_LIMIT = 56 * 1024 * 1024
LANES = 128


def apply_right(field_in, blocks, columns):
    roots_here, row_count, full_width = field_in.shape
    term_count, sectors, link_count = columns.shape
    block_size = full_width // sectors
    grouped = field_in.reshape(roots_here, row_count, sectors, block_size)
    picked = jnp.take(grouped, columns.reshape(-1), axis=2)
    picked = picked.reshape(roots_here, row_count, term_count, sectors, link_count, block_size)
    product = jnp.einsum("nrkbjq,kbjpq->knrbp", picked, blocks, preferred_element_type=jnp.float32)
    return product.reshape(term_count, roots_here, row_count, full_width).astype(jnp.bfloat16)


def take_rows(stacked, indices):
    return jnp.take(stacked, indices, axis=1)


def apply_left(arrived, blocks, columns):
    term_count, roots_here, full_width, col_count = arrived.shape
    sectors = columns.shape[1]
    link_count = columns.shape[2]
    block_size = full_width // sectors
    grouped = arrived.reshape(term_count, roots_here, sectors, block_size, col_count)
    picked = jax.vmap(take_rows)(grouped, columns.reshape(term_count, sectors * link_count))
    picked = picked.reshape(term_count, roots_here, sectors, link_count, block_size, col_count)
    product = jnp.einsum("kajpq,knajqc->napc", blocks, picked, preferred_element_type=jnp.float32)
    return product.reshape(roots_here, full_width, col_count)


def general_shards(theta, hdiag, pattern, left_blocks, left_cols, right_blocks, right_cols):
    roots_here, row_count, full_width = theta.shape
    sectors = pattern.shape[0]
    block_size = full_width // sectors
    first_row = lax.axis_index(("blk", "sub")) * row_count
    block_row = (first_row + jnp.arange(row_count, dtype=jnp.int32)) // block_size
    onehot = (block_row[:, None] == jnp.arange(sectors, dtype=jnp.int32)[None, :]).astype(
        jnp.float32
    )
    row_pattern = jnp.dot(onehot, pattern.astype(jnp.float32), preferred_element_type=jnp.float32)
    allowed = jnp.broadcast_to(row_pattern[:, :, None], (row_count, sectors, block_size))
    allowed = allowed.reshape(row_count, full_width).astype(jnp.bfloat16)
    diagonal = hdiag.astype(jnp.float32)
    peers = lax.axis_size("blk") * lax.axis_size("sub")

    def left_part(arrived):
        return apply_left(arrived, left_blocks, left_cols)

    def operate(field_in):
        images = apply_right(field_in, right_blocks, right_cols)
        partial_sum = left_part(
            lax.all_to_all(images, ("blk", "sub"), split_axis=3, concat_axis=2, tiled=True)
        )
        shares = lax.psum_scatter(partial_sum, "ops", scatter_dimension=2, tiled=True)
        returned = lax.all_to_all(
            shares.astype(jnp.bfloat16), ("blk", "sub"), split_axis=1, concat_axis=2, tiled=True
        )
        gathered = lax.all_gather(returned, "ops", axis=2, tiled=True)
        narrow = returned.shape[2] // peers
        gathered = gathered.reshape(roots_here, row_count, lax.axis_size("ops"), peers, narrow)
        offdiag = gathered.transpose(0, 1, 3, 2, 4).reshape(roots_here, row_count, full_width)
        offdiag = offdiag * allowed[None]
        return diagonal[None] * field_in.astype(jnp.float32) + offdiag.astype(jnp.float32)

    projected = theta * allowed[None]
    wave = projected.astype(jnp.float32)
    sigma_one = operate(projected)
    norm_sq, energy_sum = lax.psum(
        (jnp.sum(wave * wave, axis=(1, 2)), jnp.sum(wave * sigma_one, axis=(1, 2))), ("blk", "sub")
    )
    denominator = norm_sq + 1e-06
    energy = energy_sum / denominator
    shifted = diagonal[None] - energy[:, None, None]
    update = (sigma_one - energy[:, None, None] * wave) * shifted / (shifted * shifted + 1.0)
    correlation = lax.psum(jnp.sum(wave * update, axis=(1, 2)), ("blk", "sub"))
    factor = correlation / denominator
    orthogonal = update - factor[:, None, None] * wave
    length_sq = lax.psum(jnp.sum(orthogonal * orthogonal, axis=(1, 2)), ("blk", "sub"))
    correction = (orthogonal * jnp.sqrt(norm_sq / (length_sq + 1e-06))[:, None, None]).astype(
        jnp.bfloat16
    )
    sigma_two = operate(correction).astype(jnp.bfloat16)
    second = sigma_two.astype(jnp.float32)
    fixed = correction.astype(jnp.float32)
    cross_one, cross_two, cross_three = lax.psum(
        (
            jnp.sum(wave * second, axis=(1, 2)),
            jnp.sum(fixed * sigma_one, axis=(1, 2)),
            jnp.sum(fixed * second, axis=(1, 2)),
        ),
        ("blk", "sub"),
    )
    subspace = (
        jnp.stack([energy_sum, cross_one, cross_two, cross_three], axis=1) / denominator[:, None]
    )
    return (correction, sigma_two, subspace)


MIX_A, MIX_B = 4, 5


def halves_fit(mesh):
    sizes = dict(mesh.shape)
    return sizes["blk"] == 4 and sizes["ops"] == 2 and sizes["sub"] == 2


def across(value, axis, distance):
    size = lax.axis_size(axis)
    return lax.ppermute(value, axis, [(i, i ^ distance) for i in range(size)])


def share(stats):
    axes = ("blk", "ops")
    count = lax.axis_size("blk") * lax.axis_size("ops")
    pair = jnp.stack([stats, across(stats, "sub", 1)])
    found = [pair]
    for distance in (1, 2, 3):
        found.append(lax.ppermute(pair, axes, [(i, i ^ distance) for i in range(count)]))
    return found


def place():
    return lax.axis_index("blk"), lax.axis_index("ops"), lax.axis_index("sub")


def fold(value):
    rows, width = value.shape
    value = jnp.sum(value.reshape(rows // 8, 8, width), axis=0)
    return sum(value[:, at : at + LANES] for at in range(0, width, LANES))


def in_middle(z):
    return jnp.logical_or(z == 1, z == 2)


def row_of(dz, dx, dc):
    z, x, c = place()
    if dz in (MIX_A, MIX_B):
        far = in_middle(z) if dz == MIX_A else jnp.logical_not(in_middle(z))
        return jnp.where(far, row_of(2, 0, dc), row_of(1, 2, dc))
    return 4 * (z ^ dz) + 2 * (c ^ dc) + (x ^ dx if dx < 2 else dx - 2)


def operate_kernel(first, plan, cols, pattern, right_own, right_near, right_far, left_own, *refs):
    count = len(plan)
    pieces, refs = refs[:count], refs[count:]
    if first:
        weight_own, psi_out, off_out, stats_out = refs[:4]
        refs = refs[4:]
    else:
        hd_own, hd_far, psi_in, off_in, stats_in, near_out, far_out, late_out, stats_out = refs[:9]
        refs = refs[9:]
    field, images, right, left, diag, parts, sems = refs
    z, x, c = place()
    sectors, block, width = field.shape
    table = right.shape[1]
    links = table // sectors
    mine = 4 * z + 2 * c + x
    rows = (mine, mine ^ 8)

    copies = []

    def begin(source, target):
        copy = pltpu.make_async_copy(source, target, sems.at[len(copies)])
        copy.start()
        copies.append(copy)

    part = table // 2
    near, far = pl.ds(c * part, part), pl.ds((1 - c) * part, part)
    begin(right_own, right.at[0])
    for piece, offsets in zip(pieces, plan):
        for at, (dz, dx, dc, start, tall) in enumerate(offsets):
            target = field.at[row_of(dz, dx, dc), pl.ds(start, tall)]
            if dz in (MIX_A, MIX_B):
                begin(piece.at[at, :, pl.ds(0, width)], target)
                if dc == 0:
                    begin(
                        piece.at[at, pl.ds(0, parts.shape[1]), pl.ds(width, LANES)],
                        parts.at[dz - MIX_A],
                    )
            else:
                begin(piece.at[at], target)
    begin(right_near.at[pl.ds(0, part)], right.at[1, near])
    begin(right_far, right.at[1, far])
    early = len(copies)
    for at in range(2):
        begin(left_own.at[pl.ds(rows[at] * links, links)], left.at[0, pl.ds(at * links, links)])
    begin(right_near.at[pl.ds(part, 2 * links)], left.at[1])
    if not first:
        begin(hd_own.at[x], diag.at[0])
        begin(hd_far, diag.at[1])
    for copy in copies[:early]:
        copy.wait()

    def right_col(term, b, j):
        return cols[(2 * term) * table + b * links + j]

    def left_col(term, a, j):
        return cols[(2 * term + 1) * table + a * links + j]

    def allowed(a, q, value):
        return jnp.where(pattern[a * sectors + q] != 0, value, jnp.zeros_like(value))

    sources = [[left_col(term, rows[at], j) for at in range(2) for j in range(links)] for term in range(2)]

    deep = links * block

    def image(b, carry):
        for term in range(2):
            found = [right_col(term, b, j) for j in range(links)]
            lhs = []
            for source in sources[term]:
                line = []
                for col in found:
                    value = field[source, :, pl.ds(pl.multiple_of(col * block, block), block)]
                    line.append(allowed(source, col, value) if first else value)
                lhs.append(jnp.concatenate(line, axis=1))
            rhs = [right[term, b * links + j] for j in range(links)]
            product = lax.dot_general(
                jnp.concatenate(lhs, axis=0),
                jnp.concatenate(rhs, axis=1),
                (((1,), (1,)), ((), ())),
                preferred_element_type=jnp.float32,
            )
            product = product.astype(jnp.bfloat16)
            span = pl.ds(pl.multiple_of(b * block, block), block)
            for at in range(2):
                images[at, term * deep : (term + 1) * deep, span] = product[at * deep : (at + 1) * deep]
        return carry

    lax.fori_loop(0, sectors, image, 0, unroll=2)
    for copy in copies[early:]:
        copy.wait()

    step = 2
    half = block // 2
    zero = jnp.zeros((8, LANES), jnp.float32)

    def column(n, sums):
        start = pl.multiple_of(n * step * block, step * block)
        span = pl.ds(start, step * block)
        sums = list(sums)

        def masked(a, value):
            parts = [
                allowed(a, n * step + i, value[:, i * block : (i + 1) * block]) for i in range(step)
            ]
            return jnp.concatenate(parts, axis=1)

        for at in range(2):
            weights = [left[term, at * links + j] for term in range(2) for j in range(links)]
            total = jnp.dot(
                jnp.concatenate(weights, axis=1),
                images[at, :, span],
                preferred_element_type=jnp.float32,
            )
            offdiag = masked(rows[at], total.astype(jnp.bfloat16).astype(jnp.float32))
            own = field[rows[at], :, span].astype(jnp.float32)
            if first:
                own = masked(rows[at], own)
                psi_out[at, :, span] = own.astype(jnp.bfloat16)
                off_out[at, :, span] = offdiag.astype(jnp.bfloat16)
                sums[0] += fold(own * own)
                sums[1] += fold(own * offdiag)
            else:
                weight = diag[at, :, span].astype(jnp.float32)
                narrow = (weight * own + offdiag).astype(jnp.bfloat16)
                if at == 0:
                    near_out[:, span] = narrow
                else:
                    far_out[:, span] = narrow[:half]
                    late_out[:, span] = narrow[half:]
                second = narrow.astype(jnp.float32)
                wave = psi_in[at, :, span].astype(jnp.float32)
                sigma_one = weight * wave + off_in[at, :, span].astype(jnp.float32)
                sums[0] += fold(wave * second)
                sums[1] += fold(own * sigma_one)
                sums[2] += fold(own * second)
        return tuple(sums)

    sums = list(lax.fori_loop(0, sectors // step, column, (zero,) * (2 if first else 3)))
    if first:
        far_weight = (parts[0] + parts[1]).astype(jnp.float32)
        sums[1] += weight_own[...] + (far_weight[0:8] + far_weight[16:24] + far_weight[32:40])
    stats_out[...] = jnp.zeros_like(stats_out)
    for at, value in enumerate(sums):
        stats_out[at : at + 1, :] = jnp.sum(value, axis=0, keepdims=True)
    if not first:
        stats_out[3:5, :] = stats_in[0:2, :]


def operate(first, plan, pieces, cols, pattern, right, left, extra):
    right_own, right_near, right_far = right
    table, block, _ = right_own.shape
    width = pieces[0].shape[2]
    sectors = width // block
    links = table // sectors
    rows = jax.ShapeDtypeStruct((2, block, width), jnp.bfloat16)
    one = jax.ShapeDtypeStruct((block, width), jnp.bfloat16)
    some = jax.ShapeDtypeStruct((block // 2, width), jnp.bfloat16)
    stats = jax.ShapeDtypeStruct((8, LANES), jnp.float32)
    out_shape = (rows, rows, stats) if first else (one, some, some, stats)
    extra_specs = [VMEM] if first else [ANY, ANY, VMEM, VMEM, VMEM]
    copies = sum(len(offsets) for offsets in plan) + 9
    inner = 2 * 2 * sectors * 2 * links * links * block * block * block
    outer = 2 * 2 * 2 * links * block * block * width
    return pl.pallas_call(
        functools.partial(operate_kernel, first, plan),
        out_shape=out_shape,
        in_specs=[SMEM, SMEM] + [ANY] * (4 + len(pieces)) + extra_specs,
        out_specs=(VMEM,) * len(out_shape),
        scratch_shapes=[
            pltpu.VMEM((sectors, block, width), jnp.bfloat16),
            pltpu.VMEM((2, 2 * links * block, width), jnp.bfloat16),
            pltpu.VMEM((2, table, block, block), jnp.bfloat16),
            pltpu.VMEM((2, 2 * links, block, block), jnp.bfloat16),
            pltpu.VMEM((2, block, width), jnp.bfloat16),
            pltpu.VMEM((2, 48, LANES), jnp.bfloat16),
            pltpu.SemaphoreType.DMA((copies,)),
        ],
        compiler_params=pltpu.CompilerParams(vmem_limit_bytes=VMEM_LIMIT),
        cost_estimate=pl.CostEstimate(
            flops=inner + outer if first else 0,
            bytes_accessed=16 * 1024 * 1024 if first else 1024,
            transcendentals=0,
        ),
        name="operate_first" if first else "operate_second",
    )(cols, pattern, right_own, right_near, right_far, left, *pieces, *extra)


def prepare_kernel(
    pattern, theta, hd, right, left, cols, mix_a, mix_b, own_a, own_b, packed, own_out, waves, diag, sems
):
    z, x, c = place()
    half = z // 2
    middle = in_middle(z)
    mine = 4 * z + 2 * c + x
    block, width = own_a.shape
    sectors = width // block
    links = right.shape[0] // sectors
    part = right.shape[0] // 2
    root_a = jnp.where(middle, half, 1 - half)
    last = part + 2 * links
    rows = pl.ds(0, width)
    sources = (
        (theta.at[half, x], waves.at[0]),
        (theta.at[1 - half, x], waves.at[1]),
        (hd.at[x], diag),
        (theta.at[root_a, jnp.where(middle, 0, x)], mix_a.at[:, rows]),
        (theta.at[1 - root_a, jnp.where(middle, x, 0)], mix_b.at[:, rows]),
        (theta.at[half, 0], own_a),
        (theta.at[half, 1], own_b),
        (right.at[pl.ds(c * part, part)], packed.at[pl.ds(0, part)]),
        (left.at[pl.ds((mine ^ 1) * links, links)], packed.at[pl.ds(part, links)]),
        (left.at[pl.ds((mine ^ 9) * links, links)], packed.at[pl.ds(part + links, links)]),
    )
    copies = [
        pltpu.make_async_copy(source, target, sems.at[at])
        for at, (source, target) in enumerate(sources)
    ]
    for copy in copies:
        copy.start()
    packed[last] = jnp.zeros_like(packed[last])
    packed[last, 0 : cols.shape[0], :] = cols[...]
    for copy in copies[:3]:
        copy.wait()
    zero = jnp.zeros((8, LANES), jnp.float32)

    def column(q, sums):
        span = pl.ds(pl.multiple_of(q * block, block), block)
        weight = diag[:, span].astype(jnp.float32)
        weight = jnp.where(pattern[mine * sectors + q] != 0, weight, jnp.zeros_like(weight))
        found = []
        for root in range(2):
            wave = waves[root, :, span].astype(jnp.float32)
            found.append(sums[root] + fold(weight * wave * wave))
        return tuple(found)

    near, far = lax.fori_loop(0, sectors, column, (zero, zero), unroll=4)
    own_out[...] = near
    left_over = jnp.concatenate([far, zero], axis=0)
    parts = []
    for _ in range(3):
        piece = left_over.astype(jnp.bfloat16)
        parts.append(piece)
        left_over = left_over - piece.astype(jnp.float32)
    parts.append(jnp.zeros((block - 48, LANES), jnp.bfloat16))
    tail = jnp.concatenate(parts, axis=0)
    none = jnp.zeros_like(tail)
    mix_a[:, width:] = jnp.where(middle, none, tail)
    mix_b[:, width:] = jnp.where(middle, tail, none)
    for copy in copies[3:]:
        copy.wait()


def prepare(pattern, theta, hd, right, left, cols):
    _, _, block, width = theta.shape
    table = right.shape[0]
    links = table * block // width
    kind = jnp.bfloat16
    mix = jax.ShapeDtypeStruct((block, width + LANES), kind)
    one = jax.ShapeDtypeStruct((block, width), kind)
    packed = jax.ShapeDtypeStruct((table // 2 + 2 * links + 1, block, block), kind)
    return pl.pallas_call(
        prepare_kernel,
        out_shape=(mix, mix, one, one, packed, jax.ShapeDtypeStruct((8, LANES), jnp.float32)),
        in_specs=[SMEM, ANY, ANY, ANY, ANY, VMEM],
        out_specs=(VMEM,) * 6,
        scratch_shapes=[
            pltpu.VMEM((2, block, width), kind),
            pltpu.VMEM((block, width), kind),
            pltpu.SemaphoreType.DMA((10,)),
        ],
        compiler_params=pltpu.CompilerParams(vmem_limit_bytes=VMEM_LIMIT),
        name="prepare",
    )(pattern, theta, hd, right, left, cols)


def total_of(rows):
    return jnp.sum(rows, axis=1, keepdims=True)


def update_kernel(psi, off, hd_own, hd_far, *refs):
    stats, (t_out, stats_out, diag, sems) = refs[:4], refs[4:]
    z, x, c = place()
    copies = [
        pltpu.make_async_copy(hd_own.at[x], diag.at[0], sems.at[0]),
        pltpu.make_async_copy(hd_far, diag.at[1], sems.at[1]),
    ]
    for copy in copies:
        copy.start()
    whole = sum(ref[at, 0:2, :] for ref in stats for at in range(2))
    norm_sq, energy_sum = total_of(whole[0:1, :]), total_of(whole[1:2, :])
    energy = energy_sum / (norm_sq + 1e-06)
    mine = total_of(stats[0][0, 0:1, :])
    for copy in copies:
        copy.wait()
    _, block, width = psi.shape
    step = 16
    zero = jnp.zeros((8, LANES), jnp.float32)

    def chunk(n, total):
        span = pl.ds(pl.multiple_of(n * step, step), step)
        for at in range(2):
            wave = psi[at, span, :].astype(jnp.float32)
            weight = diag[at, span, :].astype(jnp.float32)
            sigma = weight * wave + off[at, span, :].astype(jnp.float32)
            shifted = weight - energy
            t = (sigma - energy * wave) * shifted / (shifted * shifted + 1.0)
            t_out[at, span, :] = t
            total = total + fold(wave * t)
        return total

    lanes = jnp.sum(lax.fori_loop(0, block // step, chunk, zero), axis=0, keepdims=True)
    correlation = total_of(lanes)
    local = jnp.where(mine > 0.0, correlation / jnp.where(mine > 0.0, mine, 1.0), 0.0)

    def within(n, total):
        span = pl.ds(pl.multiple_of(n * step, step), step)
        for at in range(2):
            rest = t_out[at, span, :] - local * psi[at, span, :].astype(jnp.float32)
            total = total + fold(rest * rest)
        return total

    spread = jnp.sum(lax.fori_loop(0, block // step, within, zero), axis=0, keepdims=True)
    stats_out[...] = jnp.zeros_like(stats_out)
    stats_out[0:1, :] = jnp.broadcast_to(correlation, (1, LANES))
    stats_out[1:2, :] = jnp.broadcast_to(total_of(spread), (1, LANES))
    stats_out[2:3, :] = jnp.broadcast_to(mine, (1, LANES))
    stats_out[3:4, :] = jnp.broadcast_to(local, (1, LANES))
    stats_out[4:5, :] = jnp.broadcast_to(norm_sq, (1, LANES))


def correct_kernel(psi, t, *refs):
    stats, outs = refs[:4], refs[4:]
    stats = [ref.at[at] for ref in stats for at in range(2)]
    norm_sq = stats[0][4:5, 0:1]
    factor = sum(ref[0:1, 0:1] for ref in stats) / (norm_sq + 1e-06)
    length_sq = jnp.zeros((1, 1), jnp.float32)
    for ref in stats:
        gap = factor - ref[3:4, 0:1]
        length_sq = length_sq + (ref[1:2, 0:1] + gap * gap * ref[2:3, 0:1])
    scale = jnp.sqrt(norm_sq / (length_sq + 1e-06))
    _, block, width = psi.shape
    step = 16

    def chunk(n, carry):
        span = pl.ds(pl.multiple_of(n * step, step), step)
        for at in range(2):
            wave = psi[at, span, :].astype(jnp.float32)
            outs[at][span, :] = ((t[at, span, :] - factor * wave) * scale).astype(jnp.bfloat16)
        return carry

    lax.fori_loop(0, block // step, chunk, 0)


def assemble_kernel(places, based, *refs):
    count = len(places)
    pieces, (out, sems) = refs[:count], refs[count + based :]
    z, x, c = place()
    half = z // 2
    copies = []
    for at, (root, flip, start) in enumerate(places):
        size = pieces[at].shape[0]
        target = out.at[half ^ root, x ^ flip, pl.ds(start, size)]
        copies.append(pltpu.make_async_copy(pieces[at], target, sems.at[at]))
    for copy in copies:
        copy.start()
    for copy in copies:
        copy.wait()


def assemble(block, pieces, places, base=None):
    width = pieces[0].shape[1]
    based = [] if base is None else [base]
    return pl.pallas_call(
        functools.partial(assemble_kernel, places, len(based)),
        out_shape=jax.ShapeDtypeStruct((2, 2, block, width), pieces[0].dtype),
        in_specs=[VMEM] * len(pieces) + [ANY] * len(based),
        out_specs=ANY,
        scratch_shapes=[pltpu.SemaphoreType.DMA((len(pieces),))],
        input_output_aliases={len(pieces): 0} if based else {},
        compiler_params=pltpu.CompilerParams(vmem_limit_bytes=VMEM_LIMIT),
        name="assemble",
    )(*pieces, *based)


def after(value, *others):
    return lax.optimization_barrier((value, *others))[0]


def shards(theta, hdiag, pattern, left_blocks, left_cols, right_blocks, right_cols):
    roots, row_count, width = theta.shape
    sectors = pattern.shape[0]
    block = width // sectors
    z, x, c = place()
    half = z // 2
    mine = 4 * z + 2 * c + x

    halves = theta.reshape(roots, 2, block, width)
    diag = hdiag.reshape(2, block, width)
    allowed = pattern.reshape(-1)
    chunk = block // 2
    right = right_blocks.reshape(-1, block, block)
    left = left_blocks.reshape(-1, block, block)
    table = right.shape[0]
    cols = jnp.concatenate([right_cols.reshape(-1), left_cols.reshape(-1)])
    spots = jnp.pad(cols, (0, 16 * LANES - cols.shape[0])).reshape(16, LANES).astype(jnp.bfloat16)

    mix_a, mix_b, own_a, own_b, packed, weight_own = prepare(allowed, halves, diag, right, left, spots)
    mix_a = lax.ppermute(mix_a, "blk", [(0, 2), (2, 3), (3, 1), (1, 0)])
    mix_b = lax.ppermute(mix_b, "blk", [(0, 1), (1, 3), (3, 2), (2, 0)])
    operators = across(packed, "ops", 1)
    own_core_a = across(own_a, "sub", 1)
    own_core_b = across(own_b, "sub", 1)

    mix_a, mix_b = after((mix_a, mix_b), own_core_a, own_core_b)
    far = [
        jnp.where(in_middle(z), mix_a[at : at + chunk, :width], mix_b[at : at + chunk, :width])
        for at in (0, chunk)
    ]
    far_z = [across(value, "blk", 1) for value in far]
    far_x = [across(value, "ops", 1) for value in far]
    mix_a_core = across(mix_a, "sub", 1)
    mix_b_core = across(mix_b, "sub", 1)
    operators_core = across(after(operators, mix_b_core)[: table // 2], "sub", 1)
    found = operators[-1].reshape(-1)[: cols.shape[0]].astype(jnp.int32)
    cols = jnp.concatenate([cols, found])

    near_b = across(after(own_b, far_z[0]), "blk", 1)
    far_zx = [across(far_z[0], "ops", 1), across(after(far_z[1], far_x[1]), "ops", 1)]
    crossed_core = across(jnp.stack([*far_x, *far_z]), "sub", 1)
    hd_far = lax.dynamic_index_in_dim(diag, x, 0, keepdims=False)
    hd_far = across(after(hd_far, far_z[1]), "blk", 2)
    far_zx_core = [across(value, "sub", 1) for value in far_zx]
    near_b_core = across(near_b, "sub", 1)

    operators = (right, operators, operators_core)
    pieces = []
    plan = []
    for piece, offset in (
        (own_a, (0, 2, 0)),
        (own_b, (0, 3, 0)),
        (own_core_a, (0, 2, 1)),
        (own_core_b, (0, 3, 1)),
        (mix_a, (MIX_A, 0, 0)),
        (mix_b, (MIX_B, 0, 0)),
        (mix_a_core, (MIX_A, 0, 1)),
        (mix_b_core, (MIX_B, 0, 1)),
        (near_b, (1, 3, 0)),
        (near_b_core, (1, 3, 1)),
    ):
        pieces.append(piece[None])
        plan.append((offset + (0, block),))
    for at in range(2):
        for piece, offset in (
            (far_x[at], (2, 1, 0)),
            (far_z[at], (3, 0, 0)),
            (far_zx[at], (3, 1, 0)),
            (far_zx_core[at], (3, 1, 1)),
        ):
            pieces.append(piece[None])
            plan.append((offset + (at * chunk, chunk),))
    pieces.append(crossed_core)
    plan.append(
        tuple((*offset, 1, at * chunk, chunk) for offset in ((2, 1), (3, 0)) for at in range(2))
    )
    psi, off_one, stats_one = operate(
        True, tuple(plan), pieces, cols, allowed, operators, left, (weight_own,)
    )

    found = share(stats_one)
    t, stats_two = pl.pallas_call(
        update_kernel,
        out_shape=(
            jax.ShapeDtypeStruct((2, block, width), jnp.float32),
            jax.ShapeDtypeStruct((8, LANES), jnp.float32),
        ),
        in_specs=[VMEM, VMEM, ANY, ANY] + [VMEM] * 4,
        out_specs=(VMEM, VMEM),
        scratch_shapes=[
            pltpu.VMEM((2, block, width), jnp.bfloat16),
            pltpu.SemaphoreType.DMA((2,)),
        ],
        compiler_params=pltpu.CompilerParams(vmem_limit_bytes=VMEM_LIMIT),
        name="update",
    )(psi, off_one, diag, hd_far, *found)
    found = share(stats_two)
    one = jax.ShapeDtypeStruct((block, width), jnp.bfloat16)
    changed_near, changed_far = pl.pallas_call(
        correct_kernel,
        out_shape=(one, one),
        in_specs=[VMEM, VMEM] + [VMEM] * 4,
        out_specs=(VMEM, VMEM),
        compiler_params=pltpu.CompilerParams(vmem_limit_bytes=VMEM_LIMIT),
        name="correct",
    )(psi, t, *found)

    near_z = across(changed_near, "blk", 1)
    far_x = across(changed_far, "ops", 1)
    near_core = across(changed_near, "sub", 1)
    far_core = across(changed_far, "sub", 1)
    near_zx = across(after(near_z, far_x), "ops", 1)
    far_xz = across(after(far_x, near_z), "blk", 1)
    near_x = across(after(changed_near, near_z, far_x), "ops", 1)
    far_z = across(after(changed_far, near_z, far_x), "blk", 1)
    near_z_core = across(near_z, "sub", 1)
    far_x_core = across(far_x, "sub", 1)
    near_x_core = across(near_x, "sub", 1)
    far_z_core = across(far_z, "sub", 1)
    near_zx_core = across(near_zx, "sub", 1)
    far_xz_core = across(far_xz, "sub", 1)
    other = across(after(changed_far, near_z, far_x), "blk", 2)
    pieces, plan = [], []
    for piece, offset in (
        (changed_near, (0, 0, 0)),
        (changed_far, (2, 0, 0)),
        (near_core, (0, 0, 1)),
        (far_core, (2, 0, 1)),
        (near_z, (1, 0, 0)),
        (far_z, (3, 0, 0)),
        (near_z_core, (1, 0, 1)),
        (far_z_core, (3, 0, 1)),
        (near_x, (0, 1, 0)),
        (far_x, (2, 1, 0)),
        (near_x_core, (0, 1, 1)),
        (far_x_core, (2, 1, 1)),
        (near_zx, (1, 1, 0)),
        (far_xz, (3, 1, 0)),
        (near_zx_core, (1, 1, 1)),
        (far_xz_core, (3, 1, 1)),
    ):
        pieces.append(piece[None])
        plan.append((offset + (0, block),))
    two_near, two_far, two_late, stats_three = operate(
        False, tuple(plan), pieces, cols, allowed, operators, left, (diag, hd_far, psi, off_one, stats_one)
    )

    far_in = across(two_far, "blk", 2)
    near_in = across(two_near, "ops", 1)
    late_in = across(after(two_late, far_in, near_in), "blk", 2)
    far_in_x = across(after(far_in, near_in), "ops", 1)
    other_x = across(after(other, near_in), "ops", 1)
    late_in_x = across(after(late_in, other_x, far_in_x), "ops", 1)
    sums = stats_three + across(stats_three, "sub", 1)
    sums = sums + across(sums, "blk", 1)
    both = jnp.stack([sums, across(sums, "blk", 2)])
    both = both + across(after(both, near_in), "ops", 1)
    both = jnp.sum(jnp.where(half == 0, both, both[::-1])[:, :5], axis=2)
    scale = both[:, 3:4] + 1e-06
    subspace = jnp.concatenate([both[:, 4:5], both[:, 0:3]], axis=1) / scale
    places = ((0, 0, 0), (0, 1, 0), (1, 0, 0), (1, 1, 0))
    correction = assemble(block, (changed_near, near_x, other, other_x), places)
    places = ((0, 0, 0), (0, 1, 0), (1, 0, 0), (1, 0, block // 2), (1, 1, 0))
    sigma_two = assemble(block, (two_near, near_in, far_in, late_in, far_in_x), places)
    sigma_two = assemble(block, (late_in_x,), ((1, 1, block // 2),), sigma_two)
    return correction.reshape(theta.shape), sigma_two.reshape(theta.shape), subspace


def solution(mesh):
    in_specs = (
        P("groups", ("blk", "sub"), None),
        P(("groups", "blk", "sub"), None),
        P("groups", None),
        P(("groups", "ops"), None, None, None, None),
        P(("groups", "ops"), None, None),
        P(("groups", "ops"), None, None, None, None),
        P(("groups", "ops"), None, None),
    )
    out_specs = (
        P("groups", ("blk", "sub"), None),
        P("groups", ("blk", "sub"), None),
        P("groups", None),
    )
    body = shards if halves_fit(mesh) else general_shards
    return jax.shard_map(body, mesh=mesh, in_specs=in_specs, out_specs=out_specs, check_vma=False)
```

```python
import functools

import jax
import jax.numpy as jnp
from jax import lax
from jax.experimental import pallas as pl
from jax.experimental.pallas import tpu as pltpu
from jax.sharding import PartitionSpec as P

ANY = pl.BlockSpec(memory_space=pl.ANY)
SMEM = pl.BlockSpec(memory_space=pltpu.SMEM)
VMEM = pl.BlockSpec(memory_space=pltpu.VMEM)
VMEM_LIMIT = 56 * 1024 * 1024
LANES = 128


def apply_right(field_in, blocks, columns):
    roots_here, row_count, full_width = field_in.shape
    term_count, sectors, link_count = columns.shape
    block_size = full_width // sectors
    grouped = field_in.reshape(roots_here, row_count, sectors, block_size)
    picked = jnp.take(grouped, columns.reshape(-1), axis=2)
    picked = picked.reshape(roots_here, row_count, term_count, sectors, link_count, block_size)
    product = jnp.einsum("nrkbjq,kbjpq->knrbp", picked, blocks, preferred_element_type=jnp.float32)
    return product.reshape(term_count, roots_here, row_count, full_width).astype(jnp.bfloat16)


def take_rows(stacked, indices):
    return jnp.take(stacked, indices, axis=1)


def apply_left(arrived, blocks, columns):
    term_count, roots_here, full_width, col_count = arrived.shape
    sectors = columns.shape[1]
    link_count = columns.shape[2]
    block_size = full_width // sectors
    grouped = arrived.reshape(term_count, roots_here, sectors, block_size, col_count)
    picked = jax.vmap(take_rows)(grouped, columns.reshape(term_count, sectors * link_count))
    picked = picked.reshape(term_count, roots_here, sectors, link_count, block_size, col_count)
    product = jnp.einsum("kajpq,knajqc->napc", blocks, picked, preferred_element_type=jnp.float32)
    return product.reshape(roots_here, full_width, col_count)


def general_shards(theta, hdiag, pattern, left_blocks, left_cols, right_blocks, right_cols):
    roots_here, row_count, full_width = theta.shape
    sectors = pattern.shape[0]
    block_size = full_width // sectors
    first_row = lax.axis_index(("blk", "sub")) * row_count
    block_row = (first_row + jnp.arange(row_count, dtype=jnp.int32)) // block_size
    onehot = (block_row[:, None] == jnp.arange(sectors, dtype=jnp.int32)[None, :]).astype(
        jnp.float32
    )
    row_pattern = jnp.dot(onehot, pattern.astype(jnp.float32), preferred_element_type=jnp.float32)
    allowed = jnp.broadcast_to(row_pattern[:, :, None], (row_count, sectors, block_size))
    allowed = allowed.reshape(row_count, full_width).astype(jnp.bfloat16)
    diagonal = hdiag.astype(jnp.float32)
    peers = lax.axis_size("blk") * lax.axis_size("sub")

    def left_part(arrived):
        return apply_left(arrived, left_blocks, left_cols)

    def operate(field_in):
        images = apply_right(field_in, right_blocks, right_cols)
        partial_sum = left_part(
            lax.all_to_all(images, ("blk", "sub"), split_axis=3, concat_axis=2, tiled=True)
        )
        shares = lax.psum_scatter(partial_sum, "ops", scatter_dimension=2, tiled=True)
        returned = lax.all_to_all(
            shares.astype(jnp.bfloat16), ("blk", "sub"), split_axis=1, concat_axis=2, tiled=True
        )
        gathered = lax.all_gather(returned, "ops", axis=2, tiled=True)
        narrow = returned.shape[2] // peers
        gathered = gathered.reshape(roots_here, row_count, lax.axis_size("ops"), peers, narrow)
        offdiag = gathered.transpose(0, 1, 3, 2, 4).reshape(roots_here, row_count, full_width)
        offdiag = offdiag * allowed[None]
        return diagonal[None] * field_in.astype(jnp.float32) + offdiag.astype(jnp.float32)

    projected = theta * allowed[None]
    wave = projected.astype(jnp.float32)
    sigma_one = operate(projected)
    norm_sq, energy_sum = lax.psum(
        (jnp.sum(wave * wave, axis=(1, 2)), jnp.sum(wave * sigma_one, axis=(1, 2))), ("blk", "sub")
    )
    denominator = norm_sq + 1e-06
    energy = energy_sum / denominator
    shifted = diagonal[None] - energy[:, None, None]
    update = (sigma_one - energy[:, None, None] * wave) * shifted / (shifted * shifted + 1.0)
    correlation = lax.psum(jnp.sum(wave * update, axis=(1, 2)), ("blk", "sub"))
    factor = correlation / denominator
    orthogonal = update - factor[:, None, None] * wave
    length_sq = lax.psum(jnp.sum(orthogonal * orthogonal, axis=(1, 2)), ("blk", "sub"))
    correction = (orthogonal * jnp.sqrt(norm_sq / (length_sq + 1e-06))[:, None, None]).astype(
        jnp.bfloat16
    )
    sigma_two = operate(correction).astype(jnp.bfloat16)
    second = sigma_two.astype(jnp.float32)
    fixed = correction.astype(jnp.float32)
    cross_one, cross_two, cross_three = lax.psum(
        (
            jnp.sum(wave * second, axis=(1, 2)),
            jnp.sum(fixed * sigma_one, axis=(1, 2)),
            jnp.sum(fixed * second, axis=(1, 2)),
        ),
        ("blk", "sub"),
    )
    subspace = (
        jnp.stack([energy_sum, cross_one, cross_two, cross_three], axis=1) / denominator[:, None]
    )
    return (correction, sigma_two, subspace)


MIX_A, MIX_B = 4, 5


def halves_fit(mesh):
    sizes = dict(mesh.shape)
    return sizes["blk"] == 4 and sizes["ops"] == 2 and sizes["sub"] == 2


def across(value, axis, distance):
    size = lax.axis_size(axis)
    return lax.ppermute(value, axis, [(i, i ^ distance) for i in range(size)])


def share(stats):
    axes = ("blk", "ops")
    count = lax.axis_size("blk") * lax.axis_size("ops")
    pair = jnp.stack([stats, across(stats, "sub", 1)])
    found = [pair]
    for distance in (1, 2, 3):
        found.append(lax.ppermute(pair, axes, [(i, i ^ distance) for i in range(count)]))
    return found


def place():
    return lax.axis_index("blk"), lax.axis_index("ops"), lax.axis_index("sub")


def fold(value):
    rows, width = value.shape
    value = jnp.sum(value.reshape(rows // 8, 8, width), axis=0)
    return sum(value[:, at : at + LANES] for at in range(0, width, LANES))


def in_middle(z):
    return jnp.logical_or(z == 1, z == 2)


def row_of(dz, dx, dc):
    z, x, c = place()
    if dz in (MIX_A, MIX_B):
        far = in_middle(z) if dz == MIX_A else jnp.logical_not(in_middle(z))
        return jnp.where(far, row_of(2, 0, dc), row_of(1, 2, dc))
    return 4 * (z ^ dz) + 2 * (c ^ dc) + (x ^ dx if dx < 2 else dx - 2)


def operate_kernel(first, plan, cols, pattern, right_all, left_own, left_other, *refs):
    count = len(plan)
    pieces, refs = refs[:count], refs[count:]
    if first:
        weight_own, psi_out, off_out, stats_out = refs[:4]
        refs = refs[4:]
    else:
        hd_own, hd_far, psi_in, off_in, stats_in, near_out, far_out, late_out, stats_out = refs[:9]
        refs = refs[9:]
    field, images, right, left, diag, parts, sems = refs
    z, x, c = place()
    sectors, block, width = field.shape
    table = right.shape[1]
    links = table // sectors
    mine = 4 * z + 2 * c + x
    rows = (mine, mine ^ 12)
    half = z // 2

    copies = []

    def begin(source, target):
        copy = pltpu.make_async_copy(source, target, sems.at[len(copies)])
        copy.start()
        copies.append(copy)

    begin(right_all, right)
    for piece, offsets in zip(pieces, plan):
        base = 2 * half if piece.shape[0] == 4 else 0
        for at, (dz, dx, dc, start, tall) in enumerate(offsets):
            target = field.at[row_of(dz, dx, dc), pl.ds(start, tall)]
            if dz in (MIX_A, MIX_B):
                begin(piece.at[at, :, pl.ds(0, width)], target)
                if dc == 0:
                    begin(
                        piece.at[at, pl.ds(0, parts.shape[1]), pl.ds(width, LANES)],
                        parts.at[dz - MIX_A],
                    )
            else:
                begin(piece.at[base + at], target)
    early = len(copies)
    for at in range(2):
        begin(left_own.at[pl.ds(rows[at] * links, links)], left.at[0, pl.ds(at * links, links)])
    begin(left_other.at[pl.ds(table // 2, 2 * links)], left.at[1])
    if not first:
        begin(hd_own.at[x], diag.at[0])
        begin(hd_far, diag.at[1])
    for copy in copies[:early]:
        copy.wait()

    def right_col(term, b, j):
        return cols[(2 * term) * table + b * links + j]

    def left_col(term, a, j):
        return cols[(2 * term + 1) * table + a * links + j]

    def allowed(a, q, value):
        return jnp.where(pattern[a, q] != 0, value, jnp.zeros_like(value))

    sources = [[left_col(term, rows[at], j) for at in range(2) for j in range(links)] for term in range(2)]

    deep = links * block

    none = jnp.zeros((block, block), jnp.bfloat16)
    pair = 2

    def image(n, carry):
        picks = [(i, j) for i in range(pair) for j in range(links)]
        for term in range(2):
            found = [right_col(term, n * pair + i, j) for i, j in picks]
            lhs = []
            for source in sources[term]:
                line = []
                for col in found:
                    value = field[source, :, pl.ds(pl.multiple_of(col * block, block), block)]
                    line.append(allowed(source, col, value) if first else value)
                lhs.append(jnp.concatenate(line, axis=1))
            rhs = []
            for i, j in picks:
                tile = right[term, (n * pair + i) * links + j]
                rhs.append(jnp.concatenate([tile if i == at else none for at in range(pair)], axis=1))
            product = jnp.dot(
                jnp.concatenate(lhs, axis=0),
                jnp.concatenate(rhs, axis=0),
                preferred_element_type=jnp.float32,
            )
            product = product.astype(jnp.bfloat16)
            span = pl.ds(pl.multiple_of(n * pair * block, pair * block), pair * block)
            for at in range(2):
                images[at, term * deep : (term + 1) * deep, span] = product[at * deep : (at + 1) * deep]
        return carry

    lax.fori_loop(0, sectors // pair, image, 0, unroll=2)
    for copy in copies[early:]:
        copy.wait()

    step = 2
    early_rows = block // 2
    zero = jnp.zeros((8, LANES), jnp.float32)

    def column(n, sums):
        start = pl.multiple_of(n * step * block, step * block)
        span = pl.ds(start, step * block)
        sums = list(sums)

        def masked(a, value):
            parts = [
                allowed(a, n * step + i, value[:, i * block : (i + 1) * block]) for i in range(step)
            ]
            return jnp.concatenate(parts, axis=1)

        for at in range(2):
            weights = [left[term, at * links + j] for term in range(2) for j in range(links)]
            total = jnp.dot(
                jnp.concatenate(weights, axis=1),
                images[at, :, span],
                preferred_element_type=jnp.float32,
            )
            offdiag = masked(rows[at], total.astype(jnp.bfloat16).astype(jnp.float32))
            own = field[rows[at], :, span].astype(jnp.float32)
            if first:
                own = masked(rows[at], own)
                psi_out[at, :, span] = own.astype(jnp.bfloat16)
                off_out[at, :, span] = offdiag.astype(jnp.bfloat16)
                sums[0] += fold(own * own)
                sums[1] += fold(own * offdiag)
            else:
                weight = diag[at, :, span].astype(jnp.float32)
                narrow = (weight * own + offdiag).astype(jnp.bfloat16)
                if at == 0:
                    near_out[:, span] = narrow
                else:
                    far_out[:, span] = narrow[:early_rows]
                    late_out[:, span] = narrow[early_rows:]
                second = narrow.astype(jnp.float32)
                wave = psi_in[at, :, span].astype(jnp.float32)
                sigma_one = weight * wave + off_in[at, :, span].astype(jnp.float32)
                sums[0] += fold(wave * second)
                sums[1] += fold(own * sigma_one)
                sums[2] += fold(own * second)
        return tuple(sums)

    sums = list(lax.fori_loop(0, sectors // step, column, (zero,) * (2 if first else 3)))
    if first:
        far_weight = (parts[0] + parts[1]).astype(jnp.float32)
        sums[1] += weight_own[...] + (far_weight[0:8] + far_weight[16:24] + far_weight[32:40])
    stats_out[...] = jnp.zeros_like(stats_out)
    for at, value in enumerate(sums):
        stats_out[at : at + 1, :] = jnp.sum(value, axis=0, keepdims=True)
    if not first:
        stats_out[3:5, :] = stats_in[0:2, :]


def operate(first, plan, pieces, cols, pattern, right, left, extra):
    _, table, block, _ = right.shape
    width = pieces[0].shape[2]
    sectors = width // block
    links = table // sectors
    rows = jax.ShapeDtypeStruct((2, block, width), jnp.bfloat16)
    one = jax.ShapeDtypeStruct((block, width), jnp.bfloat16)
    some = jax.ShapeDtypeStruct((block // 2, width), jnp.bfloat16)
    stats = jax.ShapeDtypeStruct((8, LANES), jnp.float32)
    out_shape = (rows, rows, stats) if first else (one, some, some, stats)
    extra_specs = [VMEM] if first else [ANY, ANY, VMEM, VMEM, VMEM]
    copies = sum(len(offsets) for offsets in plan) + 9
    inner = 2 * 2 * sectors * 2 * links * links * block * block * block
    outer = 2 * 2 * 2 * links * block * block * width
    return pl.pallas_call(
        functools.partial(operate_kernel, first, plan),
        out_shape=out_shape,
        in_specs=[SMEM, SMEM] + [ANY] * (3 + len(pieces)) + extra_specs,
        out_specs=(VMEM,) * len(out_shape),
        scratch_shapes=[
            pltpu.VMEM((sectors, block, width), jnp.bfloat16),
            pltpu.VMEM((2, 2 * links * block, width), jnp.bfloat16),
            pltpu.VMEM((2, table, block, block), jnp.bfloat16),
            pltpu.VMEM((2, 2 * links, block, block), jnp.bfloat16),
            pltpu.VMEM((2, block, width), jnp.bfloat16),
            pltpu.VMEM((2, 48, LANES), jnp.bfloat16),
            pltpu.SemaphoreType.DMA((copies,)),
        ],
        compiler_params=pltpu.CompilerParams(vmem_limit_bytes=VMEM_LIMIT),
        cost_estimate=pl.CostEstimate(
            flops=inner + outer if first else 0,
            bytes_accessed=16 * 1024 * 1024 if first else 1024,
            transcendentals=0,
        ),
        name="operate_first" if first else "operate_second",
    )(cols, pattern, right, *left, *pieces, *extra)


def arrange_kernel(own, near, far, out, found, sems):
    _, _, c = place()
    part = far.shape[0]
    copies = [
        pltpu.make_async_copy(own, found.at[0], sems.at[0]),
        pltpu.make_async_copy(near.at[pl.ds(0, part)], found.at[1, pl.ds(c * part, part)], sems.at[1]),
        pltpu.make_async_copy(far, found.at[1, pl.ds((1 - c) * part, part)], sems.at[2]),
    ]
    for copy in copies:
        copy.start()
    for copy in copies:
        copy.wait()

    def turn(at, carry):
        for term in range(2):
            out[term, at] = found[term, at].T
        return carry

    lax.fori_loop(0, found.shape[1], turn, 0, unroll=4)


def arrange(own, near, far):
    shape = (2, *own.shape)
    return pl.pallas_call(
        arrange_kernel,
        out_shape=jax.ShapeDtypeStruct(shape, own.dtype),
        in_specs=[ANY] * 3,
        out_specs=VMEM,
        scratch_shapes=[pltpu.VMEM(shape, own.dtype), pltpu.SemaphoreType.DMA((3,))],
        compiler_params=pltpu.CompilerParams(vmem_limit_bytes=VMEM_LIMIT),
        name="arrange",
    )(own, near, far)


def prepare_kernel(pattern, theta, hd, right, left, mix_a, mix_b, packed, own_out, waves, diag, sems):
    z, x, c = place()
    half = z // 2
    middle = in_middle(z)
    mine = 4 * z + 2 * c + x
    block, width = diag.shape
    sectors = width // block
    links = right.shape[0] // sectors
    part = right.shape[0] // 2
    root_a = jnp.where(middle, half, 1 - half)
    rows = pl.ds(0, width)
    sources = (
        (theta.at[half, x], waves.at[0]),
        (theta.at[1 - half, x], waves.at[1]),
        (hd.at[x], diag),
        (theta.at[root_a, jnp.where(middle, 0, x)], mix_a.at[:, rows]),
        (theta.at[1 - root_a, jnp.where(middle, x, 0)], mix_b.at[:, rows]),
        (right.at[pl.ds(c * part, part)], packed.at[pl.ds(0, part)]),
        (left.at[pl.ds((mine ^ 1) * links, links)], packed.at[pl.ds(part, links)]),
        (left.at[pl.ds((mine ^ 13) * links, links)], packed.at[pl.ds(part + links, links)]),
    )
    copies = [
        pltpu.make_async_copy(source, target, sems.at[at])
        for at, (source, target) in enumerate(sources)
    ]
    for copy in copies:
        copy.start()
    for copy in copies[:3]:
        copy.wait()
    zero = jnp.zeros((8, LANES), jnp.float32)

    def column(q, sums):
        span = pl.ds(pl.multiple_of(q * block, block), block)
        weight = diag[:, span].astype(jnp.float32)
        weight = jnp.where(pattern[mine, q] != 0, weight, jnp.zeros_like(weight))
        found = []
        for root in range(2):
            wave = waves[root, :, span].astype(jnp.float32)
            found.append(sums[root] + fold(weight * wave * wave))
        return tuple(found)

    near, far = lax.fori_loop(0, sectors, column, (zero, zero), unroll=4)
    own_out[...] = near
    left_over = jnp.concatenate([far, zero], axis=0)
    parts = []
    for _ in range(3):
        piece = left_over.astype(jnp.bfloat16)
        parts.append(piece)
        left_over = left_over - piece.astype(jnp.float32)
    parts.append(jnp.zeros((block - 48, LANES), jnp.bfloat16))
    tail = jnp.concatenate(parts, axis=0)
    none = jnp.zeros_like(tail)
    mix_a[:, width:] = jnp.where(middle, none, tail)
    mix_b[:, width:] = jnp.where(middle, tail, none)
    for copy in copies[3:]:
        copy.wait()


def prepare(pattern, theta, hd, right, left):
    _, _, block, width = theta.shape
    table = right.shape[0]
    links = table * block // width
    kind = jnp.bfloat16
    mix = jax.ShapeDtypeStruct((block, width + LANES), kind)
    packed = jax.ShapeDtypeStruct((table // 2 + 2 * links, block, block), kind)
    return pl.pallas_call(
        prepare_kernel,
        out_shape=(mix, mix, packed, jax.ShapeDtypeStruct((8, LANES), jnp.float32)),
        in_specs=[SMEM, ANY, ANY, ANY, ANY],
        out_specs=(VMEM,) * 4,
        scratch_shapes=[
            pltpu.VMEM((2, block, width), kind),
            pltpu.VMEM((block, width), kind),
            pltpu.SemaphoreType.DMA((8,)),
        ],
        compiler_params=pltpu.CompilerParams(vmem_limit_bytes=VMEM_LIMIT),
        name="prepare",
    )(pattern, theta, hd, right, left)


def total_of(rows):
    return jnp.sum(rows, axis=1, keepdims=True)


def update_kernel(psi, off, hd_own, hd_far, *refs):
    stats, (t_out, stats_out, diag, sems) = refs[:4], refs[4:]
    z, x, c = place()
    copies = [
        pltpu.make_async_copy(hd_own.at[x], diag.at[0], sems.at[0]),
        pltpu.make_async_copy(hd_far, diag.at[1], sems.at[1]),
    ]
    for copy in copies:
        copy.start()
    whole = sum(ref[at, 0:2, :] for ref in stats for at in range(2))
    norm_sq, energy_sum = total_of(whole[0:1, :]), total_of(whole[1:2, :])
    energy = energy_sum / (norm_sq + 1e-06)
    mine = total_of(stats[0][0, 0:1, :])
    for copy in copies:
        copy.wait()
    _, block, width = psi.shape
    step = 16
    zero = jnp.zeros((8, LANES), jnp.float32)

    def chunk(n, total):
        span = pl.ds(pl.multiple_of(n * step, step), step)
        for at in range(2):
            wave = psi[at, span, :].astype(jnp.float32)
            weight = diag[at, span, :].astype(jnp.float32)
            sigma = weight * wave + off[at, span, :].astype(jnp.float32)
            shifted = weight - energy
            t = (sigma - energy * wave) * shifted / (shifted * shifted + 1.0)
            t_out[at, span, :] = t
            total = total + fold(wave * t)
        return total

    lanes = jnp.sum(lax.fori_loop(0, block // step, chunk, zero), axis=0, keepdims=True)
    correlation = total_of(lanes)
    local = jnp.where(mine > 0.0, correlation / jnp.where(mine > 0.0, mine, 1.0), 0.0)

    def within(n, total):
        span = pl.ds(pl.multiple_of(n * step, step), step)
        for at in range(2):
            rest = t_out[at, span, :] - local * psi[at, span, :].astype(jnp.float32)
            total = total + fold(rest * rest)
        return total

    spread = jnp.sum(lax.fori_loop(0, block // step, within, zero), axis=0, keepdims=True)
    stats_out[...] = jnp.zeros_like(stats_out)
    stats_out[0:1, :] = jnp.broadcast_to(correlation, (1, LANES))
    stats_out[1:2, :] = jnp.broadcast_to(total_of(spread), (1, LANES))
    stats_out[2:3, :] = jnp.broadcast_to(mine, (1, LANES))
    stats_out[3:4, :] = jnp.broadcast_to(local, (1, LANES))
    stats_out[4:5, :] = jnp.broadcast_to(norm_sq, (1, LANES))


def correct_kernel(psi, t, *refs):
    stats, outs = refs[:4], refs[4:]
    stats = [ref.at[at] for ref in stats for at in range(2)]
    norm_sq = stats[0][4:5, 0:1]
    factor = sum(ref[0:1, 0:1] for ref in stats) / (norm_sq + 1e-06)
    length_sq = jnp.zeros((1, 1), jnp.float32)
    for ref in stats:
        gap = factor - ref[3:4, 0:1]
        length_sq = length_sq + (ref[1:2, 0:1] + gap * gap * ref[2:3, 0:1])
    scale = jnp.sqrt(norm_sq / (length_sq + 1e-06))
    _, block, width = psi.shape
    step = 16

    def chunk(n, carry):
        span = pl.ds(pl.multiple_of(n * step, step), step)
        for at in range(2):
            wave = psi[at, span, :].astype(jnp.float32)
            outs[at][span, :] = ((t[at, span, :] - factor * wave) * scale).astype(jnp.bfloat16)
        return carry

    lax.fori_loop(0, block // step, chunk, 0)


def assemble_kernel(places, based, *refs):
    count = len(places)
    pieces, (out, sems) = refs[:count], refs[count + based :]
    z, x, c = place()
    half = z // 2
    copies = []
    for at, (root, flip, start) in enumerate(places):
        size = pieces[at].shape[0]
        target = out.at[half ^ root, x ^ flip, pl.ds(start, size)]
        copies.append(pltpu.make_async_copy(pieces[at], target, sems.at[at]))
    for copy in copies:
        copy.start()
    for copy in copies:
        copy.wait()


def assemble(block, pieces, places, base=None):
    width = pieces[0].shape[1]
    based = [] if base is None else [base]
    return pl.pallas_call(
        functools.partial(assemble_kernel, places, len(based)),
        out_shape=jax.ShapeDtypeStruct((2, 2, block, width), pieces[0].dtype),
        in_specs=[VMEM] * len(pieces) + [ANY] * len(based),
        out_specs=ANY,
        scratch_shapes=[pltpu.SemaphoreType.DMA((len(pieces),))],
        input_output_aliases={len(pieces): 0} if based else {},
        compiler_params=pltpu.CompilerParams(vmem_limit_bytes=VMEM_LIMIT),
        name="assemble",
    )(*pieces, *based)


def after(value, *others):
    return lax.optimization_barrier((value, *others))[0]


def shards(theta, hdiag, pattern, left_blocks, left_cols, right_blocks, right_cols):
    roots, row_count, width = theta.shape
    sectors = pattern.shape[0]
    block = width // sectors
    z, x, c = place()
    half = z // 2
    mine = 4 * z + 2 * c + x

    halves = theta.reshape(roots, 2, block, width)
    diag = hdiag.reshape(2, block, width)
    chunk = block // 2
    middle = in_middle(z)
    right = right_blocks.reshape(-1, block, block)
    left = left_blocks.reshape(-1, block, block)
    cols = jnp.concatenate([right_cols.reshape(-1), left_cols.reshape(-1)])

    mix_a, mix_b, packed, weight_own = prepare(pattern, halves, diag, right, left)
    mix_a = lax.ppermute(mix_a, "blk", [(0, 2), (2, 3), (3, 1), (1, 0)])
    mix_b = lax.ppermute(mix_b, "blk", [(0, 1), (1, 3), (3, 2), (2, 0)])
    operators = across(packed, "ops", 1)
    theta_core = across(theta, "sub", 1)

    mix_a, mix_b = after((mix_a, mix_b), theta_core)
    far = jnp.where(middle, mix_a[:, :width], mix_b[:, :width])
    far_z = [across(far[at : at + chunk], "blk", 1) for at in (0, chunk)]
    far_x = across(far, "ops", 1)
    mix_a_core = across(mix_a, "sub", 1)
    mix_b_core = across(mix_b, "sub", 1)

    own_b = lax.dynamic_slice(halves, (half, 1, 0, 0), (1, 1, block, width))[0, 0]
    near_b = across(after(own_b, far_z[0], mix_a_core, mix_b_core), "blk", 1)
    far_zx = [across(value, "ops", 1) for value in far_z]
    cols_other = across(after(cols, mix_a_core, mix_b_core), "ops", 1)
    cols = jnp.concatenate([cols, cols_other])
    operators_core = across(after(operators, far_z[0])[: right.shape[0] // 2], "sub", 1)
    far_x_core = across(far_x, "sub", 1)
    far_z_core = [across(value, "sub", 1) for value in far_z]
    hd_far = lax.dynamic_index_in_dim(diag, x, 0, keepdims=False)
    hd_far = across(after(hd_far, far_z[1]), "blk", 3)
    far_zx_core = [across(value, "sub", 1) for value in far_zx]
    near_b_core = across(near_b, "sub", 1)

    turned = arrange(right, operators, operators_core)
    left = (left, operators)
    pieces = [halves.reshape(4, block, width), theta_core.reshape(4, block, width)]
    plan = [
        ((0, 2, 0, 0, block), (0, 3, 0, 0, block)),
        ((0, 2, 1, 0, block), (0, 3, 1, 0, block)),
    ]
    for piece, offset in (
        (mix_a, (MIX_A, 0, 0)),
        (mix_b, (MIX_B, 0, 0)),
        (mix_a_core, (MIX_A, 0, 1)),
        (mix_b_core, (MIX_B, 0, 1)),
        (near_b, (1, 3, 0)),
        (near_b_core, (1, 3, 1)),
        (far_x, (2, 1, 0)),
        (far_x_core, (2, 1, 1)),
    ):
        pieces.append(piece[None])
        plan.append((offset + (0, block),))
    for at in range(2):
        for piece, offset in (
            (far_z[at], (3, 0, 0)),
            (far_z_core[at], (3, 0, 1)),
            (far_zx[at], (3, 1, 0)),
            (far_zx_core[at], (3, 1, 1)),
        ):
            pieces.append(piece[None])
            plan.append((offset + (at * chunk, chunk),))
    psi, off_one, stats_one = operate(
        True, tuple(plan), pieces, cols, pattern, turned, left, (weight_own,)
    )

    found = share(stats_one)
    t, stats_two = pl.pallas_call(
        update_kernel,
        out_shape=(
            jax.ShapeDtypeStruct((2, block, width), jnp.float32),
            jax.ShapeDtypeStruct((8, LANES), jnp.float32),
        ),
        in_specs=[VMEM, VMEM, ANY, ANY] + [VMEM] * 4,
        out_specs=(VMEM, VMEM),
        scratch_shapes=[
            pltpu.VMEM((2, block, width), jnp.bfloat16),
            pltpu.SemaphoreType.DMA((2,)),
        ],
        compiler_params=pltpu.CompilerParams(vmem_limit_bytes=VMEM_LIMIT),
        name="update",
    )(psi, off_one, diag, hd_far, *found)
    found = share(stats_two)
    one = jax.ShapeDtypeStruct((block, width), jnp.bfloat16)
    changed_near, changed_far = pl.pallas_call(
        correct_kernel,
        out_shape=(one, one),
        in_specs=[VMEM, VMEM] + [VMEM] * 4,
        out_specs=(VMEM, VMEM),
        compiler_params=pltpu.CompilerParams(vmem_limit_bytes=VMEM_LIMIT),
        name="correct",
    )(psi, t, *found)

    near_z = across(changed_near, "blk", 1)
    far_x = across(changed_far, "ops", 1)
    near_core = across(changed_near, "sub", 1)
    far_core = across(changed_far, "sub", 1)
    other_middle = lax.ppermute(changed_far, "blk", [(1, 2), (2, 1)])
    near_z, far_x = after((near_z, far_x), other_middle)
    near_zx = across(near_z, "ops", 1)
    far_xz = across(far_x, "blk", 1)
    near_x = across(after(changed_near, near_z, far_x), "ops", 1)
    far_z = across(after(changed_far, near_z, far_x), "blk", 1)
    near_z_core = across(near_z, "sub", 1)
    far_x_core = across(far_x, "sub", 1)
    near_x_core = across(near_x, "sub", 1)
    far_z_core = across(far_z, "sub", 1)
    near_zx_core = across(near_zx, "sub", 1)
    far_xz_core = across(far_xz, "sub", 1)
    other_end = lax.ppermute(after(changed_far, near_z, far_x), "blk", [(0, 3), (3, 0)])
    pieces, plan = [], []
    for piece, offset in (
        (changed_near, (0, 0, 0)),
        (changed_far, (3, 0, 0)),
        (near_core, (0, 0, 1)),
        (far_core, (3, 0, 1)),
        (near_z, (1, 0, 0)),
        (far_z, (2, 0, 0)),
        (near_z_core, (1, 0, 1)),
        (far_z_core, (2, 0, 1)),
        (near_x, (0, 1, 0)),
        (far_x, (3, 1, 0)),
        (near_x_core, (0, 1, 1)),
        (far_x_core, (3, 1, 1)),
        (near_zx, (1, 1, 0)),
        (far_xz, (2, 1, 0)),
        (near_zx_core, (1, 1, 1)),
        (far_xz_core, (2, 1, 1)),
    ):
        pieces.append(piece[None])
        plan.append((offset + (0, block),))
    two_near, two_far, two_late, stats_three = operate(
        False, tuple(plan), pieces, cols, pattern, turned, left, (diag, hd_far, psi, off_one, stats_one)
    )

    other = jnp.where(middle, other_middle, other_end)
    far_in = across(two_far, "blk", 3)
    near_in = across(two_near, "ops", 1)
    late_in = across(after(two_late, far_in), "blk", 3)
    other_x = across(other, "ops", 1)
    far_in_x = across(after(far_in, near_in), "ops", 1)
    late_in_x = across(after(late_in, other_x, far_in_x), "ops", 1)
    sums = stats_three + across(stats_three, "sub", 1)
    sums = sums + across(sums, "blk", 1)
    both = jnp.stack([sums, across(sums, "blk", 2)])
    both = both + across(after(both, near_in), "ops", 1)
    both = jnp.sum(jnp.where(half == 0, both, both[::-1])[:, :5], axis=2)
    scale = both[:, 3:4] + 1e-06
    subspace = jnp.concatenate([both[:, 4:5], both[:, 0:3]], axis=1) / scale
    places = ((0, 0, 0), (0, 1, 0), (1, 0, 0), (1, 1, 0))
    correction = assemble(block, (changed_near, near_x, other, other_x), places)
    places = ((0, 0, 0), (0, 1, 0), (1, 0, 0), (1, 0, block // 2), (1, 1, 0))
    sigma_two = assemble(block, (two_near, near_in, far_in, late_in, far_in_x), places)
    sigma_two = assemble(block, (late_in_x,), ((1, 1, block // 2),), sigma_two)
    return correction.reshape(theta.shape), sigma_two.reshape(theta.shape), subspace


def solution(mesh):
    in_specs = (
        P("groups", ("blk", "sub"), None),
        P(("groups", "blk", "sub"), None),
        P("groups", None),
        P(("groups", "ops"), None, None, None, None),
        P(("groups", "ops"), None, None),
        P(("groups", "ops"), None, None, None, None),
        P(("groups", "ops"), None, None),
    )
    out_specs = (
        P("groups", ("blk", "sub"), None),
        P("groups", ("blk", "sub"), None),
        P("groups", None),
    )
    body = shards if halves_fit(mesh) else general_shards
    return jax.shard_map(body, mesh=mesh, in_specs=in_specs, out_specs=out_specs, check_vma=False)
```

```python
import functools

import jax
import jax.numpy as jnp
from jax import lax
from jax.experimental import pallas as pl
from jax.experimental.pallas import tpu as pltpu
from jax.sharding import PartitionSpec as P

ANY = pl.BlockSpec(memory_space=pl.ANY)
SMEM = pl.BlockSpec(memory_space=pltpu.SMEM)
VMEM = pl.BlockSpec(memory_space=pltpu.VMEM)
VMEM_LIMIT = 24 * 1024 * 1024
OPERATE_LIMIT = 44 * 1024 * 1024
LANES = 128


def apply_right(field_in, blocks, columns):
    roots_here, row_count, full_width = field_in.shape
    term_count, sectors, link_count = columns.shape
    block_size = full_width // sectors
    grouped = field_in.reshape(roots_here, row_count, sectors, block_size)
    picked = jnp.take(grouped, columns.reshape(-1), axis=2)
    picked = picked.reshape(roots_here, row_count, term_count, sectors, link_count, block_size)
    product = jnp.einsum("nrkbjq,kbjpq->knrbp", picked, blocks, preferred_element_type=jnp.float32)
    return product.reshape(term_count, roots_here, row_count, full_width).astype(jnp.bfloat16)


def take_rows(stacked, indices):
    return jnp.take(stacked, indices, axis=1)


def apply_left(arrived, blocks, columns):
    term_count, roots_here, full_width, col_count = arrived.shape
    sectors = columns.shape[1]
    link_count = columns.shape[2]
    block_size = full_width // sectors
    grouped = arrived.reshape(term_count, roots_here, sectors, block_size, col_count)
    picked = jax.vmap(take_rows)(grouped, columns.reshape(term_count, sectors * link_count))
    picked = picked.reshape(term_count, roots_here, sectors, link_count, block_size, col_count)
    product = jnp.einsum("kajpq,knajqc->napc", blocks, picked, preferred_element_type=jnp.float32)
    return product.reshape(roots_here, full_width, col_count)


def general_shards(theta, hdiag, pattern, left_blocks, left_cols, right_blocks, right_cols):
    roots_here, row_count, full_width = theta.shape
    sectors = pattern.shape[0]
    block_size = full_width // sectors
    first_row = lax.axis_index(("blk", "sub")) * row_count
    block_row = (first_row + jnp.arange(row_count, dtype=jnp.int32)) // block_size
    onehot = (block_row[:, None] == jnp.arange(sectors, dtype=jnp.int32)[None, :]).astype(
        jnp.float32
    )
    row_pattern = jnp.dot(onehot, pattern.astype(jnp.float32), preferred_element_type=jnp.float32)
    allowed = jnp.broadcast_to(row_pattern[:, :, None], (row_count, sectors, block_size))
    allowed = allowed.reshape(row_count, full_width).astype(jnp.bfloat16)
    diagonal = hdiag.astype(jnp.float32)
    peers = lax.axis_size("blk") * lax.axis_size("sub")

    def left_part(arrived):
        return apply_left(arrived, left_blocks, left_cols)

    def operate(field_in):
        images = apply_right(field_in, right_blocks, right_cols)
        partial_sum = left_part(
            lax.all_to_all(images, ("blk", "sub"), split_axis=3, concat_axis=2, tiled=True)
        )
        shares = lax.psum_scatter(partial_sum, "ops", scatter_dimension=2, tiled=True)
        returned = lax.all_to_all(
            shares.astype(jnp.bfloat16), ("blk", "sub"), split_axis=1, concat_axis=2, tiled=True
        )
        gathered = lax.all_gather(returned, "ops", axis=2, tiled=True)
        narrow = returned.shape[2] // peers
        gathered = gathered.reshape(roots_here, row_count, lax.axis_size("ops"), peers, narrow)
        offdiag = gathered.transpose(0, 1, 3, 2, 4).reshape(roots_here, row_count, full_width)
        offdiag = offdiag * allowed[None]
        return diagonal[None] * field_in.astype(jnp.float32) + offdiag.astype(jnp.float32)

    projected = theta * allowed[None]
    wave = projected.astype(jnp.float32)
    sigma_one = operate(projected)
    norm_sq, energy_sum = lax.psum(
        (jnp.sum(wave * wave, axis=(1, 2)), jnp.sum(wave * sigma_one, axis=(1, 2))), ("blk", "sub")
    )
    denominator = norm_sq + 1e-06
    energy = energy_sum / denominator
    shifted = diagonal[None] - energy[:, None, None]
    update = (sigma_one - energy[:, None, None] * wave) * shifted / (shifted * shifted + 1.0)
    correlation = lax.psum(jnp.sum(wave * update, axis=(1, 2)), ("blk", "sub"))
    factor = correlation / denominator
    orthogonal = update - factor[:, None, None] * wave
    length_sq = lax.psum(jnp.sum(orthogonal * orthogonal, axis=(1, 2)), ("blk", "sub"))
    correction = (orthogonal * jnp.sqrt(norm_sq / (length_sq + 1e-06))[:, None, None]).astype(
        jnp.bfloat16
    )
    sigma_two = operate(correction).astype(jnp.bfloat16)
    second = sigma_two.astype(jnp.float32)
    fixed = correction.astype(jnp.float32)
    cross_one, cross_two, cross_three = lax.psum(
        (
            jnp.sum(wave * second, axis=(1, 2)),
            jnp.sum(fixed * sigma_one, axis=(1, 2)),
            jnp.sum(fixed * second, axis=(1, 2)),
        ),
        ("blk", "sub"),
    )
    subspace = (
        jnp.stack([energy_sum, cross_one, cross_two, cross_three], axis=1) / denominator[:, None]
    )
    return (correction, sigma_two, subspace)


MIX_A, MIX_B = 4, 5
MIXES = ((MIX_A, 0, 0), (MIX_B, 0, 0))


def halves_fit(mesh):
    sizes = dict(mesh.shape)
    return sizes["blk"] == 4 and sizes["ops"] == 2 and sizes["sub"] == 2


def across(value, axis, distance):
    size = lax.axis_size(axis)
    return lax.ppermute(value, axis, [(i, i ^ distance) for i in range(size)])


def share(stats):
    axes = ("blk", "ops")
    count = lax.axis_size("blk") * lax.axis_size("ops")
    pair = jnp.stack([stats, across(stats, "sub", 1)])
    found = [pair]
    for distance in (1, 2, 3):
        found.append(lax.ppermute(pair, axes, [(i, i ^ distance) for i in range(count)]))
    return found


def place():
    return lax.axis_index("blk"), lax.axis_index("ops"), lax.axis_index("sub")


def fold(value):
    rows, width = value.shape
    value = jnp.sum(value.reshape(rows // 8, 8, width), axis=0)
    return sum(value[:, at : at + LANES] for at in range(0, width, LANES))


def in_middle(z):
    return jnp.logical_or(z == 1, z == 2)


def row_of(dz, dx, dc):
    z, x, c = place()
    if dz in (MIX_A, MIX_B):
        far = in_middle(z) if dz == MIX_A else jnp.logical_not(in_middle(z))
        return jnp.where(far, row_of(2, 0, dc), row_of(1, 2, dc))
    return 4 * (z ^ dz) + 2 * (c ^ dc) + (x ^ dx if dx < 2 else dx - 2)


def operate_kernel(first, plan, cols, pattern, right, left_own, left_other, *refs):
    count = len(plan)
    pieces, refs = refs[:count], refs[count:]
    if first:
        weight_own, psi_out, off_out, stats_out = refs[:4]
        refs = refs[4:]
    else:
        hd_own, hd_far, psi_in, off_in, stats_in, near_out, far_out, late_out, stats_out = refs[:9]
        refs = refs[9:]
    field, images, left, diag, sems = refs
    z, x, c = place()
    sectors, block, width = field.shape
    table = right.shape[1]
    links = table // sectors
    mine = 4 * z + 2 * c + x
    rows = (mine, mine ^ 12)
    half = z // 2

    copies = []

    def begin(source, target):
        copy = pltpu.make_async_copy(source, target, sems.at[len(copies)])
        copy.start()
        copies.append(copy)

    for at in range(2):
        begin(left_own.at[pl.ds(rows[at] * links, links)], left.at[0, pl.ds(at * links, links)])
    begin(left_other.at[pl.ds(table // 2, 2 * links)], left.at[1])
    if not first:
        begin(hd_own.at[x], diag.at[0])
        begin(hd_far, diag.at[1])

    def allowed(a, q, value):
        return jnp.where(pattern[a, q] != 0, value, jnp.zeros_like(value))

    for piece, offsets in zip(pieces, plan):
        base = 2 * half if piece.shape[0] == 4 else 0
        for at, (dz, dx, dc, start, tall) in enumerate(offsets):
            row = row_of(dz, dx, dc)
            for q in range(sectors):
                span = slice(q * block, (q + 1) * block)
                value = piece[base + at, :, span]
                field[row, start : start + tall, span] = allowed(row, q, value) if first else value

    def right_col(term, b, j):
        return cols[(2 * term) * table + b * links + j]

    def left_col(term, a, j):
        return cols[(2 * term + 1) * table + a * links + j]

    sources = [[left_col(term, rows[at], j) for at in range(2) for j in range(links)] for term in range(2)]

    deep = links * block

    none = jnp.zeros((block, block), jnp.bfloat16)
    pair = 2

    def image(n, carry):
        picks = [(i, j) for i in range(pair) for j in range(links)]
        for term in range(2):
            found = [right_col(term, n * pair + i, j) for i, j in picks]
            lhs = []
            for source in sources[term]:
                line = []
                for col in found:
                    value = field[source, :, pl.ds(pl.multiple_of(col * block, block), block)]
                    line.append(value)
                lhs.append(jnp.concatenate(line, axis=1))
            rhs = []
            for i, j in picks:
                tile = right[term, (n * pair + i) * links + j]
                rhs.append(jnp.concatenate([tile if i == at else none for at in range(pair)], axis=1))
            product = jnp.dot(
                jnp.concatenate(lhs, axis=0),
                jnp.concatenate(rhs, axis=0),
                preferred_element_type=jnp.float32,
            )
            product = product.astype(jnp.bfloat16)
            span = pl.ds(pl.multiple_of(n * pair * block, pair * block), pair * block)
            for at in range(2):
                images[at, term * deep : (term + 1) * deep, span] = product[at * deep : (at + 1) * deep]
        return carry

    lax.fori_loop(0, sectors // pair, image, 0, unroll=2)
    for copy in copies:
        copy.wait()

    step = 2
    early_rows = block // 2
    zero = jnp.zeros((8, LANES), jnp.float32)

    def column(n, sums):
        start = pl.multiple_of(n * step * block, step * block)
        span = pl.ds(start, step * block)
        sums = list(sums)

        def masked(a, value):
            parts = [
                allowed(a, n * step + i, value[:, i * block : (i + 1) * block]) for i in range(step)
            ]
            return jnp.concatenate(parts, axis=1)

        for at in range(2):
            weights = [left[term, at * links + j] for term in range(2) for j in range(links)]
            total = jnp.dot(
                jnp.concatenate(weights, axis=1),
                images[at, :, span],
                preferred_element_type=jnp.float32,
            )
            offdiag = masked(rows[at], total.astype(jnp.bfloat16).astype(jnp.float32))
            own = field[rows[at], :, span].astype(jnp.float32)
            if first:
                psi_out[at, :, span] = own.astype(jnp.bfloat16)
                off_out[at, :, span] = offdiag.astype(jnp.bfloat16)
                sums[0] += fold(own * own)
                sums[1] += fold(own * offdiag)
            else:
                weight = diag[at, :, span].astype(jnp.float32)
                narrow = (weight * own + offdiag).astype(jnp.bfloat16)
                if at == 0:
                    near_out[:, span] = narrow
                else:
                    far_out[:, span] = narrow[:early_rows]
                    late_out[:, span] = narrow[early_rows:]
                second = narrow.astype(jnp.float32)
                wave = psi_in[at, :, span].astype(jnp.float32)
                sigma_one = weight * wave + off_in[at, :, span].astype(jnp.float32)
                sums[0] += fold(wave * second)
                sums[1] += fold(own * sigma_one)
                sums[2] += fold(own * second)
        return tuple(sums)

    sums = list(lax.fori_loop(0, sectors // step, column, (zero,) * (2 if first else 3)))
    if first:
        parts = [
            piece[0, 0:48, width:] for piece, offsets in zip(pieces, plan) if offsets[0][:3] in MIXES
        ]
        far_weight = sum(part.astype(jnp.float32) for part in parts)
        sums[1] += weight_own[...] + (far_weight[0:8] + far_weight[16:24] + far_weight[32:40])
    stats_out[...] = jnp.zeros_like(stats_out)
    for at, value in enumerate(sums):
        stats_out[at : at + 1, :] = jnp.sum(value, axis=0, keepdims=True)
    if not first:
        stats_out[3:5, :] = stats_in[0:2, :]


def operate(first, plan, pieces, cols, pattern, right, left, extra):
    _, table, block, _ = right.shape
    width = pieces[0].shape[2]
    sectors = width // block
    links = table // sectors
    rows = jax.ShapeDtypeStruct((2, block, width), jnp.bfloat16)
    one = jax.ShapeDtypeStruct((block, width), jnp.bfloat16)
    some = jax.ShapeDtypeStruct((block // 2, width), jnp.bfloat16)
    stats = jax.ShapeDtypeStruct((8, LANES), jnp.float32)
    out_shape = (rows, rows, stats) if first else (one, some, some, stats)
    extra_specs = [VMEM] if first else [ANY, ANY, VMEM, VMEM, VMEM]
    inner = 2 * 2 * sectors * 2 * links * links * block * block * block
    outer = 2 * 2 * 2 * links * block * block * width
    return pl.pallas_call(
        functools.partial(operate_kernel, first, plan),
        out_shape=out_shape,
        in_specs=[SMEM, SMEM, VMEM, ANY, ANY] + [VMEM] * len(pieces) + extra_specs,
        out_specs=(VMEM,) * len(out_shape),
        scratch_shapes=[
            pltpu.VMEM((sectors, block, width), jnp.bfloat16),
            pltpu.VMEM((2, 2 * links * block, width), jnp.bfloat16),
            pltpu.VMEM((2, 2 * links, block, block), jnp.bfloat16),
            pltpu.VMEM((2, block, width), jnp.bfloat16),
            pltpu.SemaphoreType.DMA((5,)),
        ],
        compiler_params=pltpu.CompilerParams(vmem_limit_bytes=OPERATE_LIMIT),
        cost_estimate=pl.CostEstimate(
            flops=inner + outer if first else 0,
            bytes_accessed=16 * 1024 * 1024 if first else 1024,
            transcendentals=0,
        ),
        name="operate_first" if first else "operate_second",
    )(cols, pattern, right, *left, *pieces, *extra)


def arrange_kernel(own, near, far, out, found, sems):
    _, _, c = place()
    part = far.shape[0]
    copies = [
        pltpu.make_async_copy(own, found.at[0], sems.at[0]),
        pltpu.make_async_copy(near.at[pl.ds(0, part)], found.at[1, pl.ds(c * part, part)], sems.at[1]),
        pltpu.make_async_copy(far, found.at[1, pl.ds((1 - c) * part, part)], sems.at[2]),
    ]
    for copy in copies:
        copy.start()
    for copy in copies:
        copy.wait()

    def turn(at, carry):
        for term in range(2):
            out[term, at] = found[term, at].T
        return carry

    lax.fori_loop(0, found.shape[1], turn, 0, unroll=4)


def arrange(own, near, far):
    shape = (2, *own.shape)
    return pl.pallas_call(
        arrange_kernel,
        out_shape=jax.ShapeDtypeStruct(shape, own.dtype),
        in_specs=[ANY] * 3,
        out_specs=VMEM,
        scratch_shapes=[pltpu.VMEM(shape, own.dtype), pltpu.SemaphoreType.DMA((3,))],
        compiler_params=pltpu.CompilerParams(vmem_limit_bytes=VMEM_LIMIT),
        name="arrange",
    )(own, near, far)


def prepare_kernel(pattern, theta, hd, right, left, mix_a, mix_b, packed, own_out, waves, diag, sems):
    z, x, c = place()
    half = z // 2
    middle = in_middle(z)
    mine = 4 * z + 2 * c + x
    block, width = diag.shape
    sectors = width // block
    links = right.shape[0] // sectors
    part = right.shape[0] // 2
    root_a = jnp.where(middle, half, 1 - half)
    rows = pl.ds(0, width)
    sources = (
        (theta.at[half, x], waves.at[0]),
        (theta.at[1 - half, x], waves.at[1]),
        (hd.at[x], diag),
        (theta.at[root_a, jnp.where(middle, 0, x)], mix_a.at[:, rows]),
        (theta.at[1 - root_a, jnp.where(middle, x, 0)], mix_b.at[:, rows]),
        (right.at[pl.ds(c * part, part)], packed.at[pl.ds(0, part)]),
        (left.at[pl.ds((mine ^ 1) * links, links)], packed.at[pl.ds(part, links)]),
        (left.at[pl.ds((mine ^ 13) * links, links)], packed.at[pl.ds(part + links, links)]),
    )
    copies = [
        pltpu.make_async_copy(source, target, sems.at[at])
        for at, (source, target) in enumerate(sources)
    ]
    for copy in copies:
        copy.start()
    for copy in copies[:3]:
        copy.wait()
    zero = jnp.zeros((8, LANES), jnp.float32)

    def column(q, sums):
        span = pl.ds(pl.multiple_of(q * block, block), block)
        weight = diag[:, span].astype(jnp.float32)
        weight = jnp.where(pattern[mine, q] != 0, weight, jnp.zeros_like(weight))
        found = []
        for root in range(2):
            wave = waves[root, :, span].astype(jnp.float32)
            found.append(sums[root] + fold(weight * wave * wave))
        return tuple(found)

    near, far = lax.fori_loop(0, sectors, column, (zero, zero), unroll=4)
    own_out[...] = near
    left_over = jnp.concatenate([far, zero], axis=0)
    parts = []
    for _ in range(3):
        piece = left_over.astype(jnp.bfloat16)
        parts.append(piece)
        left_over = left_over - piece.astype(jnp.float32)
    parts.append(jnp.zeros((block - 48, LANES), jnp.bfloat16))
    tail = jnp.concatenate(parts, axis=0)
    none = jnp.zeros_like(tail)
    mix_a[:, width:] = jnp.where(middle, none, tail)
    mix_b[:, width:] = jnp.where(middle, tail, none)
    for copy in copies[3:]:
        copy.wait()


def prepare(pattern, theta, hd, right, left):
    _, _, block, width = theta.shape
    table = right.shape[0]
    links = table * block // width
    kind = jnp.bfloat16
    mix = jax.ShapeDtypeStruct((block, width + LANES), kind)
    packed = jax.ShapeDtypeStruct((table // 2 + 2 * links, block, block), kind)
    return pl.pallas_call(
        prepare_kernel,
        out_shape=(mix, mix, packed, jax.ShapeDtypeStruct((8, LANES), jnp.float32)),
        in_specs=[SMEM, ANY, ANY, ANY, ANY],
        out_specs=(VMEM,) * 4,
        scratch_shapes=[
            pltpu.VMEM((2, block, width), kind),
            pltpu.VMEM((block, width), kind),
            pltpu.SemaphoreType.DMA((8,)),
        ],
        compiler_params=pltpu.CompilerParams(vmem_limit_bytes=VMEM_LIMIT),
        name="prepare",
    )(pattern, theta, hd, right, left)


def total_of(rows):
    return jnp.sum(rows, axis=1, keepdims=True)


def update_kernel(psi, off, hd_own, hd_far, *refs):
    stats, (t_out, stats_out, diag, sems) = refs[:4], refs[4:]
    z, x, c = place()
    copies = [
        pltpu.make_async_copy(hd_own.at[x], diag.at[0], sems.at[0]),
        pltpu.make_async_copy(hd_far, diag.at[1], sems.at[1]),
    ]
    for copy in copies:
        copy.start()
    whole = sum(ref[at, 0:2, :] for ref in stats for at in range(2))
    norm_sq, energy_sum = total_of(whole[0:1, :]), total_of(whole[1:2, :])
    energy = energy_sum / (norm_sq + 1e-06)
    mine = total_of(stats[0][0, 0:1, :])
    for copy in copies:
        copy.wait()
    _, block, width = psi.shape
    step = 16
    zero = jnp.zeros((8, LANES), jnp.float32)

    def chunk(n, total):
        span = pl.ds(pl.multiple_of(n * step, step), step)
        for at in range(2):
            wave = psi[at, span, :].astype(jnp.float32)
            weight = diag[at, span, :].astype(jnp.float32)
            sigma = weight * wave + off[at, span, :].astype(jnp.float32)
            shifted = weight - energy
            t = (sigma - energy * wave) * shifted / (shifted * shifted + 1.0)
            t_out[at, span, :] = t
            total = total + fold(wave * t)
        return total

    lanes = jnp.sum(lax.fori_loop(0, block // step, chunk, zero), axis=0, keepdims=True)
    correlation = total_of(lanes)
    local = jnp.where(mine > 0.0, correlation / jnp.where(mine > 0.0, mine, 1.0), 0.0)

    def within(n, total):
        span = pl.ds(pl.multiple_of(n * step, step), step)
        for at in range(2):
            rest = t_out[at, span, :] - local * psi[at, span, :].astype(jnp.float32)
            total = total + fold(rest * rest)
        return total

    spread = jnp.sum(lax.fori_loop(0, block // step, within, zero), axis=0, keepdims=True)
    stats_out[...] = jnp.zeros_like(stats_out)
    stats_out[0:1, :] = jnp.broadcast_to(correlation, (1, LANES))
    stats_out[1:2, :] = jnp.broadcast_to(total_of(spread), (1, LANES))
    stats_out[2:3, :] = jnp.broadcast_to(mine, (1, LANES))
    stats_out[3:4, :] = jnp.broadcast_to(local, (1, LANES))
    stats_out[4:5, :] = jnp.broadcast_to(norm_sq, (1, LANES))


def correct_kernel(psi, t, *refs):
    stats, outs = refs[:4], refs[4:]
    stats = [ref.at[at] for ref in stats for at in range(2)]
    norm_sq = stats[0][4:5, 0:1]
    factor = sum(ref[0:1, 0:1] for ref in stats) / (norm_sq + 1e-06)
    length_sq = jnp.zeros((1, 1), jnp.float32)
    for ref in stats:
        gap = factor - ref[3:4, 0:1]
        length_sq = length_sq + (ref[1:2, 0:1] + gap * gap * ref[2:3, 0:1])
    scale = jnp.sqrt(norm_sq / (length_sq + 1e-06))
    _, block, width = psi.shape
    step = 16

    def chunk(n, carry):
        span = pl.ds(pl.multiple_of(n * step, step), step)
        for at in range(2):
            wave = psi[at, span, :].astype(jnp.float32)
            outs[at][span, :] = ((t[at, span, :] - factor * wave) * scale).astype(jnp.bfloat16)
        return carry

    lax.fori_loop(0, block // step, chunk, 0)


def assemble_kernel(places, based, *refs):
    count = len(places)
    pieces, (out, sems) = refs[:count], refs[count + based :]
    z, x, c = place()
    half = z // 2
    copies = []
    for at, (root, flip, start) in enumerate(places):
        size = pieces[at].shape[0]
        target = out.at[half ^ root, x ^ flip, pl.ds(start, size)]
        copies.append(pltpu.make_async_copy(pieces[at], target, sems.at[at]))
    for copy in copies:
        copy.start()
    for copy in copies:
        copy.wait()


def assemble(block, pieces, places, base=None):
    width = pieces[0].shape[1]
    based = [] if base is None else [base]
    return pl.pallas_call(
        functools.partial(assemble_kernel, places, len(based)),
        out_shape=jax.ShapeDtypeStruct((2, 2, block, width), pieces[0].dtype),
        in_specs=[VMEM] * len(pieces) + [ANY] * len(based),
        out_specs=ANY,
        scratch_shapes=[pltpu.SemaphoreType.DMA((len(pieces),))],
        input_output_aliases={len(pieces): 0} if based else {},
        compiler_params=pltpu.CompilerParams(vmem_limit_bytes=VMEM_LIMIT),
        name="assemble",
    )(*pieces, *based)


def after(value, *others):
    return lax.optimization_barrier((value, *others))[0]


def shards(theta, hdiag, pattern, left_blocks, left_cols, right_blocks, right_cols):
    roots, row_count, width = theta.shape
    sectors = pattern.shape[0]
    block = width // sectors
    z, x, c = place()
    half = z // 2
    mine = 4 * z + 2 * c + x

    halves = theta.reshape(roots, 2, block, width)
    diag = hdiag.reshape(2, block, width)
    chunk = block // 2
    middle = in_middle(z)
    right = right_blocks.reshape(-1, block, block)
    left = left_blocks.reshape(-1, block, block)
    cols = jnp.concatenate([right_cols.reshape(-1), left_cols.reshape(-1)])

    mix_a, mix_b, packed, weight_own = prepare(pattern, halves, diag, right, left)
    mix_a = lax.ppermute(mix_a, "blk", [(0, 2), (2, 3), (3, 1), (1, 0)])
    mix_b = lax.ppermute(mix_b, "blk", [(0, 1), (1, 3), (3, 2), (2, 0)])
    operators = across(packed, "ops", 1)
    theta_core = across(theta, "sub", 1)

    cols_other = across(after(cols, mix_a), "ops", 1)
    cols = jnp.concatenate([cols, cols_other])
    mix_a_core = across(mix_a, "sub", 1)
    operators_core = across(after(operators, cols_other)[: right.shape[0] // 2], "sub", 1)

    mix_b = after(mix_b, theta_core, mix_a_core, operators_core)
    far = jnp.where(middle, mix_a[:, :width], mix_b[:, :width])
    far_z = [across(far[at : at + chunk], "blk", 1) for at in (0, chunk)]
    far_x = across(far, "ops", 1)
    mix_b_core = across(mix_b, "sub", 1)
    turned = arrange(right, operators, operators_core)

    own_b = lax.dynamic_slice(halves, (half, 1, 0, 0), (1, 1, block, width))[0, 0]
    near_b = across(after(own_b, far_z[0], mix_b_core, turned), "blk", 1)
    far_zx = [across(value, "ops", 1) for value in far_z]
    far_x_core = across(far_x, "sub", 1)
    far_z_core = [across(value, "sub", 1) for value in far_z]
    hd_far = lax.dynamic_index_in_dim(diag, x, 0, keepdims=False)
    hd_far = across(after(hd_far, far_z[1]), "blk", 3)
    far_zx_core = [across(value, "sub", 1) for value in far_zx]
    near_b_core = across(near_b, "sub", 1)

    left = (left, operators)
    pieces = [halves.reshape(4, block, width), theta_core.reshape(4, block, width)]
    plan = [
        ((0, 2, 0, 0, block), (0, 3, 0, 0, block)),
        ((0, 2, 1, 0, block), (0, 3, 1, 0, block)),
    ]
    for piece, offset in (
        (mix_a, (MIX_A, 0, 0)),
        (mix_b, (MIX_B, 0, 0)),
        (mix_a_core, (MIX_A, 0, 1)),
        (mix_b_core, (MIX_B, 0, 1)),
        (near_b, (1, 3, 0)),
        (near_b_core, (1, 3, 1)),
        (far_x, (2, 1, 0)),
        (far_x_core, (2, 1, 1)),
    ):
        pieces.append(piece[None])
        plan.append((offset + (0, block),))
    for at in range(2):
        for piece, offset in (
            (far_z[at], (3, 0, 0)),
            (far_z_core[at], (3, 0, 1)),
            (far_zx[at], (3, 1, 0)),
            (far_zx_core[at], (3, 1, 1)),
        ):
            pieces.append(piece[None])
            plan.append((offset + (at * chunk, chunk),))
    psi, off_one, stats_one = operate(
        True, tuple(plan), pieces, cols, pattern, turned, left, (weight_own,)
    )

    found = share(stats_one)
    t, stats_two = pl.pallas_call(
        update_kernel,
        out_shape=(
            jax.ShapeDtypeStruct((2, block, width), jnp.float32),
            jax.ShapeDtypeStruct((8, LANES), jnp.float32),
        ),
        in_specs=[VMEM, VMEM, ANY, ANY] + [VMEM] * 4,
        out_specs=(VMEM, VMEM),
        scratch_shapes=[
            pltpu.VMEM((2, block, width), jnp.bfloat16),
            pltpu.SemaphoreType.DMA((2,)),
        ],
        compiler_params=pltpu.CompilerParams(vmem_limit_bytes=VMEM_LIMIT),
        name="update",
    )(psi, off_one, diag, hd_far, *found)
    found = share(stats_two)
    one = jax.ShapeDtypeStruct((block, width), jnp.bfloat16)
    changed_near, changed_far = pl.pallas_call(
        correct_kernel,
        out_shape=(one, one),
        in_specs=[VMEM, VMEM] + [VMEM] * 4,
        out_specs=(VMEM, VMEM),
        compiler_params=pltpu.CompilerParams(vmem_limit_bytes=VMEM_LIMIT),
        name="correct",
    )(psi, t, *found)

    near_z = across(changed_near, "blk", 1)
    far_x = across(changed_far, "ops", 1)
    near_core = across(changed_near, "sub", 1)
    far_core = across(changed_far, "sub", 1)
    other_middle = lax.ppermute(changed_far, "blk", [(1, 2), (2, 1)])
    near_z, far_x = after((near_z, far_x), other_middle)
    near_zx = across(near_z, "ops", 1)
    far_xz = across(far_x, "blk", 1)
    near_x = across(after(changed_near, near_z, far_x), "ops", 1)
    far_z = across(after(changed_far, near_z, far_x), "blk", 1)
    near_z_core = across(near_z, "sub", 1)
    far_x_core = across(far_x, "sub", 1)
    near_x_core = across(near_x, "sub", 1)
    far_z_core = across(far_z, "sub", 1)
    near_zx_core = across(near_zx, "sub", 1)
    far_xz_core = across(far_xz, "sub", 1)
    other_end = lax.ppermute(after(changed_far, near_z, far_x), "blk", [(0, 3), (3, 0)])
    pieces, plan = [], []
    for piece, offset in (
        (changed_near, (0, 0, 0)),
        (changed_far, (3, 0, 0)),
        (near_core, (0, 0, 1)),
        (far_core, (3, 0, 1)),
        (near_z, (1, 0, 0)),
        (far_z, (2, 0, 0)),
        (near_z_core, (1, 0, 1)),
        (far_z_core, (2, 0, 1)),
        (near_x, (0, 1, 0)),
        (far_x, (3, 1, 0)),
        (near_x_core, (0, 1, 1)),
        (far_x_core, (3, 1, 1)),
        (near_zx, (1, 1, 0)),
        (far_xz, (2, 1, 0)),
        (near_zx_core, (1, 1, 1)),
        (far_xz_core, (2, 1, 1)),
    ):
        pieces.append(piece[None])
        plan.append((offset + (0, block),))
    two_near, two_far, two_late, stats_three = operate(
        False, tuple(plan), pieces, cols, pattern, turned, left, (diag, hd_far, psi, off_one, stats_one)
    )

    far_in = across(two_far, "blk", 3)
    near_in = across(two_near, "ops", 1)
    sums = stats_three + across(stats_three, "sub", 1)
    other = jnp.where(middle, other_middle, after(other_end, sums))
    other_x = across(other, "ops", 1)
    sums = sums + across(sums, "blk", 1)
    both = jnp.stack([sums, across(sums, "blk", 2)])
    late_in = across(after(two_late, far_in), "blk", 3)
    far_in_x = across(after(far_in, near_in), "ops", 1)
    both = both + across(after(both, far_in), "ops", 1)
    other, other_x = after((other, other_x), late_in)
    late_in_x = across(late_in, "ops", 1)
    both = jnp.sum(jnp.where(half == 0, both, both[::-1])[:, :5], axis=2)
    scale = both[:, 3:4] + 1e-06
    subspace = jnp.concatenate([both[:, 4:5], both[:, 0:3]], axis=1) / scale
    places = ((0, 0, 0), (0, 1, 0), (1, 0, 0), (1, 1, 0))
    correction = assemble(block, (changed_near, near_x, other, other_x), places)
    places = ((0, 0, 0), (0, 1, 0), (1, 0, 0), (1, 0, block // 2), (1, 1, 0))
    sigma_two = assemble(block, (two_near, near_in, far_in, late_in, far_in_x), places)
    sigma_two = assemble(block, (late_in_x,), ((1, 1, block // 2),), sigma_two)
    return correction.reshape(theta.shape), sigma_two.reshape(theta.shape), subspace


def solution(mesh):
    in_specs = (
        P("groups", ("blk", "sub"), None),
        P(("groups", "blk", "sub"), None),
        P("groups", None),
        P(("groups", "ops"), None, None, None, None),
        P(("groups", "ops"), None, None),
        P(("groups", "ops"), None, None, None, None),
        P(("groups", "ops"), None, None),
    )
    out_specs = (
        P("groups", ("blk", "sub"), None),
        P("groups", ("blk", "sub"), None),
        P("groups", None),
    )
    body = shards if halves_fit(mesh) else general_shards
    return jax.shard_map(body, mesh=mesh, in_specs=in_specs, out_specs=out_specs, check_vma=False)
```

```python
import functools

import jax
import jax.numpy as jnp
from jax import lax
from jax.experimental import pallas as pl
from jax.experimental.pallas import tpu as pltpu
from jax.sharding import PartitionSpec as P

ANY = pl.BlockSpec(memory_space=pl.ANY)
SMEM = pl.BlockSpec(memory_space=pltpu.SMEM)
VMEM = pl.BlockSpec(memory_space=pltpu.VMEM)
VMEM_LIMIT = 24 * 1024 * 1024
OPERATE_LIMIT = 44 * 1024 * 1024
PREPARE_LIMIT = 56 * 1024 * 1024
LANES = 128


def apply_right(field_in, blocks, columns):
    roots_here, row_count, full_width = field_in.shape
    term_count, sectors, link_count = columns.shape
    block_size = full_width // sectors
    grouped = field_in.reshape(roots_here, row_count, sectors, block_size)
    picked = jnp.take(grouped, columns.reshape(-1), axis=2)
    picked = picked.reshape(roots_here, row_count, term_count, sectors, link_count, block_size)
    product = jnp.einsum("nrkbjq,kbjpq->knrbp", picked, blocks, preferred_element_type=jnp.float32)
    return product.reshape(term_count, roots_here, row_count, full_width).astype(jnp.bfloat16)


def take_rows(stacked, indices):
    return jnp.take(stacked, indices, axis=1)


def apply_left(arrived, blocks, columns):
    term_count, roots_here, full_width, col_count = arrived.shape
    sectors = columns.shape[1]
    link_count = columns.shape[2]
    block_size = full_width // sectors
    grouped = arrived.reshape(term_count, roots_here, sectors, block_size, col_count)
    picked = jax.vmap(take_rows)(grouped, columns.reshape(term_count, sectors * link_count))
    picked = picked.reshape(term_count, roots_here, sectors, link_count, block_size, col_count)
    product = jnp.einsum("kajpq,knajqc->napc", blocks, picked, preferred_element_type=jnp.float32)
    return product.reshape(roots_here, full_width, col_count)


def general_shards(theta, hdiag, pattern, left_blocks, left_cols, right_blocks, right_cols):
    roots_here, row_count, full_width = theta.shape
    sectors = pattern.shape[0]
    block_size = full_width // sectors
    first_row = lax.axis_index(("blk", "sub")) * row_count
    block_row = (first_row + jnp.arange(row_count, dtype=jnp.int32)) // block_size
    onehot = (block_row[:, None] == jnp.arange(sectors, dtype=jnp.int32)[None, :]).astype(
        jnp.float32
    )
    row_pattern = jnp.dot(onehot, pattern.astype(jnp.float32), preferred_element_type=jnp.float32)
    allowed = jnp.broadcast_to(row_pattern[:, :, None], (row_count, sectors, block_size))
    allowed = allowed.reshape(row_count, full_width).astype(jnp.bfloat16)
    diagonal = hdiag.astype(jnp.float32)
    peers = lax.axis_size("blk") * lax.axis_size("sub")

    def left_part(arrived):
        return apply_left(arrived, left_blocks, left_cols)

    def operate(field_in):
        images = apply_right(field_in, right_blocks, right_cols)
        partial_sum = left_part(
            lax.all_to_all(images, ("blk", "sub"), split_axis=3, concat_axis=2, tiled=True)
        )
        shares = lax.psum_scatter(partial_sum, "ops", scatter_dimension=2, tiled=True)
        returned = lax.all_to_all(
            shares.astype(jnp.bfloat16), ("blk", "sub"), split_axis=1, concat_axis=2, tiled=True
        )
        gathered = lax.all_gather(returned, "ops", axis=2, tiled=True)
        narrow = returned.shape[2] // peers
        gathered = gathered.reshape(roots_here, row_count, lax.axis_size("ops"), peers, narrow)
        offdiag = gathered.transpose(0, 1, 3, 2, 4).reshape(roots_here, row_count, full_width)
        offdiag = offdiag * allowed[None]
        return diagonal[None] * field_in.astype(jnp.float32) + offdiag.astype(jnp.float32)

    projected = theta * allowed[None]
    wave = projected.astype(jnp.float32)
    sigma_one = operate(projected)
    norm_sq, energy_sum = lax.psum(
        (jnp.sum(wave * wave, axis=(1, 2)), jnp.sum(wave * sigma_one, axis=(1, 2))), ("blk", "sub")
    )
    denominator = norm_sq + 1e-06
    energy = energy_sum / denominator
    shifted = diagonal[None] - energy[:, None, None]
    update = (sigma_one - energy[:, None, None] * wave) * shifted / (shifted * shifted + 1.0)
    correlation = lax.psum(jnp.sum(wave * update, axis=(1, 2)), ("blk", "sub"))
    factor = correlation / denominator
    orthogonal = update - factor[:, None, None] * wave
    length_sq = lax.psum(jnp.sum(orthogonal * orthogonal, axis=(1, 2)), ("blk", "sub"))
    correction = (orthogonal * jnp.sqrt(norm_sq / (length_sq + 1e-06))[:, None, None]).astype(
        jnp.bfloat16
    )
    sigma_two = operate(correction).astype(jnp.bfloat16)
    second = sigma_two.astype(jnp.float32)
    fixed = correction.astype(jnp.float32)
    cross_one, cross_two, cross_three = lax.psum(
        (
            jnp.sum(wave * second, axis=(1, 2)),
            jnp.sum(fixed * sigma_one, axis=(1, 2)),
            jnp.sum(fixed * second, axis=(1, 2)),
        ),
        ("blk", "sub"),
    )
    subspace = (
        jnp.stack([energy_sum, cross_one, cross_two, cross_three], axis=1) / denominator[:, None]
    )
    return (correction, sigma_two, subspace)


MIX_A, MIX_B = 4, 5
MIXES = ((MIX_A, 0, 0), (MIX_B, 0, 0))


def halves_fit(mesh):
    sizes = dict(mesh.shape)
    return sizes["blk"] == 4 and sizes["ops"] == 2 and sizes["sub"] == 2


def across(value, axis, distance):
    size = lax.axis_size(axis)
    return lax.ppermute(value, axis, [(i, i ^ distance) for i in range(size)])


def share(stats):
    axes = ("blk", "ops")
    count = lax.axis_size("blk") * lax.axis_size("ops")
    pair = jnp.stack([stats, across(stats, "sub", 1)])
    found = [pair]
    for distance in (1, 2, 3):
        found.append(lax.ppermute(pair, axes, [(i, i ^ distance) for i in range(count)]))
    return found


def place():
    return lax.axis_index("blk"), lax.axis_index("ops"), lax.axis_index("sub")


def fold(value):
    rows, width = value.shape
    value = jnp.sum(value.reshape(rows // 8, 8, width), axis=0)
    return sum(value[:, at : at + LANES] for at in range(0, width, LANES))


def in_middle(z):
    return jnp.logical_or(z == 1, z == 2)


def row_of(dz, dx, dc):
    z, x, c = place()
    if dz in (MIX_A, MIX_B):
        far = in_middle(z) if dz == MIX_A else jnp.logical_not(in_middle(z))
        return jnp.where(far, row_of(2, 0, dc), row_of(1, 2, dc))
    return 4 * (z ^ dz) + 2 * (c ^ dc) + (x ^ dx if dx < 2 else dx - 2)


def operate_kernel(first, plan, right_cols, left_cols, cols_other, pattern, right, left_own, left_other, *refs):
    count = len(plan)
    pieces, refs = refs[:count], refs[count:]
    if first:
        weight_own, psi_out, off_out, stats_out = refs[:4]
        refs = refs[4:]
    else:
        hd_own, hd_far, psi_in, off_in, stats_in, near_out, far_out, late_out, stats_out = refs[:9]
        refs = refs[9:]
    field, images, left, diag, sems = refs
    z, x, c = place()
    sectors, block, width = field.shape
    table = right.shape[1]
    links = table // sectors
    mine = 4 * z + 2 * c + x
    rows = (mine, mine ^ 12)
    half = z // 2

    copies = []

    def begin(source, target):
        copy = pltpu.make_async_copy(source, target, sems.at[len(copies)])
        copy.start()
        copies.append(copy)

    for at in range(2):
        begin(left_own.at[pl.ds(rows[at] * links, links)], left.at[0, pl.ds(at * links, links)])
    begin(left_other.at[pl.ds(table // 2, 2 * links)], left.at[1])
    if not first:
        begin(hd_own.at[x], diag.at[0])
        begin(hd_far, diag.at[1])

    def allowed(a, q, value):
        return lax.select(pattern[a, q] != 0, value, jnp.zeros_like(value))

    for piece, offsets in zip(pieces, plan):
        base = 2 * half if piece.shape[0] == 4 else 0
        for at, (dz, dx, dc, start, tall) in enumerate(offsets):
            row = row_of(dz, dx, dc)
            for q in range(sectors):
                span = slice(q * block, (q + 1) * block)
                value = piece[base + at, :, span]
                field[row, start : start + tall, span] = allowed(row, q, value) if first else value

    def right_col(term, b, j):
        return cols_other[j, b] if term else right_cols[j, 0, b]

    def left_col(term, a, j):
        return cols_other[8 + j, a] if term else left_cols[j, 0, a]

    sources = [[left_col(term, rows[at], j) for at in range(2) for j in range(links)] for term in range(2)]

    deep = links * block

    none = jnp.zeros((block, block), jnp.bfloat16)
    pair = 2

    def image(n, carry):
        picks = [(i, j) for i in range(pair) for j in range(links)]
        for term in range(2):
            found = [right_col(term, n * pair + i, j) for i, j in picks]
            lhs = []
            for source in sources[term]:
                line = []
                for col in found:
                    value = field[source, :, pl.ds(pl.multiple_of(col * block, block), block)]
                    line.append(value)
                lhs.append(jnp.concatenate(line, axis=1))
            rhs = []
            for i, j in picks:
                tile = right[term, (n * pair + i) * links + j]
                rhs.append(jnp.concatenate([tile if i == at else none for at in range(pair)], axis=1))
            product = jnp.dot(
                jnp.concatenate(lhs, axis=0),
                jnp.concatenate(rhs, axis=0),
                preferred_element_type=jnp.float32,
            )
            product = product.astype(jnp.bfloat16)
            span = pl.ds(pl.multiple_of(n * pair * block, pair * block), pair * block)
            for at in range(2):
                images[at, term * deep : (term + 1) * deep, span] = product[at * deep : (at + 1) * deep]
        return carry

    lax.fori_loop(0, sectors // pair, image, 0, unroll=2)
    for copy in copies:
        copy.wait()

    step = 2
    early_rows = block // 2
    zero = jnp.zeros((8, LANES), jnp.float32)

    def column(n, sums):
        start = pl.multiple_of(n * step * block, step * block)
        span = pl.ds(start, step * block)
        sums = list(sums)

        def masked(a, value):
            parts = [
                allowed(a, n * step + i, value[:, i * block : (i + 1) * block]) for i in range(step)
            ]
            return jnp.concatenate(parts, axis=1)

        for at in range(2):
            weights = [left[term, at * links + j] for term in range(2) for j in range(links)]
            total = jnp.dot(
                jnp.concatenate(weights, axis=1),
                images[at, :, span],
                preferred_element_type=jnp.float32,
            )
            offdiag = masked(rows[at], total.astype(jnp.bfloat16).astype(jnp.float32))
            own = field[rows[at], :, span].astype(jnp.float32)
            if first:
                psi_out[at, :, span] = own.astype(jnp.bfloat16)
                off_out[at, :, span] = offdiag.astype(jnp.bfloat16)
                sums[0] += fold(own * own)
                sums[1] += fold(own * offdiag)
            else:
                weight = diag[at, :, span].astype(jnp.float32)
                narrow = (weight * own + offdiag).astype(jnp.bfloat16)
                if at == 0:
                    near_out[:, span] = narrow
                else:
                    far_out[:, span] = narrow[:early_rows]
                    late_out[:, span] = narrow[early_rows:]
                second = narrow.astype(jnp.float32)
                wave = psi_in[at, :, span].astype(jnp.float32)
                sigma_one = weight * wave + off_in[at, :, span].astype(jnp.float32)
                sums[0] += fold(wave * second)
                sums[1] += fold(own * sigma_one)
                sums[2] += fold(own * second)
        return tuple(sums)

    sums = list(lax.fori_loop(0, sectors // step, column, (zero,) * (2 if first else 3)))
    if first:
        parts = [
            piece[0, 0:48, width:] for piece, offsets in zip(pieces, plan) if offsets[0][:3] in MIXES
        ]
        far_weight = sum(part.astype(jnp.float32) for part in parts)
        sums[1] += weight_own[...] + (far_weight[0:8] + far_weight[16:24] + far_weight[32:40])
    stats_out[...] = jnp.zeros_like(stats_out)
    for at, value in enumerate(sums):
        stats_out[at : at + 1, :] = jnp.sum(value, axis=0, keepdims=True)
    if not first:
        stats_out[3:5, :] = stats_in[0:2, :]


def operate(first, plan, pieces, cols, pattern, right, left, extra):
    _, table, block, _ = right.shape
    width = pieces[0].shape[2]
    sectors = width // block
    links = table // sectors
    rows = jax.ShapeDtypeStruct((2, block, width), jnp.bfloat16)
    one = jax.ShapeDtypeStruct((block, width), jnp.bfloat16)
    some = jax.ShapeDtypeStruct((block // 2, width), jnp.bfloat16)
    stats = jax.ShapeDtypeStruct((8, LANES), jnp.float32)
    out_shape = (rows, rows, stats) if first else (one, some, some, stats)
    extra_specs = [VMEM] if first else [ANY, ANY, VMEM, VMEM, VMEM]
    inner = 2 * 2 * sectors * 2 * links * links * block * block * block
    outer = 2 * 2 * 2 * links * block * block * width
    return pl.pallas_call(
        functools.partial(operate_kernel, first, plan),
        out_shape=out_shape,
        in_specs=[SMEM, SMEM, SMEM, SMEM, VMEM, ANY, ANY] + [VMEM] * len(pieces) + extra_specs,
        out_specs=(VMEM,) * len(out_shape),
        scratch_shapes=[
            pltpu.VMEM((sectors, block, width), jnp.bfloat16),
            pltpu.VMEM((2, 2 * links * block, width), jnp.bfloat16),
            pltpu.VMEM((2, 2 * links, block, block), jnp.bfloat16),
            pltpu.VMEM((2, block, width), jnp.bfloat16),
            pltpu.SemaphoreType.DMA((5,)),
        ],
        compiler_params=pltpu.CompilerParams(vmem_limit_bytes=OPERATE_LIMIT),
        cost_estimate=pl.CostEstimate(
            flops=inner + outer if first else 0,
            bytes_accessed=16 * 1024 * 1024 if first else 1024,
            transcendentals=0,
        ),
        name="operate_first" if first else "operate_second",
    )(*cols, pattern, right, *left, *pieces, *extra)


def arrange_kernel(own, near, far, out, found, sems):
    _, _, c = place()
    part = far.shape[0]
    copies = [
        pltpu.make_async_copy(own, found.at[0], sems.at[0]),
        pltpu.make_async_copy(near.at[pl.ds(0, part)], found.at[1, pl.ds(c * part, part)], sems.at[1]),
        pltpu.make_async_copy(far, found.at[1, pl.ds((1 - c) * part, part)], sems.at[2]),
    ]
    for copy in copies:
        copy.start()
    for copy in copies:
        copy.wait()

    def turn(at, carry):
        for term in range(2):
            out[term, at] = found[term, at].T
        return carry

    lax.fori_loop(0, found.shape[1], turn, 0, unroll=4)


def arrange(own, near, far):
    shape = (2, *own.shape)
    return pl.pallas_call(
        arrange_kernel,
        out_shape=jax.ShapeDtypeStruct(shape, own.dtype),
        in_specs=[ANY] * 3,
        out_specs=VMEM,
        scratch_shapes=[pltpu.VMEM(shape, own.dtype), pltpu.SemaphoreType.DMA((3,))],
        compiler_params=pltpu.CompilerParams(vmem_limit_bytes=VMEM_LIMIT),
        name="arrange",
    )(own, near, far)


def prepare_kernel(
    pattern, theta, hd, right, left, right_cols, left_cols, mix_a, mix_b, packed, own_out, waves, diag, spots, sems
):
    z, x, c = place()
    half = z // 2
    middle = in_middle(z)
    mine = 4 * z + 2 * c + x
    block, width = diag.shape
    sectors = width // block
    links = right.shape[0] // sectors
    part = right.shape[0] // 2
    root_a = jnp.where(middle, half, 1 - half)
    rows = pl.ds(0, width)
    sources = (
        (theta.at[half, x], waves.at[0]),
        (theta.at[1 - half, x], waves.at[1]),
        (hd.at[x], diag),
        (theta.at[root_a, jnp.where(middle, 0, x)], mix_a.at[:, rows]),
        (theta.at[1 - root_a, jnp.where(middle, x, 0)], mix_b.at[:, rows]),
        (right.at[pl.ds(c * part, part)], packed.at[pl.ds(0, part)]),
        (left.at[pl.ds((mine ^ 1) * links, links)], packed.at[pl.ds(part, links)]),
        (left.at[pl.ds((mine ^ 13) * links, links)], packed.at[pl.ds(part + links, links)]),
    )
    copies = [
        pltpu.make_async_copy(source, target, sems.at[at])
        for at, (source, target) in enumerate(sources)
    ]
    for copy in copies:
        copy.start()
    last = part + 2 * links
    spots[...] = jnp.zeros_like(spots)
    spots[0:links, 0:sectors] = right_cols[:, 0, :].astype(jnp.float32)
    spots[8 : 8 + links, 0:sectors] = left_cols[:, 0, :].astype(jnp.float32)
    packed[last] = jnp.zeros_like(packed[last])
    packed[last, 0:16, :] = spots[...].astype(jnp.bfloat16)
    for copy in copies[:3]:
        copy.wait()
    zero = jnp.zeros((8, LANES), jnp.float32)

    def column(q, sums):
        span = pl.ds(pl.multiple_of(q * block, block), block)
        weight = diag[:, span].astype(jnp.float32)
        weight = jnp.where(pattern[mine, q] != 0, weight, jnp.zeros_like(weight))
        found = []
        for root in range(2):
            wave = waves[root, :, span].astype(jnp.float32)
            found.append(sums[root] + fold(weight * wave * wave))
        return tuple(found)

    near, far = lax.fori_loop(0, sectors, column, (zero, zero), unroll=4)
    own_out[...] = near
    left_over = jnp.concatenate([far, zero], axis=0)
    parts = []
    for _ in range(3):
        piece = left_over.astype(jnp.bfloat16)
        parts.append(piece)
        left_over = left_over - piece.astype(jnp.float32)
    parts.append(jnp.zeros((block - 48, LANES), jnp.bfloat16))
    tail = jnp.concatenate(parts, axis=0)
    none = jnp.zeros_like(tail)
    mix_a[:, width:] = jnp.where(middle, none, tail)
    mix_b[:, width:] = jnp.where(middle, tail, none)
    for copy in copies[3:]:
        copy.wait()


def prepare(pattern, theta, hd, right, left, *cols):
    _, _, block, width = theta.shape
    table = right.shape[0]
    links = table * block // width
    kind = jnp.bfloat16
    mix = jax.ShapeDtypeStruct((block, width + LANES), kind)
    packed = jax.ShapeDtypeStruct((table // 2 + 2 * links + 1, block, block), kind)
    return pl.pallas_call(
        prepare_kernel,
        out_shape=(mix, mix, packed, jax.ShapeDtypeStruct((8, LANES), jnp.float32)),
        in_specs=[SMEM, ANY, ANY, ANY, ANY, VMEM, VMEM],
        out_specs=(VMEM,) * 4,
        scratch_shapes=[
            pltpu.VMEM((2, block, width), kind),
            pltpu.VMEM((block, width), kind),
            pltpu.VMEM((16, LANES), jnp.float32),
            pltpu.SemaphoreType.DMA((8,)),
        ],
        compiler_params=pltpu.CompilerParams(vmem_limit_bytes=PREPARE_LIMIT),
        name="prepare",
    )(pattern, theta, hd, right, left, *cols)


def total_of(rows):
    return jnp.sum(rows, axis=1, keepdims=True)


def update_kernel(psi, off, hd_own, hd_far, *refs):
    stats, (t_out, stats_out, diag, sems) = refs[:4], refs[4:]
    z, x, c = place()
    copies = [
        pltpu.make_async_copy(hd_own.at[x], diag.at[0], sems.at[0]),
        pltpu.make_async_copy(hd_far, diag.at[1], sems.at[1]),
    ]
    for copy in copies:
        copy.start()
    whole = sum(ref[at, 0:2, :] for ref in stats for at in range(2))
    norm_sq, energy_sum = total_of(whole[0:1, :]), total_of(whole[1:2, :])
    energy = energy_sum / (norm_sq + 1e-06)
    mine = total_of(stats[0][0, 0:1, :])
    for copy in copies:
        copy.wait()
    _, block, width = psi.shape
    step = 16
    zero = jnp.zeros((8, LANES), jnp.float32)

    def chunk(n, total):
        span = pl.ds(pl.multiple_of(n * step, step), step)
        for at in range(2):
            wave = psi[at, span, :].astype(jnp.float32)
            weight = diag[at, span, :].astype(jnp.float32)
            sigma = weight * wave + off[at, span, :].astype(jnp.float32)
            shifted = weight - energy
            t = (sigma - energy * wave) * shifted / (shifted * shifted + 1.0)
            t_out[at, span, :] = t
            total = total + fold(wave * t)
        return total

    lanes = jnp.sum(lax.fori_loop(0, block // step, chunk, zero), axis=0, keepdims=True)
    correlation = total_of(lanes)
    local = jnp.where(mine > 0.0, correlation / jnp.where(mine > 0.0, mine, 1.0), 0.0)

    def within(n, total):
        span = pl.ds(pl.multiple_of(n * step, step), step)
        for at in range(2):
            rest = t_out[at, span, :] - local * psi[at, span, :].astype(jnp.float32)
            total = total + fold(rest * rest)
        return total

    spread = jnp.sum(lax.fori_loop(0, block // step, within, zero), axis=0, keepdims=True)
    stats_out[...] = jnp.zeros_like(stats_out)
    stats_out[0:1, :] = jnp.broadcast_to(correlation, (1, LANES))
    stats_out[1:2, :] = jnp.broadcast_to(total_of(spread), (1, LANES))
    stats_out[2:3, :] = jnp.broadcast_to(mine, (1, LANES))
    stats_out[3:4, :] = jnp.broadcast_to(local, (1, LANES))
    stats_out[4:5, :] = jnp.broadcast_to(norm_sq, (1, LANES))


def correct_kernel(psi, t, *refs):
    stats, outs = refs[:4], refs[4:]
    stats = [ref.at[at] for ref in stats for at in range(2)]
    norm_sq = stats[0][4:5, 0:1]
    factor = sum(ref[0:1, 0:1] for ref in stats) / (norm_sq + 1e-06)
    length_sq = jnp.zeros((1, 1), jnp.float32)
    for ref in stats:
        gap = factor - ref[3:4, 0:1]
        length_sq = length_sq + (ref[1:2, 0:1] + gap * gap * ref[2:3, 0:1])
    scale = jnp.sqrt(norm_sq / (length_sq + 1e-06))
    _, block, width = psi.shape
    step = 16

    def chunk(n, carry):
        span = pl.ds(pl.multiple_of(n * step, step), step)
        for at in range(2):
            wave = psi[at, span, :].astype(jnp.float32)
            outs[at][span, :] = ((t[at, span, :] - factor * wave) * scale).astype(jnp.bfloat16)
        return carry

    lax.fori_loop(0, block // step, chunk, 0)


def assemble_kernel(places, based, *refs):
    count = len(places)
    pieces, (out, sems) = refs[:count], refs[count + based :]
    z, x, c = place()
    half = z // 2
    copies = []
    for at, (root, flip, start) in enumerate(places):
        size = pieces[at].shape[0]
        target = out.at[half ^ root, x ^ flip, pl.ds(start, size)]
        copies.append(pltpu.make_async_copy(pieces[at], target, sems.at[at]))
    for copy in copies:
        copy.start()
    for copy in copies:
        copy.wait()


def assemble(block, pieces, places, base=None):
    width = pieces[0].shape[1]
    based = [] if base is None else [base]
    return pl.pallas_call(
        functools.partial(assemble_kernel, places, len(based)),
        out_shape=jax.ShapeDtypeStruct((2, 2, block, width), pieces[0].dtype),
        in_specs=[VMEM] * len(pieces) + [ANY] * len(based),
        out_specs=ANY,
        scratch_shapes=[pltpu.SemaphoreType.DMA((len(pieces),))],
        input_output_aliases={len(pieces): 0} if based else {},
        compiler_params=pltpu.CompilerParams(vmem_limit_bytes=VMEM_LIMIT),
        name="assemble",
    )(*pieces, *based)


def after(value, *others):
    return lax.optimization_barrier((value, *others))[0]


def shards(theta, hdiag, pattern, left_blocks, left_cols, right_blocks, right_cols):
    roots, row_count, width = theta.shape
    sectors = pattern.shape[0]
    block = width // sectors
    z, x, c = place()
    half = z // 2
    mine = 4 * z + 2 * c + x

    halves = theta.reshape(roots, 2, block, width)
    diag = hdiag.reshape(2, block, width)
    chunk = block // 2
    middle = in_middle(z)
    right = right_blocks.reshape(-1, block, block)
    left = left_blocks.reshape(-1, block, block)
    cols = (right_cols.transpose(2, 0, 1), left_cols.transpose(2, 0, 1))

    mix_a, mix_b, packed, weight_own = prepare(pattern, halves, diag, right, left, *cols)
    mix_a = lax.ppermute(mix_a, "blk", [(0, 2), (2, 3), (3, 1), (1, 0)])
    mix_b = lax.ppermute(mix_b, "blk", [(0, 1), (1, 3), (3, 2), (2, 0)])
    operators = across(packed, "ops", 1)
    theta_core = across(theta, "sub", 1)

    mix_a, mix_b = after((mix_a, mix_b), theta_core)
    far = jnp.where(middle, mix_a[:, :width], mix_b[:, :width])
    far_z = [across(far[at : at + chunk], "blk", 1) for at in (0, chunk)]
    far_x = across(far, "ops", 1)
    mix_a_core = across(mix_a, "sub", 1)
    mix_b_core = across(mix_b, "sub", 1)
    operators = after(operators, mix_b)
    operators_core = across(operators[: right.shape[0] // 2], "sub", 1)
    turned = arrange(right, operators, operators_core)
    cols = (*cols, operators[-1, :16, :sectors].astype(jnp.int32))

    own_b = lax.dynamic_slice(halves, (half, 1, 0, 0), (1, 1, block, width))[0, 0]
    near_b = across(after(own_b, far_z[0], mix_a_core, mix_b_core, turned), "blk", 1)
    far_zx = [across(value, "ops", 1) for value in far_z]
    far_x_core = across(far_x, "sub", 1)
    far_z_core = [across(value, "sub", 1) for value in far_z]
    hd_far = lax.dynamic_index_in_dim(diag, x, 0, keepdims=False)
    hd_far = across(after(hd_far, far_z[1]), "blk", 3)
    far_zx_core = [across(value, "sub", 1) for value in far_zx]
    near_b_core = across(near_b, "sub", 1)

    left = (left, operators)
    pieces = [halves.reshape(4, block, width), theta_core.reshape(4, block, width)]
    plan = [
        ((0, 2, 0, 0, block), (0, 3, 0, 0, block)),
        ((0, 2, 1, 0, block), (0, 3, 1, 0, block)),
    ]
    for piece, offset in (
        (mix_a, (MIX_A, 0, 0)),
        (mix_b, (MIX_B, 0, 0)),
        (mix_a_core, (MIX_A, 0, 1)),
        (mix_b_core, (MIX_B, 0, 1)),
        (near_b, (1, 3, 0)),
        (near_b_core, (1, 3, 1)),
        (far_x, (2, 1, 0)),
        (far_x_core, (2, 1, 1)),
    ):
        pieces.append(piece[None])
        plan.append((offset + (0, block),))
    for at in range(2):
        for piece, offset in (
            (far_z[at], (3, 0, 0)),
            (far_z_core[at], (3, 0, 1)),
            (far_zx[at], (3, 1, 0)),
            (far_zx_core[at], (3, 1, 1)),
        ):
            pieces.append(piece[None])
            plan.append((offset + (at * chunk, chunk),))
    psi, off_one, stats_one = operate(
        True, tuple(plan), pieces, cols, pattern, turned, left, (weight_own,)
    )

    found = share(stats_one)
    t, stats_two = pl.pallas_call(
        update_kernel,
        out_shape=(
            jax.ShapeDtypeStruct((2, block, width), jnp.float32),
            jax.ShapeDtypeStruct((8, LANES), jnp.float32),
        ),
        in_specs=[VMEM, VMEM, ANY, ANY] + [VMEM] * 4,
        out_specs=(VMEM, VMEM),
        scratch_shapes=[
            pltpu.VMEM((2, block, width), jnp.bfloat16),
            pltpu.SemaphoreType.DMA((2,)),
        ],
        compiler_params=pltpu.CompilerParams(vmem_limit_bytes=VMEM_LIMIT),
        name="update",
    )(psi, off_one, diag, hd_far, *found)
    found = share(stats_two)
    one = jax.ShapeDtypeStruct((block, width), jnp.bfloat16)
    changed_near, changed_far = pl.pallas_call(
        correct_kernel,
        out_shape=(one, one),
        in_specs=[VMEM, VMEM] + [VMEM] * 4,
        out_specs=(VMEM, VMEM),
        compiler_params=pltpu.CompilerParams(vmem_limit_bytes=VMEM_LIMIT),
        name="correct",
    )(psi, t, *found)

    near_z = across(changed_near, "blk", 1)
    far_x = across(changed_far, "ops", 1)
    near_core = across(changed_near, "sub", 1)
    far_core = across(changed_far, "sub", 1)
    other_middle = lax.ppermute(changed_far, "blk", [(1, 2), (2, 1)])
    near_z, far_x = after((near_z, far_x), other_middle)
    near_zx = across(near_z, "ops", 1)
    far_xz = across(far_x, "blk", 1)
    near_x = across(after(changed_near, near_z, far_x), "ops", 1)
    far_z = across(after(changed_far, near_z, far_x), "blk", 1)
    near_z_core = across(near_z, "sub", 1)
    far_x_core = across(far_x, "sub", 1)
    near_x_core = across(near_x, "sub", 1)
    far_z_core = across(far_z, "sub", 1)
    near_zx_core = across(near_zx, "sub", 1)
    far_xz_core = across(far_xz, "sub", 1)
    other_end = lax.ppermute(after(changed_far, near_z, far_x), "blk", [(0, 3), (3, 0)])
    pieces, plan = [], []
    for piece, offset in (
        (changed_near, (0, 0, 0)),
        (changed_far, (3, 0, 0)),
        (near_core, (0, 0, 1)),
        (far_core, (3, 0, 1)),
        (near_z, (1, 0, 0)),
        (far_z, (2, 0, 0)),
        (near_z_core, (1, 0, 1)),
        (far_z_core, (2, 0, 1)),
        (near_x, (0, 1, 0)),
        (far_x, (3, 1, 0)),
        (near_x_core, (0, 1, 1)),
        (far_x_core, (3, 1, 1)),
        (near_zx, (1, 1, 0)),
        (far_xz, (2, 1, 0)),
        (near_zx_core, (1, 1, 1)),
        (far_xz_core, (2, 1, 1)),
    ):
        pieces.append(piece[None])
        plan.append((offset + (0, block),))
    two_near, two_far, two_late, stats_three = operate(
        False, tuple(plan), pieces, cols, pattern, turned, left, (diag, hd_far, psi, off_one, stats_one)
    )

    far_in = across(two_far, "blk", 3)
    near_in = across(two_near, "ops", 1)
    late_in = across(after(two_late, far_in, near_in), "blk", 3)
    far_in_x = across(after(far_in, near_in), "ops", 1)
    other = jnp.where(middle, other_middle, after(other_end, near_in))
    other_x = across(other, "ops", 1)
    sums = after(stats_three, far_in, near_in)
    sums = sums + across(sums, "sub", 1)
    sums = sums + across(sums, "blk", 1)
    both = jnp.stack([sums, across(sums, "blk", 2)])
    both = both + across(both, "ops", 1)
    other, other_x = after((other, other_x), late_in)
    late_in_x = across(late_in, "ops", 1)
    both = jnp.sum(jnp.where(half == 0, both, both[::-1])[:, :5], axis=2)
    scale = both[:, 3:4] + 1e-06
    subspace = jnp.concatenate([both[:, 4:5], both[:, 0:3]], axis=1) / scale
    places = ((0, 0, 0), (0, 1, 0), (1, 0, 0), (1, 1, 0))
    correction = assemble(block, (changed_near, near_x, other, other_x), places)
    places = ((0, 0, 0), (0, 1, 0), (1, 0, 0), (1, 0, block // 2), (1, 1, 0))
    sigma_two = assemble(block, (two_near, near_in, far_in, late_in, far_in_x), places)
    sigma_two = assemble(block, (late_in_x,), ((1, 1, block // 2),), sigma_two)
    return correction.reshape(theta.shape), sigma_two.reshape(theta.shape), subspace


def solution(mesh):
    in_specs = (
        P("groups", ("blk", "sub"), None),
        P(("groups", "blk", "sub"), None),
        P("groups", None),
        P(("groups", "ops"), None, None, None, None),
        P(("groups", "ops"), None, None),
        P(("groups", "ops"), None, None, None, None),
        P(("groups", "ops"), None, None),
    )
    out_specs = (
        P("groups", ("blk", "sub"), None),
        P("groups", ("blk", "sub"), None),
        P("groups", None),
    )
    body = shards if halves_fit(mesh) else general_shards
    return jax.shard_map(body, mesh=mesh, in_specs=in_specs, out_specs=out_specs, check_vma=False)
```

```python
import functools

import jax
import jax.numpy as jnp
from jax import lax
from jax.experimental import pallas as pl
from jax.experimental.pallas import tpu as pltpu
from jax.sharding import PartitionSpec as P

ANY = pl.BlockSpec(memory_space=pl.ANY)
SMEM = pl.BlockSpec(memory_space=pltpu.SMEM)
VMEM = pl.BlockSpec(memory_space=pltpu.VMEM)
VMEM_LIMIT = 24 * 1024 * 1024
OPERATE_LIMIT = 44 * 1024 * 1024
PREPARE_LIMIT = 56 * 1024 * 1024
LANES = 128


def apply_right(field_in, blocks, columns):
    roots_here, row_count, full_width = field_in.shape
    term_count, sectors, link_count = columns.shape
    block_size = full_width // sectors
    grouped = field_in.reshape(roots_here, row_count, sectors, block_size)
    picked = jnp.take(grouped, columns.reshape(-1), axis=2)
    picked = picked.reshape(roots_here, row_count, term_count, sectors, link_count, block_size)
    product = jnp.einsum("nrkbjq,kbjpq->knrbp", picked, blocks, preferred_element_type=jnp.float32)
    return product.reshape(term_count, roots_here, row_count, full_width).astype(jnp.bfloat16)


def take_rows(stacked, indices):
    return jnp.take(stacked, indices, axis=1)


def apply_left(arrived, blocks, columns):
    term_count, roots_here, full_width, col_count = arrived.shape
    sectors = columns.shape[1]
    link_count = columns.shape[2]
    block_size = full_width // sectors
    grouped = arrived.reshape(term_count, roots_here, sectors, block_size, col_count)
    picked = jax.vmap(take_rows)(grouped, columns.reshape(term_count, sectors * link_count))
    picked = picked.reshape(term_count, roots_here, sectors, link_count, block_size, col_count)
    product = jnp.einsum("kajpq,knajqc->napc", blocks, picked, preferred_element_type=jnp.float32)
    return product.reshape(roots_here, full_width, col_count)


def general_shards(theta, hdiag, pattern, left_blocks, left_cols, right_blocks, right_cols):
    roots_here, row_count, full_width = theta.shape
    sectors = pattern.shape[0]
    block_size = full_width // sectors
    first_row = lax.axis_index(("blk", "sub")) * row_count
    block_row = (first_row + jnp.arange(row_count, dtype=jnp.int32)) // block_size
    onehot = (block_row[:, None] == jnp.arange(sectors, dtype=jnp.int32)[None, :]).astype(
        jnp.float32
    )
    row_pattern = jnp.dot(onehot, pattern.astype(jnp.float32), preferred_element_type=jnp.float32)
    allowed = jnp.broadcast_to(row_pattern[:, :, None], (row_count, sectors, block_size))
    allowed = allowed.reshape(row_count, full_width).astype(jnp.bfloat16)
    diagonal = hdiag.astype(jnp.float32)
    peers = lax.axis_size("blk") * lax.axis_size("sub")

    def left_part(arrived):
        return apply_left(arrived, left_blocks, left_cols)

    def operate(field_in):
        images = apply_right(field_in, right_blocks, right_cols)
        partial_sum = left_part(
            lax.all_to_all(images, ("blk", "sub"), split_axis=3, concat_axis=2, tiled=True)
        )
        shares = lax.psum_scatter(partial_sum, "ops", scatter_dimension=2, tiled=True)
        returned = lax.all_to_all(
            shares.astype(jnp.bfloat16), ("blk", "sub"), split_axis=1, concat_axis=2, tiled=True
        )
        gathered = lax.all_gather(returned, "ops", axis=2, tiled=True)
        narrow = returned.shape[2] // peers
        gathered = gathered.reshape(roots_here, row_count, lax.axis_size("ops"), peers, narrow)
        offdiag = gathered.transpose(0, 1, 3, 2, 4).reshape(roots_here, row_count, full_width)
        offdiag = offdiag * allowed[None]
        return diagonal[None] * field_in.astype(jnp.float32) + offdiag.astype(jnp.float32)

    projected = theta * allowed[None]
    wave = projected.astype(jnp.float32)
    sigma_one = operate(projected)
    norm_sq, energy_sum = lax.psum(
        (jnp.sum(wave * wave, axis=(1, 2)), jnp.sum(wave * sigma_one, axis=(1, 2))), ("blk", "sub")
    )
    denominator = norm_sq + 1e-06
    energy = energy_sum / denominator
    shifted = diagonal[None] - energy[:, None, None]
    update = (sigma_one - energy[:, None, None] * wave) * shifted / (shifted * shifted + 1.0)
    correlation = lax.psum(jnp.sum(wave * update, axis=(1, 2)), ("blk", "sub"))
    factor = correlation / denominator
    orthogonal = update - factor[:, None, None] * wave
    length_sq = lax.psum(jnp.sum(orthogonal * orthogonal, axis=(1, 2)), ("blk", "sub"))
    correction = (orthogonal * jnp.sqrt(norm_sq / (length_sq + 1e-06))[:, None, None]).astype(
        jnp.bfloat16
    )
    sigma_two = operate(correction).astype(jnp.bfloat16)
    second = sigma_two.astype(jnp.float32)
    fixed = correction.astype(jnp.float32)
    cross_one, cross_two, cross_three = lax.psum(
        (
            jnp.sum(wave * second, axis=(1, 2)),
            jnp.sum(fixed * sigma_one, axis=(1, 2)),
            jnp.sum(fixed * second, axis=(1, 2)),
        ),
        ("blk", "sub"),
    )
    subspace = (
        jnp.stack([energy_sum, cross_one, cross_two, cross_three], axis=1) / denominator[:, None]
    )
    return (correction, sigma_two, subspace)


MIX_A, MIX_B = 4, 5
MIXES = ((MIX_A, 0, 0), (MIX_B, 0, 0))


def halves_fit(mesh):
    sizes = dict(mesh.shape)
    return sizes["blk"] == 4 and sizes["ops"] == 2 and sizes["sub"] == 2


def across(value, axis, distance):
    size = lax.axis_size(axis)
    return lax.ppermute(value, axis, [(i, i ^ distance) for i in range(size)])


def share(stats):
    axes = ("blk", "ops")
    count = lax.axis_size("blk") * lax.axis_size("ops")
    pair = jnp.stack([stats, across(stats, "sub", 1)])
    found = [pair]
    for distance in (1, 2, 3):
        found.append(lax.ppermute(pair, axes, [(i, i ^ distance) for i in range(count)]))
    return found


def place():
    return lax.axis_index("blk"), lax.axis_index("ops"), lax.axis_index("sub")


def fold(value):
    rows, width = value.shape
    value = jnp.sum(value.reshape(rows // 8, 8, width), axis=0)
    return sum(value[:, at : at + LANES] for at in range(0, width, LANES))


def in_middle(z):
    return jnp.logical_or(z == 1, z == 2)


def row_of(dz, dx, dc):
    z, x, c = place()
    if dz in (MIX_A, MIX_B):
        far = in_middle(z) if dz == MIX_A else jnp.logical_not(in_middle(z))
        return jnp.where(far, row_of(2, 0, dc), row_of(1, 2, dc))
    return 4 * (z ^ dz) + 2 * (c ^ dc) + (x ^ dx if dx < 2 else dx - 2)


def operate_kernel(first, plan, right_cols, left_cols, cols_other, pattern, right, left_own, left_other, *refs):
    count = len(plan)
    pieces, refs = refs[:count], refs[count:]
    if first:
        masks, weight_own, psi_out, off_out, stats_out = refs[:5]
        refs = refs[5:]
    else:
        hd_own, hd_far, psi_in, off_in, stats_in, near_out, far_out, late_out, stats_out = refs[:9]
        refs = refs[9:]
    field, images, left, diag, sems = refs
    z, x, c = place()
    sectors, block, width = field.shape
    table = right.shape[1]
    links = table // sectors
    mine = 4 * z + 2 * c + x
    rows = (mine, mine ^ 12)
    half = z // 2

    copies = []

    def begin(source, target):
        copy = pltpu.make_async_copy(source, target, sems.at[len(copies)])
        copy.start()
        copies.append(copy)

    for at in range(2):
        begin(left_own.at[pl.ds(rows[at] * links, links)], left.at[0, pl.ds(at * links, links)])
    begin(left_other.at[pl.ds(table // 2, 2 * links)], left.at[1])
    if not first:
        begin(hd_own.at[x], diag.at[0])
        begin(hd_far, diag.at[1])

    def allowed(a, q, value):
        return lax.select(pattern[a, q] != 0, value, jnp.zeros_like(value))

    for piece, offsets in zip(pieces, plan):
        base = 2 * half if piece.shape[0] == 4 else 0
        for at, (dz, dx, dc, start, tall) in enumerate(offsets):
            row = row_of(dz, dx, dc)
            for line in range(0, tall, 16):
                value = piece[base + at, line : line + 16, 0:width]
                if first:
                    value = value * masks[row]
                field[row, start + line : start + line + 16, :] = value

    def right_col(term, b, j):
        return cols_other[j, b] if term else right_cols[j, 0, b]

    def left_col(term, a, j):
        return cols_other[8 + j, a] if term else left_cols[j, 0, a]

    sources = [[left_col(term, rows[at], j) for at in range(2) for j in range(links)] for term in range(2)]

    deep = links * block

    none = jnp.zeros((block, block), jnp.bfloat16)
    pair = 2

    def image(n, carry):
        picks = [(i, j) for i in range(pair) for j in range(links)]
        for term in range(2):
            found = [right_col(term, n * pair + i, j) for i, j in picks]
            lhs = []
            for source in sources[term]:
                line = []
                for col in found:
                    value = field[source, :, pl.ds(pl.multiple_of(col * block, block), block)]
                    line.append(value)
                lhs.append(jnp.concatenate(line, axis=1))
            rhs = []
            for i, j in picks:
                tile = right[term, (n * pair + i) * links + j]
                rhs.append(jnp.concatenate([tile if i == at else none for at in range(pair)], axis=1))
            product = jnp.dot(
                jnp.concatenate(lhs, axis=0),
                jnp.concatenate(rhs, axis=0),
                preferred_element_type=jnp.float32,
            )
            product = product.astype(jnp.bfloat16)
            span = pl.ds(pl.multiple_of(n * pair * block, pair * block), pair * block)
            for at in range(2):
                images[at, term * deep : (term + 1) * deep, span] = product[at * deep : (at + 1) * deep]
        return carry

    lax.fori_loop(0, sectors // pair, image, 0, unroll=2)
    for copy in copies:
        copy.wait()

    step = 2
    early_rows = block // 2
    zero = jnp.zeros((8, LANES), jnp.float32)

    def column(n, sums):
        start = pl.multiple_of(n * step * block, step * block)
        span = pl.ds(start, step * block)
        sums = list(sums)

        def masked(a, value):
            parts = [
                allowed(a, n * step + i, value[:, i * block : (i + 1) * block]) for i in range(step)
            ]
            return jnp.concatenate(parts, axis=1)

        for at in range(2):
            weights = [left[term, at * links + j] for term in range(2) for j in range(links)]
            total = jnp.dot(
                jnp.concatenate(weights, axis=1),
                images[at, :, span],
                preferred_element_type=jnp.float32,
            )
            offdiag = masked(rows[at], total.astype(jnp.bfloat16).astype(jnp.float32))
            own = field[rows[at], :, span].astype(jnp.float32)
            if first:
                psi_out[at, :, span] = own.astype(jnp.bfloat16)
                off_out[at, :, span] = offdiag.astype(jnp.bfloat16)
                sums[0] += fold(own * own)
                sums[1] += fold(own * offdiag)
            else:
                weight = diag[at, :, span].astype(jnp.float32)
                narrow = (weight * own + offdiag).astype(jnp.bfloat16)
                if at == 0:
                    near_out[:, span] = narrow
                else:
                    far_out[:, span] = narrow[:early_rows]
                    late_out[:, span] = narrow[early_rows:]
                second = narrow.astype(jnp.float32)
                wave = psi_in[at, :, span].astype(jnp.float32)
                sigma_one = weight * wave + off_in[at, :, span].astype(jnp.float32)
                sums[0] += fold(wave * second)
                sums[1] += fold(own * sigma_one)
                sums[2] += fold(own * second)
        return tuple(sums)

    sums = list(lax.fori_loop(0, sectors // step, column, (zero,) * (2 if first else 3)))
    if first:
        parts = [
            piece[0, 0:48, width:] for piece, offsets in zip(pieces, plan) if offsets[0][:3] in MIXES
        ]
        far_weight = sum(part.astype(jnp.float32) for part in parts)
        sums[1] += weight_own[...] + (far_weight[0:8] + far_weight[16:24] + far_weight[32:40])
    stats_out[...] = jnp.zeros_like(stats_out)
    for at, value in enumerate(sums):
        stats_out[at : at + 1, :] = jnp.sum(value, axis=0, keepdims=True)
    if not first:
        stats_out[3:5, :] = stats_in[0:2, :]


def operate(first, plan, pieces, cols, pattern, right, left, extra):
    _, table, block, _ = right.shape
    width = pieces[0].shape[2]
    sectors = width // block
    links = table // sectors
    rows = jax.ShapeDtypeStruct((2, block, width), jnp.bfloat16)
    one = jax.ShapeDtypeStruct((block, width), jnp.bfloat16)
    some = jax.ShapeDtypeStruct((block // 2, width), jnp.bfloat16)
    stats = jax.ShapeDtypeStruct((8, LANES), jnp.float32)
    out_shape = (rows, rows, stats) if first else (one, some, some, stats)
    extra_specs = [VMEM, VMEM] if first else [ANY, ANY, VMEM, VMEM, VMEM]
    inner = 2 * 2 * sectors * 2 * links * links * block * block * block
    outer = 2 * 2 * 2 * links * block * block * width
    return pl.pallas_call(
        functools.partial(operate_kernel, first, plan),
        out_shape=out_shape,
        in_specs=[SMEM, SMEM, SMEM, SMEM, VMEM, ANY, ANY] + [VMEM] * len(pieces) + extra_specs,
        out_specs=(VMEM,) * len(out_shape),
        scratch_shapes=[
            pltpu.VMEM((sectors, block, width), jnp.bfloat16),
            pltpu.VMEM((2, 2 * links * block, width), jnp.bfloat16),
            pltpu.VMEM((2, 2 * links, block, block), jnp.bfloat16),
            pltpu.VMEM((2, block, width), jnp.bfloat16),
            pltpu.SemaphoreType.DMA((5,)),
        ],
        compiler_params=pltpu.CompilerParams(vmem_limit_bytes=OPERATE_LIMIT),
        cost_estimate=pl.CostEstimate(
            flops=inner + outer if first else 0,
            bytes_accessed=16 * 1024 * 1024 if first else 1024,
            transcendentals=0,
        ),
        name="operate_first" if first else "operate_second",
    )(*cols, pattern, right, *left, *pieces, *extra)


def arrange_kernel(own, near, far, out, found, sems):
    _, _, c = place()
    part = own.shape[0] // 2
    copies = [
        pltpu.make_async_copy(own, found.at[0], sems.at[0]),
        pltpu.make_async_copy(near.at[pl.ds(0, part)], found.at[1, pl.ds(c * part, part)], sems.at[1]),
        pltpu.make_async_copy(far.at[pl.ds(0, part)], found.at[1, pl.ds((1 - c) * part, part)], sems.at[2]),
    ]
    for copy in copies:
        copy.start()
    for copy in copies:
        copy.wait()

    def turn(at, carry):
        for term in range(2):
            out[term, at] = found[term, at].T
        return carry

    lax.fori_loop(0, found.shape[1], turn, 0, unroll=4)


def arrange(own, near, far):
    shape = (2, *own.shape)
    return pl.pallas_call(
        arrange_kernel,
        out_shape=jax.ShapeDtypeStruct(shape, own.dtype),
        in_specs=[ANY] * 3,
        out_specs=VMEM,
        scratch_shapes=[pltpu.VMEM(shape, own.dtype), pltpu.SemaphoreType.DMA((3,))],
        compiler_params=pltpu.CompilerParams(vmem_limit_bytes=VMEM_LIMIT),
        name="arrange",
    )(own, near, far)


def prepare_kernel(
    pattern, theta, hd, right, left, right_cols, left_cols, mix_a, mix_b, packed, own_out, waves, diag, spots, sems
):
    z, x, c = place()
    half = z // 2
    middle = in_middle(z)
    mine = 4 * z + 2 * c + x
    block, width = diag.shape
    sectors = width // block
    links = right.shape[0] // sectors
    part = right.shape[0] // 2
    root_a = jnp.where(middle, half, 1 - half)
    rows = pl.ds(0, width)
    sources = (
        (theta.at[half, x], waves.at[0]),
        (theta.at[1 - half, x], waves.at[1]),
        (hd.at[x], diag),
        (theta.at[root_a, jnp.where(middle, 0, x)], mix_a.at[:, rows]),
        (theta.at[1 - root_a, jnp.where(middle, x, 0)], mix_b.at[:, rows]),
        (right.at[pl.ds(c * part, part)], packed.at[pl.ds(0, part)]),
        (left.at[pl.ds((mine ^ 1) * links, links)], packed.at[pl.ds(part, links)]),
        (left.at[pl.ds((mine ^ 13) * links, links)], packed.at[pl.ds(part + links, links)]),
    )
    copies = [
        pltpu.make_async_copy(source, target, sems.at[at])
        for at, (source, target) in enumerate(sources)
    ]
    for copy in copies:
        copy.start()
    last = part + 2 * links
    spots[...] = jnp.zeros_like(spots)
    spots[0:links, 0:sectors] = right_cols[:, 0, :].astype(jnp.float32)
    spots[8 : 8 + links, 0:sectors] = left_cols[:, 0, :].astype(jnp.float32)
    packed[last] = jnp.zeros_like(packed[last])
    packed[last, 0:16, :] = spots[...].astype(jnp.bfloat16)
    for copy in copies[:3]:
        copy.wait()
    zero = jnp.zeros((8, LANES), jnp.float32)

    def column(q, sums):
        span = pl.ds(pl.multiple_of(q * block, block), block)
        weight = diag[:, span].astype(jnp.float32)
        weight = jnp.where(pattern[mine, q] != 0, weight, jnp.zeros_like(weight))
        found = []
        for root in range(2):
            wave = waves[root, :, span].astype(jnp.float32)
            found.append(sums[root] + fold(weight * wave * wave))
        return tuple(found)

    near, far = lax.fori_loop(0, sectors, column, (zero, zero), unroll=4)
    own_out[...] = near
    left_over = jnp.concatenate([far, zero], axis=0)
    parts = []
    for _ in range(3):
        piece = left_over.astype(jnp.bfloat16)
        parts.append(piece)
        left_over = left_over - piece.astype(jnp.float32)
    parts.append(jnp.zeros((block - 48, LANES), jnp.bfloat16))
    tail = jnp.concatenate(parts, axis=0)
    none = jnp.zeros_like(tail)
    mix_a[:, width:] = jnp.where(middle, none, tail)
    mix_b[:, width:] = jnp.where(middle, tail, none)
    for copy in copies[3:]:
        copy.wait()


def prepare(pattern, theta, hd, right, left, *cols):
    _, _, block, width = theta.shape
    table = right.shape[0]
    links = table * block // width
    kind = jnp.bfloat16
    mix = jax.ShapeDtypeStruct((block, width + LANES), kind)
    packed = jax.ShapeDtypeStruct((table // 2 + 2 * links + 1, block, block), kind)
    return pl.pallas_call(
        prepare_kernel,
        out_shape=(mix, mix, packed, jax.ShapeDtypeStruct((8, LANES), jnp.float32)),
        in_specs=[SMEM, ANY, ANY, ANY, ANY, VMEM, VMEM],
        out_specs=(VMEM,) * 4,
        scratch_shapes=[
            pltpu.VMEM((2, block, width), kind),
            pltpu.VMEM((block, width), kind),
            pltpu.VMEM((16, LANES), jnp.float32),
            pltpu.SemaphoreType.DMA((8,)),
        ],
        compiler_params=pltpu.CompilerParams(vmem_limit_bytes=PREPARE_LIMIT),
        name="prepare",
    )(pattern, theta, hd, right, left, *cols)


def total_of(rows):
    return jnp.sum(rows, axis=1, keepdims=True)


def update_kernel(psi, off, hd_own, hd_far, *refs):
    stats, (t_out, stats_out, diag, sems) = refs[:4], refs[4:]
    z, x, c = place()
    copies = [
        pltpu.make_async_copy(hd_own.at[x], diag.at[0], sems.at[0]),
        pltpu.make_async_copy(hd_far, diag.at[1], sems.at[1]),
    ]
    for copy in copies:
        copy.start()
    whole = sum(ref[at, 0:2, :] for ref in stats for at in range(2))
    norm_sq, energy_sum = total_of(whole[0:1, :]), total_of(whole[1:2, :])
    energy = energy_sum / (norm_sq + 1e-06)
    mine = total_of(stats[0][0, 0:1, :])
    for copy in copies:
        copy.wait()
    _, block, width = psi.shape
    step = 16
    zero = jnp.zeros((8, LANES), jnp.float32)

    def chunk(n, total):
        span = pl.ds(pl.multiple_of(n * step, step), step)
        for at in range(2):
            wave = psi[at, span, :].astype(jnp.float32)
            weight = diag[at, span, :].astype(jnp.float32)
            sigma = weight * wave + off[at, span, :].astype(jnp.float32)
            shifted = weight - energy
            t = (sigma - energy * wave) * shifted / (shifted * shifted + 1.0)
            t_out[at, span, :] = t
            total = total + fold(wave * t)
        return total

    lanes = jnp.sum(lax.fori_loop(0, block // step, chunk, zero), axis=0, keepdims=True)
    correlation = total_of(lanes)
    local = jnp.where(mine > 0.0, correlation / jnp.where(mine > 0.0, mine, 1.0), 0.0)

    def within(n, total):
        span = pl.ds(pl.multiple_of(n * step, step), step)
        for at in range(2):
            rest = t_out[at, span, :] - local * psi[at, span, :].astype(jnp.float32)
            total = total + fold(rest * rest)
        return total

    spread = jnp.sum(lax.fori_loop(0, block // step, within, zero), axis=0, keepdims=True)
    stats_out[...] = jnp.zeros_like(stats_out)
    stats_out[0:1, :] = jnp.broadcast_to(correlation, (1, LANES))
    stats_out[1:2, :] = jnp.broadcast_to(total_of(spread), (1, LANES))
    stats_out[2:3, :] = jnp.broadcast_to(mine, (1, LANES))
    stats_out[3:4, :] = jnp.broadcast_to(local, (1, LANES))
    stats_out[4:5, :] = jnp.broadcast_to(norm_sq, (1, LANES))


def correct_kernel(psi, t, *refs):
    stats, outs = refs[:4], refs[4:]
    stats = [ref.at[at] for ref in stats for at in range(2)]
    norm_sq = stats[0][4:5, 0:1]
    factor = sum(ref[0:1, 0:1] for ref in stats) / (norm_sq + 1e-06)
    length_sq = jnp.zeros((1, 1), jnp.float32)
    for ref in stats:
        gap = factor - ref[3:4, 0:1]
        length_sq = length_sq + (ref[1:2, 0:1] + gap * gap * ref[2:3, 0:1])
    scale = jnp.sqrt(norm_sq / (length_sq + 1e-06))
    _, block, width = psi.shape
    step = 16

    def chunk(n, carry):
        span = pl.ds(pl.multiple_of(n * step, step), step)
        for at in range(2):
            wave = psi[at, span, :].astype(jnp.float32)
            outs[at][span, :] = ((t[at, span, :] - factor * wave) * scale).astype(jnp.bfloat16)
        return carry

    lax.fori_loop(0, block // step, chunk, 0)


def assemble_kernel(places, based, *refs):
    count = len(places)
    pieces, (out, sems) = refs[:count], refs[count + based :]
    z, x, c = place()
    half = z // 2
    copies = []
    for at, (root, flip, start) in enumerate(places):
        size = pieces[at].shape[0]
        target = out.at[half ^ root, x ^ flip, pl.ds(start, size)]
        copies.append(pltpu.make_async_copy(pieces[at], target, sems.at[at]))
    for copy in copies:
        copy.start()
    for copy in copies:
        copy.wait()


def assemble(block, pieces, places, base=None):
    width = pieces[0].shape[1]
    based = [] if base is None else [base]
    return pl.pallas_call(
        functools.partial(assemble_kernel, places, len(based)),
        out_shape=jax.ShapeDtypeStruct((2, 2, block, width), pieces[0].dtype),
        in_specs=[VMEM] * len(pieces) + [ANY] * len(based),
        out_specs=ANY,
        scratch_shapes=[pltpu.SemaphoreType.DMA((len(pieces),))],
        input_output_aliases={len(pieces): 0} if based else {},
        compiler_params=pltpu.CompilerParams(vmem_limit_bytes=VMEM_LIMIT),
        name="assemble",
    )(*pieces, *based)


def after(value, *others):
    return lax.optimization_barrier((value, *others))[0]


def shards(theta, hdiag, pattern, left_blocks, left_cols, right_blocks, right_cols):
    roots, row_count, width = theta.shape
    sectors = pattern.shape[0]
    block = width // sectors
    z, x, c = place()
    half = z // 2
    mine = 4 * z + 2 * c + x

    halves = theta.reshape(roots, 2, block, width)
    diag = hdiag.reshape(2, block, width)
    middle = in_middle(z)
    right = right_blocks.reshape(-1, block, block)
    left = left_blocks.reshape(-1, block, block)
    cols = (right_cols.transpose(2, 0, 1), left_cols.transpose(2, 0, 1))

    mix_a, mix_b, packed, weight_own = prepare(pattern, halves, diag, right, left, *cols)
    mix_a = lax.ppermute(mix_a, "blk", [(0, 2), (2, 3), (3, 1), (1, 0)])
    mix_b = lax.ppermute(mix_b, "blk", [(0, 1), (1, 3), (3, 2), (2, 0)])
    operators = across(packed, "ops", 1)
    theta_core = across(theta, "sub", 1)

    mix_a, mix_b = after((mix_a, mix_b), theta_core)
    far = jnp.where(middle, mix_a[:, :width], mix_b[:, :width])
    far_z = across(far, "blk", 1)
    far_x = across(far, "ops", 1)
    mix_a_core = across(mix_a, "sub", 1)
    mix_b_core = across(mix_b, "sub", 1)
    operators = after(operators, mix_b)
    operators_core = across(operators, "sub", 1)
    turned = arrange(right, operators, operators_core)
    cols = (*cols, operators[-1, :16, :sectors].astype(jnp.int32))
    masks = jnp.repeat(pattern.astype(jnp.bfloat16), block, axis=1)
    masks = jnp.broadcast_to(masks[:, None, :], (sectors, 16, width))

    own_b = lax.dynamic_slice(halves, (half, 1, 0, 0), (1, 1, block, width))[0, 0]
    near_b = across(after(own_b, mix_a_core, mix_b_core, turned), "blk", 1)
    far_zx = across(far_z, "ops", 1)
    far_x_core = across(far_x, "sub", 1)
    far_z_core = across(far_z, "sub", 1)
    hd_far = lax.dynamic_index_in_dim(diag, x, 0, keepdims=False)
    hd_far = across(after(hd_far, far_z), "blk", 3)
    far_zx_core = across(far_zx, "sub", 1)
    near_b_core = across(near_b, "sub", 1)

    left = (left, operators)
    pieces = [halves.reshape(4, block, width), theta_core.reshape(4, block, width)]
    plan = [
        ((0, 2, 0, 0, block), (0, 3, 0, 0, block)),
        ((0, 2, 1, 0, block), (0, 3, 1, 0, block)),
    ]
    for piece, offset in (
        (mix_a, (MIX_A, 0, 0)),
        (mix_b, (MIX_B, 0, 0)),
        (mix_a_core, (MIX_A, 0, 1)),
        (mix_b_core, (MIX_B, 0, 1)),
        (near_b, (1, 3, 0)),
        (near_b_core, (1, 3, 1)),
        (far_x, (2, 1, 0)),
        (far_x_core, (2, 1, 1)),
        (far_z, (3, 0, 0)),
        (far_z_core, (3, 0, 1)),
        (far_zx, (3, 1, 0)),
        (far_zx_core, (3, 1, 1)),
    ):
        pieces.append(piece[None])
        plan.append((offset + (0, block),))
    psi, off_one, stats_one = operate(
        True, tuple(plan), pieces, cols, pattern, turned, left, (masks, weight_own)
    )

    found = share(stats_one)
    t, stats_two = pl.pallas_call(
        update_kernel,
        out_shape=(
            jax.ShapeDtypeStruct((2, block, width), jnp.float32),
            jax.ShapeDtypeStruct((8, LANES), jnp.float32),
        ),
        in_specs=[VMEM, VMEM, ANY, ANY] + [VMEM] * 4,
        out_specs=(VMEM, VMEM),
        scratch_shapes=[
            pltpu.VMEM((2, block, width), jnp.bfloat16),
            pltpu.SemaphoreType.DMA((2,)),
        ],
        compiler_params=pltpu.CompilerParams(vmem_limit_bytes=VMEM_LIMIT),
        name="update",
    )(psi, off_one, diag, hd_far, *found)
    found = share(stats_two)
    one = jax.ShapeDtypeStruct((block, width), jnp.bfloat16)
    changed_near, changed_far = pl.pallas_call(
        correct_kernel,
        out_shape=(one, one),
        in_specs=[VMEM, VMEM] + [VMEM] * 4,
        out_specs=(VMEM, VMEM),
        compiler_params=pltpu.CompilerParams(vmem_limit_bytes=VMEM_LIMIT),
        name="correct",
    )(psi, t, *found)

    near_z = across(changed_near, "blk", 1)
    far_x = across(changed_far, "ops", 1)
    near_core = across(changed_near, "sub", 1)
    far_core = across(changed_far, "sub", 1)
    other_middle = lax.ppermute(changed_far, "blk", [(1, 2), (2, 1)])
    near_z, far_x = after((near_z, far_x), other_middle)
    near_zx = across(near_z, "ops", 1)
    far_xz = across(far_x, "blk", 1)
    near_x = across(after(changed_near, near_z, far_x), "ops", 1)
    far_z = across(after(changed_far, near_z, far_x), "blk", 1)
    near_z_core = across(near_z, "sub", 1)
    far_x_core = across(far_x, "sub", 1)
    near_x_core = across(near_x, "sub", 1)
    far_z_core = across(far_z, "sub", 1)
    near_zx_core = across(near_zx, "sub", 1)
    far_xz_core = across(far_xz, "sub", 1)
    other_end = lax.ppermute(after(changed_far, near_z, far_x), "blk", [(0, 3), (3, 0)])
    pieces, plan = [], []
    for piece, offset in (
        (changed_near, (0, 0, 0)),
        (changed_far, (3, 0, 0)),
        (near_core, (0, 0, 1)),
        (far_core, (3, 0, 1)),
        (near_z, (1, 0, 0)),
        (far_z, (2, 0, 0)),
        (near_z_core, (1, 0, 1)),
        (far_z_core, (2, 0, 1)),
        (near_x, (0, 1, 0)),
        (far_x, (3, 1, 0)),
        (near_x_core, (0, 1, 1)),
        (far_x_core, (3, 1, 1)),
        (near_zx, (1, 1, 0)),
        (far_xz, (2, 1, 0)),
        (near_zx_core, (1, 1, 1)),
        (far_xz_core, (2, 1, 1)),
    ):
        pieces.append(piece[None])
        plan.append((offset + (0, block),))
    two_near, two_far, two_late, stats_three = operate(
        False, tuple(plan), pieces, cols, pattern, turned, left, (diag, hd_far, psi, off_one, stats_one)
    )

    far_in = across(two_far, "blk", 3)
    near_in = across(two_near, "ops", 1)
    late_in = across(after(two_late, far_in), "blk", 3)
    far_in_x = across(after(far_in, near_in), "ops", 1)
    sums = stats_three + across(stats_three, "sub", 1)
    other = jnp.where(middle, other_middle, after(other_end, sums))
    other_x = across(other, "ops", 1)
    sums = after(sums, far_in)
    both = jnp.stack([sums + across(sums, "blk", 1), across(sums, "blk", 2) + across(sums, "blk", 3)])
    both = after(both, late_in)
    both = both + across(both, "ops", 1)
    other, other_x = after((other, other_x), late_in)
    late_in_x = across(late_in, "ops", 1)
    both = jnp.sum(jnp.where(half == 0, both, both[::-1])[:, :5], axis=2)
    scale = both[:, 3:4] + 1e-06
    subspace = jnp.concatenate([both[:, 4:5], both[:, 0:3]], axis=1) / scale
    places = ((0, 0, 0), (0, 1, 0), (1, 0, 0), (1, 1, 0))
    correction = assemble(block, (changed_near, near_x, other, other_x), places)
    places = ((0, 0, 0), (0, 1, 0), (1, 0, 0), (1, 0, block // 2), (1, 1, 0))
    sigma_two = assemble(block, (two_near, near_in, far_in, late_in, far_in_x), places)
    sigma_two = assemble(block, (late_in_x,), ((1, 1, block // 2),), sigma_two)
    return correction.reshape(theta.shape), sigma_two.reshape(theta.shape), subspace


def solution(mesh):
    in_specs = (
        P("groups", ("blk", "sub"), None),
        P(("groups", "blk", "sub"), None),
        P("groups", None),
        P(("groups", "ops"), None, None, None, None),
        P(("groups", "ops"), None, None),
        P(("groups", "ops"), None, None, None, None),
        P(("groups", "ops"), None, None),
    )
    out_specs = (
        P("groups", ("blk", "sub"), None),
        P("groups", ("blk", "sub"), None),
        P("groups", None),
    )
    body = shards if halves_fit(mesh) else general_shards
    return jax.shard_map(body, mesh=mesh, in_specs=in_specs, out_specs=out_specs, check_vma=False)
```

```python
import functools

import jax
import jax.numpy as jnp
from jax import lax
from jax.experimental import pallas as pl
from jax.experimental.pallas import tpu as pltpu
from jax.sharding import PartitionSpec as P

ANY = pl.BlockSpec(memory_space=pl.ANY)
SMEM = pl.BlockSpec(memory_space=pltpu.SMEM)
VMEM = pl.BlockSpec(memory_space=pltpu.VMEM)
VMEM_LIMIT = 24 * 1024 * 1024
OPERATE_LIMIT = 44 * 1024 * 1024
PREPARE_LIMIT = 56 * 1024 * 1024
LANES = 128


def apply_right(field_in, blocks, columns):
    roots_here, row_count, full_width = field_in.shape
    term_count, sectors, link_count = columns.shape
    block_size = full_width // sectors
    grouped = field_in.reshape(roots_here, row_count, sectors, block_size)
    picked = jnp.take(grouped, columns.reshape(-1), axis=2)
    picked = picked.reshape(roots_here, row_count, term_count, sectors, link_count, block_size)
    product = jnp.einsum("nrkbjq,kbjpq->knrbp", picked, blocks, preferred_element_type=jnp.float32)
    return product.reshape(term_count, roots_here, row_count, full_width).astype(jnp.bfloat16)


def take_rows(stacked, indices):
    return jnp.take(stacked, indices, axis=1)


def apply_left(arrived, blocks, columns):
    term_count, roots_here, full_width, col_count = arrived.shape
    sectors = columns.shape[1]
    link_count = columns.shape[2]
    block_size = full_width // sectors
    grouped = arrived.reshape(term_count, roots_here, sectors, block_size, col_count)
    picked = jax.vmap(take_rows)(grouped, columns.reshape(term_count, sectors * link_count))
    picked = picked.reshape(term_count, roots_here, sectors, link_count, block_size, col_count)
    product = jnp.einsum("kajpq,knajqc->napc", blocks, picked, preferred_element_type=jnp.float32)
    return product.reshape(roots_here, full_width, col_count)


def general_shards(theta, hdiag, pattern, left_blocks, left_cols, right_blocks, right_cols):
    roots_here, row_count, full_width = theta.shape
    sectors = pattern.shape[0]
    block_size = full_width // sectors
    first_row = lax.axis_index(("blk", "sub")) * row_count
    block_row = (first_row + jnp.arange(row_count, dtype=jnp.int32)) // block_size
    onehot = (block_row[:, None] == jnp.arange(sectors, dtype=jnp.int32)[None, :]).astype(
        jnp.float32
    )
    row_pattern = jnp.dot(onehot, pattern.astype(jnp.float32), preferred_element_type=jnp.float32)
    allowed = jnp.broadcast_to(row_pattern[:, :, None], (row_count, sectors, block_size))
    allowed = allowed.reshape(row_count, full_width).astype(jnp.bfloat16)
    diagonal = hdiag.astype(jnp.float32)
    peers = lax.axis_size("blk") * lax.axis_size("sub")

    def left_part(arrived):
        return apply_left(arrived, left_blocks, left_cols)

    def operate(field_in):
        images = apply_right(field_in, right_blocks, right_cols)
        partial_sum = left_part(
            lax.all_to_all(images, ("blk", "sub"), split_axis=3, concat_axis=2, tiled=True)
        )
        shares = lax.psum_scatter(partial_sum, "ops", scatter_dimension=2, tiled=True)
        returned = lax.all_to_all(
            shares.astype(jnp.bfloat16), ("blk", "sub"), split_axis=1, concat_axis=2, tiled=True
        )
        gathered = lax.all_gather(returned, "ops", axis=2, tiled=True)
        narrow = returned.shape[2] // peers
        gathered = gathered.reshape(roots_here, row_count, lax.axis_size("ops"), peers, narrow)
        offdiag = gathered.transpose(0, 1, 3, 2, 4).reshape(roots_here, row_count, full_width)
        offdiag = offdiag * allowed[None]
        return diagonal[None] * field_in.astype(jnp.float32) + offdiag.astype(jnp.float32)

    projected = theta * allowed[None]
    wave = projected.astype(jnp.float32)
    sigma_one = operate(projected)
    norm_sq, energy_sum = lax.psum(
        (jnp.sum(wave * wave, axis=(1, 2)), jnp.sum(wave * sigma_one, axis=(1, 2))), ("blk", "sub")
    )
    denominator = norm_sq + 1e-06
    energy = energy_sum / denominator
    shifted = diagonal[None] - energy[:, None, None]
    update = (sigma_one - energy[:, None, None] * wave) * shifted / (shifted * shifted + 1.0)
    correlation = lax.psum(jnp.sum(wave * update, axis=(1, 2)), ("blk", "sub"))
    factor = correlation / denominator
    orthogonal = update - factor[:, None, None] * wave
    length_sq = lax.psum(jnp.sum(orthogonal * orthogonal, axis=(1, 2)), ("blk", "sub"))
    correction = (orthogonal * jnp.sqrt(norm_sq / (length_sq + 1e-06))[:, None, None]).astype(
        jnp.bfloat16
    )
    sigma_two = operate(correction).astype(jnp.bfloat16)
    second = sigma_two.astype(jnp.float32)
    fixed = correction.astype(jnp.float32)
    cross_one, cross_two, cross_three = lax.psum(
        (
            jnp.sum(wave * second, axis=(1, 2)),
            jnp.sum(fixed * sigma_one, axis=(1, 2)),
            jnp.sum(fixed * second, axis=(1, 2)),
        ),
        ("blk", "sub"),
    )
    subspace = (
        jnp.stack([energy_sum, cross_one, cross_two, cross_three], axis=1) / denominator[:, None]
    )
    return (correction, sigma_two, subspace)


MIX_A, MIX_B = 4, 5
MIXES = ((MIX_A, 0, 0), (MIX_B, 0, 0))


def halves_fit(mesh):
    sizes = dict(mesh.shape)
    return sizes["blk"] == 4 and sizes["ops"] == 2 and sizes["sub"] == 2


def across(value, axis, distance):
    size = lax.axis_size(axis)
    return lax.ppermute(value, axis, [(i, i ^ distance) for i in range(size)])


def share(stats):
    axes = ("blk", "ops")
    count = lax.axis_size("blk") * lax.axis_size("ops")
    pair = jnp.stack([stats, across(stats, "sub", 1)])
    found = [pair]
    for distance in (1, 2, 3):
        found.append(lax.ppermute(pair, axes, [(i, i ^ distance) for i in range(count)]))
    return found


def place():
    return lax.axis_index("blk"), lax.axis_index("ops"), lax.axis_index("sub")


def fold(value):
    rows, width = value.shape
    value = jnp.sum(value.reshape(rows // 8, 8, width), axis=0)
    return sum(value[:, at : at + LANES] for at in range(0, width, LANES))


def in_middle(z):
    return jnp.logical_or(z == 1, z == 2)


def row_of(dz, dx, dc):
    z, x, c = place()
    if dz in (MIX_A, MIX_B):
        far = in_middle(z) if dz == MIX_A else jnp.logical_not(in_middle(z))
        return jnp.where(far, row_of(2, 0, dc), row_of(1, 2, dc))
    return 4 * (z ^ dz) + 2 * (c ^ dc) + (x ^ dx if dx < 2 else dx - 2)


def operate_kernel(first, ats, plan, right_cols, left_cols, cols_other, pattern, right, left_own, left_other, *refs):
    count = len(plan)
    pieces, refs = refs[:count], refs[count:]
    if first:
        masks, weight_own, psi_out, off_out, stats_out = refs[:5]
        refs = refs[5:]
    else:
        hd_own, hd_far, psi_in, off_in, stats_in = refs[:5]
        result_outs, stats_out, refs = refs[5:-6], refs[-6], refs[-5:]
    field, images, left, diag, sems = refs
    z, x, c = place()
    sectors, block, width = field.shape
    table = right.shape[1]
    links = table // sectors
    mine = 4 * z + 2 * c + x
    rows = (mine, mine ^ 12)
    half = z // 2

    copies = []

    def begin(source, target):
        copy = pltpu.make_async_copy(source, target, sems.at[len(copies)])
        copy.start()
        copies.append(copy)

    for at in ats:
        begin(left_own.at[pl.ds(rows[at] * links, links)], left.at[0, pl.ds(at * links, links)])
    begin(left_other.at[pl.ds(table // 2, 2 * links)], left.at[1])
    if not first:
        begin(hd_own.at[x], diag.at[0])
        begin(hd_far, diag.at[1])

    def allowed(a, q, value):
        return lax.select(pattern[a, q] != 0, value, jnp.zeros_like(value))

    for piece, offsets in zip(pieces, plan):
        base = 2 * half if piece.shape[0] == 4 else 0
        for at, (dz, dx, dc, start, tall) in enumerate(offsets):
            row = row_of(dz, dx, dc)
            for line in range(0, tall, 16):
                value = piece[base + at, line : line + 16, 0:width]
                if first:
                    value = value * masks[row]
                field[row, start + line : start + line + 16, :] = value

    def right_col(term, b, j):
        return cols_other[j, b] if term else right_cols[j, 0, b]

    def left_col(term, a, j):
        return cols_other[8 + j, a] if term else left_cols[j, 0, a]

    sources = [[left_col(term, rows[at], j) for at in ats for j in range(links)] for term in range(2)]

    deep = links * block

    none = jnp.zeros((block, block), jnp.bfloat16)
    pair = 2

    def image(n, carry):
        picks = [(i, j) for i in range(pair) for j in range(links)]
        for term in range(2):
            found = [right_col(term, n * pair + i, j) for i, j in picks]
            lhs = []
            for source in sources[term]:
                line = []
                for col in found:
                    value = field[source, :, pl.ds(pl.multiple_of(col * block, block), block)]
                    line.append(value)
                lhs.append(jnp.concatenate(line, axis=1))
            rhs = []
            for i, j in picks:
                tile = right[term, (n * pair + i) * links + j]
                rhs.append(jnp.concatenate([tile if i == at else none for at in range(pair)], axis=1))
            product = jnp.dot(
                jnp.concatenate(lhs, axis=0),
                jnp.concatenate(rhs, axis=0),
                preferred_element_type=jnp.float32,
            )
            product = product.astype(jnp.bfloat16)
            span = pl.ds(pl.multiple_of(n * pair * block, pair * block), pair * block)
            for at in range(len(ats)):
                images[at, term * deep : (term + 1) * deep, span] = product[at * deep : (at + 1) * deep]
        return carry

    lax.fori_loop(0, sectors // pair, image, 0, unroll=2)
    for copy in copies:
        copy.wait()

    step = 2
    zero = jnp.zeros((8, LANES), jnp.float32)

    def column(n, sums):
        start = pl.multiple_of(n * step * block, step * block)
        span = pl.ds(start, step * block)
        sums = list(sums)

        def masked(a, value):
            parts = [
                allowed(a, n * step + i, value[:, i * block : (i + 1) * block]) for i in range(step)
            ]
            return jnp.concatenate(parts, axis=1)

        for spot, at in enumerate(ats):
            weights = [left[term, at * links + j] for term in range(2) for j in range(links)]
            total = jnp.dot(
                jnp.concatenate(weights, axis=1),
                images[spot, :, span],
                preferred_element_type=jnp.float32,
            )
            offdiag = masked(rows[at], total.astype(jnp.bfloat16).astype(jnp.float32))
            own = field[rows[at], :, span].astype(jnp.float32)
            if first:
                psi_out[at, :, span] = own.astype(jnp.bfloat16)
                off_out[at, :, span] = offdiag.astype(jnp.bfloat16)
                sums[0] += fold(own * own)
                sums[1] += fold(own * offdiag)
            else:
                weight = diag[at, :, span].astype(jnp.float32)
                narrow = (weight * own + offdiag).astype(jnp.bfloat16)
                tall = block // len(result_outs)
                for part, out in enumerate(result_outs):
                    out[:, span] = narrow[part * tall : (part + 1) * tall]
                second = narrow.astype(jnp.float32)
                wave = psi_in[at, :, span].astype(jnp.float32)
                sigma_one = weight * wave + off_in[at, :, span].astype(jnp.float32)
                sums[0] += fold(wave * second)
                sums[1] += fold(own * sigma_one)
                sums[2] += fold(own * second)
        return tuple(sums)

    sums = list(lax.fori_loop(0, sectors // step, column, (zero,) * (2 if first else 3)))
    if first:
        parts = [
            piece[0, 0:48, width:] for piece, offsets in zip(pieces, plan) if offsets[0][:3] in MIXES
        ]
        far_weight = sum(part.astype(jnp.float32) for part in parts)
        sums[1] += weight_own[...] + (far_weight[0:8] + far_weight[16:24] + far_weight[32:40])
    stats_out[...] = jnp.zeros_like(stats_out)
    for at, value in enumerate(sums):
        stats_out[at : at + 1, :] = jnp.sum(value, axis=0, keepdims=True)
    if not first:
        if len(result_outs) == 2:
            stats_out[3:5, :] = stats_in[0:2, :]
        else:
            stats_out[...] = stats_out[...] + stats_in[...]


def operate(first, ats, plan, pieces, cols, pattern, right, left, extra):
    _, table, block, _ = right.shape
    width = pieces[0].shape[2]
    sectors = width // block
    links = table // sectors
    rows = jax.ShapeDtypeStruct((2, block, width), jnp.bfloat16)
    one = jax.ShapeDtypeStruct((block, width), jnp.bfloat16)
    some = jax.ShapeDtypeStruct((block // 2, width), jnp.bfloat16)
    stats = jax.ShapeDtypeStruct((8, LANES), jnp.float32)
    out_shape = (rows, rows, stats) if first else ((some, some, stats) if ats == (1,) else (one, stats))
    extra_specs = [VMEM, VMEM] if first else [ANY, ANY, VMEM, VMEM, VMEM]
    inner = 2 * 2 * sectors * 2 * links * links * block * block * block
    outer = 2 * 2 * 2 * links * block * block * width
    return pl.pallas_call(
        functools.partial(operate_kernel, first, ats, plan),
        out_shape=out_shape,
        in_specs=[SMEM, SMEM, SMEM, SMEM, VMEM, ANY, ANY] + [VMEM] * len(pieces) + extra_specs,
        out_specs=(VMEM,) * len(out_shape),
        scratch_shapes=[
            pltpu.VMEM((sectors, block, width), jnp.bfloat16),
            pltpu.VMEM((len(ats), 2 * links * block, width), jnp.bfloat16),
            pltpu.VMEM((2, 2 * links, block, block), jnp.bfloat16),
            pltpu.VMEM((2, block, width), jnp.bfloat16),
            pltpu.SemaphoreType.DMA((5,)),
        ],
        compiler_params=pltpu.CompilerParams(vmem_limit_bytes=OPERATE_LIMIT),
        cost_estimate=pl.CostEstimate(
            flops=inner + outer if 0 in ats else 0,
            bytes_accessed=64 * 1024 * 1024 if 0 in ats else 1024,
            transcendentals=0,
        ),
        name="operate_first" if first else "operate_second",
    )(*cols, pattern, right, *left, *pieces, *extra)


def arrange_kernel(own, near, far, out, found, sems):
    _, _, c = place()
    part = own.shape[0] // 2
    copies = [
        pltpu.make_async_copy(own, found.at[0], sems.at[0]),
        pltpu.make_async_copy(near.at[pl.ds(0, part)], found.at[1, pl.ds(c * part, part)], sems.at[1]),
        pltpu.make_async_copy(far.at[pl.ds(0, part)], found.at[1, pl.ds((1 - c) * part, part)], sems.at[2]),
    ]
    for copy in copies:
        copy.start()
    for copy in copies:
        copy.wait()

    def turn(at, carry):
        for term in range(2):
            out[term, at] = found[term, at].T
        return carry

    lax.fori_loop(0, found.shape[1], turn, 0, unroll=4)


def arrange(own, near, far):
    shape = (2, *own.shape)
    return pl.pallas_call(
        arrange_kernel,
        out_shape=jax.ShapeDtypeStruct(shape, own.dtype),
        in_specs=[ANY] * 3,
        out_specs=VMEM,
        scratch_shapes=[pltpu.VMEM(shape, own.dtype), pltpu.SemaphoreType.DMA((3,))],
        compiler_params=pltpu.CompilerParams(vmem_limit_bytes=VMEM_LIMIT),
        name="arrange",
    )(own, near, far)


def prepare_kernel(
    pattern, theta, hd, right, left, right_cols, left_cols, mix_a, mix_b, packed, own_out, waves, diag, spots, sems
):
    z, x, c = place()
    half = z // 2
    middle = in_middle(z)
    mine = 4 * z + 2 * c + x
    block, width = diag.shape
    sectors = width // block
    links = right.shape[0] // sectors
    part = right.shape[0] // 2
    root_a = jnp.where(middle, half, 1 - half)
    rows = pl.ds(0, width)
    sources = (
        (theta.at[half, x], waves.at[0]),
        (theta.at[1 - half, x], waves.at[1]),
        (hd.at[x], diag),
        (theta.at[root_a, jnp.where(middle, 0, x)], mix_a.at[:, rows]),
        (theta.at[1 - root_a, jnp.where(middle, x, 0)], mix_b.at[:, rows]),
        (right.at[pl.ds(c * part, part)], packed.at[pl.ds(0, part)]),
        (left.at[pl.ds((mine ^ 1) * links, links)], packed.at[pl.ds(part, links)]),
        (left.at[pl.ds((mine ^ 13) * links, links)], packed.at[pl.ds(part + links, links)]),
    )
    copies = [
        pltpu.make_async_copy(source, target, sems.at[at])
        for at, (source, target) in enumerate(sources)
    ]
    for copy in copies:
        copy.start()
    last = part + 2 * links
    spots[...] = jnp.zeros_like(spots)
    spots[0:links, 0:sectors] = right_cols[:, 0, :].astype(jnp.float32)
    spots[8 : 8 + links, 0:sectors] = left_cols[:, 0, :].astype(jnp.float32)
    packed[last] = jnp.zeros_like(packed[last])
    packed[last, 0:16, :] = spots[...].astype(jnp.bfloat16)
    for copy in copies[:3]:
        copy.wait()
    zero = jnp.zeros((8, LANES), jnp.float32)

    def column(q, sums):
        span = pl.ds(pl.multiple_of(q * block, block), block)
        weight = diag[:, span].astype(jnp.float32)
        weight = jnp.where(pattern[mine, q] != 0, weight, jnp.zeros_like(weight))
        found = []
        for root in range(2):
            wave = waves[root, :, span].astype(jnp.float32)
            found.append(sums[root] + fold(weight * wave * wave))
        return tuple(found)

    near, far = lax.fori_loop(0, sectors, column, (zero, zero), unroll=4)
    own_out[...] = near
    left_over = jnp.concatenate([far, zero], axis=0)
    parts = []
    for _ in range(3):
        piece = left_over.astype(jnp.bfloat16)
        parts.append(piece)
        left_over = left_over - piece.astype(jnp.float32)
    parts.append(jnp.zeros((block - 48, LANES), jnp.bfloat16))
    tail = jnp.concatenate(parts, axis=0)
    none = jnp.zeros_like(tail)
    mix_a[:, width:] = jnp.where(middle, none, tail)
    mix_b[:, width:] = jnp.where(middle, tail, none)
    for copy in copies[3:]:
        copy.wait()


def prepare(pattern, theta, hd, right, left, *cols):
    _, _, block, width = theta.shape
    table = right.shape[0]
    links = table * block // width
    kind = jnp.bfloat16
    mix = jax.ShapeDtypeStruct((block, width + LANES), kind)
    packed = jax.ShapeDtypeStruct((table // 2 + 2 * links + 1, block, block), kind)
    return pl.pallas_call(
        prepare_kernel,
        out_shape=(mix, mix, packed, jax.ShapeDtypeStruct((8, LANES), jnp.float32)),
        in_specs=[SMEM, ANY, ANY, ANY, ANY, VMEM, VMEM],
        out_specs=(VMEM,) * 4,
        scratch_shapes=[
            pltpu.VMEM((2, block, width), kind),
            pltpu.VMEM((block, width), kind),
            pltpu.VMEM((16, LANES), jnp.float32),
            pltpu.SemaphoreType.DMA((8,)),
        ],
        compiler_params=pltpu.CompilerParams(vmem_limit_bytes=PREPARE_LIMIT),
        name="prepare",
    )(pattern, theta, hd, right, left, *cols)


def total_of(rows):
    return jnp.sum(rows, axis=1, keepdims=True)


def update_kernel(psi, off, hd_own, hd_far, *refs):
    stats, (t_out, stats_out, diag, sems) = refs[:4], refs[4:]
    z, x, c = place()
    copies = [
        pltpu.make_async_copy(hd_own.at[x], diag.at[0], sems.at[0]),
        pltpu.make_async_copy(hd_far, diag.at[1], sems.at[1]),
    ]
    for copy in copies:
        copy.start()
    whole = sum(ref[at, 0:2, :] for ref in stats for at in range(2))
    norm_sq, energy_sum = total_of(whole[0:1, :]), total_of(whole[1:2, :])
    energy = energy_sum / (norm_sq + 1e-06)
    mine = total_of(stats[0][0, 0:1, :])
    for copy in copies:
        copy.wait()
    _, block, width = psi.shape
    step = 16
    zero = jnp.zeros((8, LANES), jnp.float32)

    def chunk(n, total):
        span = pl.ds(pl.multiple_of(n * step, step), step)
        for at in range(2):
            wave = psi[at, span, :].astype(jnp.float32)
            weight = diag[at, span, :].astype(jnp.float32)
            sigma = weight * wave + off[at, span, :].astype(jnp.float32)
            shifted = weight - energy
            t = (sigma - energy * wave) * shifted / (shifted * shifted + 1.0)
            t_out[at, span, :] = t
            total = total + fold(wave * t)
        return total

    lanes = jnp.sum(lax.fori_loop(0, block // step, chunk, zero), axis=0, keepdims=True)
    correlation = total_of(lanes)
    local = jnp.where(mine > 0.0, correlation / jnp.where(mine > 0.0, mine, 1.0), 0.0)

    def within(n, total):
        span = pl.ds(pl.multiple_of(n * step, step), step)
        for at in range(2):
            rest = t_out[at, span, :] - local * psi[at, span, :].astype(jnp.float32)
            total = total + fold(rest * rest)
        return total

    spread = jnp.sum(lax.fori_loop(0, block // step, within, zero), axis=0, keepdims=True)
    stats_out[...] = jnp.zeros_like(stats_out)
    stats_out[0:1, :] = jnp.broadcast_to(correlation, (1, LANES))
    stats_out[1:2, :] = jnp.broadcast_to(total_of(spread), (1, LANES))
    stats_out[2:3, :] = jnp.broadcast_to(mine, (1, LANES))
    stats_out[3:4, :] = jnp.broadcast_to(local, (1, LANES))
    stats_out[4:5, :] = jnp.broadcast_to(norm_sq, (1, LANES))


def correct_kernel(psi, t, *refs):
    stats, outs = refs[:4], refs[4:]
    stats = [ref.at[at] for ref in stats for at in range(2)]
    norm_sq = stats[0][4:5, 0:1]
    factor = sum(ref[0:1, 0:1] for ref in stats) / (norm_sq + 1e-06)
    length_sq = jnp.zeros((1, 1), jnp.float32)
    for ref in stats:
        gap = factor - ref[3:4, 0:1]
        length_sq = length_sq + (ref[1:2, 0:1] + gap * gap * ref[2:3, 0:1])
    scale = jnp.sqrt(norm_sq / (length_sq + 1e-06))
    _, block, width = psi.shape
    step = 16

    def chunk(n, carry):
        span = pl.ds(pl.multiple_of(n * step, step), step)
        for at in range(2):
            wave = psi[at, span, :].astype(jnp.float32)
            outs[at][span, :] = ((t[at, span, :] - factor * wave) * scale).astype(jnp.bfloat16)
        return carry

    lax.fori_loop(0, block // step, chunk, 0)


def assemble_kernel(places, based, *refs):
    count = len(places)
    pieces, (out, sems) = refs[:count], refs[count + based :]
    z, x, c = place()
    half = z // 2
    copies = []
    for at, (root, flip, start) in enumerate(places):
        size = pieces[at].shape[0]
        target = out.at[half ^ root, x ^ flip, pl.ds(start, size)]
        copies.append(pltpu.make_async_copy(pieces[at], target, sems.at[at]))
    for copy in copies:
        copy.start()
    for copy in copies:
        copy.wait()


def assemble(block, pieces, places, base=None):
    width = pieces[0].shape[1]
    based = [] if base is None else [base]
    return pl.pallas_call(
        functools.partial(assemble_kernel, places, len(based)),
        out_shape=jax.ShapeDtypeStruct((2, 2, block, width), pieces[0].dtype),
        in_specs=[VMEM] * len(pieces) + [ANY] * len(based),
        out_specs=ANY,
        scratch_shapes=[pltpu.SemaphoreType.DMA((len(pieces),))],
        input_output_aliases={len(pieces): 0} if based else {},
        compiler_params=pltpu.CompilerParams(vmem_limit_bytes=VMEM_LIMIT),
        name="assemble",
    )(*pieces, *based)


def after(value, *others):
    return lax.optimization_barrier((value, *others))[0]


def shards(theta, hdiag, pattern, left_blocks, left_cols, right_blocks, right_cols):
    roots, row_count, width = theta.shape
    sectors = pattern.shape[0]
    block = width // sectors
    z, x, c = place()
    half = z // 2
    mine = 4 * z + 2 * c + x

    halves = theta.reshape(roots, 2, block, width)
    diag = hdiag.reshape(2, block, width)
    middle = in_middle(z)
    chunk = block // 2
    right = right_blocks.reshape(-1, block, block)
    left = left_blocks.reshape(-1, block, block)
    cols = (right_cols.transpose(2, 0, 1), left_cols.transpose(2, 0, 1))

    mix_a, mix_b, packed, weight_own = prepare(pattern, halves, diag, right, left, *cols)
    mix_a = lax.ppermute(mix_a, "blk", [(0, 2), (2, 3), (3, 1), (1, 0)])
    mix_b = lax.ppermute(mix_b, "blk", [(0, 1), (1, 3), (3, 2), (2, 0)])
    operators = across(packed, "ops", 1)
    theta_core = across(theta, "sub", 1)

    mix_a, mix_b = after((mix_a, mix_b), theta_core)
    far = jnp.where(middle, mix_a[:, :width], mix_b[:, :width])
    far_z = [across(far[at : at + chunk], "blk", 1) for at in (0, chunk)]
    far_x = across(far, "ops", 1)
    masks = jnp.repeat(pattern.astype(jnp.bfloat16), block, axis=1)
    masks = jnp.broadcast_to(masks[:, None, :], (sectors, 16, width))
    own_b = lax.dynamic_slice(halves, (half, 1, 0, 0), (1, 1, block, width))[0, 0]
    near_b = across(after(own_b, far_z[0], masks), "blk", 1)
    far_zx = [across(value, "ops", 1) for value in far_z]
    mix_a_core = across(after(mix_a, far_z[0]), "sub", 1)
    mix_b_core = across(after(mix_b, far_z[0]), "sub", 1)
    operators = after(operators, far_z[0])
    operators_core = across(operators, "sub", 1)
    turned = arrange(right, operators, operators_core)
    cols = (*cols, operators[-1, :16, :sectors].astype(jnp.int32))
    far_x_core = across(far_x, "sub", 1)
    far_z_core = [across(value, "sub", 1) for value in far_z]
    hd_far = lax.dynamic_index_in_dim(diag, x, 0, keepdims=False)
    hd_far = across(after(hd_far, far_z[1]), "blk", 3)
    far_zx_core = [across(value, "sub", 1) for value in far_zx]
    near_b_core = across(after(near_b, turned), "sub", 1)

    left = (left, operators)
    pieces = [halves.reshape(4, block, width), theta_core.reshape(4, block, width)]
    plan = [
        ((0, 2, 0, 0, block), (0, 3, 0, 0, block)),
        ((0, 2, 1, 0, block), (0, 3, 1, 0, block)),
    ]
    for piece, offset in (
        (mix_a, (MIX_A, 0, 0)),
        (mix_b, (MIX_B, 0, 0)),
        (mix_a_core, (MIX_A, 0, 1)),
        (mix_b_core, (MIX_B, 0, 1)),
        (near_b, (1, 3, 0)),
        (near_b_core, (1, 3, 1)),
        (far_x, (2, 1, 0)),
        (far_x_core, (2, 1, 1)),
    ):
        pieces.append(piece[None])
        plan.append((offset + (0, block),))
    for at in range(2):
        for piece, offset in (
            (far_z[at], (3, 0, 0)),
            (far_z_core[at], (3, 0, 1)),
            (far_zx[at], (3, 1, 0)),
            (far_zx_core[at], (3, 1, 1)),
        ):
            pieces.append(piece[None])
            plan.append((offset + (at * chunk, chunk),))
    psi, off_one, stats_one = operate(
        True, (0, 1), tuple(plan), pieces, cols, pattern, turned, left, (masks, weight_own)
    )

    found = share(stats_one)
    t, stats_two = pl.pallas_call(
        update_kernel,
        out_shape=(
            jax.ShapeDtypeStruct((2, block, width), jnp.float32),
            jax.ShapeDtypeStruct((8, LANES), jnp.float32),
        ),
        in_specs=[VMEM, VMEM, ANY, ANY] + [VMEM] * 4,
        out_specs=(VMEM, VMEM),
        scratch_shapes=[
            pltpu.VMEM((2, block, width), jnp.bfloat16),
            pltpu.SemaphoreType.DMA((2,)),
        ],
        compiler_params=pltpu.CompilerParams(vmem_limit_bytes=VMEM_LIMIT),
        name="update",
    )(psi, off_one, diag, hd_far, *found)
    found = share(stats_two)
    one = jax.ShapeDtypeStruct((block, width), jnp.bfloat16)
    changed_near, changed_far = pl.pallas_call(
        correct_kernel,
        out_shape=(one, one),
        in_specs=[VMEM, VMEM] + [VMEM] * 4,
        out_specs=(VMEM, VMEM),
        compiler_params=pltpu.CompilerParams(vmem_limit_bytes=VMEM_LIMIT),
        name="correct",
    )(psi, t, *found)

    near_z = across(changed_near, "blk", 1)
    far_x = across(changed_far, "ops", 1)
    near_core = across(changed_near, "sub", 1)
    far_core = across(changed_far, "sub", 1)
    other_middle = lax.ppermute(changed_far, "blk", [(1, 2), (2, 1)])
    near_z, far_x = after((near_z, far_x), other_middle)
    near_zx = across(near_z, "ops", 1)
    far_xz = across(far_x, "blk", 1)
    near_x = across(after(changed_near, near_z, far_x), "ops", 1)
    far_z = across(after(changed_far, near_z, far_x), "blk", 1)
    near_z_core = across(near_z, "sub", 1)
    far_x_core = across(far_x, "sub", 1)
    near_x_core = across(near_x, "sub", 1)
    far_z_core = across(far_z, "sub", 1)
    near_zx_core = across(near_zx, "sub", 1)
    far_xz_core = across(far_xz, "sub", 1)
    other_end = lax.ppermute(after(changed_far, near_z, far_x), "blk", [(0, 3), (3, 0)])
    pieces, plan = [], []
    for piece, offset in (
        (changed_near, (0, 0, 0)),
        (changed_far, (3, 0, 0)),
        (near_core, (0, 0, 1)),
        (far_core, (3, 0, 1)),
        (near_z, (1, 0, 0)),
        (far_z, (2, 0, 0)),
        (near_z_core, (1, 0, 1)),
        (far_z_core, (2, 0, 1)),
        (near_x, (0, 1, 0)),
        (far_x, (3, 1, 0)),
        (near_x_core, (0, 1, 1)),
        (far_x_core, (3, 1, 1)),
        (near_zx, (1, 1, 0)),
        (far_xz, (2, 1, 0)),
        (near_zx_core, (1, 1, 1)),
        (far_xz_core, (2, 1, 1)),
    ):
        pieces.append(piece[None])
        plan.append((offset + (0, block),))
    extra = (diag, hd_far, psi, off_one)
    two_far, two_late, stats_far = operate(
        False, (1,), tuple(plan), pieces, cols, pattern, turned, left, (*extra, stats_one)
    )
    far_in = across(two_far, "blk", 3)
    other = jnp.where(middle, other_middle, after(other_end, two_far))
    other_x = across(other, "ops", 1)
    pieces[0] = after(pieces[0], other)
    two_near, stats_three = operate(
        False, (0,), tuple(plan), pieces, cols, pattern, turned, left, (*extra, stats_far)
    )
    near_in = across(two_near, "ops", 1)
    late_in = across(after(two_late, far_in), "blk", 3)
    far_in_x = across(far_in, "ops", 1)
    sums = stats_three + across(stats_three, "sub", 1)
    sums = after(sums, far_in)
    both = jnp.stack([sums + across(sums, "blk", 1), across(sums, "blk", 2) + across(sums, "blk", 3)])
    both = after(both, late_in)
    both = both + across(both, "ops", 1)
    other, other_x = after((other, other_x), late_in)
    late_in_x = across(late_in, "ops", 1)
    both = jnp.sum(jnp.where(half == 0, both, both[::-1])[:, :5], axis=2)
    scale = both[:, 3:4] + 1e-06
    subspace = jnp.concatenate([both[:, 4:5], both[:, 0:3]], axis=1) / scale
    places = ((0, 0, 0), (0, 1, 0), (1, 0, 0), (1, 1, 0))
    correction = assemble(block, (changed_near, near_x, other, other_x), places)
    places = ((0, 0, 0), (0, 1, 0), (1, 0, 0), (1, 0, block // 2), (1, 1, 0))
    sigma_two = assemble(block, (two_near, near_in, far_in, late_in, far_in_x), places)
    sigma_two = assemble(block, (late_in_x,), ((1, 1, block // 2),), sigma_two)
    return correction.reshape(theta.shape), sigma_two.reshape(theta.shape), subspace


def solution(mesh):
    in_specs = (
        P("groups", ("blk", "sub"), None),
        P(("groups", "blk", "sub"), None),
        P("groups", None),
        P(("groups", "ops"), None, None, None, None),
        P(("groups", "ops"), None, None),
        P(("groups", "ops"), None, None, None, None),
        P(("groups", "ops"), None, None),
    )
    out_specs = (
        P("groups", ("blk", "sub"), None),
        P("groups", ("blk", "sub"), None),
        P("groups", None),
    )
    body = shards if halves_fit(mesh) else general_shards
    return jax.shard_map(body, mesh=mesh, in_specs=in_specs, out_specs=out_specs, check_vma=False)
```

```python
import functools

import jax
import jax.numpy as jnp
from jax import lax
from jax.experimental import pallas as pl
from jax.experimental.pallas import tpu as pltpu
from jax.sharding import PartitionSpec as P

ANY = pl.BlockSpec(memory_space=pl.ANY)
SMEM = pl.BlockSpec(memory_space=pltpu.SMEM)
VMEM = pl.BlockSpec(memory_space=pltpu.VMEM)
VMEM_LIMIT = 24 * 1024 * 1024
OPERATE_LIMIT = 44 * 1024 * 1024
PREPARE_LIMIT = 56 * 1024 * 1024
LANES = 128


def apply_right(field_in, blocks, columns):
    roots_here, row_count, full_width = field_in.shape
    term_count, sectors, link_count = columns.shape
    block_size = full_width // sectors
    grouped = field_in.reshape(roots_here, row_count, sectors, block_size)
    picked = jnp.take(grouped, columns.reshape(-1), axis=2)
    picked = picked.reshape(roots_here, row_count, term_count, sectors, link_count, block_size)
    product = jnp.einsum("nrkbjq,kbjpq->knrbp", picked, blocks, preferred_element_type=jnp.float32)
    return product.reshape(term_count, roots_here, row_count, full_width).astype(jnp.bfloat16)


def take_rows(stacked, indices):
    return jnp.take(stacked, indices, axis=1)


def apply_left(arrived, blocks, columns):
    term_count, roots_here, full_width, col_count = arrived.shape
    sectors = columns.shape[1]
    link_count = columns.shape[2]
    block_size = full_width // sectors
    grouped = arrived.reshape(term_count, roots_here, sectors, block_size, col_count)
    picked = jax.vmap(take_rows)(grouped, columns.reshape(term_count, sectors * link_count))
    picked = picked.reshape(term_count, roots_here, sectors, link_count, block_size, col_count)
    product = jnp.einsum("kajpq,knajqc->napc", blocks, picked, preferred_element_type=jnp.float32)
    return product.reshape(roots_here, full_width, col_count)


def general_shards(theta, hdiag, pattern, left_blocks, left_cols, right_blocks, right_cols):
    roots_here, row_count, full_width = theta.shape
    sectors = pattern.shape[0]
    block_size = full_width // sectors
    first_row = lax.axis_index(("blk", "sub")) * row_count
    block_row = (first_row + jnp.arange(row_count, dtype=jnp.int32)) // block_size
    onehot = (block_row[:, None] == jnp.arange(sectors, dtype=jnp.int32)[None, :]).astype(
        jnp.float32
    )
    row_pattern = jnp.dot(onehot, pattern.astype(jnp.float32), preferred_element_type=jnp.float32)
    allowed = jnp.broadcast_to(row_pattern[:, :, None], (row_count, sectors, block_size))
    allowed = allowed.reshape(row_count, full_width).astype(jnp.bfloat16)
    diagonal = hdiag.astype(jnp.float32)
    peers = lax.axis_size("blk") * lax.axis_size("sub")

    def left_part(arrived):
        return apply_left(arrived, left_blocks, left_cols)

    def operate(field_in):
        images = apply_right(field_in, right_blocks, right_cols)
        partial_sum = left_part(
            lax.all_to_all(images, ("blk", "sub"), split_axis=3, concat_axis=2, tiled=True)
        )
        shares = lax.psum_scatter(partial_sum, "ops", scatter_dimension=2, tiled=True)
        returned = lax.all_to_all(
            shares.astype(jnp.bfloat16), ("blk", "sub"), split_axis=1, concat_axis=2, tiled=True
        )
        gathered = lax.all_gather(returned, "ops", axis=2, tiled=True)
        narrow = returned.shape[2] // peers
        gathered = gathered.reshape(roots_here, row_count, lax.axis_size("ops"), peers, narrow)
        offdiag = gathered.transpose(0, 1, 3, 2, 4).reshape(roots_here, row_count, full_width)
        offdiag = offdiag * allowed[None]
        return diagonal[None] * field_in.astype(jnp.float32) + offdiag.astype(jnp.float32)

    projected = theta * allowed[None]
    wave = projected.astype(jnp.float32)
    sigma_one = operate(projected)
    norm_sq, energy_sum = lax.psum(
        (jnp.sum(wave * wave, axis=(1, 2)), jnp.sum(wave * sigma_one, axis=(1, 2))), ("blk", "sub")
    )
    denominator = norm_sq + 1e-06
    energy = energy_sum / denominator
    shifted = diagonal[None] - energy[:, None, None]
    update = (sigma_one - energy[:, None, None] * wave) * shifted / (shifted * shifted + 1.0)
    correlation = lax.psum(jnp.sum(wave * update, axis=(1, 2)), ("blk", "sub"))
    factor = correlation / denominator
    orthogonal = update - factor[:, None, None] * wave
    length_sq = lax.psum(jnp.sum(orthogonal * orthogonal, axis=(1, 2)), ("blk", "sub"))
    correction = (orthogonal * jnp.sqrt(norm_sq / (length_sq + 1e-06))[:, None, None]).astype(
        jnp.bfloat16
    )
    sigma_two = operate(correction).astype(jnp.bfloat16)
    second = sigma_two.astype(jnp.float32)
    fixed = correction.astype(jnp.float32)
    cross_one, cross_two, cross_three = lax.psum(
        (
            jnp.sum(wave * second, axis=(1, 2)),
            jnp.sum(fixed * sigma_one, axis=(1, 2)),
            jnp.sum(fixed * second, axis=(1, 2)),
        ),
        ("blk", "sub"),
    )
    subspace = (
        jnp.stack([energy_sum, cross_one, cross_two, cross_three], axis=1) / denominator[:, None]
    )
    return (correction, sigma_two, subspace)


def halves_fit(mesh):
    sizes = dict(mesh.shape)
    return sizes["blk"] == 4 and sizes["ops"] == 2 and sizes["sub"] == 2


def across(value, axis, distance):
    size = lax.axis_size(axis)
    return lax.ppermute(value, axis, [(i, i ^ distance) for i in range(size)])


def share(stats):
    axes = ("blk", "ops")
    count = lax.axis_size("blk") * lax.axis_size("ops")
    pair = jnp.stack([stats, across(stats, "sub", 1)])
    found = [pair]
    for distance in (1, 2, 3):
        found.append(lax.ppermute(pair, axes, [(i, i ^ distance) for i in range(count)]))
    return found


def place():
    return lax.axis_index("blk"), lax.axis_index("ops"), lax.axis_index("sub")


def fold(value):
    rows, width = value.shape
    value = jnp.sum(value.reshape(rows // 8, 8, width), axis=0)
    return sum(value[:, at : at + LANES] for at in range(0, width, LANES))


def in_middle(z):
    return jnp.logical_or(z == 1, z == 2)


def row_of(dz, dx, dc):
    z, x, c = place()
    return 4 * (z ^ dz) + 2 * (c ^ dc) + (x ^ dx if dx < 2 else dx - 2)


def operate_kernel(first, plan, right_cols, left_cols, cols_other, pattern, right, left_own, left_other, *refs):
    count = len(plan)
    pieces, refs = refs[:count], refs[count:]
    if first:
        mix_a, mix_b, weight_own, psi_out, off_out, stats_out = refs[:6]
        refs = refs[6:]
    else:
        hd_own, hd_far, psi_in, off_in, stats_in, near_out, far_out, late_out, stats_out = refs[:9]
        refs = refs[9:]
    field, images, left, diag, sems = refs
    z, x, c = place()
    sectors, block, width = field.shape
    table = right.shape[1]
    links = table // sectors
    mine = 4 * z + 2 * c + x
    rows = (mine, mine ^ 12)

    copies = []

    def begin(source, target):
        copy = pltpu.make_async_copy(source, target, sems.at[len(copies)])
        copy.start()
        copies.append(copy)

    for at in range(2):
        begin(left_own.at[pl.ds(rows[at] * links, links)], left.at[0, pl.ds(at * links, links)])
    begin(left_other.at[pl.ds(table // 2, 2 * links)], left.at[1])
    if not first:
        begin(hd_own.at[x], diag.at[0])
        begin(hd_far, diag.at[1])

    def allowed(a, q, value):
        return lax.select(pattern[a, q] != 0, value, jnp.zeros_like(value))

    for piece, offsets in zip(pieces, plan):
        for at, (dz, dx, dc, start, tall) in enumerate(offsets):
            row = row_of(dz, dx, dc)
            for line in range(0, tall, 16):
                value = piece[at, line : line + 16, :]
                field[row, start + line : start + line + 16, :] = value

    def right_col(term, b, j):
        return cols_other[j, b] if term else right_cols[j, 0, b]

    def left_col(term, a, j):
        return cols_other[8 + j, a] if term else left_cols[j, 0, a]

    sources = [[left_col(term, rows[at], j) for at in range(2) for j in range(links)] for term in range(2)]

    deep = links * block

    none = jnp.zeros((block, block), jnp.bfloat16)
    pair = 2

    def image(n, carry):
        picks = [(i, j) for i in range(pair) for j in range(links)]
        for term in range(2):
            found = [right_col(term, n * pair + i, j) for i, j in picks]
            lhs = []
            for source in sources[term]:
                line = []
                for col in found:
                    value = field[source, :, pl.ds(pl.multiple_of(col * block, block), block)]
                    line.append(value)
                lhs.append(jnp.concatenate(line, axis=1))
            rhs = []
            for i, j in picks:
                tile = right[term, (n * pair + i) * links + j]
                rhs.append(jnp.concatenate([tile if i == at else none for at in range(pair)], axis=1))
            product = jnp.dot(
                jnp.concatenate(lhs, axis=0),
                jnp.concatenate(rhs, axis=0),
                preferred_element_type=jnp.float32,
            )
            product = product.astype(jnp.bfloat16)
            span = pl.ds(pl.multiple_of(n * pair * block, pair * block), pair * block)
            for at in range(2):
                images[at, term * deep : (term + 1) * deep, span] = product[at * deep : (at + 1) * deep]
        return carry

    lax.fori_loop(0, sectors // pair, image, 0, unroll=2)
    for copy in copies:
        copy.wait()

    step = 2
    early_rows = block // 2
    zero = jnp.zeros((8, LANES), jnp.float32)

    def column(n, sums):
        start = pl.multiple_of(n * step * block, step * block)
        span = pl.ds(start, step * block)
        sums = list(sums)

        def masked(a, value):
            parts = [
                allowed(a, n * step + i, value[:, i * block : (i + 1) * block]) for i in range(step)
            ]
            return jnp.concatenate(parts, axis=1)

        for at in range(2):
            weights = [left[term, at * links + j] for term in range(2) for j in range(links)]
            total = jnp.dot(
                jnp.concatenate(weights, axis=1),
                images[at, :, span],
                preferred_element_type=jnp.float32,
            )
            offdiag = masked(rows[at], total.astype(jnp.bfloat16).astype(jnp.float32))
            own = field[rows[at], :, span].astype(jnp.float32)
            if first:
                psi_out[at, :, span] = own.astype(jnp.bfloat16)
                off_out[at, :, span] = offdiag.astype(jnp.bfloat16)
                sums[0] += fold(own * own)
                sums[1] += fold(own * offdiag)
            else:
                weight = diag[at, :, span].astype(jnp.float32)
                narrow = (weight * own + offdiag).astype(jnp.bfloat16)
                if at == 0:
                    near_out[:, span] = narrow
                else:
                    far_out[:, span] = narrow[:early_rows]
                    late_out[:, span] = narrow[early_rows:]
                second = narrow.astype(jnp.float32)
                wave = psi_in[at, :, span].astype(jnp.float32)
                sigma_one = weight * wave + off_in[at, :, span].astype(jnp.float32)
                sums[0] += fold(wave * second)
                sums[1] += fold(own * sigma_one)
                sums[2] += fold(own * second)
        return tuple(sums)

    sums = list(lax.fori_loop(0, sectors // step, column, (zero,) * (2 if first else 3)))
    if first:
        far_weight = sum(mix[0:48, width:].astype(jnp.float32) for mix in (mix_a, mix_b))
        sums[1] += weight_own[...] + (far_weight[0:8] + far_weight[16:24] + far_weight[32:40])
    stats_out[...] = jnp.zeros_like(stats_out)
    for at, value in enumerate(sums):
        stats_out[at : at + 1, :] = jnp.sum(value, axis=0, keepdims=True)
    if not first:
        stats_out[3:5, :] = stats_in[0:2, :]


def operate(first, plan, pieces, cols, pattern, right, left, extra):
    _, table, block, _ = right.shape
    width = pieces[0].shape[2]
    sectors = width // block
    links = table // sectors
    rows = jax.ShapeDtypeStruct((2, block, width), jnp.bfloat16)
    one = jax.ShapeDtypeStruct((block, width), jnp.bfloat16)
    some = jax.ShapeDtypeStruct((block // 2, width), jnp.bfloat16)
    stats = jax.ShapeDtypeStruct((8, LANES), jnp.float32)
    out_shape = (rows, rows, stats) if first else (one, some, some, stats)
    extra_specs = [VMEM] * 3 if first else [ANY, ANY, VMEM, VMEM, VMEM]
    inner = 2 * 2 * sectors * 2 * links * links * block * block * block
    outer = 2 * 2 * 2 * links * block * block * width
    return pl.pallas_call(
        functools.partial(operate_kernel, first, plan),
        out_shape=out_shape,
        in_specs=[SMEM, SMEM, SMEM, SMEM, VMEM, ANY, ANY] + [VMEM] * len(pieces) + extra_specs,
        out_specs=(VMEM,) * len(out_shape),
        scratch_shapes=[
            pltpu.VMEM((sectors, block, width), jnp.bfloat16),
            pltpu.VMEM((2, 2 * links * block, width), jnp.bfloat16),
            pltpu.VMEM((2, 2 * links, block, block), jnp.bfloat16),
            pltpu.VMEM((2, block, width), jnp.bfloat16),
            pltpu.SemaphoreType.DMA((5,)),
        ],
        compiler_params=pltpu.CompilerParams(vmem_limit_bytes=OPERATE_LIMIT),
        cost_estimate=pl.CostEstimate(
            flops=inner + outer if first else 0,
            bytes_accessed=16 * 1024 * 1024 if first else 1024,
            transcendentals=0,
        ),
        name="operate_first" if first else "operate_second",
    )(*cols, pattern, right, *left, *pieces, *extra)


def arrange_kernel(own, near, far, out, found, sems):
    _, _, c = place()
    part = own.shape[0] // 2
    copies = [
        pltpu.make_async_copy(own, found.at[0], sems.at[0]),
        pltpu.make_async_copy(near.at[pl.ds(0, part)], found.at[1, pl.ds(c * part, part)], sems.at[1]),
        pltpu.make_async_copy(far.at[pl.ds(0, part)], found.at[1, pl.ds((1 - c) * part, part)], sems.at[2]),
    ]
    for copy in copies:
        copy.start()
    for copy in copies:
        copy.wait()

    def turn(at, carry):
        for term in range(2):
            out[term, at] = found[term, at].T
        return carry

    lax.fori_loop(0, found.shape[1], turn, 0, unroll=4)


def arrange(own, near, far):
    shape = (2, *own.shape)
    return pl.pallas_call(
        arrange_kernel,
        out_shape=jax.ShapeDtypeStruct(shape, own.dtype),
        in_specs=[ANY] * 3,
        out_specs=VMEM,
        scratch_shapes=[pltpu.VMEM(shape, own.dtype), pltpu.SemaphoreType.DMA((3,))],
        compiler_params=pltpu.CompilerParams(vmem_limit_bytes=VMEM_LIMIT),
        name="arrange",
    )(own, near, far)


def prepare_kernel(
    pattern, theta, hd, right, left, right_cols, left_cols, mix_a, mix_b, packed, own_out, waves, diag, spots, sems
):
    z, x, c = place()
    half = z // 2
    middle = in_middle(z)
    mine = 4 * z + 2 * c + x
    block, width = diag.shape
    sectors = width // block
    links = right.shape[0] // sectors
    part = right.shape[0] // 2
    root_a = jnp.where(middle, half, 1 - half)
    rows = pl.ds(0, width)
    sources = (
        (theta.at[half, x], waves.at[0]),
        (theta.at[1 - half, x], waves.at[1]),
        (hd.at[x], diag),
        (theta.at[root_a, jnp.where(middle, 0, x)], mix_a.at[:, rows]),
        (theta.at[1 - root_a, jnp.where(middle, x, 0)], mix_b.at[:, rows]),
        (right.at[pl.ds(c * part, part)], packed.at[pl.ds(0, part)]),
        (left.at[pl.ds((mine ^ 1) * links, links)], packed.at[pl.ds(part, links)]),
        (left.at[pl.ds((mine ^ 13) * links, links)], packed.at[pl.ds(part + links, links)]),
    )
    copies = [
        pltpu.make_async_copy(source, target, sems.at[at])
        for at, (source, target) in enumerate(sources)
    ]
    for copy in copies:
        copy.start()
    last = part + 2 * links
    spots[...] = jnp.zeros_like(spots)
    spots[0:links, 0:sectors] = right_cols[:, 0, :].astype(jnp.float32)
    spots[8 : 8 + links, 0:sectors] = left_cols[:, 0, :].astype(jnp.float32)
    packed[last] = jnp.zeros_like(packed[last])
    packed[last, 0:16, :] = spots[...].astype(jnp.bfloat16)
    for copy in copies[:3]:
        copy.wait()
    zero = jnp.zeros((8, LANES), jnp.float32)

    def column(q, sums):
        span = pl.ds(pl.multiple_of(q * block, block), block)
        weight = diag[:, span].astype(jnp.float32)
        weight = jnp.where(pattern[mine, q] != 0, weight, jnp.zeros_like(weight))
        found = []
        for root in range(2):
            wave = waves[root, :, span].astype(jnp.float32)
            found.append(sums[root] + fold(weight * wave * wave))
        return tuple(found)

    near, far = lax.fori_loop(0, sectors, column, (zero, zero), unroll=4)
    own_out[...] = near
    left_over = jnp.concatenate([far, zero], axis=0)
    parts = []
    for _ in range(3):
        piece = left_over.astype(jnp.bfloat16)
        parts.append(piece)
        left_over = left_over - piece.astype(jnp.float32)
    parts.append(jnp.zeros((block - 48, LANES), jnp.bfloat16))
    tail = jnp.concatenate(parts, axis=0)
    none = jnp.zeros_like(tail)
    mix_a[:, width:] = jnp.where(middle, none, tail)
    mix_b[:, width:] = jnp.where(middle, tail, none)
    for copy in copies[3:]:
        copy.wait()


def prepare(pattern, theta, hd, right, left, *cols):
    _, _, block, width = theta.shape
    table = right.shape[0]
    links = table * block // width
    kind = jnp.bfloat16
    mix = jax.ShapeDtypeStruct((block, width + LANES), kind)
    packed = jax.ShapeDtypeStruct((table // 2 + 2 * links + 1, block, block), kind)
    return pl.pallas_call(
        prepare_kernel,
        out_shape=(mix, mix, packed, jax.ShapeDtypeStruct((8, LANES), jnp.float32)),
        in_specs=[SMEM, ANY, ANY, ANY, ANY, VMEM, VMEM],
        out_specs=(VMEM,) * 4,
        scratch_shapes=[
            pltpu.VMEM((2, block, width), kind),
            pltpu.VMEM((block, width), kind),
            pltpu.VMEM((16, LANES), jnp.float32),
            pltpu.SemaphoreType.DMA((8,)),
        ],
        compiler_params=pltpu.CompilerParams(vmem_limit_bytes=PREPARE_LIMIT),
        name="prepare",
    )(pattern, theta, hd, right, left, *cols)


def total_of(rows):
    return jnp.sum(rows, axis=1, keepdims=True)


def update_kernel(psi, off, hd_own, hd_far, *refs):
    stats, (t_out, stats_out, diag, sems) = refs[:4], refs[4:]
    z, x, c = place()
    copies = [
        pltpu.make_async_copy(hd_own.at[x], diag.at[0], sems.at[0]),
        pltpu.make_async_copy(hd_far, diag.at[1], sems.at[1]),
    ]
    for copy in copies:
        copy.start()
    whole = sum(ref[at, 0:2, :] for ref in stats for at in range(2))
    norm_sq, energy_sum = total_of(whole[0:1, :]), total_of(whole[1:2, :])
    energy = energy_sum / (norm_sq + 1e-06)
    mine = total_of(stats[0][0, 0:1, :])
    for copy in copies:
        copy.wait()
    _, block, width = psi.shape
    step = 16
    zero = jnp.zeros((8, LANES), jnp.float32)

    def chunk(n, total):
        span = pl.ds(pl.multiple_of(n * step, step), step)
        for at in range(2):
            wave = psi[at, span, :].astype(jnp.float32)
            weight = diag[at, span, :].astype(jnp.float32)
            sigma = weight * wave + off[at, span, :].astype(jnp.float32)
            shifted = weight - energy
            t = (sigma - energy * wave) * shifted / (shifted * shifted + 1.0)
            t_out[at, span, :] = t
            total = total + fold(wave * t)
        return total

    lanes = jnp.sum(lax.fori_loop(0, block // step, chunk, zero), axis=0, keepdims=True)
    correlation = total_of(lanes)
    local = jnp.where(mine > 0.0, correlation / jnp.where(mine > 0.0, mine, 1.0), 0.0)

    def within(n, total):
        span = pl.ds(pl.multiple_of(n * step, step), step)
        for at in range(2):
            rest = t_out[at, span, :] - local * psi[at, span, :].astype(jnp.float32)
            total = total + fold(rest * rest)
        return total

    spread = jnp.sum(lax.fori_loop(0, block // step, within, zero), axis=0, keepdims=True)
    stats_out[...] = jnp.zeros_like(stats_out)
    stats_out[0:1, :] = jnp.broadcast_to(correlation, (1, LANES))
    stats_out[1:2, :] = jnp.broadcast_to(total_of(spread), (1, LANES))
    stats_out[2:3, :] = jnp.broadcast_to(mine, (1, LANES))
    stats_out[3:4, :] = jnp.broadcast_to(local, (1, LANES))
    stats_out[4:5, :] = jnp.broadcast_to(norm_sq, (1, LANES))


def correct_kernel(psi, t, *refs):
    stats, outs = refs[:4], refs[4:]
    stats = [ref.at[at] for ref in stats for at in range(2)]
    norm_sq = stats[0][4:5, 0:1]
    factor = sum(ref[0:1, 0:1] for ref in stats) / (norm_sq + 1e-06)
    length_sq = jnp.zeros((1, 1), jnp.float32)
    for ref in stats:
        gap = factor - ref[3:4, 0:1]
        length_sq = length_sq + (ref[1:2, 0:1] + gap * gap * ref[2:3, 0:1])
    scale = jnp.sqrt(norm_sq / (length_sq + 1e-06))
    _, block, width = psi.shape
    step = 16

    def chunk(n, carry):
        span = pl.ds(pl.multiple_of(n * step, step), step)
        for at in range(2):
            wave = psi[at, span, :].astype(jnp.float32)
            outs[at][span, :] = ((t[at, span, :] - factor * wave) * scale).astype(jnp.bfloat16)
        return carry

    lax.fori_loop(0, block // step, chunk, 0)


def assemble_kernel(places, based, *refs):
    count = len(places)
    pieces, (out, sems) = refs[:count], refs[count + based :]
    z, x, c = place()
    half = z // 2
    copies = []
    for at, (root, flip, start) in enumerate(places):
        size = pieces[at].shape[0]
        target = out.at[half ^ root, x ^ flip, pl.ds(start, size)]
        copies.append(pltpu.make_async_copy(pieces[at], target, sems.at[at]))
    for copy in copies:
        copy.start()
    for copy in copies:
        copy.wait()


def assemble(block, pieces, places, base=None):
    width = pieces[0].shape[1]
    based = [] if base is None else [base]
    return pl.pallas_call(
        functools.partial(assemble_kernel, places, len(based)),
        out_shape=jax.ShapeDtypeStruct((2, 2, block, width), pieces[0].dtype),
        in_specs=[VMEM] * len(pieces) + [ANY] * len(based),
        out_specs=ANY,
        scratch_shapes=[pltpu.SemaphoreType.DMA((len(pieces),))],
        input_output_aliases={len(pieces): 0} if based else {},
        compiler_params=pltpu.CompilerParams(vmem_limit_bytes=VMEM_LIMIT),
        name="assemble",
    )(*pieces, *based)


def after(value, *others):
    return lax.optimization_barrier((value, *others))[0]


def shards(theta, hdiag, pattern, left_blocks, left_cols, right_blocks, right_cols):
    roots, row_count, width = theta.shape
    sectors = pattern.shape[0]
    block = width // sectors
    z, x, c = place()
    half = z // 2
    mine = 4 * z + 2 * c + x

    halves = theta.reshape(roots, 2, block, width)
    diag = hdiag.reshape(2, block, width)
    middle = in_middle(z)
    right = right_blocks.reshape(-1, block, block)
    left = left_blocks.reshape(-1, block, block)
    cols = (right_cols.transpose(2, 0, 1), left_cols.transpose(2, 0, 1))

    mix_a, mix_b, packed, weight_own = prepare(pattern, halves, diag, right, left, *cols)
    mix_a = lax.ppermute(mix_a, "blk", [(0, 2), (2, 3), (3, 1), (1, 0)])
    mix_b = lax.ppermute(mix_b, "blk", [(0, 1), (1, 3), (3, 2), (2, 0)])
    operators = across(packed, "ops", 1)

    def masked(row, value):
        line = lax.dynamic_index_in_dim(pattern, row, 0, keepdims=False).astype(jnp.bfloat16)
        return value * jnp.repeat(line, block)[None, :]

    own = [
        masked(row_of(0, 2 + at, 0), lax.dynamic_slice(halves, (half, at, 0, 0), (1, 1, block, width))[0, 0])
        for at in range(2)
    ]
    own_core = [across(value, "sub", 1) for value in own]

    mix_a, mix_b = after((mix_a, mix_b), *own_core)
    far = masked(row_of(2, 0, 0), jnp.where(middle, mix_a[:, :width], mix_b[:, :width]))
    far_z = across(far, "blk", 1)
    far_x = across(far, "ops", 1)
    near_a = masked(row_of(1, 2, 0), jnp.where(middle, mix_b[:, :width], mix_a[:, :width]))
    far_core = across(far, "sub", 1)
    near_a_core = across(near_a, "sub", 1)

    near_b = across(after(own[1], far_z, far_core, near_a_core), "blk", 1)
    far_zx = across(far_z, "ops", 1)
    operators = after(operators, far_z)
    operators_core = across(operators, "sub", 1)
    turned = arrange(right, operators, operators_core)
    cols = (*cols, operators[-1, :16, :sectors].astype(jnp.int32))
    far_x_core = across(far_x, "sub", 1)
    far_z_core = across(far_z, "sub", 1)
    hd_far = lax.dynamic_index_in_dim(diag, x, 0, keepdims=False)
    hd_far = across(after(hd_far, far_z), "blk", 3)
    far_zx_core = across(far_zx, "sub", 1)
    near_b_core = across(near_b, "sub", 1)

    left = (left, operators)
    pieces = []
    plan = []
    for piece, offset in (
        (own[0], (0, 2, 0)),
        (own[1], (0, 3, 0)),
        (own_core[0], (0, 2, 1)),
        (own_core[1], (0, 3, 1)),
        (near_a, (1, 2, 0)),
        (near_b, (1, 3, 0)),
        (near_a_core, (1, 2, 1)),
        (near_b_core, (1, 3, 1)),
        (far, (2, 0, 0)),
        (far_core, (2, 0, 1)),
        (far_x, (2, 1, 0)),
        (far_x_core, (2, 1, 1)),
        (far_z, (3, 0, 0)),
        (far_z_core, (3, 0, 1)),
        (far_zx, (3, 1, 0)),
        (far_zx_core, (3, 1, 1)),
    ):
        pieces.append(piece[None])
        plan.append((offset + (0, block),))
    psi, off_one, stats_one = operate(
        True, tuple(plan), pieces, cols, pattern, turned, left, (mix_a, mix_b, weight_own)
    )

    found = share(stats_one)
    t, stats_two = pl.pallas_call(
        update_kernel,
        out_shape=(
            jax.ShapeDtypeStruct((2, block, width), jnp.float32),
            jax.ShapeDtypeStruct((8, LANES), jnp.float32),
        ),
        in_specs=[VMEM, VMEM, ANY, ANY] + [VMEM] * 4,
        out_specs=(VMEM, VMEM),
        scratch_shapes=[
            pltpu.VMEM((2, block, width), jnp.bfloat16),
            pltpu.SemaphoreType.DMA((2,)),
        ],
        compiler_params=pltpu.CompilerParams(vmem_limit_bytes=VMEM_LIMIT),
        name="update",
    )(psi, off_one, diag, hd_far, *found)
    found = share(stats_two)
    one = jax.ShapeDtypeStruct((block, width), jnp.bfloat16)
    changed_near, changed_far = pl.pallas_call(
        correct_kernel,
        out_shape=(one, one),
        in_specs=[VMEM, VMEM] + [VMEM] * 4,
        out_specs=(VMEM, VMEM),
        compiler_params=pltpu.CompilerParams(vmem_limit_bytes=VMEM_LIMIT),
        name="correct",
    )(psi, t, *found)

    near_z = across(changed_near, "blk", 1)
    far_x = across(changed_far, "ops", 1)
    near_core = across(changed_near, "sub", 1)
    far_core = across(changed_far, "sub", 1)
    other_middle = lax.ppermute(changed_far, "blk", [(1, 2), (2, 1)])
    near_z, far_x = after((near_z, far_x), other_middle)
    near_zx = across(near_z, "ops", 1)
    far_xz = across(far_x, "blk", 1)
    near_x = across(after(changed_near, near_z, far_x), "ops", 1)
    far_z = across(after(changed_far, near_z, far_x), "blk", 1)
    near_z_core = across(near_z, "sub", 1)
    far_x_core = across(far_x, "sub", 1)
    near_x_core = across(near_x, "sub", 1)
    far_z_core = across(far_z, "sub", 1)
    near_zx_core = across(near_zx, "sub", 1)
    far_xz_core = across(far_xz, "sub", 1)
    other_end = lax.ppermute(after(changed_far, near_z, far_x), "blk", [(0, 3), (3, 0)])
    pieces, plan = [], []
    for piece, offset in (
        (changed_near, (0, 0, 0)),
        (changed_far, (3, 0, 0)),
        (near_core, (0, 0, 1)),
        (far_core, (3, 0, 1)),
        (near_z, (1, 0, 0)),
        (far_z, (2, 0, 0)),
        (near_z_core, (1, 0, 1)),
        (far_z_core, (2, 0, 1)),
        (near_x, (0, 1, 0)),
        (far_x, (3, 1, 0)),
        (near_x_core, (0, 1, 1)),
        (far_x_core, (3, 1, 1)),
        (near_zx, (1, 1, 0)),
        (far_xz, (2, 1, 0)),
        (near_zx_core, (1, 1, 1)),
        (far_xz_core, (2, 1, 1)),
    ):
        pieces.append(piece[None])
        plan.append((offset + (0, block),))
    two_near, two_far, two_late, stats_three = operate(
        False, tuple(plan), pieces, cols, pattern, turned, left, (diag, hd_far, psi, off_one, stats_one)
    )

    far_in = across(two_far, "blk", 3)
    near_in = across(two_near, "ops", 1)
    late_in = across(after(two_late, far_in), "blk", 3)
    far_in_x = across(after(far_in, near_in), "ops", 1)
    sums = stats_three + across(stats_three, "sub", 1)
    other = jnp.where(middle, other_middle, after(other_end, sums))
    other_x = across(other, "ops", 1)
    sums = after(sums, far_in)
    both = jnp.stack([sums + across(sums, "blk", 1), across(sums, "blk", 2) + across(sums, "blk", 3)])
    both = after(both, late_in)
    both = both + across(both, "ops", 1)
    other, other_x = after((other, other_x), late_in)
    late_in_x = across(late_in, "ops", 1)
    both = jnp.sum(jnp.where(half == 0, both, both[::-1])[:, :5], axis=2)
    scale = both[:, 3:4] + 1e-06
    subspace = jnp.concatenate([both[:, 4:5], both[:, 0:3]], axis=1) / scale
    places = ((0, 0, 0), (0, 1, 0), (1, 0, 0), (1, 1, 0))
    correction = assemble(block, (changed_near, near_x, other, other_x), places)
    places = ((0, 0, 0), (0, 1, 0), (1, 0, 0), (1, 0, block // 2), (1, 1, 0))
    sigma_two = assemble(block, (two_near, near_in, far_in, late_in, far_in_x), places)
    sigma_two = assemble(block, (late_in_x,), ((1, 1, block // 2),), sigma_two)
    return correction.reshape(theta.shape), sigma_two.reshape(theta.shape), subspace


def solution(mesh):
    in_specs = (
        P("groups", ("blk", "sub"), None),
        P(("groups", "blk", "sub"), None),
        P("groups", None),
        P(("groups", "ops"), None, None, None, None),
        P(("groups", "ops"), None, None),
        P(("groups", "ops"), None, None, None, None),
        P(("groups", "ops"), None, None),
    )
    out_specs = (
        P("groups", ("blk", "sub"), None),
        P("groups", ("blk", "sub"), None),
        P("groups", None),
    )
    body = shards if halves_fit(mesh) else general_shards
    return jax.shard_map(body, mesh=mesh, in_specs=in_specs, out_specs=out_specs, check_vma=False)
```

```python
import functools

import jax
import jax.numpy as jnp
from jax import lax
from jax.experimental import pallas as pl
from jax.experimental.pallas import tpu as pltpu
from jax.sharding import PartitionSpec as P

ANY = pl.BlockSpec(memory_space=pl.ANY)
SMEM = pl.BlockSpec(memory_space=pltpu.SMEM)
VMEM = pl.BlockSpec(memory_space=pltpu.VMEM)
VMEM_LIMIT = 24 * 1024 * 1024
OPERATE_LIMIT = 32 * 1024 * 1024
PREPARE_LIMIT = 56 * 1024 * 1024
LANES = 128


def apply_right(field_in, blocks, columns):
    roots_here, row_count, full_width = field_in.shape
    term_count, sectors, link_count = columns.shape
    block_size = full_width // sectors
    grouped = field_in.reshape(roots_here, row_count, sectors, block_size)
    picked = jnp.take(grouped, columns.reshape(-1), axis=2)
    picked = picked.reshape(roots_here, row_count, term_count, sectors, link_count, block_size)
    product = jnp.einsum("nrkbjq,kbjpq->knrbp", picked, blocks, preferred_element_type=jnp.float32)
    return product.reshape(term_count, roots_here, row_count, full_width).astype(jnp.bfloat16)


def take_rows(stacked, indices):
    return jnp.take(stacked, indices, axis=1)


def apply_left(arrived, blocks, columns):
    term_count, roots_here, full_width, col_count = arrived.shape
    sectors = columns.shape[1]
    link_count = columns.shape[2]
    block_size = full_width // sectors
    grouped = arrived.reshape(term_count, roots_here, sectors, block_size, col_count)
    picked = jax.vmap(take_rows)(grouped, columns.reshape(term_count, sectors * link_count))
    picked = picked.reshape(term_count, roots_here, sectors, link_count, block_size, col_count)
    product = jnp.einsum("kajpq,knajqc->napc", blocks, picked, preferred_element_type=jnp.float32)
    return product.reshape(roots_here, full_width, col_count)


def general_shards(theta, hdiag, pattern, left_blocks, left_cols, right_blocks, right_cols):
    roots_here, row_count, full_width = theta.shape
    sectors = pattern.shape[0]
    block_size = full_width // sectors
    first_row = lax.axis_index(("blk", "sub")) * row_count
    block_row = (first_row + jnp.arange(row_count, dtype=jnp.int32)) // block_size
    onehot = (block_row[:, None] == jnp.arange(sectors, dtype=jnp.int32)[None, :]).astype(
        jnp.float32
    )
    row_pattern = jnp.dot(onehot, pattern.astype(jnp.float32), preferred_element_type=jnp.float32)
    allowed = jnp.broadcast_to(row_pattern[:, :, None], (row_count, sectors, block_size))
    allowed = allowed.reshape(row_count, full_width).astype(jnp.bfloat16)
    diagonal = hdiag.astype(jnp.float32)
    peers = lax.axis_size("blk") * lax.axis_size("sub")

    def left_part(arrived):
        return apply_left(arrived, left_blocks, left_cols)

    def operate(field_in):
        images = apply_right(field_in, right_blocks, right_cols)
        partial_sum = left_part(
            lax.all_to_all(images, ("blk", "sub"), split_axis=3, concat_axis=2, tiled=True)
        )
        shares = lax.psum_scatter(partial_sum, "ops", scatter_dimension=2, tiled=True)
        returned = lax.all_to_all(
            shares.astype(jnp.bfloat16), ("blk", "sub"), split_axis=1, concat_axis=2, tiled=True
        )
        gathered = lax.all_gather(returned, "ops", axis=2, tiled=True)
        narrow = returned.shape[2] // peers
        gathered = gathered.reshape(roots_here, row_count, lax.axis_size("ops"), peers, narrow)
        offdiag = gathered.transpose(0, 1, 3, 2, 4).reshape(roots_here, row_count, full_width)
        offdiag = offdiag * allowed[None]
        return diagonal[None] * field_in.astype(jnp.float32) + offdiag.astype(jnp.float32)

    projected = theta * allowed[None]
    wave = projected.astype(jnp.float32)
    sigma_one = operate(projected)
    norm_sq, energy_sum = lax.psum(
        (jnp.sum(wave * wave, axis=(1, 2)), jnp.sum(wave * sigma_one, axis=(1, 2))), ("blk", "sub")
    )
    denominator = norm_sq + 1e-06
    energy = energy_sum / denominator
    shifted = diagonal[None] - energy[:, None, None]
    update = (sigma_one - energy[:, None, None] * wave) * shifted / (shifted * shifted + 1.0)
    correlation = lax.psum(jnp.sum(wave * update, axis=(1, 2)), ("blk", "sub"))
    factor = correlation / denominator
    orthogonal = update - factor[:, None, None] * wave
    length_sq = lax.psum(jnp.sum(orthogonal * orthogonal, axis=(1, 2)), ("blk", "sub"))
    correction = (orthogonal * jnp.sqrt(norm_sq / (length_sq + 1e-06))[:, None, None]).astype(
        jnp.bfloat16
    )
    sigma_two = operate(correction).astype(jnp.bfloat16)
    second = sigma_two.astype(jnp.float32)
    fixed = correction.astype(jnp.float32)
    cross_one, cross_two, cross_three = lax.psum(
        (
            jnp.sum(wave * second, axis=(1, 2)),
            jnp.sum(fixed * sigma_one, axis=(1, 2)),
            jnp.sum(fixed * second, axis=(1, 2)),
        ),
        ("blk", "sub"),
    )
    subspace = (
        jnp.stack([energy_sum, cross_one, cross_two, cross_three], axis=1) / denominator[:, None]
    )
    return (correction, sigma_two, subspace)


def halves_fit(mesh):
    sizes = dict(mesh.shape)
    return sizes["blk"] == 4 and sizes["ops"] == 2 and sizes["sub"] == 2


def across(value, axis, distance):
    size = lax.axis_size(axis)
    return lax.ppermute(value, axis, [(i, i ^ distance) for i in range(size)])


def share(stats):
    axes = ("blk", "ops")
    count = lax.axis_size("blk") * lax.axis_size("ops")
    pair = jnp.stack([stats, across(stats, "sub", 1)])
    found = [pair]
    for distance in (1, 2, 3):
        found.append(lax.ppermute(pair, axes, [(i, i ^ distance) for i in range(count)]))
    return found


def place():
    return lax.axis_index("blk"), lax.axis_index("ops"), lax.axis_index("sub")


def fold(value):
    rows, width = value.shape
    value = jnp.sum(value.reshape(rows // 8, 8, width), axis=0)
    return sum(value[:, at : at + LANES] for at in range(0, width, LANES))


def in_middle(z):
    return jnp.logical_or(z == 1, z == 2)


def row_of(dz, dx, dc):
    z, x, c = place()
    return 4 * (z ^ dz) + 2 * (c ^ dc) + (x ^ dx if dx < 2 else dx - 2)


def operate_kernel(first, plan, right_cols, left_cols, cols_other, pattern, right, left_own, left_other, *refs):
    count = len(plan)
    pieces, refs = refs[:count], refs[count:]
    if first:
        mix_a, mix_b, weight_own, psi_out, off_out, stats_out = refs[:6]
        refs = refs[6:]
    else:
        hd_own, hd_far, psi_in, off_in, stats_in, near_out, far_out, late_out, stats_out = refs[:9]
        refs = refs[9:]
    field, images, left, diag, parts, sems = refs
    z, x, c = place()
    sectors, block, width = field.shape
    table = right.shape[1]
    links = table // sectors
    mine = 4 * z + 2 * c + x
    rows = (mine, mine ^ 12)

    copies = []

    def begin(source, target):
        copy = pltpu.make_async_copy(source, target, sems.at[len(copies)])
        copy.start()
        copies.append(copy)

    for at in range(2):
        begin(left_own.at[pl.ds(rows[at] * links, links)], left.at[0, pl.ds(at * links, links)])
    begin(left_other.at[pl.ds(table // 2, 2 * links)], left.at[1])
    if first:
        for at, mix in enumerate((mix_a, mix_b)):
            begin(mix.at[pl.ds(0, parts.shape[1]), pl.ds(width, LANES)], parts.at[at])
    else:
        begin(hd_own.at[x], diag.at[0])
        begin(hd_far, diag.at[1])

    def allowed(a, q, value):
        return lax.select(pattern[a, q] != 0, value, jnp.zeros_like(value))

    for piece, offset in zip(pieces, plan):
        row = row_of(*offset)
        for line in range(0, block, 16):
            field[row, line : line + 16, :] = piece[line : line + 16, :]

    def right_col(term, b, j):
        return cols_other[j, b] if term else right_cols[j, 0, b]

    def left_col(term, a, j):
        return cols_other[8 + j, a] if term else left_cols[j, 0, a]

    sources = [[left_col(term, rows[at], j) for at in range(2) for j in range(links)] for term in range(2)]

    deep = links * block

    none = jnp.zeros((block, block), jnp.bfloat16)
    pair = 2

    def image(n, carry):
        picks = [(i, j) for i in range(pair) for j in range(links)]
        for term in range(2):
            found = [right_col(term, n * pair + i, j) for i, j in picks]
            lhs = []
            for source in sources[term]:
                line = []
                for col in found:
                    value = field[source, :, pl.ds(pl.multiple_of(col * block, block), block)]
                    line.append(value)
                lhs.append(jnp.concatenate(line, axis=1))
            rhs = []
            for i, j in picks:
                tile = right[term, (n * pair + i) * links + j]
                rhs.append(jnp.concatenate([tile if i == at else none for at in range(pair)], axis=1))
            product = jnp.dot(
                jnp.concatenate(lhs, axis=0),
                jnp.concatenate(rhs, axis=0),
                preferred_element_type=jnp.float32,
            )
            product = product.astype(jnp.bfloat16)
            span = pl.ds(pl.multiple_of(n * pair * block, pair * block), pair * block)
            for at in range(2):
                images[at, term * deep : (term + 1) * deep, span] = product[at * deep : (at + 1) * deep]
        return carry

    lax.fori_loop(0, sectors // pair, image, 0, unroll=2)
    for copy in copies:
        copy.wait()

    step = 2
    early_rows = block // 2
    zero = jnp.zeros((8, LANES), jnp.float32)

    def column(n, sums):
        start = pl.multiple_of(n * step * block, step * block)
        span = pl.ds(start, step * block)
        sums = list(sums)

        def masked(a, value):
            parts = [
                allowed(a, n * step + i, value[:, i * block : (i + 1) * block]) for i in range(step)
            ]
            return jnp.concatenate(parts, axis=1)

        for at in range(2):
            weights = [left[term, at * links + j] for term in range(2) for j in range(links)]
            total = jnp.dot(
                jnp.concatenate(weights, axis=1),
                images[at, :, span],
                preferred_element_type=jnp.float32,
            )
            offdiag = masked(rows[at], total.astype(jnp.bfloat16).astype(jnp.float32))
            own = field[rows[at], :, span].astype(jnp.float32)
            if first:
                psi_out[at, :, span] = own.astype(jnp.bfloat16)
                off_out[at, :, span] = offdiag.astype(jnp.bfloat16)
                sums[0] += fold(own * own)
                sums[1] += fold(own * offdiag)
            else:
                weight = diag[at, :, span].astype(jnp.float32)
                narrow = (weight * own + offdiag).astype(jnp.bfloat16)
                if at == 0:
                    near_out[:, span] = narrow
                else:
                    far_out[:, span] = narrow[:early_rows]
                    late_out[:, span] = narrow[early_rows:]
                second = narrow.astype(jnp.float32)
                wave = psi_in[at, :, span].astype(jnp.float32)
                sigma_one = weight * wave + off_in[at, :, span].astype(jnp.float32)
                sums[0] += fold(wave * second)
                sums[1] += fold(own * sigma_one)
                sums[2] += fold(own * second)
        return tuple(sums)

    sums = list(lax.fori_loop(0, sectors // step, column, (zero,) * (2 if first else 3)))
    if first:
        far_weight = (parts[0] + parts[1]).astype(jnp.float32)
        sums[1] += weight_own[...] + (far_weight[0:8] + far_weight[16:24] + far_weight[32:40])
    stats_out[...] = jnp.zeros_like(stats_out)
    for at, value in enumerate(sums):
        stats_out[at : at + 1, :] = jnp.sum(value, axis=0, keepdims=True)
    if not first:
        stats_out[3:5, :] = stats_in[0:2, :]


def operate(first, plan, pieces, cols, pattern, right, left, extra):
    _, table, block, _ = right.shape
    width = pieces[0].shape[1]
    sectors = width // block
    links = table // sectors
    rows = jax.ShapeDtypeStruct((2, block, width), jnp.bfloat16)
    one = jax.ShapeDtypeStruct((block, width), jnp.bfloat16)
    some = jax.ShapeDtypeStruct((block // 2, width), jnp.bfloat16)
    stats = jax.ShapeDtypeStruct((8, LANES), jnp.float32)
    out_shape = (rows, rows, stats) if first else (one, some, some, stats)
    extra_specs = [ANY, ANY, VMEM] if first else [ANY, ANY, VMEM, VMEM, VMEM]
    inner = 2 * 2 * sectors * 2 * links * links * block * block * block
    outer = 2 * 2 * 2 * links * block * block * width
    return pl.pallas_call(
        functools.partial(operate_kernel, first, plan),
        out_shape=out_shape,
        in_specs=[SMEM, SMEM, SMEM, SMEM, VMEM, ANY, ANY] + [VMEM] * len(pieces) + extra_specs,
        out_specs=(VMEM,) * len(out_shape),
        scratch_shapes=[
            pltpu.VMEM((sectors, block, width), jnp.bfloat16),
            pltpu.VMEM((2, 2 * links * block, width), jnp.bfloat16),
            pltpu.VMEM((2, 2 * links, block, block), jnp.bfloat16),
            pltpu.VMEM((2, block, width), jnp.bfloat16),
            pltpu.VMEM((2, 48, LANES), jnp.bfloat16),
            pltpu.SemaphoreType.DMA((5,)),
        ],
        compiler_params=pltpu.CompilerParams(vmem_limit_bytes=OPERATE_LIMIT),
        cost_estimate=pl.CostEstimate(
            flops=inner + outer if first else 0,
            bytes_accessed=16 * 1024 * 1024 if first else 1024,
            transcendentals=0,
        ),
        name="operate_first" if first else "operate_second",
    )(*cols, pattern, right, *left, *pieces, *extra)


def arrange_kernel(own, near, far, out, found, sems):
    _, _, c = place()
    part = own.shape[0] // 2
    copies = [
        pltpu.make_async_copy(own, found.at[0], sems.at[0]),
        pltpu.make_async_copy(near.at[pl.ds(0, part)], found.at[1, pl.ds(c * part, part)], sems.at[1]),
        pltpu.make_async_copy(far.at[pl.ds(0, part)], found.at[1, pl.ds((1 - c) * part, part)], sems.at[2]),
    ]
    for copy in copies:
        copy.start()
    for copy in copies:
        copy.wait()

    def turn(at, carry):
        for term in range(2):
            out[term, at] = found[term, at].T
        return carry

    lax.fori_loop(0, found.shape[1], turn, 0, unroll=4)


def arrange(own, near, far):
    shape = (2, *own.shape)
    return pl.pallas_call(
        arrange_kernel,
        out_shape=jax.ShapeDtypeStruct(shape, own.dtype),
        in_specs=[ANY] * 3,
        out_specs=VMEM,
        scratch_shapes=[pltpu.VMEM(shape, own.dtype), pltpu.SemaphoreType.DMA((3,))],
        compiler_params=pltpu.CompilerParams(vmem_limit_bytes=VMEM_LIMIT),
        name="arrange",
    )(own, near, far)


def prepare_kernel(
    pattern, theta, hd, right, left, right_cols, left_cols, mix_a, mix_b, packed, own_out, waves, diag, spots, sems
):
    z, x, c = place()
    half = z // 2
    middle = in_middle(z)
    mine = 4 * z + 2 * c + x
    block, width = diag.shape
    sectors = width // block
    links = right.shape[0] // sectors
    part = right.shape[0] // 2
    root_a = jnp.where(middle, half, 1 - half)
    rows = pl.ds(0, width)
    sources = (
        (theta.at[half, x], waves.at[0]),
        (theta.at[1 - half, x], waves.at[1]),
        (hd.at[x], diag),
        (theta.at[root_a, jnp.where(middle, 0, x)], mix_a.at[:, rows]),
        (theta.at[1 - root_a, jnp.where(middle, x, 0)], mix_b.at[:, rows]),
        (right.at[pl.ds(c * part, part)], packed.at[pl.ds(0, part)]),
        (left.at[pl.ds((mine ^ 1) * links, links)], packed.at[pl.ds(part, links)]),
        (left.at[pl.ds((mine ^ 13) * links, links)], packed.at[pl.ds(part + links, links)]),
    )
    copies = [
        pltpu.make_async_copy(source, target, sems.at[at])
        for at, (source, target) in enumerate(sources)
    ]
    for copy in copies:
        copy.start()
    last = part + 2 * links
    spots[...] = jnp.zeros_like(spots)
    spots[0:links, 0:sectors] = right_cols[:, 0, :].astype(jnp.float32)
    spots[8 : 8 + links, 0:sectors] = left_cols[:, 0, :].astype(jnp.float32)
    packed[last] = jnp.zeros_like(packed[last])
    packed[last, 0:16, :] = spots[...].astype(jnp.bfloat16)
    for copy in copies[:3]:
        copy.wait()
    zero = jnp.zeros((8, LANES), jnp.float32)

    def column(q, sums):
        span = pl.ds(pl.multiple_of(q * block, block), block)
        weight = diag[:, span].astype(jnp.float32)
        weight = jnp.where(pattern[mine, q] != 0, weight, jnp.zeros_like(weight))
        found = []
        for root in range(2):
            wave = waves[root, :, span].astype(jnp.float32)
            found.append(sums[root] + fold(weight * wave * wave))
        return tuple(found)

    near, far = lax.fori_loop(0, sectors, column, (zero, zero), unroll=4)
    own_out[...] = near
    left_over = jnp.concatenate([far, zero], axis=0)
    parts = []
    for _ in range(3):
        piece = left_over.astype(jnp.bfloat16)
        parts.append(piece)
        left_over = left_over - piece.astype(jnp.float32)
    parts.append(jnp.zeros((block - 48, LANES), jnp.bfloat16))
    tail = jnp.concatenate(parts, axis=0)
    none = jnp.zeros_like(tail)
    mix_a[:, width:] = jnp.where(middle, none, tail)
    mix_b[:, width:] = jnp.where(middle, tail, none)
    for copy in copies[3:]:
        copy.wait()


def prepare(pattern, theta, hd, right, left, *cols):
    _, _, block, width = theta.shape
    table = right.shape[0]
    links = table * block // width
    kind = jnp.bfloat16
    mix = jax.ShapeDtypeStruct((block, width + LANES), kind)
    packed = jax.ShapeDtypeStruct((table // 2 + 2 * links + 1, block, block), kind)
    return pl.pallas_call(
        prepare_kernel,
        out_shape=(mix, mix, packed, jax.ShapeDtypeStruct((8, LANES), jnp.float32)),
        in_specs=[SMEM, ANY, ANY, ANY, ANY, VMEM, VMEM],
        out_specs=(VMEM,) * 4,
        scratch_shapes=[
            pltpu.VMEM((2, block, width), kind),
            pltpu.VMEM((block, width), kind),
            pltpu.VMEM((16, LANES), jnp.float32),
            pltpu.SemaphoreType.DMA((8,)),
        ],
        compiler_params=pltpu.CompilerParams(vmem_limit_bytes=PREPARE_LIMIT),
        name="prepare",
    )(pattern, theta, hd, right, left, *cols)


def total_of(rows):
    return jnp.sum(rows, axis=1, keepdims=True)


def update_kernel(psi, off, hd_own, hd_far, *refs):
    stats, (t_out, stats_out, diag, sems) = refs[:4], refs[4:]
    z, x, c = place()
    copies = [
        pltpu.make_async_copy(hd_own.at[x], diag.at[0], sems.at[0]),
        pltpu.make_async_copy(hd_far, diag.at[1], sems.at[1]),
    ]
    for copy in copies:
        copy.start()
    whole = sum(ref[at, 0:2, :] for ref in stats for at in range(2))
    norm_sq, energy_sum = total_of(whole[0:1, :]), total_of(whole[1:2, :])
    energy = energy_sum / (norm_sq + 1e-06)
    mine = total_of(stats[0][0, 0:1, :])
    for copy in copies:
        copy.wait()
    _, block, width = psi.shape
    step = 16
    zero = jnp.zeros((8, LANES), jnp.float32)

    def chunk(n, total):
        span = pl.ds(pl.multiple_of(n * step, step), step)
        for at in range(2):
            wave = psi[at, span, :].astype(jnp.float32)
            weight = diag[at, span, :].astype(jnp.float32)
            sigma = weight * wave + off[at, span, :].astype(jnp.float32)
            shifted = weight - energy
            t = (sigma - energy * wave) * shifted / (shifted * shifted + 1.0)
            t_out[at, span, :] = t
            total = total + fold(wave * t)
        return total

    lanes = jnp.sum(lax.fori_loop(0, block // step, chunk, zero), axis=0, keepdims=True)
    correlation = total_of(lanes)
    local = jnp.where(mine > 0.0, correlation / jnp.where(mine > 0.0, mine, 1.0), 0.0)

    def within(n, total):
        span = pl.ds(pl.multiple_of(n * step, step), step)
        for at in range(2):
            rest = t_out[at, span, :] - local * psi[at, span, :].astype(jnp.float32)
            total = total + fold(rest * rest)
        return total

    spread = jnp.sum(lax.fori_loop(0, block // step, within, zero), axis=0, keepdims=True)
    stats_out[...] = jnp.zeros_like(stats_out)
    stats_out[0:1, :] = jnp.broadcast_to(correlation, (1, LANES))
    stats_out[1:2, :] = jnp.broadcast_to(total_of(spread), (1, LANES))
    stats_out[2:3, :] = jnp.broadcast_to(mine, (1, LANES))
    stats_out[3:4, :] = jnp.broadcast_to(local, (1, LANES))
    stats_out[4:5, :] = jnp.broadcast_to(norm_sq, (1, LANES))


def correct_kernel(psi, t, *refs):
    stats, outs = refs[:4], refs[4:]
    stats = [ref.at[at] for ref in stats for at in range(2)]
    norm_sq = stats[0][4:5, 0:1]
    factor = sum(ref[0:1, 0:1] for ref in stats) / (norm_sq + 1e-06)
    length_sq = jnp.zeros((1, 1), jnp.float32)
    for ref in stats:
        gap = factor - ref[3:4, 0:1]
        length_sq = length_sq + (ref[1:2, 0:1] + gap * gap * ref[2:3, 0:1])
    scale = jnp.sqrt(norm_sq / (length_sq + 1e-06))
    _, block, width = psi.shape
    step = 16

    def chunk(n, carry):
        span = pl.ds(pl.multiple_of(n * step, step), step)
        for at in range(2):
            wave = psi[at, span, :].astype(jnp.float32)
            outs[at][span, :] = ((t[at, span, :] - factor * wave) * scale).astype(jnp.bfloat16)
        return carry

    lax.fori_loop(0, block // step, chunk, 0)


def assemble_kernel(places, based, *refs):
    count = len(places)
    pieces, (out, sems) = refs[:count], refs[count + based :]
    z, x, c = place()
    half = z // 2
    copies = []
    for at, (root, flip, start) in enumerate(places):
        size = pieces[at].shape[0]
        target = out.at[half ^ root, x ^ flip, pl.ds(start, size)]
        copies.append(pltpu.make_async_copy(pieces[at], target, sems.at[at]))
    for copy in copies:
        copy.start()
    for copy in copies:
        copy.wait()


def assemble(block, pieces, places, base=None):
    width = pieces[0].shape[1]
    based = [] if base is None else [base]
    return pl.pallas_call(
        functools.partial(assemble_kernel, places, len(based)),
        out_shape=jax.ShapeDtypeStruct((2, 2, block, width), pieces[0].dtype),
        in_specs=[VMEM] * len(pieces) + [ANY] * len(based),
        out_specs=ANY,
        scratch_shapes=[pltpu.SemaphoreType.DMA((len(pieces),))],
        input_output_aliases={len(pieces): 0} if based else {},
        compiler_params=pltpu.CompilerParams(vmem_limit_bytes=VMEM_LIMIT),
        name="assemble",
    )(*pieces, *based)


def after(value, *others):
    return lax.optimization_barrier((value, *others))[0]


def shards(theta, hdiag, pattern, left_blocks, left_cols, right_blocks, right_cols):
    roots, row_count, width = theta.shape
    sectors = pattern.shape[0]
    block = width // sectors
    z, x, c = place()
    half = z // 2
    mine = 4 * z + 2 * c + x

    halves = theta.reshape(roots, 2, block, width)
    diag = hdiag.reshape(2, block, width)
    middle = in_middle(z)
    right = right_blocks.reshape(-1, block, block)
    left = left_blocks.reshape(-1, block, block)
    cols = (right_cols.transpose(2, 0, 1), left_cols.transpose(2, 0, 1))

    mix_a, mix_b, packed, weight_own = prepare(pattern, halves, diag, right, left, *cols)
    mix_a = lax.ppermute(mix_a, "blk", [(0, 2), (2, 3), (3, 1), (1, 0)])
    mix_b = lax.ppermute(mix_b, "blk", [(0, 1), (1, 3), (3, 2), (2, 0)])
    operators = across(packed, "ops", 1)

    def masked(row, value):
        line = lax.dynamic_index_in_dim(pattern, row, 0, keepdims=False).astype(jnp.bfloat16)
        return value * jnp.repeat(line, block)[None, :]

    own = [
        masked(row_of(0, 2 + at, 0), lax.dynamic_slice(halves, (half, at, 0, 0), (1, 1, block, width))[0, 0])
        for at in range(2)
    ]
    own_core = [across(value, "sub", 1) for value in own]

    mix_a, mix_b = after((mix_a, mix_b), *own_core)
    far = masked(row_of(2, 0, 0), jnp.where(middle, mix_a[:, :width], mix_b[:, :width]))
    far_z = across(far, "blk", 1)
    far_x = across(far, "ops", 1)
    near_a = masked(row_of(1, 2, 0), jnp.where(middle, mix_b[:, :width], mix_a[:, :width]))
    far_core = across(far, "sub", 1)
    near_a_core = across(near_a, "sub", 1)

    near_b = across(after(own[1], far_z, far_core, near_a_core), "blk", 1)
    far_zx = across(far_z, "ops", 1)
    operators = after(operators, far_z)
    operators_core = across(operators, "sub", 1)
    turned = arrange(right, operators, operators_core)
    cols = (*cols, operators[-1, :16, :sectors].astype(jnp.int32))
    far_x_core = across(far_x, "sub", 1)
    far_z_core = across(far_z, "sub", 1)
    hd_far = lax.dynamic_index_in_dim(diag, x, 0, keepdims=False)
    hd_far = across(after(hd_far, far_z), "blk", 3)
    far_zx_core = across(far_zx, "sub", 1)
    near_b_core = across(after(near_b, turned), "sub", 1)

    left = (left, operators)
    pieces = []
    plan = []
    for piece, offset in (
        (own[0], (0, 2, 0)),
        (own[1], (0, 3, 0)),
        (own_core[0], (0, 2, 1)),
        (own_core[1], (0, 3, 1)),
        (near_a, (1, 2, 0)),
        (near_b, (1, 3, 0)),
        (near_a_core, (1, 2, 1)),
        (near_b_core, (1, 3, 1)),
        (far, (2, 0, 0)),
        (far_core, (2, 0, 1)),
        (far_x, (2, 1, 0)),
        (far_x_core, (2, 1, 1)),
        (far_z, (3, 0, 0)),
        (far_z_core, (3, 0, 1)),
        (far_zx, (3, 1, 0)),
        (far_zx_core, (3, 1, 1)),
    ):
        pieces.append(piece)
        plan.append(offset)
    psi, off_one, stats_one = operate(
        True, tuple(plan), pieces, cols, pattern, turned, left, (mix_a, mix_b, weight_own)
    )

    found = share(stats_one)
    t, stats_two = pl.pallas_call(
        update_kernel,
        out_shape=(
            jax.ShapeDtypeStruct((2, block, width), jnp.float32),
            jax.ShapeDtypeStruct((8, LANES), jnp.float32),
        ),
        in_specs=[VMEM, VMEM, ANY, ANY] + [VMEM] * 4,
        out_specs=(VMEM, VMEM),
        scratch_shapes=[
            pltpu.VMEM((2, block, width), jnp.bfloat16),
            pltpu.SemaphoreType.DMA((2,)),
        ],
        compiler_params=pltpu.CompilerParams(vmem_limit_bytes=VMEM_LIMIT),
        name="update",
    )(psi, off_one, diag, hd_far, *found)
    found = share(stats_two)
    one = jax.ShapeDtypeStruct((block, width), jnp.bfloat16)
    changed_near, changed_far = pl.pallas_call(
        correct_kernel,
        out_shape=(one, one),
        in_specs=[VMEM, VMEM] + [VMEM] * 4,
        out_specs=(VMEM, VMEM),
        compiler_params=pltpu.CompilerParams(vmem_limit_bytes=VMEM_LIMIT),
        name="correct",
    )(psi, t, *found)

    near_z = across(changed_near, "blk", 1)
    far_x = across(changed_far, "ops", 1)
    near_core = across(changed_near, "sub", 1)
    far_core = across(changed_far, "sub", 1)
    other_middle = lax.ppermute(changed_far, "blk", [(1, 2), (2, 1)])
    near_z, far_x = after((near_z, far_x), other_middle)
    near_zx = across(near_z, "ops", 1)
    far_xz = across(far_x, "blk", 1)
    near_x = across(after(changed_near, near_z, far_x), "ops", 1)
    far_z = across(after(changed_far, near_z, far_x), "blk", 1)
    near_z_core = across(near_z, "sub", 1)
    far_x_core = across(far_x, "sub", 1)
    near_x_core = across(near_x, "sub", 1)
    far_z_core = across(far_z, "sub", 1)
    near_zx_core = across(near_zx, "sub", 1)
    far_xz_core = across(far_xz, "sub", 1)
    other_end = lax.ppermute(after(changed_far, near_z, far_x), "blk", [(0, 3), (3, 0)])
    pieces, plan = [], []
    for piece, offset in (
        (changed_near, (0, 0, 0)),
        (changed_far, (3, 0, 0)),
        (near_core, (0, 0, 1)),
        (far_core, (3, 0, 1)),
        (near_z, (1, 0, 0)),
        (far_z, (2, 0, 0)),
        (near_z_core, (1, 0, 1)),
        (far_z_core, (2, 0, 1)),
        (near_x, (0, 1, 0)),
        (far_x, (3, 1, 0)),
        (near_x_core, (0, 1, 1)),
        (far_x_core, (3, 1, 1)),
        (near_zx, (1, 1, 0)),
        (far_xz, (2, 1, 0)),
        (near_zx_core, (1, 1, 1)),
        (far_xz_core, (2, 1, 1)),
    ):
        pieces.append(piece)
        plan.append(offset)
    two_near, two_far, two_late, stats_three = operate(
        False, tuple(plan), pieces, cols, pattern, turned, left, (diag, hd_far, psi, off_one, stats_one)
    )

    far_in = across(two_far, "blk", 3)
    near_in = across(two_near, "ops", 1)
    late_in = across(after(two_late, far_in), "blk", 3)
    far_in_x = across(far_in, "ops", 1)
    other = jnp.where(middle, other_middle, after(other_end, two_near))
    other_x = across(other, "ops", 1)
    sums = stats_three + across(stats_three, "sub", 1)
    sums = sums + across(sums, "ops", 1)
    sums = after(sums, late_in)
    both = jnp.stack([sums + across(sums, "blk", 1), across(sums, "blk", 2) + across(sums, "blk", 3)])
    other, other_x = after((other, other_x), late_in)
    late_in_x = across(late_in, "ops", 1)
    both = jnp.sum(jnp.where(half == 0, both, both[::-1])[:, :5], axis=2)
    scale = both[:, 3:4] + 1e-06
    subspace = jnp.concatenate([both[:, 4:5], both[:, 0:3]], axis=1) / scale
    places = ((0, 0, 0), (0, 1, 0), (1, 0, 0), (1, 1, 0))
    correction = assemble(block, (changed_near, near_x, other, other_x), places)
    places = ((0, 0, 0), (0, 1, 0), (1, 0, 0), (1, 0, block // 2), (1, 1, 0))
    sigma_two = assemble(block, (two_near, near_in, far_in, late_in, far_in_x), places)
    sigma_two = assemble(block, (late_in_x,), ((1, 1, block // 2),), sigma_two)
    return correction.reshape(theta.shape), sigma_two.reshape(theta.shape), subspace


def solution(mesh):
    in_specs = (
        P("groups", ("blk", "sub"), None),
        P(("groups", "blk", "sub"), None),
        P("groups", None),
        P(("groups", "ops"), None, None, None, None),
        P(("groups", "ops"), None, None),
        P(("groups", "ops"), None, None, None, None),
        P(("groups", "ops"), None, None),
    )
    out_specs = (
        P("groups", ("blk", "sub"), None),
        P("groups", ("blk", "sub"), None),
        P("groups", None),
    )
    body = shards if halves_fit(mesh) else general_shards
    return jax.shard_map(body, mesh=mesh, in_specs=in_specs, out_specs=out_specs, check_vma=False)
```

```python
import functools

import jax
import jax.numpy as jnp
from jax import lax
from jax.experimental import pallas as pl
from jax.experimental.pallas import tpu as pltpu
from jax.sharding import PartitionSpec as P

ANY = pl.BlockSpec(memory_space=pl.ANY)
SMEM = pl.BlockSpec(memory_space=pltpu.SMEM)
VMEM = pl.BlockSpec(memory_space=pltpu.VMEM)
VMEM_LIMIT = 24 * 1024 * 1024
OPERATE_LIMIT = 44 * 1024 * 1024
PREPARE_LIMIT = 56 * 1024 * 1024
LANES = 128


def apply_right(field_in, blocks, columns):
    roots_here, row_count, full_width = field_in.shape
    term_count, sectors, link_count = columns.shape
    block_size = full_width // sectors
    grouped = field_in.reshape(roots_here, row_count, sectors, block_size)
    picked = jnp.take(grouped, columns.reshape(-1), axis=2)
    picked = picked.reshape(roots_here, row_count, term_count, sectors, link_count, block_size)
    product = jnp.einsum("nrkbjq,kbjpq->knrbp", picked, blocks, preferred_element_type=jnp.float32)
    return product.reshape(term_count, roots_here, row_count, full_width).astype(jnp.bfloat16)


def take_rows(stacked, indices):
    return jnp.take(stacked, indices, axis=1)


def apply_left(arrived, blocks, columns):
    term_count, roots_here, full_width, col_count = arrived.shape
    sectors = columns.shape[1]
    link_count = columns.shape[2]
    block_size = full_width // sectors
    grouped = arrived.reshape(term_count, roots_here, sectors, block_size, col_count)
    picked = jax.vmap(take_rows)(grouped, columns.reshape(term_count, sectors * link_count))
    picked = picked.reshape(term_count, roots_here, sectors, link_count, block_size, col_count)
    product = jnp.einsum("kajpq,knajqc->napc", blocks, picked, preferred_element_type=jnp.float32)
    return product.reshape(roots_here, full_width, col_count)


def general_shards(theta, hdiag, pattern, left_blocks, left_cols, right_blocks, right_cols):
    roots_here, row_count, full_width = theta.shape
    sectors = pattern.shape[0]
    block_size = full_width // sectors
    first_row = lax.axis_index(("blk", "sub")) * row_count
    block_row = (first_row + jnp.arange(row_count, dtype=jnp.int32)) // block_size
    onehot = (block_row[:, None] == jnp.arange(sectors, dtype=jnp.int32)[None, :]).astype(
        jnp.float32
    )
    row_pattern = jnp.dot(onehot, pattern.astype(jnp.float32), preferred_element_type=jnp.float32)
    allowed = jnp.broadcast_to(row_pattern[:, :, None], (row_count, sectors, block_size))
    allowed = allowed.reshape(row_count, full_width).astype(jnp.bfloat16)
    diagonal = hdiag.astype(jnp.float32)
    peers = lax.axis_size("blk") * lax.axis_size("sub")

    def left_part(arrived):
        return apply_left(arrived, left_blocks, left_cols)

    def operate(field_in):
        images = apply_right(field_in, right_blocks, right_cols)
        partial_sum = left_part(
            lax.all_to_all(images, ("blk", "sub"), split_axis=3, concat_axis=2, tiled=True)
        )
        shares = lax.psum_scatter(partial_sum, "ops", scatter_dimension=2, tiled=True)
        returned = lax.all_to_all(
            shares.astype(jnp.bfloat16), ("blk", "sub"), split_axis=1, concat_axis=2, tiled=True
        )
        gathered = lax.all_gather(returned, "ops", axis=2, tiled=True)
        narrow = returned.shape[2] // peers
        gathered = gathered.reshape(roots_here, row_count, lax.axis_size("ops"), peers, narrow)
        offdiag = gathered.transpose(0, 1, 3, 2, 4).reshape(roots_here, row_count, full_width)
        offdiag = offdiag * allowed[None]
        return diagonal[None] * field_in.astype(jnp.float32) + offdiag.astype(jnp.float32)

    projected = theta * allowed[None]
    wave = projected.astype(jnp.float32)
    sigma_one = operate(projected)
    norm_sq, energy_sum = lax.psum(
        (jnp.sum(wave * wave, axis=(1, 2)), jnp.sum(wave * sigma_one, axis=(1, 2))), ("blk", "sub")
    )
    denominator = norm_sq + 1e-06
    energy = energy_sum / denominator
    shifted = diagonal[None] - energy[:, None, None]
    update = (sigma_one - energy[:, None, None] * wave) * shifted / (shifted * shifted + 1.0)
    correlation = lax.psum(jnp.sum(wave * update, axis=(1, 2)), ("blk", "sub"))
    factor = correlation / denominator
    orthogonal = update - factor[:, None, None] * wave
    length_sq = lax.psum(jnp.sum(orthogonal * orthogonal, axis=(1, 2)), ("blk", "sub"))
    correction = (orthogonal * jnp.sqrt(norm_sq / (length_sq + 1e-06))[:, None, None]).astype(
        jnp.bfloat16
    )
    sigma_two = operate(correction).astype(jnp.bfloat16)
    second = sigma_two.astype(jnp.float32)
    fixed = correction.astype(jnp.float32)
    cross_one, cross_two, cross_three = lax.psum(
        (
            jnp.sum(wave * second, axis=(1, 2)),
            jnp.sum(fixed * sigma_one, axis=(1, 2)),
            jnp.sum(fixed * second, axis=(1, 2)),
        ),
        ("blk", "sub"),
    )
    subspace = (
        jnp.stack([energy_sum, cross_one, cross_two, cross_three], axis=1) / denominator[:, None]
    )
    return (correction, sigma_two, subspace)


def halves_fit(mesh):
    sizes = dict(mesh.shape)
    return sizes["blk"] == 4 and sizes["ops"] == 2 and sizes["sub"] == 2


def across(value, axis, distance):
    size = lax.axis_size(axis)
    return lax.ppermute(value, axis, [(i, i ^ distance) for i in range(size)])


def share(stats):
    axes = ("blk", "ops")
    count = lax.axis_size("blk") * lax.axis_size("ops")
    pair = jnp.stack([stats, across(stats, "sub", 1)])
    found = [pair]
    for distance in (1, 2, 3):
        found.append(lax.ppermute(pair, axes, [(i, i ^ distance) for i in range(count)]))
    return found


def place():
    return lax.axis_index("blk"), lax.axis_index("ops"), lax.axis_index("sub")


def fold(value):
    rows, width = value.shape
    value = jnp.sum(value.reshape(rows // 8, 8, width), axis=0)
    return sum(value[:, at : at + LANES] for at in range(0, width, LANES))


def in_middle(z):
    return jnp.logical_or(z == 1, z == 2)


def row_of(dz, dx, dc):
    z, x, c = place()
    return 4 * (z ^ dz) + 2 * (c ^ dc) + (x ^ dx if dx < 2 else dx - 2)


def operate_kernel(first, plan, right_cols, left_cols, cols_other, pattern, right, left_own, left_other, *refs):
    count = len(plan)
    pieces, refs = refs[:count], refs[count:]
    if first:
        mix_a, mix_b, weight_own, psi_out, off_out, stats_out = refs[:6]
        refs = refs[6:]
    else:
        hd_own, hd_far, psi_in, off_in, stats_in, near_out, far_out, late_out, stats_out = refs[:9]
        refs = refs[9:]
    field, images, left, diag, sems = refs
    z, x, c = place()
    sectors, block, width = field.shape
    table = right.shape[1]
    links = table // sectors
    mine = 4 * z + 2 * c + x
    rows = (mine, mine ^ 12)

    copies = []

    def begin(source, target):
        copy = pltpu.make_async_copy(source, target, sems.at[len(copies)])
        copy.start()
        copies.append(copy)

    for at in range(2):
        begin(left_own.at[pl.ds(rows[at] * links, links)], left.at[0, pl.ds(at * links, links)])
    begin(left_other.at[pl.ds(table // 2, 2 * links)], left.at[1])
    if not first:
        begin(hd_own.at[x], diag.at[0])
        begin(hd_far, diag.at[1])

    def allowed(a, q, value):
        return lax.select(pattern[a, q] != 0, value, jnp.zeros_like(value))

    for piece, offsets in zip(pieces, plan):
        for at, (dz, dx, dc, start, tall) in enumerate(offsets):
            row = row_of(dz, dx, dc)
            for line in range(0, tall, 16):
                value = piece[at, line : line + 16, :]
                field[row, start + line : start + line + 16, :] = value

    def right_col(term, b, j):
        return cols_other[j, b] if term else right_cols[j, 0, b]

    def left_col(term, a, j):
        return cols_other[8 + j, a] if term else left_cols[j, 0, a]

    sources = [[left_col(term, rows[at], j) for at in range(2) for j in range(links)] for term in range(2)]

    deep = links * block

    none = jnp.zeros((block, block), jnp.bfloat16)
    pair = 2

    def image(n, carry):
        picks = [(i, j) for i in range(pair) for j in range(links)]
        for term in range(2):
            found = [right_col(term, n * pair + i, j) for i, j in picks]
            lhs = []
            for source in sources[term]:
                line = []
                for col in found:
                    value = field[source, :, pl.ds(pl.multiple_of(col * block, block), block)]
                    line.append(value)
                lhs.append(jnp.concatenate(line, axis=1))
            rhs = []
            for i, j in picks:
                tile = right[term, (n * pair + i) * links + j]
                rhs.append(jnp.concatenate([tile if i == at else none for at in range(pair)], axis=1))
            product = jnp.dot(
                jnp.concatenate(lhs, axis=0),
                jnp.concatenate(rhs, axis=0),
                preferred_element_type=jnp.float32,
            )
            product = product.astype(jnp.bfloat16)
            span = pl.ds(pl.multiple_of(n * pair * block, pair * block), pair * block)
            for at in range(2):
                images[at, term * deep : (term + 1) * deep, span] = product[at * deep : (at + 1) * deep]
        return carry

    lax.fori_loop(0, sectors // pair, image, 0, unroll=2)
    for copy in copies:
        copy.wait()

    step = 2
    early_rows = block // 2
    zero = jnp.zeros((8, LANES), jnp.float32)

    def column(n, sums):
        start = pl.multiple_of(n * step * block, step * block)
        span = pl.ds(start, step * block)
        sums = list(sums)

        def masked(a, value):
            parts = [
                allowed(a, n * step + i, value[:, i * block : (i + 1) * block]) for i in range(step)
            ]
            return jnp.concatenate(parts, axis=1)

        for at in range(2):
            weights = [left[term, at * links + j] for term in range(2) for j in range(links)]
            total = jnp.dot(
                jnp.concatenate(weights, axis=1),
                images[at, :, span],
                preferred_element_type=jnp.float32,
            )
            offdiag = masked(rows[at], total.astype(jnp.bfloat16).astype(jnp.float32))
            own = field[rows[at], :, span].astype(jnp.float32)
            if first:
                psi_out[at, :, span] = own.astype(jnp.bfloat16)
                off_out[at, :, span] = offdiag.astype(jnp.bfloat16)
                sums[0] += fold(own * own)
                sums[1] += fold(own * offdiag)
            else:
                weight = diag[at, :, span].astype(jnp.float32)
                narrow = (weight * own + offdiag).astype(jnp.bfloat16)
                if at == 0:
                    near_out[:, span] = narrow
                else:
                    far_out[:, span] = narrow[:early_rows]
                    late_out[:, span] = narrow[early_rows:]
                second = narrow.astype(jnp.float32)
                wave = psi_in[at, :, span].astype(jnp.float32)
                sigma_one = weight * wave + off_in[at, :, span].astype(jnp.float32)
                sums[0] += fold(wave * second)
                sums[1] += fold(own * sigma_one)
                sums[2] += fold(own * second)
        return tuple(sums)

    sums = list(lax.fori_loop(0, sectors // step, column, (zero,) * (2 if first else 3)))
    if first:
        far_weight = sum(mix[0:48, width:].astype(jnp.float32) for mix in (mix_a, mix_b))
        sums[1] += weight_own[...] + (far_weight[0:8] + far_weight[16:24] + far_weight[32:40])
    stats_out[...] = jnp.zeros_like(stats_out)
    for at, value in enumerate(sums):
        stats_out[at : at + 1, :] = jnp.sum(value, axis=0, keepdims=True)
    if not first:
        stats_out[3:5, :] = stats_in[0:2, :]


def operate(first, plan, pieces, cols, pattern, right, left, extra):
    _, table, block, _ = right.shape
    width = pieces[0].shape[2]
    sectors = width // block
    links = table // sectors
    rows = jax.ShapeDtypeStruct((2, block, width), jnp.bfloat16)
    one = jax.ShapeDtypeStruct((block, width), jnp.bfloat16)
    some = jax.ShapeDtypeStruct((block // 2, width), jnp.bfloat16)
    stats = jax.ShapeDtypeStruct((8, LANES), jnp.float32)
    out_shape = (rows, rows, stats) if first else (one, some, some, stats)
    extra_specs = [VMEM] * 3 if first else [ANY, ANY, VMEM, VMEM, VMEM]
    inner = 2 * 2 * sectors * 2 * links * links * block * block * block
    outer = 2 * 2 * 2 * links * block * block * width
    return pl.pallas_call(
        functools.partial(operate_kernel, first, plan),
        out_shape=out_shape,
        in_specs=[SMEM, SMEM, SMEM, SMEM, VMEM, ANY, ANY] + [VMEM] * len(pieces) + extra_specs,
        out_specs=(VMEM,) * len(out_shape),
        scratch_shapes=[
            pltpu.VMEM((sectors, block, width), jnp.bfloat16),
            pltpu.VMEM((2, 2 * links * block, width), jnp.bfloat16),
            pltpu.VMEM((2, 2 * links, block, block), jnp.bfloat16),
            pltpu.VMEM((2, block, width), jnp.bfloat16),
            pltpu.SemaphoreType.DMA((5,)),
        ],
        compiler_params=pltpu.CompilerParams(vmem_limit_bytes=OPERATE_LIMIT),
        cost_estimate=pl.CostEstimate(
            flops=inner + outer if first else 0,
            bytes_accessed=16 * 1024 * 1024 if first else 1024,
            transcendentals=0,
        ),
        name="operate_first" if first else "operate_second",
    )(*cols, pattern, right, *left, *pieces, *extra)


def arrange_kernel(own, near, far, out, found, sems):
    _, _, c = place()
    part = own.shape[0] // 2
    copies = [
        pltpu.make_async_copy(own, found.at[0], sems.at[0]),
        pltpu.make_async_copy(near.at[pl.ds(0, part)], found.at[1, pl.ds(c * part, part)], sems.at[1]),
        pltpu.make_async_copy(far.at[pl.ds(0, part)], found.at[1, pl.ds((1 - c) * part, part)], sems.at[2]),
    ]
    for copy in copies:
        copy.start()
    for copy in copies:
        copy.wait()

    def turn(at, carry):
        for term in range(2):
            out[term, at] = found[term, at].T
        return carry

    lax.fori_loop(0, found.shape[1], turn, 0, unroll=4)


def arrange(own, near, far):
    shape = (2, *own.shape)
    return pl.pallas_call(
        arrange_kernel,
        out_shape=jax.ShapeDtypeStruct(shape, own.dtype),
        in_specs=[ANY] * 3,
        out_specs=VMEM,
        scratch_shapes=[pltpu.VMEM(shape, own.dtype), pltpu.SemaphoreType.DMA((3,))],
        compiler_params=pltpu.CompilerParams(vmem_limit_bytes=VMEM_LIMIT),
        name="arrange",
    )(own, near, far)


def prepare_kernel(
    pattern, theta, hd, right, left, right_cols, left_cols, mix_a, mix_b, packed, own_out, waves, diag, spots, sems
):
    z, x, c = place()
    half = z // 2
    middle = in_middle(z)
    mine = 4 * z + 2 * c + x
    block, width = diag.shape
    sectors = width // block
    links = right.shape[0] // sectors
    part = right.shape[0] // 2
    root_a = jnp.where(middle, half, 1 - half)
    rows = pl.ds(0, width)
    sources = (
        (theta.at[half, x], waves.at[0]),
        (theta.at[1 - half, x], waves.at[1]),
        (hd.at[x], diag),
        (theta.at[root_a, jnp.where(middle, 0, x)], mix_a.at[:, rows]),
        (theta.at[1 - root_a, jnp.where(middle, x, 0)], mix_b.at[:, rows]),
        (right.at[pl.ds(c * part, part)], packed.at[pl.ds(0, part)]),
        (left.at[pl.ds((mine ^ 1) * links, links)], packed.at[pl.ds(part, links)]),
        (left.at[pl.ds((mine ^ 13) * links, links)], packed.at[pl.ds(part + links, links)]),
    )
    copies = [
        pltpu.make_async_copy(source, target, sems.at[at])
        for at, (source, target) in enumerate(sources)
    ]
    for copy in copies:
        copy.start()
    last = part + 2 * links
    spots[...] = jnp.zeros_like(spots)
    spots[0:links, 0:sectors] = right_cols[:, 0, :].astype(jnp.float32)
    spots[8 : 8 + links, 0:sectors] = left_cols[:, 0, :].astype(jnp.float32)
    packed[last] = jnp.zeros_like(packed[last])
    packed[last, 0:16, :] = spots[...].astype(jnp.bfloat16)
    for copy in copies[:3]:
        copy.wait()
    zero = jnp.zeros((8, LANES), jnp.float32)

    def column(q, sums):
        span = pl.ds(pl.multiple_of(q * block, block), block)
        weight = diag[:, span].astype(jnp.float32)
        weight = jnp.where(pattern[mine, q] != 0, weight, jnp.zeros_like(weight))
        found = []
        for root in range(2):
            wave = waves[root, :, span].astype(jnp.float32)
            found.append(sums[root] + fold(weight * wave * wave))
        return tuple(found)

    near, far = lax.fori_loop(0, sectors, column, (zero, zero), unroll=4)
    own_out[...] = near
    left_over = jnp.concatenate([far, zero], axis=0)
    parts = []
    for _ in range(3):
        piece = left_over.astype(jnp.bfloat16)
        parts.append(piece)
        left_over = left_over - piece.astype(jnp.float32)
    parts.append(jnp.zeros((block - 48, LANES), jnp.bfloat16))
    tail = jnp.concatenate(parts, axis=0)
    none = jnp.zeros_like(tail)
    mix_a[:, width:] = jnp.where(middle, none, tail)
    mix_b[:, width:] = jnp.where(middle, tail, none)
    for copy in copies[3:]:
        copy.wait()


def prepare(pattern, theta, hd, right, left, *cols):
    _, _, block, width = theta.shape
    table = right.shape[0]
    links = table * block // width
    kind = jnp.bfloat16
    mix = jax.ShapeDtypeStruct((block, width + LANES), kind)
    packed = jax.ShapeDtypeStruct((table // 2 + 2 * links + 1, block, block), kind)
    return pl.pallas_call(
        prepare_kernel,
        out_shape=(mix, mix, packed, jax.ShapeDtypeStruct((8, LANES), jnp.float32)),
        in_specs=[SMEM, ANY, ANY, ANY, ANY, VMEM, VMEM],
        out_specs=(VMEM,) * 4,
        scratch_shapes=[
            pltpu.VMEM((2, block, width), kind),
            pltpu.VMEM((block, width), kind),
            pltpu.VMEM((16, LANES), jnp.float32),
            pltpu.SemaphoreType.DMA((8,)),
        ],
        compiler_params=pltpu.CompilerParams(vmem_limit_bytes=PREPARE_LIMIT),
        name="prepare",
    )(pattern, theta, hd, right, left, *cols)


def total_of(rows):
    return jnp.sum(rows, axis=1, keepdims=True)


def update_kernel(psi, off, hd_own, hd_far, *refs):
    stats, (t_out, stats_out, diag, sems) = refs[:4], refs[4:]
    z, x, c = place()
    copies = [
        pltpu.make_async_copy(hd_own.at[x], diag.at[0], sems.at[0]),
        pltpu.make_async_copy(hd_far, diag.at[1], sems.at[1]),
    ]
    for copy in copies:
        copy.start()
    whole = sum(ref[at, 0:2, :] for ref in stats for at in range(2))
    norm_sq, energy_sum = total_of(whole[0:1, :]), total_of(whole[1:2, :])
    energy = energy_sum / (norm_sq + 1e-06)
    mine = total_of(stats[0][0, 0:1, :])
    for copy in copies:
        copy.wait()
    _, block, width = psi.shape
    step = 16
    zero = jnp.zeros((8, LANES), jnp.float32)

    def chunk(n, total):
        span = pl.ds(pl.multiple_of(n * step, step), step)
        for at in range(2):
            wave = psi[at, span, :].astype(jnp.float32)
            weight = diag[at, span, :].astype(jnp.float32)
            sigma = weight * wave + off[at, span, :].astype(jnp.float32)
            shifted = weight - energy
            t = (sigma - energy * wave) * shifted / (shifted * shifted + 1.0)
            t_out[at, span, :] = t
            total = total + fold(wave * t)
        return total

    lanes = jnp.sum(lax.fori_loop(0, block // step, chunk, zero), axis=0, keepdims=True)
    correlation = total_of(lanes)
    local = jnp.where(mine > 0.0, correlation / jnp.where(mine > 0.0, mine, 1.0), 0.0)

    def within(n, total):
        span = pl.ds(pl.multiple_of(n * step, step), step)
        for at in range(2):
            rest = t_out[at, span, :] - local * psi[at, span, :].astype(jnp.float32)
            total = total + fold(rest * rest)
        return total

    spread = jnp.sum(lax.fori_loop(0, block // step, within, zero), axis=0, keepdims=True)
    stats_out[...] = jnp.zeros_like(stats_out)
    stats_out[0:1, :] = jnp.broadcast_to(correlation, (1, LANES))
    stats_out[1:2, :] = jnp.broadcast_to(total_of(spread), (1, LANES))
    stats_out[2:3, :] = jnp.broadcast_to(mine, (1, LANES))
    stats_out[3:4, :] = jnp.broadcast_to(local, (1, LANES))
    stats_out[4:5, :] = jnp.broadcast_to(norm_sq, (1, LANES))


def correct_kernel(psi, t, *refs):
    stats, outs = refs[:4], refs[4:]
    stats = [ref.at[at] for ref in stats for at in range(2)]
    norm_sq = stats[0][4:5, 0:1]
    factor = sum(ref[0:1, 0:1] for ref in stats) / (norm_sq + 1e-06)
    length_sq = jnp.zeros((1, 1), jnp.float32)
    for ref in stats:
        gap = factor - ref[3:4, 0:1]
        length_sq = length_sq + (ref[1:2, 0:1] + gap * gap * ref[2:3, 0:1])
    scale = jnp.sqrt(norm_sq / (length_sq + 1e-06))
    _, block, width = psi.shape
    step = 16

    def chunk(n, carry):
        span = pl.ds(pl.multiple_of(n * step, step), step)
        for at in range(2):
            wave = psi[at, span, :].astype(jnp.float32)
            outs[at][span, :] = ((t[at, span, :] - factor * wave) * scale).astype(jnp.bfloat16)
        return carry

    lax.fori_loop(0, block // step, chunk, 0)


def assemble_kernel(places, based, *refs):
    count = len(places)
    pieces, (out, sems) = refs[:count], refs[count + based :]
    z, x, c = place()
    half = z // 2
    copies = []
    for at, (root, flip, start) in enumerate(places):
        size = pieces[at].shape[0]
        target = out.at[half ^ root, x ^ flip, pl.ds(start, size)]
        copies.append(pltpu.make_async_copy(pieces[at], target, sems.at[at]))
    for copy in copies:
        copy.start()
    for copy in copies:
        copy.wait()


def assemble(block, pieces, places, base=None):
    width = pieces[0].shape[1]
    based = [] if base is None else [base]
    return pl.pallas_call(
        functools.partial(assemble_kernel, places, len(based)),
        out_shape=jax.ShapeDtypeStruct((2, 2, block, width), pieces[0].dtype),
        in_specs=[VMEM] * len(pieces) + [ANY] * len(based),
        out_specs=ANY,
        scratch_shapes=[pltpu.SemaphoreType.DMA((len(pieces),))],
        input_output_aliases={len(pieces): 0} if based else {},
        compiler_params=pltpu.CompilerParams(vmem_limit_bytes=VMEM_LIMIT),
        name="assemble",
    )(*pieces, *based)


def after(value, *others):
    return lax.optimization_barrier((value, *others))[0]


def shards(theta, hdiag, pattern, left_blocks, left_cols, right_blocks, right_cols):
    roots, row_count, width = theta.shape
    sectors = pattern.shape[0]
    block = width // sectors
    z, x, c = place()
    half = z // 2
    mine = 4 * z + 2 * c + x

    halves = theta.reshape(roots, 2, block, width)
    diag = hdiag.reshape(2, block, width)
    middle = in_middle(z)
    right = right_blocks.reshape(-1, block, block)
    left = left_blocks.reshape(-1, block, block)
    cols = (right_cols.transpose(2, 0, 1), left_cols.transpose(2, 0, 1))

    mix_a, mix_b, packed, weight_own = prepare(pattern, halves, diag, right, left, *cols)
    mix_a = lax.ppermute(mix_a, "blk", [(0, 2), (2, 3), (3, 1), (1, 0)])
    mix_b = lax.ppermute(mix_b, "blk", [(0, 1), (1, 3), (3, 2), (2, 0)])
    operators = across(packed, "ops", 1)

    def masked(row, value):
        line = lax.dynamic_index_in_dim(pattern, row, 0, keepdims=False).astype(jnp.bfloat16)
        return value * jnp.repeat(line, block)[None, :]

    own = [
        masked(row_of(0, 2 + at, 0), lax.dynamic_slice(halves, (half, at, 0, 0), (1, 1, block, width))[0, 0])
        for at in range(2)
    ]
    own = list(lax.optimization_barrier(tuple(own)))
    own_core = [across(value, "sub", 1) for value in own]

    mix_a, mix_b = after((mix_a, mix_b), *own_core)
    far = masked(row_of(2, 0, 0), jnp.where(middle, mix_a[:, :width], mix_b[:, :width]))
    far_z = across(far, "blk", 1)
    far_x = across(far, "ops", 1)
    near_a = masked(row_of(1, 2, 0), jnp.where(middle, mix_b[:, :width], mix_a[:, :width]))
    far_core = across(far, "sub", 1)
    near_a_core = across(near_a, "sub", 1)

    operators = after(operators, mix_b)
    operators_core = across(operators, "sub", 1)
    turned = arrange(right, operators, operators_core)
    near_b = across(after(own[1], far_z, far_core, near_a_core, turned), "blk", 1)
    far_zx = across(far_z, "ops", 1)
    cols = (*cols, operators[-1, :16, :sectors].astype(jnp.int32))
    far_x_core = across(far_x, "sub", 1)
    far_z_core = across(far_z, "sub", 1)
    hd_far = lax.dynamic_index_in_dim(diag, x, 0, keepdims=False)
    hd_far = across(after(hd_far, far_z), "blk", 3)
    far_zx_core = across(far_zx, "sub", 1)
    near_b_core = across(near_b, "sub", 1)

    left = (left, operators)
    pieces = []
    plan = []
    for piece, offset in (
        (own[0], (0, 2, 0)),
        (own[1], (0, 3, 0)),
        (own_core[0], (0, 2, 1)),
        (own_core[1], (0, 3, 1)),
        (near_a, (1, 2, 0)),
        (near_b, (1, 3, 0)),
        (near_a_core, (1, 2, 1)),
        (near_b_core, (1, 3, 1)),
        (far, (2, 0, 0)),
        (far_core, (2, 0, 1)),
        (far_x, (2, 1, 0)),
        (far_x_core, (2, 1, 1)),
        (far_z, (3, 0, 0)),
        (far_z_core, (3, 0, 1)),
        (far_zx, (3, 1, 0)),
        (far_zx_core, (3, 1, 1)),
    ):
        pieces.append(piece[None])
        plan.append((offset + (0, block),))
    psi, off_one, stats_one = operate(
        True, tuple(plan), pieces, cols, pattern, turned, left, (mix_a, mix_b, weight_own)
    )

    found = share(stats_one)
    t, stats_two = pl.pallas_call(
        update_kernel,
        out_shape=(
            jax.ShapeDtypeStruct((2, block, width), jnp.float32),
            jax.ShapeDtypeStruct((8, LANES), jnp.float32),
        ),
        in_specs=[VMEM, VMEM, ANY, ANY] + [VMEM] * 4,
        out_specs=(VMEM, VMEM),
        scratch_shapes=[
            pltpu.VMEM((2, block, width), jnp.bfloat16),
            pltpu.SemaphoreType.DMA((2,)),
        ],
        compiler_params=pltpu.CompilerParams(vmem_limit_bytes=VMEM_LIMIT),
        name="update",
    )(psi, off_one, diag, hd_far, *found)
    found = share(stats_two)
    one = jax.ShapeDtypeStruct((block, width), jnp.bfloat16)
    changed_near, changed_far = pl.pallas_call(
        correct_kernel,
        out_shape=(one, one),
        in_specs=[VMEM, VMEM] + [VMEM] * 4,
        out_specs=(VMEM, VMEM),
        compiler_params=pltpu.CompilerParams(vmem_limit_bytes=VMEM_LIMIT),
        name="correct",
    )(psi, t, *found)

    near_z = across(changed_near, "blk", 1)
    far_x = across(changed_far, "ops", 1)
    near_core = across(changed_near, "sub", 1)
    far_core = across(changed_far, "sub", 1)
    other_middle = lax.ppermute(changed_far, "blk", [(1, 2), (2, 1)])
    near_z, far_x = after((near_z, far_x), other_middle)
    near_zx = across(near_z, "ops", 1)
    far_xz = across(far_x, "blk", 1)
    near_x = across(after(changed_near, near_z, far_x), "ops", 1)
    far_z = across(after(changed_far, near_z, far_x), "blk", 1)
    near_z_core = across(near_z, "sub", 1)
    far_x_core = across(far_x, "sub", 1)
    near_x_core = across(near_x, "sub", 1)
    far_z_core = across(far_z, "sub", 1)
    near_zx_core = across(near_zx, "sub", 1)
    far_xz_core = across(far_xz, "sub", 1)
    other_end = lax.ppermute(after(changed_far, near_z, far_x), "blk", [(0, 3), (3, 0)])
    pieces, plan = [], []
    for piece, offset in (
        (changed_near, (0, 0, 0)),
        (changed_far, (3, 0, 0)),
        (near_core, (0, 0, 1)),
        (far_core, (3, 0, 1)),
        (near_z, (1, 0, 0)),
        (far_z, (2, 0, 0)),
        (near_z_core, (1, 0, 1)),
        (far_z_core, (2, 0, 1)),
        (near_x, (0, 1, 0)),
        (far_x, (3, 1, 0)),
        (near_x_core, (0, 1, 1)),
        (far_x_core, (3, 1, 1)),
        (near_zx, (1, 1, 0)),
        (far_xz, (2, 1, 0)),
        (near_zx_core, (1, 1, 1)),
        (far_xz_core, (2, 1, 1)),
    ):
        pieces.append(piece[None])
        plan.append((offset + (0, block),))
    two_near, two_far, two_late, stats_three = operate(
        False, tuple(plan), pieces, cols, pattern, turned, left, (diag, hd_far, psi, off_one, stats_one)
    )

    far_in = across(two_far, "blk", 3)
    near_in = across(two_near, "ops", 1)
    late_in = across(after(two_late, far_in), "blk", 3)
    far_in_x = across(far_in, "ops", 1)
    other = jnp.where(middle, other_middle, after(other_end, two_near))
    other_x = across(other, "ops", 1)
    sums = stats_three + across(stats_three, "sub", 1)
    sums = after(sums, late_in)
    both = jnp.stack([sums + across(sums, "blk", 1), across(sums, "blk", 2) + across(sums, "blk", 3)])
    both = both + across(both, "ops", 1)
    other, other_x = after((other, other_x), late_in)
    late_in_x = across(late_in, "ops", 1)
    both = jnp.sum(jnp.where(half == 0, both, both[::-1])[:, :5], axis=2)
    scale = both[:, 3:4] + 1e-06
    subspace = jnp.concatenate([both[:, 4:5], both[:, 0:3]], axis=1) / scale
    places = ((0, 0, 0), (0, 1, 0), (1, 0, 0), (1, 1, 0))
    correction = assemble(block, (changed_near, near_x, other, other_x), places)
    places = ((0, 0, 0), (0, 1, 0), (1, 0, 0), (1, 0, block // 2), (1, 1, 0))
    sigma_two = assemble(block, (two_near, near_in, far_in, late_in, far_in_x), places)
    sigma_two = assemble(block, (late_in_x,), ((1, 1, block // 2),), sigma_two)
    return correction.reshape(theta.shape), sigma_two.reshape(theta.shape), subspace


def solution(mesh):
    in_specs = (
        P("groups", ("blk", "sub"), None),
        P(("groups", "blk", "sub"), None),
        P("groups", None),
        P(("groups", "ops"), None, None, None, None),
        P(("groups", "ops"), None, None),
        P(("groups", "ops"), None, None, None, None),
        P(("groups", "ops"), None, None),
    )
    out_specs = (
        P("groups", ("blk", "sub"), None),
        P("groups", ("blk", "sub"), None),
        P("groups", None),
    )
    body = shards if halves_fit(mesh) else general_shards
    return jax.shard_map(body, mesh=mesh, in_specs=in_specs, out_specs=out_specs, check_vma=False)
```

```python
import functools

import jax
import jax.numpy as jnp
from jax import lax
from jax.experimental import pallas as pl
from jax.experimental.pallas import tpu as pltpu
from jax.sharding import PartitionSpec as P

ANY = pl.BlockSpec(memory_space=pl.ANY)
SMEM = pl.BlockSpec(memory_space=pltpu.SMEM)
VMEM = pl.BlockSpec(memory_space=pltpu.VMEM)
VMEM_LIMIT = 24 * 1024 * 1024
OPERATE_LIMIT = 44 * 1024 * 1024
PREPARE_LIMIT = 56 * 1024 * 1024
LANES = 128


def apply_right(field_in, blocks, columns):
    roots_here, row_count, full_width = field_in.shape
    term_count, sectors, link_count = columns.shape
    block_size = full_width // sectors
    grouped = field_in.reshape(roots_here, row_count, sectors, block_size)
    picked = jnp.take(grouped, columns.reshape(-1), axis=2)
    picked = picked.reshape(roots_here, row_count, term_count, sectors, link_count, block_size)
    product = jnp.einsum("nrkbjq,kbjpq->knrbp", picked, blocks, preferred_element_type=jnp.float32)
    return product.reshape(term_count, roots_here, row_count, full_width).astype(jnp.bfloat16)


def take_rows(stacked, indices):
    return jnp.take(stacked, indices, axis=1)


def apply_left(arrived, blocks, columns):
    term_count, roots_here, full_width, col_count = arrived.shape
    sectors = columns.shape[1]
    link_count = columns.shape[2]
    block_size = full_width // sectors
    grouped = arrived.reshape(term_count, roots_here, sectors, block_size, col_count)
    picked = jax.vmap(take_rows)(grouped, columns.reshape(term_count, sectors * link_count))
    picked = picked.reshape(term_count, roots_here, sectors, link_count, block_size, col_count)
    product = jnp.einsum("kajpq,knajqc->napc", blocks, picked, preferred_element_type=jnp.float32)
    return product.reshape(roots_here, full_width, col_count)


def general_shards(theta, hdiag, pattern, left_blocks, left_cols, right_blocks, right_cols):
    roots_here, row_count, full_width = theta.shape
    sectors = pattern.shape[0]
    block_size = full_width // sectors
    first_row = lax.axis_index(("blk", "sub")) * row_count
    block_row = (first_row + jnp.arange(row_count, dtype=jnp.int32)) // block_size
    onehot = (block_row[:, None] == jnp.arange(sectors, dtype=jnp.int32)[None, :]).astype(
        jnp.float32
    )
    row_pattern = jnp.dot(onehot, pattern.astype(jnp.float32), preferred_element_type=jnp.float32)
    allowed = jnp.broadcast_to(row_pattern[:, :, None], (row_count, sectors, block_size))
    allowed = allowed.reshape(row_count, full_width).astype(jnp.bfloat16)
    diagonal = hdiag.astype(jnp.float32)
    peers = lax.axis_size("blk") * lax.axis_size("sub")

    def left_part(arrived):
        return apply_left(arrived, left_blocks, left_cols)

    def operate(field_in):
        images = apply_right(field_in, right_blocks, right_cols)
        partial_sum = left_part(
            lax.all_to_all(images, ("blk", "sub"), split_axis=3, concat_axis=2, tiled=True)
        )
        shares = lax.psum_scatter(partial_sum, "ops", scatter_dimension=2, tiled=True)
        returned = lax.all_to_all(
            shares.astype(jnp.bfloat16), ("blk", "sub"), split_axis=1, concat_axis=2, tiled=True
        )
        gathered = lax.all_gather(returned, "ops", axis=2, tiled=True)
        narrow = returned.shape[2] // peers
        gathered = gathered.reshape(roots_here, row_count, lax.axis_size("ops"), peers, narrow)
        offdiag = gathered.transpose(0, 1, 3, 2, 4).reshape(roots_here, row_count, full_width)
        offdiag = offdiag * allowed[None]
        return diagonal[None] * field_in.astype(jnp.float32) + offdiag.astype(jnp.float32)

    projected = theta * allowed[None]
    wave = projected.astype(jnp.float32)
    sigma_one = operate(projected)
    norm_sq, energy_sum = lax.psum(
        (jnp.sum(wave * wave, axis=(1, 2)), jnp.sum(wave * sigma_one, axis=(1, 2))), ("blk", "sub")
    )
    denominator = norm_sq + 1e-06
    energy = energy_sum / denominator
    shifted = diagonal[None] - energy[:, None, None]
    update = (sigma_one - energy[:, None, None] * wave) * shifted / (shifted * shifted + 1.0)
    correlation = lax.psum(jnp.sum(wave * update, axis=(1, 2)), ("blk", "sub"))
    factor = correlation / denominator
    orthogonal = update - factor[:, None, None] * wave
    length_sq = lax.psum(jnp.sum(orthogonal * orthogonal, axis=(1, 2)), ("blk", "sub"))
    correction = (orthogonal * jnp.sqrt(norm_sq / (length_sq + 1e-06))[:, None, None]).astype(
        jnp.bfloat16
    )
    sigma_two = operate(correction).astype(jnp.bfloat16)
    second = sigma_two.astype(jnp.float32)
    fixed = correction.astype(jnp.float32)
    cross_one, cross_two, cross_three = lax.psum(
        (
            jnp.sum(wave * second, axis=(1, 2)),
            jnp.sum(fixed * sigma_one, axis=(1, 2)),
            jnp.sum(fixed * second, axis=(1, 2)),
        ),
        ("blk", "sub"),
    )
    subspace = (
        jnp.stack([energy_sum, cross_one, cross_two, cross_three], axis=1) / denominator[:, None]
    )
    return (correction, sigma_two, subspace)


def halves_fit(mesh):
    sizes = dict(mesh.shape)
    return sizes["blk"] == 4 and sizes["ops"] == 2 and sizes["sub"] == 2


def across(value, axis, distance):
    size = lax.axis_size(axis)
    return lax.ppermute(value, axis, [(i, i ^ distance) for i in range(size)])


def share(stats):
    axes = ("blk", "ops")
    count = lax.axis_size("blk") * lax.axis_size("ops")
    pair = jnp.stack([stats, across(stats, "sub", 1)])
    found = [pair]
    for distance in (1, 2, 3):
        found.append(lax.ppermute(pair, axes, [(i, i ^ distance) for i in range(count)]))
    return found


def place():
    return lax.axis_index("blk"), lax.axis_index("ops"), lax.axis_index("sub")


def fold(value):
    rows, width = value.shape
    value = jnp.sum(value.reshape(rows // 8, 8, width), axis=0)
    return sum(value[:, at : at + LANES] for at in range(0, width, LANES))


def in_middle(z):
    return jnp.logical_or(z == 1, z == 2)


def row_of(dz, dx, dc):
    z, x, c = place()
    return 4 * (z ^ dz) + 2 * (c ^ dc) + (x ^ dx if dx < 2 else dx - 2)


def operate_kernel(first, plan, right_cols, left_cols, cols_other, pattern, right, left_own, left_other, *refs):
    count = len(plan)
    pieces, refs = refs[:count], refs[count:]
    if first:
        mix_a, mix_b, weight_own, psi_out, off_out, stats_out = refs[:6]
        refs = refs[6:]
    else:
        hd_own, hd_far, psi_in, off_in, stats_in, near_out, far_out, late_out, stats_out = refs[:9]
        refs = refs[9:]
    field, images, left, diag, sems = refs
    z, x, c = place()
    sectors, block, width = field.shape
    table = right.shape[1]
    links = table // sectors
    mine = 4 * z + 2 * c + x
    rows = (mine, mine ^ 12)

    copies = []

    def begin(source, target):
        copy = pltpu.make_async_copy(source, target, sems.at[len(copies)])
        copy.start()
        copies.append(copy)

    for at in range(2):
        begin(left_own.at[pl.ds(rows[at] * links, links)], left.at[0, pl.ds(at * links, links)])
    begin(left_other.at[pl.ds(table // 2, 2 * links)], left.at[1])
    if not first:
        begin(hd_own.at[x], diag.at[0])
        begin(hd_far, diag.at[1])

    def allowed(a, q, value):
        return lax.select(pattern[a, q] != 0, value, jnp.zeros_like(value))

    for piece, offsets in zip(pieces, plan):
        for at, (dz, dx, dc, start, tall) in enumerate(offsets):
            row = row_of(dz, dx, dc)
            for line in range(0, tall, 16):
                value = piece[at, line : line + 16, :]
                field[row, start + line : start + line + 16, :] = value

    def right_col(term, b, j):
        return cols_other[j, b] if term else right_cols[j, 0, b]

    def left_col(term, a, j):
        return cols_other[8 + j, a] if term else left_cols[j, 0, a]

    sources = [[left_col(term, rows[at], j) for at in range(2) for j in range(links)] for term in range(2)]

    deep = links * block

    none = jnp.zeros((block, block), jnp.bfloat16)
    pair = 2

    def image(n, carry):
        picks = [(i, j) for i in range(pair) for j in range(links)]
        for term in range(2):
            found = [right_col(term, n * pair + i, j) for i, j in picks]
            lhs = []
            for source in sources[term]:
                line = []
                for col in found:
                    value = field[source, :, pl.ds(pl.multiple_of(col * block, block), block)]
                    line.append(value)
                lhs.append(jnp.concatenate(line, axis=1))
            rhs = []
            for i, j in picks:
                tile = right[term, (n * pair + i) * links + j]
                rhs.append(jnp.concatenate([tile if i == at else none for at in range(pair)], axis=1))
            product = jnp.dot(
                jnp.concatenate(lhs, axis=0),
                jnp.concatenate(rhs, axis=0),
                preferred_element_type=jnp.float32,
            )
            product = product.astype(jnp.bfloat16)
            span = pl.ds(pl.multiple_of(n * pair * block, pair * block), pair * block)
            for at in range(2):
                images[at, term * deep : (term + 1) * deep, span] = product[at * deep : (at + 1) * deep]
        return carry

    lax.fori_loop(0, sectors // pair, image, 0, unroll=2)
    for copy in copies:
        copy.wait()

    step = 2
    early_rows = block // 2
    zero = jnp.zeros((8, LANES), jnp.float32)

    def column(n, sums):
        start = pl.multiple_of(n * step * block, step * block)
        span = pl.ds(start, step * block)
        sums = list(sums)

        def masked(a, value):
            parts = [
                allowed(a, n * step + i, value[:, i * block : (i + 1) * block]) for i in range(step)
            ]
            return jnp.concatenate(parts, axis=1)

        for at in range(2):
            weights = [left[term, at * links + j] for term in range(2) for j in range(links)]
            total = jnp.dot(
                jnp.concatenate(weights, axis=1),
                images[at, :, span],
                preferred_element_type=jnp.float32,
            )
            offdiag = masked(rows[at], total.astype(jnp.bfloat16).astype(jnp.float32))
            own = field[rows[at], :, span].astype(jnp.float32)
            if first:
                psi_out[at, :, span] = own.astype(jnp.bfloat16)
                off_out[at, :, span] = offdiag.astype(jnp.bfloat16)
                sums[0] += fold(own * own)
                sums[1] += fold(own * offdiag)
            else:
                weight = diag[at, :, span].astype(jnp.float32)
                narrow = (weight * own + offdiag).astype(jnp.bfloat16)
                if at == 0:
                    near_out[:, span] = narrow
                else:
                    far_out[:, span] = narrow[:early_rows]
                    late_out[:, span] = narrow[early_rows:]
                second = narrow.astype(jnp.float32)
                wave = psi_in[at, :, span].astype(jnp.float32)
                sigma_one = weight * wave + off_in[at, :, span].astype(jnp.float32)
                sums[0] += fold(wave * second)
                sums[1] += fold(own * sigma_one)
                sums[2] += fold(own * second)
        return tuple(sums)

    sums = list(lax.fori_loop(0, sectors // step, column, (zero,) * (2 if first else 3)))
    if first:
        far_weight = sum(mix[0:48, width:].astype(jnp.float32) for mix in (mix_a, mix_b))
        sums[1] += weight_own[...] + (far_weight[0:8] + far_weight[16:24] + far_weight[32:40])
    stats_out[...] = jnp.zeros_like(stats_out)
    for at, value in enumerate(sums):
        stats_out[at : at + 1, :] = jnp.sum(value, axis=0, keepdims=True)
    if not first:
        stats_out[3:5, :] = stats_in[0:2, :]


def operate(first, plan, pieces, cols, pattern, right, left, extra):
    _, table, block, _ = right.shape
    width = pieces[0].shape[2]
    sectors = width // block
    links = table // sectors
    rows = jax.ShapeDtypeStruct((2, block, width), jnp.bfloat16)
    one = jax.ShapeDtypeStruct((block, width), jnp.bfloat16)
    some = jax.ShapeDtypeStruct((block // 2, width), jnp.bfloat16)
    stats = jax.ShapeDtypeStruct((8, LANES), jnp.float32)
    out_shape = (rows, rows, stats) if first else (one, some, some, stats)
    extra_specs = [VMEM] * 3 if first else [ANY, ANY, VMEM, VMEM, VMEM]
    inner = 2 * 2 * sectors * 2 * links * links * block * block * block
    outer = 2 * 2 * 2 * links * block * block * width
    return pl.pallas_call(
        functools.partial(operate_kernel, first, plan),
        out_shape=out_shape,
        in_specs=[SMEM, SMEM, SMEM, SMEM, VMEM, ANY, ANY] + [VMEM] * len(pieces) + extra_specs,
        out_specs=(VMEM,) * len(out_shape),
        scratch_shapes=[
            pltpu.VMEM((sectors, block, width), jnp.bfloat16),
            pltpu.VMEM((2, 2 * links * block, width), jnp.bfloat16),
            pltpu.VMEM((2, 2 * links, block, block), jnp.bfloat16),
            pltpu.VMEM((2, block, width), jnp.bfloat16),
            pltpu.SemaphoreType.DMA((5,)),
        ],
        compiler_params=pltpu.CompilerParams(vmem_limit_bytes=OPERATE_LIMIT),
        cost_estimate=pl.CostEstimate(
            flops=inner + outer if first else 0,
            bytes_accessed=16 * 1024 * 1024 if first else 1024,
            transcendentals=0,
        ),
        name="operate_first" if first else "operate_second",
    )(*cols, pattern, right, *left, *pieces, *extra)


def arrange_kernel(own, near, far, out, found, sems):
    _, _, c = place()
    part = own.shape[0] // 2
    copies = [
        pltpu.make_async_copy(own, found.at[0], sems.at[0]),
        pltpu.make_async_copy(near.at[pl.ds(0, part)], found.at[1, pl.ds(c * part, part)], sems.at[1]),
        pltpu.make_async_copy(far.at[pl.ds(0, part)], found.at[1, pl.ds((1 - c) * part, part)], sems.at[2]),
    ]
    for copy in copies:
        copy.start()
    for copy in copies:
        copy.wait()

    def turn(at, carry):
        for term in range(2):
            out[term, at] = found[term, at].T
        return carry

    lax.fori_loop(0, found.shape[1], turn, 0, unroll=4)


def arrange(own, near, far):
    shape = (2, *own.shape)
    return pl.pallas_call(
        arrange_kernel,
        out_shape=jax.ShapeDtypeStruct(shape, own.dtype),
        in_specs=[ANY] * 3,
        out_specs=VMEM,
        scratch_shapes=[pltpu.VMEM(shape, own.dtype), pltpu.SemaphoreType.DMA((3,))],
        compiler_params=pltpu.CompilerParams(vmem_limit_bytes=VMEM_LIMIT),
        name="arrange",
    )(own, near, far)


def prepare_kernel(
    pattern, theta, hd, right, left, right_cols, left_cols, mix_a, mix_b, packed, own_out, waves, diag, spots, sems
):
    z, x, c = place()
    half = z // 2
    middle = in_middle(z)
    mine = 4 * z + 2 * c + x
    block, width = diag.shape
    sectors = width // block
    links = right.shape[0] // sectors
    part = right.shape[0] // 2
    root_a = jnp.where(middle, half, 1 - half)
    rows = pl.ds(0, width)
    sources = (
        (theta.at[half, x], waves.at[0]),
        (theta.at[1 - half, x], waves.at[1]),
        (hd.at[x], diag),
        (theta.at[root_a, jnp.where(middle, 0, x)], mix_a.at[:, rows]),
        (theta.at[1 - root_a, jnp.where(middle, x, 0)], mix_b.at[:, rows]),
        (right.at[pl.ds(c * part, part)], packed.at[pl.ds(0, part)]),
        (left.at[pl.ds((mine ^ 1) * links, links)], packed.at[pl.ds(part, links)]),
        (left.at[pl.ds((mine ^ 13) * links, links)], packed.at[pl.ds(part + links, links)]),
    )
    copies = [
        pltpu.make_async_copy(source, target, sems.at[at])
        for at, (source, target) in enumerate(sources)
    ]
    for copy in copies:
        copy.start()
    last = part + 2 * links
    spots[...] = jnp.zeros_like(spots)
    spots[0:links, 0:sectors] = right_cols[:, 0, :].astype(jnp.float32)
    spots[8 : 8 + links, 0:sectors] = left_cols[:, 0, :].astype(jnp.float32)
    packed[last] = jnp.zeros_like(packed[last])
    packed[last, 0:16, :] = spots[...].astype(jnp.bfloat16)
    for copy in copies[:3]:
        copy.wait()
    zero = jnp.zeros((8, LANES), jnp.float32)

    def column(q, sums):
        span = pl.ds(pl.multiple_of(q * block, block), block)
        weight = diag[:, span].astype(jnp.float32)
        weight = jnp.where(pattern[mine, q] != 0, weight, jnp.zeros_like(weight))
        found = []
        for root in range(2):
            wave = waves[root, :, span].astype(jnp.float32)
            found.append(sums[root] + fold(weight * wave * wave))
        return tuple(found)

    near, far = lax.fori_loop(0, sectors, column, (zero, zero), unroll=4)
    own_out[...] = near
    left_over = jnp.concatenate([far, zero], axis=0)
    parts = []
    for _ in range(3):
        piece = left_over.astype(jnp.bfloat16)
        parts.append(piece)
        left_over = left_over - piece.astype(jnp.float32)
    parts.append(jnp.zeros((block - 48, LANES), jnp.bfloat16))
    tail = jnp.concatenate(parts, axis=0)
    none = jnp.zeros_like(tail)
    mix_a[:, width:] = jnp.where(middle, none, tail)
    mix_b[:, width:] = jnp.where(middle, tail, none)
    for copy in copies[3:]:
        copy.wait()


def prepare(pattern, theta, hd, right, left, *cols):
    _, _, block, width = theta.shape
    table = right.shape[0]
    links = table * block // width
    kind = jnp.bfloat16
    mix = jax.ShapeDtypeStruct((block, width + LANES), kind)
    packed = jax.ShapeDtypeStruct((table // 2 + 2 * links + 1, block, block), kind)
    return pl.pallas_call(
        prepare_kernel,
        out_shape=(mix, mix, packed, jax.ShapeDtypeStruct((8, LANES), jnp.float32)),
        in_specs=[SMEM, ANY, ANY, ANY, ANY, VMEM, VMEM],
        out_specs=(VMEM,) * 4,
        scratch_shapes=[
            pltpu.VMEM((2, block, width), kind),
            pltpu.VMEM((block, width), kind),
            pltpu.VMEM((16, LANES), jnp.float32),
            pltpu.SemaphoreType.DMA((8,)),
        ],
        compiler_params=pltpu.CompilerParams(vmem_limit_bytes=PREPARE_LIMIT),
        name="prepare",
    )(pattern, theta, hd, right, left, *cols)


def total_of(rows):
    return jnp.sum(rows, axis=1, keepdims=True)


def update_kernel(psi, off, hd_own, hd_far, *refs):
    stats, (t_out, stats_out, diag, sems) = refs[:4], refs[4:]
    z, x, c = place()
    copies = [
        pltpu.make_async_copy(hd_own.at[x], diag.at[0], sems.at[0]),
        pltpu.make_async_copy(hd_far, diag.at[1], sems.at[1]),
    ]
    for copy in copies:
        copy.start()
    whole = sum(ref[at, 0:2, :] for ref in stats for at in range(2))
    norm_sq, energy_sum = total_of(whole[0:1, :]), total_of(whole[1:2, :])
    energy = energy_sum / (norm_sq + 1e-06)
    mine = total_of(stats[0][0, 0:1, :])
    for copy in copies:
        copy.wait()
    _, block, width = psi.shape
    step = 16
    zero = jnp.zeros((8, LANES), jnp.float32)

    def chunk(n, total):
        span = pl.ds(pl.multiple_of(n * step, step), step)
        for at in range(2):
            wave = psi[at, span, :].astype(jnp.float32)
            weight = diag[at, span, :].astype(jnp.float32)
            sigma = weight * wave + off[at, span, :].astype(jnp.float32)
            shifted = weight - energy
            t = (sigma - energy * wave) * shifted / (shifted * shifted + 1.0)
            t_out[at, span, :] = t
            total = total + fold(wave * t)
        return total

    lanes = jnp.sum(lax.fori_loop(0, block // step, chunk, zero), axis=0, keepdims=True)
    correlation = total_of(lanes)
    local = jnp.where(mine > 0.0, correlation / jnp.where(mine > 0.0, mine, 1.0), 0.0)

    def within(n, total):
        span = pl.ds(pl.multiple_of(n * step, step), step)
        for at in range(2):
            rest = t_out[at, span, :] - local * psi[at, span, :].astype(jnp.float32)
            total = total + fold(rest * rest)
        return total

    spread = jnp.sum(lax.fori_loop(0, block // step, within, zero), axis=0, keepdims=True)
    stats_out[...] = jnp.zeros_like(stats_out)
    stats_out[0:1, :] = jnp.broadcast_to(correlation, (1, LANES))
    stats_out[1:2, :] = jnp.broadcast_to(total_of(spread), (1, LANES))
    stats_out[2:3, :] = jnp.broadcast_to(mine, (1, LANES))
    stats_out[3:4, :] = jnp.broadcast_to(local, (1, LANES))
    stats_out[4:5, :] = jnp.broadcast_to(norm_sq, (1, LANES))


def correct_kernel(psi, t, *refs):
    stats, outs = refs[:4], refs[4:]
    stats = [ref.at[at] for ref in stats for at in range(2)]
    norm_sq = stats[0][4:5, 0:1]
    factor = sum(ref[0:1, 0:1] for ref in stats) / (norm_sq + 1e-06)
    length_sq = jnp.zeros((1, 1), jnp.float32)
    for ref in stats:
        gap = factor - ref[3:4, 0:1]
        length_sq = length_sq + (ref[1:2, 0:1] + gap * gap * ref[2:3, 0:1])
    scale = jnp.sqrt(norm_sq / (length_sq + 1e-06))
    _, block, width = psi.shape
    step = 16

    def chunk(n, carry):
        span = pl.ds(pl.multiple_of(n * step, step), step)
        for at in range(2):
            wave = psi[at, span, :].astype(jnp.float32)
            outs[at][span, :] = ((t[at, span, :] - factor * wave) * scale).astype(jnp.bfloat16)
        return carry

    lax.fori_loop(0, block // step, chunk, 0)


def assemble_kernel(places, based, *refs):
    count = len(places)
    pieces, (out, sems) = refs[:count], refs[count + based :]
    z, x, c = place()
    half = z // 2
    copies = []
    for at, (root, flip, start) in enumerate(places):
        size = pieces[at].shape[0]
        target = out.at[half ^ root, x ^ flip, pl.ds(start, size)]
        copies.append(pltpu.make_async_copy(pieces[at], target, sems.at[at]))
    for copy in copies:
        copy.start()
    for copy in copies:
        copy.wait()


def assemble(block, pieces, places, base=None):
    width = pieces[0].shape[1]
    based = [] if base is None else [base]
    return pl.pallas_call(
        functools.partial(assemble_kernel, places, len(based)),
        out_shape=jax.ShapeDtypeStruct((2, 2, block, width), pieces[0].dtype),
        in_specs=[VMEM] * len(pieces) + [ANY] * len(based),
        out_specs=ANY,
        scratch_shapes=[pltpu.SemaphoreType.DMA((len(pieces),))],
        input_output_aliases={len(pieces): 0} if based else {},
        compiler_params=pltpu.CompilerParams(vmem_limit_bytes=VMEM_LIMIT),
        name="assemble",
    )(*pieces, *based)


def after(value, *others):
    return lax.optimization_barrier((value, *others))[0]


def shards(theta, hdiag, pattern, left_blocks, left_cols, right_blocks, right_cols):
    roots, row_count, width = theta.shape
    sectors = pattern.shape[0]
    block = width // sectors
    z, x, c = place()
    half = z // 2
    mine = 4 * z + 2 * c + x

    halves = theta.reshape(roots, 2, block, width)
    diag = hdiag.reshape(2, block, width)
    middle = in_middle(z)
    right = right_blocks.reshape(-1, block, block)
    left = left_blocks.reshape(-1, block, block)
    cols = (right_cols.transpose(2, 0, 1), left_cols.transpose(2, 0, 1))

    mix_a, mix_b, packed, weight_own = prepare(pattern, halves, diag, right, left, *cols)
    mix_a = lax.ppermute(mix_a, "blk", [(0, 2), (2, 3), (3, 1), (1, 0)])
    mix_b = lax.ppermute(mix_b, "blk", [(0, 1), (1, 3), (3, 2), (2, 0)])
    operators = across(packed, "ops", 1)

    def masked(row, value):
        line = lax.dynamic_index_in_dim(pattern, row, 0, keepdims=False).astype(jnp.bfloat16)
        return value * jnp.repeat(line, block)[None, :]

    own = [
        masked(row_of(0, 2 + at, 0), lax.dynamic_slice(halves, (half, at, 0, 0), (1, 1, block, width))[0, 0])
        for at in range(2)
    ]
    own_core = [across(value, "sub", 1) for value in own]

    mix_a, mix_b = after((mix_a, mix_b), *own_core)
    far = masked(row_of(2, 0, 0), jnp.where(middle, mix_a[:, :width], mix_b[:, :width]))
    far_z = across(far, "blk", 1)
    far_x = across(far, "ops", 1)
    near_a = masked(row_of(1, 2, 0), jnp.where(middle, mix_b[:, :width], mix_a[:, :width]))
    far_core = across(far, "sub", 1)
    near_a_core = across(near_a, "sub", 1)

    operators = after(operators, mix_b)
    operators_core = across(operators, "sub", 1)
    turned = arrange(right, operators, operators_core)
    next_b, far_z = after((own[1], far_z), far_core, near_a_core, turned)
    near_b = across(next_b, "blk", 1)
    far_zx = across(far_z, "ops", 1)
    cols = (*cols, operators[-1, :16, :sectors].astype(jnp.int32))
    far_x_core = across(far_x, "sub", 1)
    far_z_core = across(far_z, "sub", 1)
    hd_far = lax.dynamic_index_in_dim(diag, x, 0, keepdims=False)
    hd_far = across(after(hd_far, far_z), "blk", 3)
    far_zx_core = across(far_zx, "sub", 1)
    near_b_core = across(near_b, "sub", 1)

    left = (left, operators)
    pieces = []
    plan = []
    for piece, offset in (
        (own[0], (0, 2, 0)),
        (own[1], (0, 3, 0)),
        (own_core[0], (0, 2, 1)),
        (own_core[1], (0, 3, 1)),
        (near_a, (1, 2, 0)),
        (near_b, (1, 3, 0)),
        (near_a_core, (1, 2, 1)),
        (near_b_core, (1, 3, 1)),
        (far, (2, 0, 0)),
        (far_core, (2, 0, 1)),
        (far_x, (2, 1, 0)),
        (far_x_core, (2, 1, 1)),
        (far_z, (3, 0, 0)),
        (far_z_core, (3, 0, 1)),
        (far_zx, (3, 1, 0)),
        (far_zx_core, (3, 1, 1)),
    ):
        pieces.append(piece[None])
        plan.append((offset + (0, block),))
    psi, off_one, stats_one = operate(
        True, tuple(plan), pieces, cols, pattern, turned, left, (mix_a, mix_b, weight_own)
    )

    found = share(stats_one)
    t, stats_two = pl.pallas_call(
        update_kernel,
        out_shape=(
            jax.ShapeDtypeStruct((2, block, width), jnp.float32),
            jax.ShapeDtypeStruct((8, LANES), jnp.float32),
        ),
        in_specs=[VMEM, VMEM, ANY, ANY] + [VMEM] * 4,
        out_specs=(VMEM, VMEM),
        scratch_shapes=[
            pltpu.VMEM((2, block, width), jnp.bfloat16),
            pltpu.SemaphoreType.DMA((2,)),
        ],
        compiler_params=pltpu.CompilerParams(vmem_limit_bytes=VMEM_LIMIT),
        name="update",
    )(psi, off_one, diag, hd_far, *found)
    found = share(stats_two)
    one = jax.ShapeDtypeStruct((block, width), jnp.bfloat16)
    changed_near, changed_far = pl.pallas_call(
        correct_kernel,
        out_shape=(one, one),
        in_specs=[VMEM, VMEM] + [VMEM] * 4,
        out_specs=(VMEM, VMEM),
        compiler_params=pltpu.CompilerParams(vmem_limit_bytes=VMEM_LIMIT),
        name="correct",
    )(psi, t, *found)

    near_z = across(changed_near, "blk", 1)
    far_x = across(changed_far, "ops", 1)
    near_core = across(changed_near, "sub", 1)
    far_core = across(changed_far, "sub", 1)
    other_middle = lax.ppermute(changed_far, "blk", [(1, 2), (2, 1)])
    near_z, far_x = after((near_z, far_x), other_middle)
    near_zx = across(near_z, "ops", 1)
    far_xz = across(far_x, "blk", 1)
    near_x = across(after(changed_near, near_z, far_x), "ops", 1)
    far_z = across(after(changed_far, near_z, far_x), "blk", 1)
    near_z_core = across(near_z, "sub", 1)
    far_x_core = across(far_x, "sub", 1)
    near_x_core = across(near_x, "sub", 1)
    far_z_core = across(far_z, "sub", 1)
    near_zx_core = across(near_zx, "sub", 1)
    far_xz_core = across(far_xz, "sub", 1)
    other_end = lax.ppermute(after(changed_far, near_z, far_x), "blk", [(0, 3), (3, 0)])
    pieces, plan = [], []
    for piece, offset in (
        (changed_near, (0, 0, 0)),
        (changed_far, (3, 0, 0)),
        (near_core, (0, 0, 1)),
        (far_core, (3, 0, 1)),
        (near_z, (1, 0, 0)),
        (far_z, (2, 0, 0)),
        (near_z_core, (1, 0, 1)),
        (far_z_core, (2, 0, 1)),
        (near_x, (0, 1, 0)),
        (far_x, (3, 1, 0)),
        (near_x_core, (0, 1, 1)),
        (far_x_core, (3, 1, 1)),
        (near_zx, (1, 1, 0)),
        (far_xz, (2, 1, 0)),
        (near_zx_core, (1, 1, 1)),
        (far_xz_core, (2, 1, 1)),
    ):
        pieces.append(piece[None])
        plan.append((offset + (0, block),))
    two_near, two_far, two_late, stats_three = operate(
        False, tuple(plan), pieces, cols, pattern, turned, left, (diag, hd_far, psi, off_one, stats_one)
    )

    far_in = across(two_far, "blk", 3)
    near_in = across(two_near, "ops", 1)
    late_in = across(after(two_late, far_in), "blk", 3)
    far_in_x = across(after(far_in, near_in), "ops", 1)
    sums = stats_three + across(stats_three, "sub", 1)
    other = jnp.where(middle, other_middle, after(other_end, two_near))
    other_x = across(other, "ops", 1)
    sums = after(sums, far_in)
    both = jnp.stack([sums + across(sums, "blk", 1), across(sums, "blk", 2) + across(sums, "blk", 3)])
    both = after(both, late_in)
    both = both + across(both, "ops", 1)
    other, other_x = after((other, other_x), late_in)
    late_in_x = across(late_in, "ops", 1)
    both = jnp.sum(jnp.where(half == 0, both, both[::-1])[:, :5], axis=2)
    scale = both[:, 3:4] + 1e-06
    subspace = jnp.concatenate([both[:, 4:5], both[:, 0:3]], axis=1) / scale
    places = ((0, 0, 0), (0, 1, 0), (1, 0, 0), (1, 1, 0))
    correction = assemble(block, (changed_near, near_x, other, other_x), places)
    places = ((0, 0, 0), (0, 1, 0), (1, 0, 0), (1, 0, block // 2), (1, 1, 0))
    sigma_two = assemble(block, (two_near, near_in, far_in, late_in, far_in_x), places)
    sigma_two = assemble(block, (late_in_x,), ((1, 1, block // 2),), sigma_two)
    return correction.reshape(theta.shape), sigma_two.reshape(theta.shape), subspace


def solution(mesh):
    in_specs = (
        P("groups", ("blk", "sub"), None),
        P(("groups", "blk", "sub"), None),
        P("groups", None),
        P(("groups", "ops"), None, None, None, None),
        P(("groups", "ops"), None, None),
        P(("groups", "ops"), None, None, None, None),
        P(("groups", "ops"), None, None),
    )
    out_specs = (
        P("groups", ("blk", "sub"), None),
        P("groups", ("blk", "sub"), None),
        P("groups", None),
    )
    body = shards if halves_fit(mesh) else general_shards
    return jax.shard_map(body, mesh=mesh, in_specs=in_specs, out_specs=out_specs, check_vma=False)
```

```python
import functools

import jax
import jax.numpy as jnp
from jax import lax
from jax.experimental import pallas as pl
from jax.experimental.pallas import tpu as pltpu
from jax.sharding import PartitionSpec as P

ANY = pl.BlockSpec(memory_space=pl.ANY)
SMEM = pl.BlockSpec(memory_space=pltpu.SMEM)
VMEM = pl.BlockSpec(memory_space=pltpu.VMEM)
VMEM_LIMIT = 24 * 1024 * 1024
OPERATE_LIMIT = 44 * 1024 * 1024
PREPARE_LIMIT = 56 * 1024 * 1024
LANES = 128


def apply_right(field_in, blocks, columns):
    roots_here, row_count, full_width = field_in.shape
    term_count, sectors, link_count = columns.shape
    block_size = full_width // sectors
    grouped = field_in.reshape(roots_here, row_count, sectors, block_size)
    picked = jnp.take(grouped, columns.reshape(-1), axis=2)
    picked = picked.reshape(roots_here, row_count, term_count, sectors, link_count, block_size)
    product = jnp.einsum("nrkbjq,kbjpq->knrbp", picked, blocks, preferred_element_type=jnp.float32)
    return product.reshape(term_count, roots_here, row_count, full_width).astype(jnp.bfloat16)


def take_rows(stacked, indices):
    return jnp.take(stacked, indices, axis=1)


def apply_left(arrived, blocks, columns):
    term_count, roots_here, full_width, col_count = arrived.shape
    sectors = columns.shape[1]
    link_count = columns.shape[2]
    block_size = full_width // sectors
    grouped = arrived.reshape(term_count, roots_here, sectors, block_size, col_count)
    picked = jax.vmap(take_rows)(grouped, columns.reshape(term_count, sectors * link_count))
    picked = picked.reshape(term_count, roots_here, sectors, link_count, block_size, col_count)
    product = jnp.einsum("kajpq,knajqc->napc", blocks, picked, preferred_element_type=jnp.float32)
    return product.reshape(roots_here, full_width, col_count)


def general_shards(theta, hdiag, pattern, left_blocks, left_cols, right_blocks, right_cols):
    roots_here, row_count, full_width = theta.shape
    sectors = pattern.shape[0]
    block_size = full_width // sectors
    first_row = lax.axis_index(("blk", "sub")) * row_count
    block_row = (first_row + jnp.arange(row_count, dtype=jnp.int32)) // block_size
    onehot = (block_row[:, None] == jnp.arange(sectors, dtype=jnp.int32)[None, :]).astype(
        jnp.float32
    )
    row_pattern = jnp.dot(onehot, pattern.astype(jnp.float32), preferred_element_type=jnp.float32)
    allowed = jnp.broadcast_to(row_pattern[:, :, None], (row_count, sectors, block_size))
    allowed = allowed.reshape(row_count, full_width).astype(jnp.bfloat16)
    diagonal = hdiag.astype(jnp.float32)
    peers = lax.axis_size("blk") * lax.axis_size("sub")

    def left_part(arrived):
        return apply_left(arrived, left_blocks, left_cols)

    def operate(field_in):
        images = apply_right(field_in, right_blocks, right_cols)
        partial_sum = left_part(
            lax.all_to_all(images, ("blk", "sub"), split_axis=3, concat_axis=2, tiled=True)
        )
        shares = lax.psum_scatter(partial_sum, "ops", scatter_dimension=2, tiled=True)
        returned = lax.all_to_all(
            shares.astype(jnp.bfloat16), ("blk", "sub"), split_axis=1, concat_axis=2, tiled=True
        )
        gathered = lax.all_gather(returned, "ops", axis=2, tiled=True)
        narrow = returned.shape[2] // peers
        gathered = gathered.reshape(roots_here, row_count, lax.axis_size("ops"), peers, narrow)
        offdiag = gathered.transpose(0, 1, 3, 2, 4).reshape(roots_here, row_count, full_width)
        offdiag = offdiag * allowed[None]
        return diagonal[None] * field_in.astype(jnp.float32) + offdiag.astype(jnp.float32)

    projected = theta * allowed[None]
    wave = projected.astype(jnp.float32)
    sigma_one = operate(projected)
    norm_sq, energy_sum = lax.psum(
        (jnp.sum(wave * wave, axis=(1, 2)), jnp.sum(wave * sigma_one, axis=(1, 2))), ("blk", "sub")
    )
    denominator = norm_sq + 1e-06
    energy = energy_sum / denominator
    shifted = diagonal[None] - energy[:, None, None]
    update = (sigma_one - energy[:, None, None] * wave) * shifted / (shifted * shifted + 1.0)
    correlation = lax.psum(jnp.sum(wave * update, axis=(1, 2)), ("blk", "sub"))
    factor = correlation / denominator
    orthogonal = update - factor[:, None, None] * wave
    length_sq = lax.psum(jnp.sum(orthogonal * orthogonal, axis=(1, 2)), ("blk", "sub"))
    correction = (orthogonal * jnp.sqrt(norm_sq / (length_sq + 1e-06))[:, None, None]).astype(
        jnp.bfloat16
    )
    sigma_two = operate(correction).astype(jnp.bfloat16)
    second = sigma_two.astype(jnp.float32)
    fixed = correction.astype(jnp.float32)
    cross_one, cross_two, cross_three = lax.psum(
        (
            jnp.sum(wave * second, axis=(1, 2)),
            jnp.sum(fixed * sigma_one, axis=(1, 2)),
            jnp.sum(fixed * second, axis=(1, 2)),
        ),
        ("blk", "sub"),
    )
    subspace = (
        jnp.stack([energy_sum, cross_one, cross_two, cross_three], axis=1) / denominator[:, None]
    )
    return (correction, sigma_two, subspace)


def halves_fit(mesh):
    sizes = dict(mesh.shape)
    return sizes["blk"] == 4 and sizes["ops"] == 2 and sizes["sub"] == 2


def across(value, axis, distance):
    size = lax.axis_size(axis)
    return lax.ppermute(value, axis, [(i, i ^ distance) for i in range(size)])


def share(stats):
    axes = ("blk", "ops")
    count = lax.axis_size("blk") * lax.axis_size("ops")
    pair = jnp.stack([stats, across(stats, "sub", 1)])
    found = [pair]
    for distance in (1, 2, 3):
        found.append(lax.ppermute(pair, axes, [(i, i ^ distance) for i in range(count)]))
    return found


def place():
    return lax.axis_index("blk"), lax.axis_index("ops"), lax.axis_index("sub")


def fold(value):
    rows, width = value.shape
    value = jnp.sum(value.reshape(rows // 8, 8, width), axis=0)
    return sum(value[:, at : at + LANES] for at in range(0, width, LANES))


def in_middle(z):
    return jnp.logical_or(z == 1, z == 2)


def row_of(dz, dx, dc):
    z, x, c = place()
    return 4 * (z ^ dz) + 2 * (c ^ dc) + (x ^ dx if dx < 2 else dx - 2)


def operate_kernel(first, plan, right_cols, left_cols, cols_other, pattern, right, left_own, left_other, *refs):
    count = len(plan)
    pieces, refs = refs[:count], refs[count:]
    if first:
        mix_a, mix_b, weight_own, psi_out, off_out, stats_out = refs[:6]
        refs = refs[6:]
    else:
        hd_own, hd_far, psi_in, off_in, stats_in, near_out, far_out, late_out, stats_out = refs[:9]
        refs = refs[9:]
    field, images, left, diag, parts, sems = refs
    z, x, c = place()
    sectors, block, width = field.shape
    table = right.shape[1]
    links = table // sectors
    mine = 4 * z + 2 * c + x
    rows = (mine, mine ^ 12)

    copies = []

    def begin(source, target):
        copy = pltpu.make_async_copy(source, target, sems.at[len(copies)])
        copy.start()
        copies.append(copy)

    for at in range(2):
        begin(left_own.at[pl.ds(rows[at] * links, links)], left.at[0, pl.ds(at * links, links)])
    begin(left_other.at[pl.ds(table // 2, 2 * links)], left.at[1])
    if first:
        for at, mix in enumerate((mix_a, mix_b)):
            begin(mix.at[pl.ds(0, parts.shape[1]), pl.ds(width, LANES)], parts.at[at])
    else:
        begin(hd_own.at[x], diag.at[0])
        begin(hd_far, diag.at[1])

    def allowed(a, q, value):
        return lax.select(pattern[a, q] != 0, value, jnp.zeros_like(value))

    later = len(copies)
    for piece, offsets in zip(pieces, plan):
        for at, (dz, dx, dc, start, tall) in enumerate(offsets):
            row = row_of(dz, dx, dc)
            if first:
                begin(piece.at[at], field.at[row, pl.ds(start, tall)])
                continue
            for line in range(0, tall, 16):
                field[row, start + line : start + line + 16, :] = piece[at, line : line + 16, :]
    for copy in copies[later:]:
        copy.wait()

    def right_col(term, b, j):
        return cols_other[j, b] if term else right_cols[j, 0, b]

    def left_col(term, a, j):
        return cols_other[8 + j, a] if term else left_cols[j, 0, a]

    sources = [[left_col(term, rows[at], j) for at in range(2) for j in range(links)] for term in range(2)]

    deep = links * block

    none = jnp.zeros((block, block), jnp.bfloat16)
    pair = 2

    def image(n, carry):
        picks = [(i, j) for i in range(pair) for j in range(links)]
        for term in range(2):
            found = [right_col(term, n * pair + i, j) for i, j in picks]
            lhs = []
            for source in sources[term]:
                line = []
                for col in found:
                    value = field[source, :, pl.ds(pl.multiple_of(col * block, block), block)]
                    line.append(value)
                lhs.append(jnp.concatenate(line, axis=1))
            rhs = []
            for i, j in picks:
                tile = right[term, (n * pair + i) * links + j]
                rhs.append(jnp.concatenate([tile if i == at else none for at in range(pair)], axis=1))
            product = jnp.dot(
                jnp.concatenate(lhs, axis=0),
                jnp.concatenate(rhs, axis=0),
                preferred_element_type=jnp.float32,
            )
            product = product.astype(jnp.bfloat16)
            span = pl.ds(pl.multiple_of(n * pair * block, pair * block), pair * block)
            for at in range(2):
                images[at, term * deep : (term + 1) * deep, span] = product[at * deep : (at + 1) * deep]
        return carry

    lax.fori_loop(0, sectors // pair, image, 0, unroll=2)
    for copy in copies[:later]:
        copy.wait()

    step = 2
    early_rows = block // 2
    zero = jnp.zeros((8, LANES), jnp.float32)

    def column(n, sums):
        start = pl.multiple_of(n * step * block, step * block)
        span = pl.ds(start, step * block)
        sums = list(sums)

        def masked(a, value):
            parts = [
                allowed(a, n * step + i, value[:, i * block : (i + 1) * block]) for i in range(step)
            ]
            return jnp.concatenate(parts, axis=1)

        for at in range(2):
            weights = [left[term, at * links + j] for term in range(2) for j in range(links)]
            total = jnp.dot(
                jnp.concatenate(weights, axis=1),
                images[at, :, span],
                preferred_element_type=jnp.float32,
            )
            offdiag = masked(rows[at], total.astype(jnp.bfloat16).astype(jnp.float32))
            own = field[rows[at], :, span].astype(jnp.float32)
            if first:
                psi_out[at, :, span] = own.astype(jnp.bfloat16)
                off_out[at, :, span] = offdiag.astype(jnp.bfloat16)
                sums[0] += fold(own * own)
                sums[1] += fold(own * offdiag)
            else:
                weight = diag[at, :, span].astype(jnp.float32)
                narrow = (weight * own + offdiag).astype(jnp.bfloat16)
                if at == 0:
                    near_out[:, span] = narrow
                else:
                    far_out[:, span] = narrow[:early_rows]
                    late_out[:, span] = narrow[early_rows:]
                second = narrow.astype(jnp.float32)
                wave = psi_in[at, :, span].astype(jnp.float32)
                sigma_one = weight * wave + off_in[at, :, span].astype(jnp.float32)
                sums[0] += fold(wave * second)
                sums[1] += fold(own * sigma_one)
                sums[2] += fold(own * second)
        return tuple(sums)

    sums = list(lax.fori_loop(0, sectors // step, column, (zero,) * (2 if first else 3)))
    if first:
        far_weight = (parts[0] + parts[1]).astype(jnp.float32)
        sums[1] += weight_own[...] + (far_weight[0:8] + far_weight[16:24] + far_weight[32:40])
    stats_out[...] = jnp.zeros_like(stats_out)
    for at, value in enumerate(sums):
        stats_out[at : at + 1, :] = jnp.sum(value, axis=0, keepdims=True)
    if not first:
        stats_out[3:5, :] = stats_in[0:2, :]


def operate(first, plan, pieces, cols, pattern, right, left, extra):
    _, table, block, _ = right.shape
    width = pieces[0].shape[2]
    sectors = width // block
    links = table // sectors
    rows = jax.ShapeDtypeStruct((2, block, width), jnp.bfloat16)
    one = jax.ShapeDtypeStruct((block, width), jnp.bfloat16)
    some = jax.ShapeDtypeStruct((block // 2, width), jnp.bfloat16)
    stats = jax.ShapeDtypeStruct((8, LANES), jnp.float32)
    out_shape = (rows, rows, stats) if first else (one, some, some, stats)
    extra_specs = [ANY, ANY, VMEM] if first else [ANY, ANY, VMEM, VMEM, VMEM]
    inner = 2 * 2 * sectors * 2 * links * links * block * block * block
    outer = 2 * 2 * 2 * links * block * block * width
    return pl.pallas_call(
        functools.partial(operate_kernel, first, plan),
        out_shape=out_shape,
        in_specs=[SMEM, SMEM, SMEM, SMEM, VMEM, ANY, ANY] + [ANY if first else VMEM] * len(pieces) + extra_specs,
        out_specs=(VMEM,) * len(out_shape),
        scratch_shapes=[
            pltpu.VMEM((sectors, block, width), jnp.bfloat16),
            pltpu.VMEM((2, 2 * links * block, width), jnp.bfloat16),
            pltpu.VMEM((2, 2 * links, block, block), jnp.bfloat16),
            pltpu.VMEM((2, block, width), jnp.bfloat16),
            pltpu.VMEM((2, 48, LANES), jnp.bfloat16),
            pltpu.SemaphoreType.DMA((5 + len(plan),)),
        ],
        compiler_params=pltpu.CompilerParams(vmem_limit_bytes=PREPARE_LIMIT if first else OPERATE_LIMIT),
        cost_estimate=pl.CostEstimate(
            flops=inner + outer if first else 0,
            bytes_accessed=16 * 1024 * 1024 if first else 1024,
            transcendentals=0,
        ),
        name="operate_first" if first else "operate_second",
    )(*cols, pattern, right, *left, *pieces, *extra)


def arrange_kernel(own, near, far, out, found, sems):
    _, _, c = place()
    part = own.shape[0] // 2
    copies = [
        pltpu.make_async_copy(own, found.at[0], sems.at[0]),
        pltpu.make_async_copy(near.at[pl.ds(0, part)], found.at[1, pl.ds(c * part, part)], sems.at[1]),
        pltpu.make_async_copy(far.at[pl.ds(0, part)], found.at[1, pl.ds((1 - c) * part, part)], sems.at[2]),
    ]
    for copy in copies:
        copy.start()
    for copy in copies:
        copy.wait()

    def turn(at, carry):
        for term in range(2):
            out[term, at] = found[term, at].T
        return carry

    lax.fori_loop(0, found.shape[1], turn, 0, unroll=4)


def arrange(own, near, far):
    shape = (2, *own.shape)
    return pl.pallas_call(
        arrange_kernel,
        out_shape=jax.ShapeDtypeStruct(shape, own.dtype),
        in_specs=[ANY] * 3,
        out_specs=VMEM,
        scratch_shapes=[pltpu.VMEM(shape, own.dtype), pltpu.SemaphoreType.DMA((3,))],
        compiler_params=pltpu.CompilerParams(vmem_limit_bytes=VMEM_LIMIT),
        name="arrange",
    )(own, near, far)


def prepare_kernel(
    pattern, theta, hd, right, left, right_cols, left_cols, mix_a, mix_b, packed, own_out, waves, diag, spots, sems
):
    z, x, c = place()
    half = z // 2
    middle = in_middle(z)
    mine = 4 * z + 2 * c + x
    block, width = diag.shape
    sectors = width // block
    links = right.shape[0] // sectors
    part = right.shape[0] // 2
    root_a = jnp.where(middle, half, 1 - half)
    rows = pl.ds(0, width)
    sources = (
        (theta.at[half, x], waves.at[0]),
        (theta.at[1 - half, x], waves.at[1]),
        (hd.at[x], diag),
        (theta.at[root_a, jnp.where(middle, 0, x)], mix_a.at[:, rows]),
        (theta.at[1 - root_a, jnp.where(middle, x, 0)], mix_b.at[:, rows]),
        (right.at[pl.ds(c * part, part)], packed.at[pl.ds(0, part)]),
        (left.at[pl.ds((mine ^ 1) * links, links)], packed.at[pl.ds(part, links)]),
        (left.at[pl.ds((mine ^ 13) * links, links)], packed.at[pl.ds(part + links, links)]),
    )
    copies = [
        pltpu.make_async_copy(source, target, sems.at[at])
        for at, (source, target) in enumerate(sources)
    ]
    for copy in copies:
        copy.start()
    last = part + 2 * links
    spots[...] = jnp.zeros_like(spots)
    spots[0:links, 0:sectors] = right_cols[:, 0, :].astype(jnp.float32)
    spots[8 : 8 + links, 0:sectors] = left_cols[:, 0, :].astype(jnp.float32)
    packed[last] = jnp.zeros_like(packed[last])
    packed[last, 0:16, :] = spots[...].astype(jnp.bfloat16)
    for copy in copies[:3]:
        copy.wait()
    zero = jnp.zeros((8, LANES), jnp.float32)

    def column(q, sums):
        span = pl.ds(pl.multiple_of(q * block, block), block)
        weight = diag[:, span].astype(jnp.float32)
        weight = jnp.where(pattern[mine, q] != 0, weight, jnp.zeros_like(weight))
        found = []
        for root in range(2):
            wave = waves[root, :, span].astype(jnp.float32)
            found.append(sums[root] + fold(weight * wave * wave))
        return tuple(found)

    near, far = lax.fori_loop(0, sectors, column, (zero, zero), unroll=4)
    own_out[...] = near
    left_over = jnp.concatenate([far, zero], axis=0)
    parts = []
    for _ in range(3):
        piece = left_over.astype(jnp.bfloat16)
        parts.append(piece)
        left_over = left_over - piece.astype(jnp.float32)
    parts.append(jnp.zeros((block - 48, LANES), jnp.bfloat16))
    tail = jnp.concatenate(parts, axis=0)
    none = jnp.zeros_like(tail)
    mix_a[:, width:] = jnp.where(middle, none, tail)
    mix_b[:, width:] = jnp.where(middle, tail, none)
    for copy in copies[3:]:
        copy.wait()


def prepare(pattern, theta, hd, right, left, *cols):
    _, _, block, width = theta.shape
    table = right.shape[0]
    links = table * block // width
    kind = jnp.bfloat16
    mix = jax.ShapeDtypeStruct((block, width + LANES), kind)
    packed = jax.ShapeDtypeStruct((table // 2 + 2 * links + 1, block, block), kind)
    return pl.pallas_call(
        prepare_kernel,
        out_shape=(mix, mix, packed, jax.ShapeDtypeStruct((8, LANES), jnp.float32)),
        in_specs=[SMEM, ANY, ANY, ANY, ANY, VMEM, VMEM],
        out_specs=(VMEM,) * 4,
        scratch_shapes=[
            pltpu.VMEM((2, block, width), kind),
            pltpu.VMEM((block, width), kind),
            pltpu.VMEM((16, LANES), jnp.float32),
            pltpu.SemaphoreType.DMA((8,)),
        ],
        compiler_params=pltpu.CompilerParams(vmem_limit_bytes=PREPARE_LIMIT),
        name="prepare",
    )(pattern, theta, hd, right, left, *cols)


def total_of(rows):
    return jnp.sum(rows, axis=1, keepdims=True)


def update_kernel(psi, off, hd_own, hd_far, *refs):
    stats, (t_out, stats_out, diag, sems) = refs[:4], refs[4:]
    z, x, c = place()
    copies = [
        pltpu.make_async_copy(hd_own.at[x], diag.at[0], sems.at[0]),
        pltpu.make_async_copy(hd_far, diag.at[1], sems.at[1]),
    ]
    for copy in copies:
        copy.start()
    whole = sum(ref[at, 0:2, :] for ref in stats for at in range(2))
    norm_sq, energy_sum = total_of(whole[0:1, :]), total_of(whole[1:2, :])
    energy = energy_sum / (norm_sq + 1e-06)
    mine = total_of(stats[0][0, 0:1, :])
    for copy in copies:
        copy.wait()
    _, block, width = psi.shape
    step = 16
    zero = jnp.zeros((8, LANES), jnp.float32)

    def chunk(n, total):
        span = pl.ds(pl.multiple_of(n * step, step), step)
        for at in range(2):
            wave = psi[at, span, :].astype(jnp.float32)
            weight = diag[at, span, :].astype(jnp.float32)
            sigma = weight * wave + off[at, span, :].astype(jnp.float32)
            shifted = weight - energy
            t = (sigma - energy * wave) * shifted / (shifted * shifted + 1.0)
            t_out[at, span, :] = t
            total = total + fold(wave * t)
        return total

    lanes = jnp.sum(lax.fori_loop(0, block // step, chunk, zero), axis=0, keepdims=True)
    correlation = total_of(lanes)
    local = jnp.where(mine > 0.0, correlation / jnp.where(mine > 0.0, mine, 1.0), 0.0)

    def within(n, total):
        span = pl.ds(pl.multiple_of(n * step, step), step)
        for at in range(2):
            rest = t_out[at, span, :] - local * psi[at, span, :].astype(jnp.float32)
            total = total + fold(rest * rest)
        return total

    spread = jnp.sum(lax.fori_loop(0, block // step, within, zero), axis=0, keepdims=True)
    stats_out[...] = jnp.zeros_like(stats_out)
    stats_out[0:1, :] = jnp.broadcast_to(correlation, (1, LANES))
    stats_out[1:2, :] = jnp.broadcast_to(total_of(spread), (1, LANES))
    stats_out[2:3, :] = jnp.broadcast_to(mine, (1, LANES))
    stats_out[3:4, :] = jnp.broadcast_to(local, (1, LANES))
    stats_out[4:5, :] = jnp.broadcast_to(norm_sq, (1, LANES))


def correct_kernel(psi, t, *refs):
    stats, outs = refs[:4], refs[4:]
    stats = [ref.at[at] for ref in stats for at in range(2)]
    norm_sq = stats[0][4:5, 0:1]
    factor = sum(ref[0:1, 0:1] for ref in stats) / (norm_sq + 1e-06)
    length_sq = jnp.zeros((1, 1), jnp.float32)
    for ref in stats:
        gap = factor - ref[3:4, 0:1]
        length_sq = length_sq + (ref[1:2, 0:1] + gap * gap * ref[2:3, 0:1])
    scale = jnp.sqrt(norm_sq / (length_sq + 1e-06))
    _, block, width = psi.shape
    step = 16

    def chunk(n, carry):
        span = pl.ds(pl.multiple_of(n * step, step), step)
        for at in range(2):
            wave = psi[at, span, :].astype(jnp.float32)
            outs[at][span, :] = ((t[at, span, :] - factor * wave) * scale).astype(jnp.bfloat16)
        return carry

    lax.fori_loop(0, block // step, chunk, 0)


def assemble_kernel(places, based, *refs):
    count = len(places)
    pieces, (out, sems) = refs[:count], refs[count + based :]
    z, x, c = place()
    half = z // 2
    copies = []
    for at, (root, flip, start) in enumerate(places):
        size = pieces[at].shape[0]
        target = out.at[half ^ root, x ^ flip, pl.ds(start, size)]
        copies.append(pltpu.make_async_copy(pieces[at], target, sems.at[at]))
    for copy in copies:
        copy.start()
    for copy in copies:
        copy.wait()


def assemble(block, pieces, places, base=None):
    width = pieces[0].shape[1]
    based = [] if base is None else [base]
    return pl.pallas_call(
        functools.partial(assemble_kernel, places, len(based)),
        out_shape=jax.ShapeDtypeStruct((2, 2, block, width), pieces[0].dtype),
        in_specs=[VMEM] * len(pieces) + [ANY] * len(based),
        out_specs=ANY,
        scratch_shapes=[pltpu.SemaphoreType.DMA((len(pieces),))],
        input_output_aliases={len(pieces): 0} if based else {},
        compiler_params=pltpu.CompilerParams(vmem_limit_bytes=VMEM_LIMIT),
        name="assemble",
    )(*pieces, *based)


def after(value, *others):
    return lax.optimization_barrier((value, *others))[0]


def shards(theta, hdiag, pattern, left_blocks, left_cols, right_blocks, right_cols):
    roots, row_count, width = theta.shape
    sectors = pattern.shape[0]
    block = width // sectors
    z, x, c = place()
    half = z // 2
    mine = 4 * z + 2 * c + x

    halves = theta.reshape(roots, 2, block, width)
    diag = hdiag.reshape(2, block, width)
    middle = in_middle(z)
    right = right_blocks.reshape(-1, block, block)
    left = left_blocks.reshape(-1, block, block)
    cols = (right_cols.transpose(2, 0, 1), left_cols.transpose(2, 0, 1))

    mix_a, mix_b, packed, weight_own = prepare(pattern, halves, diag, right, left, *cols)
    mix_a = lax.ppermute(mix_a, "blk", [(0, 2), (2, 3), (3, 1), (1, 0)])
    mix_b = lax.ppermute(mix_b, "blk", [(0, 1), (1, 3), (3, 2), (2, 0)])
    operators = across(packed, "ops", 1)

    def masked(row, value):
        line = lax.dynamic_index_in_dim(pattern, row, 0, keepdims=False).astype(jnp.bfloat16)
        return value * jnp.repeat(line, block)[None, :]

    own = [
        masked(row_of(0, 2 + at, 0), lax.dynamic_slice(halves, (half, at, 0, 0), (1, 1, block, width))[0, 0])
        for at in range(2)
    ]
    own_core = [across(value, "sub", 1) for value in own]

    mix_a, mix_b = after((mix_a, mix_b), *own_core)
    far = masked(row_of(2, 0, 0), jnp.where(middle, mix_a[:, :width], mix_b[:, :width]))
    far_z = across(far, "blk", 1)
    far_x = across(far, "ops", 1)
    near_a = masked(row_of(1, 2, 0), jnp.where(middle, mix_b[:, :width], mix_a[:, :width]))
    far_core = across(far, "sub", 1)
    near_a_core = across(near_a, "sub", 1)

    operators = after(operators, mix_b)
    operators_core = across(operators, "sub", 1)
    turned = arrange(right, operators, operators_core)
    next_b, far_z = after((own[1], far_z), far_core, near_a_core, turned)
    near_b = across(next_b, "blk", 1)
    far_zx = across(far_z, "ops", 1)
    cols = (*cols, operators[-1, :16, :sectors].astype(jnp.int32))
    far_x_core = across(far_x, "sub", 1)
    far_z_core = across(far_z, "sub", 1)
    hd_far = lax.dynamic_index_in_dim(diag, x, 0, keepdims=False)
    hd_far = across(after(hd_far, far_z), "blk", 3)
    far_zx_core = across(far_zx, "sub", 1)
    near_b_core = across(near_b, "sub", 1)

    left = (left, operators)
    pieces = []
    plan = []
    for piece, offset in (
        (own[0], (0, 2, 0)),
        (own[1], (0, 3, 0)),
        (own_core[0], (0, 2, 1)),
        (own_core[1], (0, 3, 1)),
        (near_a, (1, 2, 0)),
        (near_b, (1, 3, 0)),
        (near_a_core, (1, 2, 1)),
        (near_b_core, (1, 3, 1)),
        (far, (2, 0, 0)),
        (far_core, (2, 0, 1)),
        (far_x, (2, 1, 0)),
        (far_x_core, (2, 1, 1)),
        (far_z, (3, 0, 0)),
        (far_z_core, (3, 0, 1)),
        (far_zx, (3, 1, 0)),
        (far_zx_core, (3, 1, 1)),
    ):
        pieces.append(piece[None])
        plan.append((offset + (0, block),))
    psi, off_one, stats_one = operate(
        True, tuple(plan), pieces, cols, pattern, turned, left, (mix_a, mix_b, weight_own)
    )

    found = share(stats_one)
    t, stats_two = pl.pallas_call(
        update_kernel,
        out_shape=(
            jax.ShapeDtypeStruct((2, block, width), jnp.float32),
            jax.ShapeDtypeStruct((8, LANES), jnp.float32),
        ),
        in_specs=[VMEM, VMEM, ANY, ANY] + [VMEM] * 4,
        out_specs=(VMEM, VMEM),
        scratch_shapes=[
            pltpu.VMEM((2, block, width), jnp.bfloat16),
            pltpu.SemaphoreType.DMA((2,)),
        ],
        compiler_params=pltpu.CompilerParams(vmem_limit_bytes=VMEM_LIMIT),
        name="update",
    )(psi, off_one, diag, hd_far, *found)
    found = share(stats_two)
    one = jax.ShapeDtypeStruct((block, width), jnp.bfloat16)
    changed_near, changed_far = pl.pallas_call(
        correct_kernel,
        out_shape=(one, one),
        in_specs=[VMEM, VMEM] + [VMEM] * 4,
        out_specs=(VMEM, VMEM),
        compiler_params=pltpu.CompilerParams(vmem_limit_bytes=VMEM_LIMIT),
        name="correct",
    )(psi, t, *found)

    near_z = across(changed_near, "blk", 1)
    far_x = across(changed_far, "ops", 1)
    near_core = across(changed_near, "sub", 1)
    far_core = across(changed_far, "sub", 1)
    other_middle = lax.ppermute(changed_far, "blk", [(1, 2), (2, 1)])
    near_z, far_x = after((near_z, far_x), other_middle)
    near_zx = across(near_z, "ops", 1)
    far_xz = across(far_x, "blk", 1)
    near_x = across(after(changed_near, near_z, far_x), "ops", 1)
    far_z = across(after(changed_far, near_z, far_x), "blk", 1)
    near_z_core = across(near_z, "sub", 1)
    far_x_core = across(far_x, "sub", 1)
    near_x_core = across(near_x, "sub", 1)
    far_z_core = across(far_z, "sub", 1)
    near_zx_core = across(near_zx, "sub", 1)
    far_xz_core = across(far_xz, "sub", 1)
    other_end = lax.ppermute(after(changed_far, near_z, far_x), "blk", [(0, 3), (3, 0)])
    pieces, plan = [], []
    for piece, offset in (
        (changed_near, (0, 0, 0)),
        (changed_far, (3, 0, 0)),
        (near_core, (0, 0, 1)),
        (far_core, (3, 0, 1)),
        (near_z, (1, 0, 0)),
        (far_z, (2, 0, 0)),
        (near_z_core, (1, 0, 1)),
        (far_z_core, (2, 0, 1)),
        (near_x, (0, 1, 0)),
        (far_x, (3, 1, 0)),
        (near_x_core, (0, 1, 1)),
        (far_x_core, (3, 1, 1)),
        (near_zx, (1, 1, 0)),
        (far_xz, (2, 1, 0)),
        (near_zx_core, (1, 1, 1)),
        (far_xz_core, (2, 1, 1)),
    ):
        pieces.append(piece[None])
        plan.append((offset + (0, block),))
    two_near, two_far, two_late, stats_three = operate(
        False, tuple(plan), pieces, cols, pattern, turned, left, (diag, hd_far, psi, off_one, stats_one)
    )

    far_in = across(two_far, "blk", 3)
    near_in = across(two_near, "ops", 1)
    late_in = across(after(two_late, far_in), "blk", 3)
    far_in_x = across(after(far_in, near_in), "ops", 1)
    sums = stats_three + across(stats_three, "sub", 1)
    other = jnp.where(middle, other_middle, after(other_end, two_near))
    other_x = across(other, "ops", 1)
    sums = after(sums, far_in)
    both = jnp.stack([sums + across(sums, "blk", 1), across(sums, "blk", 2) + across(sums, "blk", 3)])
    both = after(both, late_in)
    both = both + across(both, "ops", 1)
    other, other_x = after((other, other_x), late_in)
    late_in_x = across(late_in, "ops", 1)
    both = jnp.sum(jnp.where(half == 0, both, both[::-1])[:, :5], axis=2)
    scale = both[:, 3:4] + 1e-06
    subspace = jnp.concatenate([both[:, 4:5], both[:, 0:3]], axis=1) / scale
    places = ((0, 0, 0), (0, 1, 0), (1, 0, 0), (1, 1, 0))
    correction = assemble(block, (changed_near, near_x, other, other_x), places)
    places = ((0, 0, 0), (0, 1, 0), (1, 0, 0), (1, 0, block // 2), (1, 1, 0))
    sigma_two = assemble(block, (two_near, near_in, far_in, late_in, far_in_x), places)
    sigma_two = assemble(block, (late_in_x,), ((1, 1, block // 2),), sigma_two)
    return correction.reshape(theta.shape), sigma_two.reshape(theta.shape), subspace


def solution(mesh):
    in_specs = (
        P("groups", ("blk", "sub"), None),
        P(("groups", "blk", "sub"), None),
        P("groups", None),
        P(("groups", "ops"), None, None, None, None),
        P(("groups", "ops"), None, None),
        P(("groups", "ops"), None, None, None, None),
        P(("groups", "ops"), None, None),
    )
    out_specs = (
        P("groups", ("blk", "sub"), None),
        P("groups", ("blk", "sub"), None),
        P("groups", None),
    )
    body = shards if halves_fit(mesh) else general_shards
    return jax.shard_map(body, mesh=mesh, in_specs=in_specs, out_specs=out_specs, check_vma=False)
```

```python
import functools

import jax
import jax.numpy as jnp
from jax import lax
from jax.experimental import pallas as pl
from jax.experimental.pallas import tpu as pltpu
from jax.sharding import PartitionSpec as P

ANY = pl.BlockSpec(memory_space=pl.ANY)
SMEM = pl.BlockSpec(memory_space=pltpu.SMEM)
VMEM = pl.BlockSpec(memory_space=pltpu.VMEM)
VMEM_LIMIT = 24 * 1024 * 1024
OPERATE_LIMIT = 44 * 1024 * 1024
PREPARE_LIMIT = 56 * 1024 * 1024
LANES = 128


def apply_right(field_in, blocks, columns):
    roots_here, row_count, full_width = field_in.shape
    term_count, sectors, link_count = columns.shape
    block_size = full_width // sectors
    grouped = field_in.reshape(roots_here, row_count, sectors, block_size)
    picked = jnp.take(grouped, columns.reshape(-1), axis=2)
    picked = picked.reshape(roots_here, row_count, term_count, sectors, link_count, block_size)
    product = jnp.einsum("nrkbjq,kbjpq->knrbp", picked, blocks, preferred_element_type=jnp.float32)
    return product.reshape(term_count, roots_here, row_count, full_width).astype(jnp.bfloat16)


def take_rows(stacked, indices):
    return jnp.take(stacked, indices, axis=1)


def apply_left(arrived, blocks, columns):
    term_count, roots_here, full_width, col_count = arrived.shape
    sectors = columns.shape[1]
    link_count = columns.shape[2]
    block_size = full_width // sectors
    grouped = arrived.reshape(term_count, roots_here, sectors, block_size, col_count)
    picked = jax.vmap(take_rows)(grouped, columns.reshape(term_count, sectors * link_count))
    picked = picked.reshape(term_count, roots_here, sectors, link_count, block_size, col_count)
    product = jnp.einsum("kajpq,knajqc->napc", blocks, picked, preferred_element_type=jnp.float32)
    return product.reshape(roots_here, full_width, col_count)


def general_shards(theta, hdiag, pattern, left_blocks, left_cols, right_blocks, right_cols):
    roots_here, row_count, full_width = theta.shape
    sectors = pattern.shape[0]
    block_size = full_width // sectors
    first_row = lax.axis_index(("blk", "sub")) * row_count
    block_row = (first_row + jnp.arange(row_count, dtype=jnp.int32)) // block_size
    onehot = (block_row[:, None] == jnp.arange(sectors, dtype=jnp.int32)[None, :]).astype(
        jnp.float32
    )
    row_pattern = jnp.dot(onehot, pattern.astype(jnp.float32), preferred_element_type=jnp.float32)
    allowed = jnp.broadcast_to(row_pattern[:, :, None], (row_count, sectors, block_size))
    allowed = allowed.reshape(row_count, full_width).astype(jnp.bfloat16)
    diagonal = hdiag.astype(jnp.float32)
    peers = lax.axis_size("blk") * lax.axis_size("sub")

    def left_part(arrived):
        return apply_left(arrived, left_blocks, left_cols)

    def operate(field_in):
        images = apply_right(field_in, right_blocks, right_cols)
        partial_sum = left_part(
            lax.all_to_all(images, ("blk", "sub"), split_axis=3, concat_axis=2, tiled=True)
        )
        shares = lax.psum_scatter(partial_sum, "ops", scatter_dimension=2, tiled=True)
        returned = lax.all_to_all(
            shares.astype(jnp.bfloat16), ("blk", "sub"), split_axis=1, concat_axis=2, tiled=True
        )
        gathered = lax.all_gather(returned, "ops", axis=2, tiled=True)
        narrow = returned.shape[2] // peers
        gathered = gathered.reshape(roots_here, row_count, lax.axis_size("ops"), peers, narrow)
        offdiag = gathered.transpose(0, 1, 3, 2, 4).reshape(roots_here, row_count, full_width)
        offdiag = offdiag * allowed[None]
        return diagonal[None] * field_in.astype(jnp.float32) + offdiag.astype(jnp.float32)

    projected = theta * allowed[None]
    wave = projected.astype(jnp.float32)
    sigma_one = operate(projected)
    norm_sq, energy_sum = lax.psum(
        (jnp.sum(wave * wave, axis=(1, 2)), jnp.sum(wave * sigma_one, axis=(1, 2))), ("blk", "sub")
    )
    denominator = norm_sq + 1e-06
    energy = energy_sum / denominator
    shifted = diagonal[None] - energy[:, None, None]
    update = (sigma_one - energy[:, None, None] * wave) * shifted / (shifted * shifted + 1.0)
    correlation = lax.psum(jnp.sum(wave * update, axis=(1, 2)), ("blk", "sub"))
    factor = correlation / denominator
    orthogonal = update - factor[:, None, None] * wave
    length_sq = lax.psum(jnp.sum(orthogonal * orthogonal, axis=(1, 2)), ("blk", "sub"))
    correction = (orthogonal * jnp.sqrt(norm_sq / (length_sq + 1e-06))[:, None, None]).astype(
        jnp.bfloat16
    )
    sigma_two = operate(correction).astype(jnp.bfloat16)
    second = sigma_two.astype(jnp.float32)
    fixed = correction.astype(jnp.float32)
    cross_one, cross_two, cross_three = lax.psum(
        (
            jnp.sum(wave * second, axis=(1, 2)),
            jnp.sum(fixed * sigma_one, axis=(1, 2)),
            jnp.sum(fixed * second, axis=(1, 2)),
        ),
        ("blk", "sub"),
    )
    subspace = (
        jnp.stack([energy_sum, cross_one, cross_two, cross_three], axis=1) / denominator[:, None]
    )
    return (correction, sigma_two, subspace)


def halves_fit(mesh):
    sizes = dict(mesh.shape)
    return sizes["blk"] == 4 and sizes["ops"] == 2 and sizes["sub"] == 2


def across(value, axis, distance):
    size = lax.axis_size(axis)
    return lax.ppermute(value, axis, [(i, i ^ distance) for i in range(size)])


def share(stats):
    axes = ("blk", "ops")
    count = lax.axis_size("blk") * lax.axis_size("ops")
    pair = jnp.stack([stats, across(stats, "sub", 1)])
    found = [pair]
    for distance in (1, 2, 3):
        found.append(lax.ppermute(pair, axes, [(i, i ^ distance) for i in range(count)]))
    return found


def place():
    return lax.axis_index("blk"), lax.axis_index("ops"), lax.axis_index("sub")


def fold(value):
    rows, width = value.shape
    value = jnp.sum(value.reshape(rows // 8, 8, width), axis=0)
    return sum(value[:, at : at + LANES] for at in range(0, width, LANES))


def in_middle(z):
    return jnp.logical_or(z == 1, z == 2)


def row_of(dz, dx, dc):
    z, x, c = place()
    return 4 * (z ^ dz) + 2 * (c ^ dc) + (x ^ dx if dx < 2 else dx - 2)


def operate_kernel(first, plan, right_cols, left_cols, cols_other, pattern, right, left_own, left_other, *refs):
    count = len(plan)
    pieces, refs = refs[:count], refs[count:]
    if first:
        mix_a, mix_b, weight_own, psi_out, off_out, stats_out = refs[:6]
        refs = refs[6:]
    else:
        hd_own, hd_far, psi_in, off_in, stats_in, near_out, far_out, late_out, stats_out = refs[:9]
        refs = refs[9:]
    field, images, left, diag, parts, sems = refs
    z, x, c = place()
    sectors, block, width = field.shape
    table = right.shape[1]
    links = table // sectors
    mine = 4 * z + 2 * c + x
    rows = (mine, mine ^ 12)

    copies = []

    def begin(source, target):
        copy = pltpu.make_async_copy(source, target, sems.at[len(copies)])
        copy.start()
        copies.append(copy)

    for at in range(2):
        begin(left_own.at[pl.ds(rows[at] * links, links)], left.at[0, pl.ds(at * links, links)])
    begin(left_other.at[pl.ds(table // 2, 2 * links)], left.at[1])
    if first:
        for at, mix in enumerate((mix_a, mix_b)):
            begin(mix.at[pl.ds(0, parts.shape[1]), pl.ds(width, LANES)], parts.at[at])
    else:
        begin(hd_own.at[x], diag.at[0])
        begin(hd_far, diag.at[1])

    def allowed(a, q, value):
        return lax.select(pattern[a, q] != 0, value, jnp.zeros_like(value))

    later = len(copies)
    for piece, offsets in zip(pieces, plan):
        for at, (dz, dx, dc, start, tall) in enumerate(offsets):
            row = row_of(dz, dx, dc)
            if first:
                begin(piece.at[at], field.at[row, pl.ds(start, tall)])
                continue
            for line in range(0, tall, 16):
                field[row, start + line : start + line + 16, :] = piece[at, line : line + 16, :]
    for copy in copies[later:]:
        copy.wait()

    def right_col(term, b, j):
        return cols_other[j, b] if term else right_cols[j, 0, b]

    def left_col(term, a, j):
        return cols_other[8 + j, a] if term else left_cols[j, 0, a]

    sources = [[left_col(term, rows[at], j) for at in range(2) for j in range(links)] for term in range(2)]

    deep = links * block

    none = jnp.zeros((block, block), jnp.bfloat16)
    pair = 2

    def image(n, carry):
        picks = [(i, j) for i in range(pair) for j in range(links)]
        for term in range(2):
            found = [right_col(term, n * pair + i, j) for i, j in picks]
            lhs = []
            for source in sources[term]:
                line = []
                for col in found:
                    value = field[source, :, pl.ds(pl.multiple_of(col * block, block), block)]
                    line.append(value)
                lhs.append(jnp.concatenate(line, axis=1))
            rhs = []
            for i, j in picks:
                tile = right[term, (n * pair + i) * links + j]
                rhs.append(jnp.concatenate([tile if i == at else none for at in range(pair)], axis=1))
            product = jnp.dot(
                jnp.concatenate(lhs, axis=0),
                jnp.concatenate(rhs, axis=0),
                preferred_element_type=jnp.float32,
            )
            product = product.astype(jnp.bfloat16)
            span = pl.ds(pl.multiple_of(n * pair * block, pair * block), pair * block)
            for at in range(2):
                images[at, term * deep : (term + 1) * deep, span] = product[at * deep : (at + 1) * deep]
        return carry

    lax.fori_loop(0, sectors // pair, image, 0, unroll=2)
    for copy in copies[:later]:
        copy.wait()

    step = 2
    early_rows = block // 2
    zero = jnp.zeros((8, LANES), jnp.float32)

    def column(n, sums):
        start = pl.multiple_of(n * step * block, step * block)
        span = pl.ds(start, step * block)
        sums = list(sums)

        def masked(a, value):
            parts = [
                allowed(a, n * step + i, value[:, i * block : (i + 1) * block]) for i in range(step)
            ]
            return jnp.concatenate(parts, axis=1)

        for at in range(2):
            weights = [left[term, at * links + j] for term in range(2) for j in range(links)]
            total = jnp.dot(
                jnp.concatenate(weights, axis=1),
                images[at, :, span],
                preferred_element_type=jnp.float32,
            )
            offdiag = masked(rows[at], total.astype(jnp.bfloat16).astype(jnp.float32))
            own = field[rows[at], :, span].astype(jnp.float32)
            if first:
                psi_out[at, :, span] = own.astype(jnp.bfloat16)
                off_out[at, :, span] = offdiag.astype(jnp.bfloat16)
                sums[0] += fold(own * own)
                sums[1] += fold(own * offdiag)
            else:
                weight = diag[at, :, span].astype(jnp.float32)
                narrow = (weight * own + offdiag).astype(jnp.bfloat16)
                if at == 0:
                    near_out[:, span] = narrow
                else:
                    far_out[:, span] = narrow[:early_rows]
                    late_out[:, span] = narrow[early_rows:]
                second = narrow.astype(jnp.float32)
                wave = psi_in[at, :, span].astype(jnp.float32)
                sigma_one = weight * wave + off_in[at, :, span].astype(jnp.float32)
                sums[0] += fold(wave * second)
                sums[1] += fold(own * sigma_one)
                sums[2] += fold(own * second)
        return tuple(sums)

    sums = list(lax.fori_loop(0, sectors // step, column, (zero,) * (2 if first else 3)))
    if first:
        far_weight = (parts[0] + parts[1]).astype(jnp.float32)
        sums[1] += weight_own[...] + (far_weight[0:8] + far_weight[16:24] + far_weight[32:40])
    stats_out[...] = jnp.zeros_like(stats_out)
    for at, value in enumerate(sums):
        stats_out[at : at + 1, :] = jnp.sum(value, axis=0, keepdims=True)
    if not first:
        stats_out[3:5, :] = stats_in[0:2, :]


def operate(first, plan, pieces, cols, pattern, right, left, extra):
    _, table, block, _ = right.shape
    width = pieces[0].shape[2]
    sectors = width // block
    links = table // sectors
    rows = jax.ShapeDtypeStruct((2, block, width), jnp.bfloat16)
    one = jax.ShapeDtypeStruct((block, width), jnp.bfloat16)
    some = jax.ShapeDtypeStruct((block // 2, width), jnp.bfloat16)
    stats = jax.ShapeDtypeStruct((8, LANES), jnp.float32)
    out_shape = (rows, rows, stats) if first else (one, some, some, stats)
    extra_specs = [ANY, ANY, VMEM] if first else [ANY, ANY, VMEM, VMEM, VMEM]
    inner = 2 * 2 * sectors * 2 * links * links * block * block * block
    outer = 2 * 2 * 2 * links * block * block * width
    return pl.pallas_call(
        functools.partial(operate_kernel, first, plan),
        out_shape=out_shape,
        in_specs=[SMEM, SMEM, SMEM, SMEM, VMEM, ANY, ANY] + [ANY if first else VMEM] * len(pieces) + extra_specs,
        out_specs=(VMEM,) * len(out_shape),
        scratch_shapes=[
            pltpu.VMEM((sectors, block, width), jnp.bfloat16),
            pltpu.VMEM((2, 2 * links * block, width), jnp.bfloat16),
            pltpu.VMEM((2, 2 * links, block, block), jnp.bfloat16),
            pltpu.VMEM((2, block, width), jnp.bfloat16),
            pltpu.VMEM((2, 48, LANES), jnp.bfloat16),
            pltpu.SemaphoreType.DMA((5 + len(plan),)),
        ],
        compiler_params=pltpu.CompilerParams(vmem_limit_bytes=PREPARE_LIMIT if first else OPERATE_LIMIT),
        cost_estimate=pl.CostEstimate(
            flops=inner + outer if first else 0,
            bytes_accessed=16 * 1024 * 1024 if first else 1024,
            transcendentals=0,
        ),
        name="operate_first" if first else "operate_second",
    )(*cols, pattern, right, *left, *pieces, *extra)


def arrange_kernel(own, near, far, out, found, sems):
    _, _, c = place()
    part = own.shape[0] // 2
    copies = [
        pltpu.make_async_copy(own, found.at[0], sems.at[0]),
        pltpu.make_async_copy(near.at[pl.ds(0, part)], found.at[1, pl.ds(c * part, part)], sems.at[1]),
        pltpu.make_async_copy(far.at[pl.ds(0, part)], found.at[1, pl.ds((1 - c) * part, part)], sems.at[2]),
    ]
    for copy in copies:
        copy.start()
    for copy in copies:
        copy.wait()

    def turn(at, carry):
        for term in range(2):
            out[term, at] = found[term, at].T
        return carry

    lax.fori_loop(0, found.shape[1], turn, 0, unroll=4)


def arrange(own, near, far):
    shape = (2, *own.shape)
    return pl.pallas_call(
        arrange_kernel,
        out_shape=jax.ShapeDtypeStruct(shape, own.dtype),
        in_specs=[ANY] * 3,
        out_specs=VMEM,
        scratch_shapes=[pltpu.VMEM(shape, own.dtype), pltpu.SemaphoreType.DMA((3,))],
        compiler_params=pltpu.CompilerParams(vmem_limit_bytes=VMEM_LIMIT),
        name="arrange",
    )(own, near, far)


def prepare_kernel(
    pattern, theta, hd, right, left, right_cols, left_cols, mix_a, mix_b, packed, own_out, waves, diag, spots, sems
):
    z, x, c = place()
    half = z // 2
    middle = in_middle(z)
    mine = 4 * z + 2 * c + x
    block, width = diag.shape
    sectors = width // block
    links = right.shape[0] // sectors
    part = right.shape[0] // 2
    root_a = jnp.where(middle, half, 1 - half)
    rows = pl.ds(0, width)
    sources = (
        (theta.at[half, x], waves.at[0]),
        (theta.at[1 - half, x], waves.at[1]),
        (hd.at[x], diag),
        (theta.at[root_a, jnp.where(middle, 0, x)], mix_a.at[:, rows]),
        (theta.at[1 - root_a, jnp.where(middle, x, 0)], mix_b.at[:, rows]),
        (right.at[pl.ds(c * part, part)], packed.at[pl.ds(0, part)]),
        (left.at[pl.ds((mine ^ 1) * links, links)], packed.at[pl.ds(part, links)]),
        (left.at[pl.ds((mine ^ 13) * links, links)], packed.at[pl.ds(part + links, links)]),
    )
    copies = [
        pltpu.make_async_copy(source, target, sems.at[at])
        for at, (source, target) in enumerate(sources)
    ]
    for copy in copies:
        copy.start()
    last = part + 2 * links
    spots[...] = jnp.zeros_like(spots)
    spots[0:links, 0:sectors] = right_cols[:, 0, :].astype(jnp.float32)
    spots[8 : 8 + links, 0:sectors] = left_cols[:, 0, :].astype(jnp.float32)
    packed[last] = jnp.zeros_like(packed[last])
    packed[last, 0:16, :] = spots[...].astype(jnp.bfloat16)
    for copy in copies[:3]:
        copy.wait()
    zero = jnp.zeros((8, LANES), jnp.float32)

    def column(q, sums):
        span = pl.ds(pl.multiple_of(q * block, block), block)
        weight = diag[:, span].astype(jnp.float32)
        weight = jnp.where(pattern[mine, q] != 0, weight, jnp.zeros_like(weight))
        found = []
        for root in range(2):
            wave = waves[root, :, span].astype(jnp.float32)
            found.append(sums[root] + fold(weight * wave * wave))
        return tuple(found)

    near, far = lax.fori_loop(0, sectors, column, (zero, zero), unroll=4)
    own_out[...] = near
    left_over = jnp.concatenate([far, zero], axis=0)
    parts = []
    for _ in range(3):
        piece = left_over.astype(jnp.bfloat16)
        parts.append(piece)
        left_over = left_over - piece.astype(jnp.float32)
    parts.append(jnp.zeros((block - 48, LANES), jnp.bfloat16))
    tail = jnp.concatenate(parts, axis=0)
    none = jnp.zeros_like(tail)
    mix_a[:, width:] = jnp.where(middle, none, tail)
    mix_b[:, width:] = jnp.where(middle, tail, none)
    for copy in copies[3:]:
        copy.wait()


def prepare(pattern, theta, hd, right, left, *cols):
    _, _, block, width = theta.shape
    table = right.shape[0]
    links = table * block // width
    kind = jnp.bfloat16
    mix = jax.ShapeDtypeStruct((block, width + LANES), kind)
    packed = jax.ShapeDtypeStruct((table // 2 + 2 * links + 1, block, block), kind)
    return pl.pallas_call(
        prepare_kernel,
        out_shape=(mix, mix, packed, jax.ShapeDtypeStruct((8, LANES), jnp.float32)),
        in_specs=[SMEM, ANY, ANY, ANY, ANY, VMEM, VMEM],
        out_specs=(VMEM,) * 4,
        scratch_shapes=[
            pltpu.VMEM((2, block, width), kind),
            pltpu.VMEM((block, width), kind),
            pltpu.VMEM((16, LANES), jnp.float32),
            pltpu.SemaphoreType.DMA((8,)),
        ],
        compiler_params=pltpu.CompilerParams(vmem_limit_bytes=PREPARE_LIMIT),
        name="prepare",
    )(pattern, theta, hd, right, left, *cols)


def total_of(rows):
    return jnp.sum(rows, axis=1, keepdims=True)


def update_kernel(psi, off, hd_own, hd_far, *refs):
    stats, (t_out, stats_out, diag, sems) = refs[:4], refs[4:]
    z, x, c = place()
    copies = [
        pltpu.make_async_copy(hd_own.at[x], diag.at[0], sems.at[0]),
        pltpu.make_async_copy(hd_far, diag.at[1], sems.at[1]),
    ]
    for copy in copies:
        copy.start()
    whole = sum(ref[at, 0:2, :] for ref in stats for at in range(2))
    norm_sq, energy_sum = total_of(whole[0:1, :]), total_of(whole[1:2, :])
    energy = energy_sum / (norm_sq + 1e-06)
    mine = total_of(stats[0][0, 0:1, :])
    for copy in copies:
        copy.wait()
    _, block, width = psi.shape
    step = 16
    zero = jnp.zeros((8, LANES), jnp.float32)

    def chunk(n, total):
        span = pl.ds(pl.multiple_of(n * step, step), step)
        for at in range(2):
            wave = psi[at, span, :].astype(jnp.float32)
            weight = diag[at, span, :].astype(jnp.float32)
            sigma = weight * wave + off[at, span, :].astype(jnp.float32)
            shifted = weight - energy
            t = (sigma - energy * wave) * shifted / (shifted * shifted + 1.0)
            t_out[at, span, :] = t
            total = total + fold(wave * t)
        return total

    lanes = jnp.sum(lax.fori_loop(0, block // step, chunk, zero), axis=0, keepdims=True)
    correlation = total_of(lanes)
    local = jnp.where(mine > 0.0, correlation / jnp.where(mine > 0.0, mine, 1.0), 0.0)

    def within(n, total):
        span = pl.ds(pl.multiple_of(n * step, step), step)
        for at in range(2):
            rest = t_out[at, span, :] - local * psi[at, span, :].astype(jnp.float32)
            total = total + fold(rest * rest)
        return total

    spread = jnp.sum(lax.fori_loop(0, block // step, within, zero), axis=0, keepdims=True)
    stats_out[...] = jnp.zeros_like(stats_out)
    stats_out[0:1, :] = jnp.broadcast_to(correlation, (1, LANES))
    stats_out[1:2, :] = jnp.broadcast_to(total_of(spread), (1, LANES))
    stats_out[2:3, :] = jnp.broadcast_to(mine, (1, LANES))
    stats_out[3:4, :] = jnp.broadcast_to(local, (1, LANES))
    stats_out[4:5, :] = jnp.broadcast_to(norm_sq, (1, LANES))


def correct_kernel(psi, t, *refs):
    stats, outs = refs[:4], refs[4:]
    stats = [ref.at[at] for ref in stats for at in range(2)]
    norm_sq = stats[0][4:5, 0:1]
    factor = sum(ref[0:1, 0:1] for ref in stats) / (norm_sq + 1e-06)
    length_sq = jnp.zeros((1, 1), jnp.float32)
    for ref in stats:
        gap = factor - ref[3:4, 0:1]
        length_sq = length_sq + (ref[1:2, 0:1] + gap * gap * ref[2:3, 0:1])
    scale = jnp.sqrt(norm_sq / (length_sq + 1e-06))
    _, block, width = psi.shape
    step = 16

    def chunk(n, carry):
        span = pl.ds(pl.multiple_of(n * step, step), step)
        for at in range(2):
            wave = psi[at, span, :].astype(jnp.float32)
            outs[at][span, :] = ((t[at, span, :] - factor * wave) * scale).astype(jnp.bfloat16)
        return carry

    lax.fori_loop(0, block // step, chunk, 0)


def assemble_kernel(places, based, *refs):
    count = len(places)
    pieces, (out, sems) = refs[:count], refs[count + based :]
    z, x, c = place()
    half = z // 2
    copies = []
    for at, (root, flip, start) in enumerate(places):
        size = pieces[at].shape[0]
        target = out.at[half ^ root, x ^ flip, pl.ds(start, size)]
        copies.append(pltpu.make_async_copy(pieces[at], target, sems.at[at]))
    for copy in copies:
        copy.start()
    for copy in copies:
        copy.wait()


def assemble(block, pieces, places, base=None):
    width = pieces[0].shape[1]
    based = [] if base is None else [base]
    return pl.pallas_call(
        functools.partial(assemble_kernel, places, len(based)),
        out_shape=jax.ShapeDtypeStruct((2, 2, block, width), pieces[0].dtype),
        in_specs=[VMEM] * len(pieces) + [ANY] * len(based),
        out_specs=ANY,
        scratch_shapes=[pltpu.SemaphoreType.DMA((len(pieces),))],
        input_output_aliases={len(pieces): 0} if based else {},
        compiler_params=pltpu.CompilerParams(vmem_limit_bytes=VMEM_LIMIT),
        name="assemble",
    )(*pieces, *based)


def after(value, *others):
    return lax.optimization_barrier((value, *others))[0]


def shards(theta, hdiag, pattern, left_blocks, left_cols, right_blocks, right_cols):
    roots, row_count, width = theta.shape
    sectors = pattern.shape[0]
    block = width // sectors
    z, x, c = place()
    half = z // 2
    mine = 4 * z + 2 * c + x

    halves = theta.reshape(roots, 2, block, width)
    diag = hdiag.reshape(2, block, width)
    middle = in_middle(z)
    right = right_blocks.reshape(-1, block, block)
    left = left_blocks.reshape(-1, block, block)
    cols = (right_cols.transpose(2, 0, 1), left_cols.transpose(2, 0, 1))

    mix_a, mix_b, packed, weight_own = prepare(pattern, halves, diag, right, left, *cols)
    mix_a = lax.ppermute(mix_a, "blk", [(0, 2), (2, 3), (3, 1), (1, 0)])
    mix_b = lax.ppermute(mix_b, "blk", [(0, 1), (1, 3), (3, 2), (2, 0)])
    operators = across(packed, "ops", 1)

    def masked(row, value):
        line = lax.dynamic_index_in_dim(pattern, row, 0, keepdims=False).astype(jnp.bfloat16)
        return value * jnp.repeat(line, block)[None, :]

    own = [
        masked(row_of(0, 2 + at, 0), lax.dynamic_slice(halves, (half, at, 0, 0), (1, 1, block, width))[0, 0])
        for at in range(2)
    ]
    own = list(lax.optimization_barrier(tuple(own)))
    own_core = [across(value, "sub", 1) for value in own]

    mix_a, mix_b = after((mix_a, mix_b), *own_core)
    far = masked(row_of(2, 0, 0), jnp.where(middle, mix_a[:, :width], mix_b[:, :width]))
    far_z = across(far, "blk", 1)
    far_x = across(far, "ops", 1)
    near_a = masked(row_of(1, 2, 0), jnp.where(middle, mix_b[:, :width], mix_a[:, :width]))
    far_core = across(far, "sub", 1)
    near_a_core = across(near_a, "sub", 1)

    operators = after(operators, mix_b)
    operators_core = across(operators, "sub", 1)
    turned = arrange(right, operators, operators_core)
    cols_other = operators[-1, :16, :sectors].astype(jnp.int32)
    cols = (*cols, cols_other)
    next_b, far_z = after((own[1], far_z), far_core, near_a_core, turned, cols_other)
    near_b = across(next_b, "blk", 1)
    far_zx = across(far_z, "ops", 1)
    far_x_core = across(far_x, "sub", 1)
    far_z_core = across(far_z, "sub", 1)
    hd_far = lax.dynamic_index_in_dim(diag, x, 0, keepdims=False)
    hd_far = across(after(hd_far, far_z), "blk", 3)
    far_zx_core = across(far_zx, "sub", 1)
    near_b_core = across(near_b, "sub", 1)

    left = (left, operators)
    pieces = []
    plan = []
    for piece, offset in (
        (own[0], (0, 2, 0)),
        (own[1], (0, 3, 0)),
        (own_core[0], (0, 2, 1)),
        (own_core[1], (0, 3, 1)),
        (near_a, (1, 2, 0)),
        (near_b, (1, 3, 0)),
        (near_a_core, (1, 2, 1)),
        (near_b_core, (1, 3, 1)),
        (far, (2, 0, 0)),
        (far_core, (2, 0, 1)),
        (far_x, (2, 1, 0)),
        (far_x_core, (2, 1, 1)),
        (far_z, (3, 0, 0)),
        (far_z_core, (3, 0, 1)),
        (far_zx, (3, 1, 0)),
        (far_zx_core, (3, 1, 1)),
    ):
        pieces.append(piece[None])
        plan.append((offset + (0, block),))
    psi, off_one, stats_one = operate(
        True, tuple(plan), pieces, cols, pattern, turned, left, (mix_a, mix_b, weight_own)
    )

    found = share(stats_one)
    t, stats_two = pl.pallas_call(
        update_kernel,
        out_shape=(
            jax.ShapeDtypeStruct((2, block, width), jnp.float32),
            jax.ShapeDtypeStruct((8, LANES), jnp.float32),
        ),
        in_specs=[VMEM, VMEM, ANY, ANY] + [VMEM] * 4,
        out_specs=(VMEM, VMEM),
        scratch_shapes=[
            pltpu.VMEM((2, block, width), jnp.bfloat16),
            pltpu.SemaphoreType.DMA((2,)),
        ],
        compiler_params=pltpu.CompilerParams(vmem_limit_bytes=VMEM_LIMIT),
        name="update",
    )(psi, off_one, diag, hd_far, *found)
    found = share(stats_two)
    one = jax.ShapeDtypeStruct((block, width), jnp.bfloat16)
    changed_near, changed_far = pl.pallas_call(
        correct_kernel,
        out_shape=(one, one),
        in_specs=[VMEM, VMEM] + [VMEM] * 4,
        out_specs=(VMEM, VMEM),
        compiler_params=pltpu.CompilerParams(vmem_limit_bytes=VMEM_LIMIT),
        name="correct",
    )(psi, t, *found)

    near_z = across(changed_near, "blk", 1)
    far_x = across(changed_far, "ops", 1)
    near_core = across(changed_near, "sub", 1)
    far_core = across(changed_far, "sub", 1)
    other_middle = lax.ppermute(changed_far, "blk", [(1, 2), (2, 1)])
    near_z, far_x = after((near_z, far_x), other_middle)
    near_zx = across(near_z, "ops", 1)
    far_xz = across(far_x, "blk", 1)
    near_x = across(after(changed_near, near_z, far_x), "ops", 1)
    far_z = across(after(changed_far, near_z, far_x), "blk", 1)
    near_z_core = across(near_z, "sub", 1)
    far_x_core = across(far_x, "sub", 1)
    near_x_core = across(near_x, "sub", 1)
    far_z_core = across(far_z, "sub", 1)
    near_zx_core = across(near_zx, "sub", 1)
    far_xz_core = across(far_xz, "sub", 1)
    other_end = lax.ppermute(after(changed_far, near_z, far_x), "blk", [(0, 3), (3, 0)])
    pieces, plan = [], []
    for piece, offset in (
        (changed_near, (0, 0, 0)),
        (changed_far, (3, 0, 0)),
        (near_core, (0, 0, 1)),
        (far_core, (3, 0, 1)),
        (near_z, (1, 0, 0)),
        (far_z, (2, 0, 0)),
        (near_z_core, (1, 0, 1)),
        (far_z_core, (2, 0, 1)),
        (near_x, (0, 1, 0)),
        (far_x, (3, 1, 0)),
        (near_x_core, (0, 1, 1)),
        (far_x_core, (3, 1, 1)),
        (near_zx, (1, 1, 0)),
        (far_xz, (2, 1, 0)),
        (near_zx_core, (1, 1, 1)),
        (far_xz_core, (2, 1, 1)),
    ):
        pieces.append(piece[None])
        plan.append((offset + (0, block),))
    two_near, two_far, two_late, stats_three = operate(
        False, tuple(plan), pieces, cols, pattern, turned, left, (diag, hd_far, psi, off_one, stats_one)
    )

    far_in = across(two_far, "blk", 3)
    near_in = across(two_near, "ops", 1)
    late_in = across(after(two_late, far_in), "blk", 3)
    far_in_x = across(after(far_in, near_in), "ops", 1)
    sums = stats_three + across(stats_three, "sub", 1)
    other = jnp.where(middle, other_middle, after(other_end, two_near))
    other_x = across(other, "ops", 1)
    sums = after(sums, far_in)
    both = jnp.stack([sums + across(sums, "blk", 1), across(sums, "blk", 2) + across(sums, "blk", 3)])
    both = after(both, late_in)
    both = both + across(both, "ops", 1)
    other, other_x = after((other, other_x), late_in)
    late_in_x = across(late_in, "ops", 1)
    both = jnp.sum(jnp.where(half == 0, both, both[::-1])[:, :5], axis=2)
    scale = both[:, 3:4] + 1e-06
    subspace = jnp.concatenate([both[:, 4:5], both[:, 0:3]], axis=1) / scale
    places = ((0, 0, 0), (0, 1, 0), (1, 0, 0), (1, 1, 0))
    correction = assemble(block, (changed_near, near_x, other, other_x), places)
    places = ((0, 0, 0), (0, 1, 0), (1, 0, 0), (1, 0, block // 2), (1, 1, 0))
    sigma_two = assemble(block, (two_near, near_in, far_in, late_in, far_in_x), places)
    sigma_two = assemble(block, (late_in_x,), ((1, 1, block // 2),), sigma_two)
    return correction.reshape(theta.shape), sigma_two.reshape(theta.shape), subspace


def solution(mesh):
    in_specs = (
        P("groups", ("blk", "sub"), None),
        P(("groups", "blk", "sub"), None),
        P("groups", None),
        P(("groups", "ops"), None, None, None, None),
        P(("groups", "ops"), None, None),
        P(("groups", "ops"), None, None, None, None),
        P(("groups", "ops"), None, None),
    )
    out_specs = (
        P("groups", ("blk", "sub"), None),
        P("groups", ("blk", "sub"), None),
        P("groups", None),
    )
    body = shards if halves_fit(mesh) else general_shards
    return jax.shard_map(body, mesh=mesh, in_specs=in_specs, out_specs=out_specs, check_vma=False)
```

```python
import functools

import jax
import jax.numpy as jnp
from jax import lax
from jax.experimental import pallas as pl
from jax.experimental.pallas import tpu as pltpu
from jax.sharding import PartitionSpec as P

ANY = pl.BlockSpec(memory_space=pl.ANY)
SMEM = pl.BlockSpec(memory_space=pltpu.SMEM)
VMEM = pl.BlockSpec(memory_space=pltpu.VMEM)
VMEM_LIMIT = 24 * 1024 * 1024
OPERATE_LIMIT = 44 * 1024 * 1024
PREPARE_LIMIT = 56 * 1024 * 1024
LANES = 128


def apply_right(field_in, blocks, columns):
    roots_here, row_count, full_width = field_in.shape
    term_count, sectors, link_count = columns.shape
    block_size = full_width // sectors
    grouped = field_in.reshape(roots_here, row_count, sectors, block_size)
    picked = jnp.take(grouped, columns.reshape(-1), axis=2)
    picked = picked.reshape(roots_here, row_count, term_count, sectors, link_count, block_size)
    product = jnp.einsum("nrkbjq,kbjpq->knrbp", picked, blocks, preferred_element_type=jnp.float32)
    return product.reshape(term_count, roots_here, row_count, full_width).astype(jnp.bfloat16)


def take_rows(stacked, indices):
    return jnp.take(stacked, indices, axis=1)


def apply_left(arrived, blocks, columns):
    term_count, roots_here, full_width, col_count = arrived.shape
    sectors = columns.shape[1]
    link_count = columns.shape[2]
    block_size = full_width // sectors
    grouped = arrived.reshape(term_count, roots_here, sectors, block_size, col_count)
    picked = jax.vmap(take_rows)(grouped, columns.reshape(term_count, sectors * link_count))
    picked = picked.reshape(term_count, roots_here, sectors, link_count, block_size, col_count)
    product = jnp.einsum("kajpq,knajqc->napc", blocks, picked, preferred_element_type=jnp.float32)
    return product.reshape(roots_here, full_width, col_count)


def general_shards(theta, hdiag, pattern, left_blocks, left_cols, right_blocks, right_cols):
    roots_here, row_count, full_width = theta.shape
    sectors = pattern.shape[0]
    block_size = full_width // sectors
    first_row = lax.axis_index(("blk", "sub")) * row_count
    block_row = (first_row + jnp.arange(row_count, dtype=jnp.int32)) // block_size
    onehot = (block_row[:, None] == jnp.arange(sectors, dtype=jnp.int32)[None, :]).astype(
        jnp.float32
    )
    row_pattern = jnp.dot(onehot, pattern.astype(jnp.float32), preferred_element_type=jnp.float32)
    allowed = jnp.broadcast_to(row_pattern[:, :, None], (row_count, sectors, block_size))
    allowed = allowed.reshape(row_count, full_width).astype(jnp.bfloat16)
    diagonal = hdiag.astype(jnp.float32)
    peers = lax.axis_size("blk") * lax.axis_size("sub")

    def left_part(arrived):
        return apply_left(arrived, left_blocks, left_cols)

    def operate(field_in):
        images = apply_right(field_in, right_blocks, right_cols)
        partial_sum = left_part(
            lax.all_to_all(images, ("blk", "sub"), split_axis=3, concat_axis=2, tiled=True)
        )
        shares = lax.psum_scatter(partial_sum, "ops", scatter_dimension=2, tiled=True)
        returned = lax.all_to_all(
            shares.astype(jnp.bfloat16), ("blk", "sub"), split_axis=1, concat_axis=2, tiled=True
        )
        gathered = lax.all_gather(returned, "ops", axis=2, tiled=True)
        narrow = returned.shape[2] // peers
        gathered = gathered.reshape(roots_here, row_count, lax.axis_size("ops"), peers, narrow)
        offdiag = gathered.transpose(0, 1, 3, 2, 4).reshape(roots_here, row_count, full_width)
        offdiag = offdiag * allowed[None]
        return diagonal[None] * field_in.astype(jnp.float32) + offdiag.astype(jnp.float32)

    projected = theta * allowed[None]
    wave = projected.astype(jnp.float32)
    sigma_one = operate(projected)
    norm_sq, energy_sum = lax.psum(
        (jnp.sum(wave * wave, axis=(1, 2)), jnp.sum(wave * sigma_one, axis=(1, 2))), ("blk", "sub")
    )
    denominator = norm_sq + 1e-06
    energy = energy_sum / denominator
    shifted = diagonal[None] - energy[:, None, None]
    update = (sigma_one - energy[:, None, None] * wave) * shifted / (shifted * shifted + 1.0)
    correlation = lax.psum(jnp.sum(wave * update, axis=(1, 2)), ("blk", "sub"))
    factor = correlation / denominator
    orthogonal = update - factor[:, None, None] * wave
    length_sq = lax.psum(jnp.sum(orthogonal * orthogonal, axis=(1, 2)), ("blk", "sub"))
    correction = (orthogonal * jnp.sqrt(norm_sq / (length_sq + 1e-06))[:, None, None]).astype(
        jnp.bfloat16
    )
    sigma_two = operate(correction).astype(jnp.bfloat16)
    second = sigma_two.astype(jnp.float32)
    fixed = correction.astype(jnp.float32)
    cross_one, cross_two, cross_three = lax.psum(
        (
            jnp.sum(wave * second, axis=(1, 2)),
            jnp.sum(fixed * sigma_one, axis=(1, 2)),
            jnp.sum(fixed * second, axis=(1, 2)),
        ),
        ("blk", "sub"),
    )
    subspace = (
        jnp.stack([energy_sum, cross_one, cross_two, cross_three], axis=1) / denominator[:, None]
    )
    return (correction, sigma_two, subspace)


def halves_fit(mesh):
    sizes = dict(mesh.shape)
    return sizes["blk"] == 4 and sizes["ops"] == 2 and sizes["sub"] == 2


def across(value, axis, distance):
    size = lax.axis_size(axis)
    return lax.ppermute(value, axis, [(i, i ^ distance) for i in range(size)])


def share(stats):
    axes = ("blk", "ops")
    count = lax.axis_size("blk") * lax.axis_size("ops")
    pair = jnp.stack([stats, across(stats, "sub", 1)])
    found = [pair]
    for distance in (1, 2, 3):
        found.append(lax.ppermute(pair, axes, [(i, i ^ distance) for i in range(count)]))
    return found


def place():
    return lax.axis_index("blk"), lax.axis_index("ops"), lax.axis_index("sub")


def fold(value):
    rows, width = value.shape
    value = jnp.sum(value.reshape(rows // 8, 8, width), axis=0)
    return sum(value[:, at : at + LANES] for at in range(0, width, LANES))


def in_middle(z):
    return jnp.logical_or(z == 1, z == 2)


def row_of(dz, dx, dc):
    z, x, c = place()
    return 4 * (z ^ dz) + 2 * (c ^ dc) + (x ^ dx if dx < 2 else dx - 2)


def operate_kernel(first, plan, right_cols, left_cols, cols_other, pattern, right, left_own, left_other, *refs):
    count = len(plan)
    pieces, refs = refs[:count], refs[count:]
    if first:
        mix_a, mix_b, weight_own, psi_out, off_out, stats_out = refs[:6]
        refs = refs[6:]
    else:
        hd_own, hd_far, psi_in, off_in, stats_in, near_out, far_out, late_out, stats_out = refs[:9]
        refs = refs[9:]
    field, images, left, diag, parts, sems = refs
    z, x, c = place()
    sectors, block, width = field.shape
    table = right.shape[1]
    links = table // sectors
    mine = 4 * z + 2 * c + x
    rows = (mine, mine ^ 12)

    copies = []

    def begin(source, target):
        copy = pltpu.make_async_copy(source, target, sems.at[len(copies)])
        copy.start()
        copies.append(copy)

    for at in range(2):
        begin(left_own.at[pl.ds(rows[at] * links, links)], left.at[0, pl.ds(at * links, links)])
    begin(left_other.at[pl.ds(table // 2, 2 * links)], left.at[1])
    if first:
        for at, mix in enumerate((mix_a, mix_b)):
            begin(mix.at[pl.ds(0, parts.shape[1]), pl.ds(width, LANES)], parts.at[at])
    else:
        begin(hd_own.at[x], diag.at[0])
        begin(hd_far, diag.at[1])

    def allowed(a, q, value):
        return lax.select(pattern[a, q] != 0, value, jnp.zeros_like(value))

    later = len(copies)
    for piece, offsets in zip(pieces, plan):
        for at, (dz, dx, dc, start, tall) in enumerate(offsets):
            row = row_of(dz, dx, dc)
            if first:
                begin(piece.at[at], field.at[row, pl.ds(start, tall)])
                continue
            for line in range(0, tall, 16):
                field[row, start + line : start + line + 16, :] = piece[at, line : line + 16, :]
    for copy in copies[later:]:
        copy.wait()

    def right_col(term, b, j):
        return cols_other[j, b] if term else right_cols[j, 0, b]

    def left_col(term, a, j):
        return cols_other[8 + j, a] if term else left_cols[j, 0, a]

    sources = [[left_col(term, rows[at], j) for at in range(2) for j in range(links)] for term in range(2)]

    deep = links * block

    none = jnp.zeros((block, block), jnp.bfloat16)
    pair = 2

    def image(n, carry):
        picks = [(i, j) for i in range(pair) for j in range(links)]
        for term in range(2):
            found = [right_col(term, n * pair + i, j) for i, j in picks]
            lhs = []
            for source in sources[term]:
                line = []
                for col in found:
                    value = field[source, :, pl.ds(pl.multiple_of(col * block, block), block)]
                    line.append(value)
                lhs.append(jnp.concatenate(line, axis=1))
            rhs = []
            for i, j in picks:
                tile = right[term, (n * pair + i) * links + j]
                rhs.append(jnp.concatenate([tile if i == at else none for at in range(pair)], axis=1))
            product = jnp.dot(
                jnp.concatenate(lhs, axis=0),
                jnp.concatenate(rhs, axis=0),
                preferred_element_type=jnp.float32,
            )
            product = product.astype(jnp.bfloat16)
            span = pl.ds(pl.multiple_of(n * pair * block, pair * block), pair * block)
            for at in range(2):
                images[at, term * deep : (term + 1) * deep, span] = product[at * deep : (at + 1) * deep]
        return carry

    lax.fori_loop(0, sectors // pair, image, 0, unroll=2)
    for copy in copies[:later]:
        copy.wait()

    step = 2
    early_rows = block // 2
    zero = jnp.zeros((8, LANES), jnp.float32)

    def column(n, sums):
        start = pl.multiple_of(n * step * block, step * block)
        span = pl.ds(start, step * block)
        sums = list(sums)

        def masked(a, value):
            parts = [
                allowed(a, n * step + i, value[:, i * block : (i + 1) * block]) for i in range(step)
            ]
            return jnp.concatenate(parts, axis=1)

        for at in range(2):
            weights = [left[term, at * links + j] for term in range(2) for j in range(links)]
            total = jnp.dot(
                jnp.concatenate(weights, axis=1),
                images[at, :, span],
                preferred_element_type=jnp.float32,
            )
            offdiag = masked(rows[at], total.astype(jnp.bfloat16).astype(jnp.float32))
            own = field[rows[at], :, span].astype(jnp.float32)
            if first:
                psi_out[at, :, span] = own.astype(jnp.bfloat16)
                off_out[at, :, span] = offdiag.astype(jnp.bfloat16)
                sums[0] += fold(own * own)
                sums[1] += fold(own * offdiag)
            else:
                weight = diag[at, :, span].astype(jnp.float32)
                narrow = (weight * own + offdiag).astype(jnp.bfloat16)
                if at == 0:
                    near_out[:, span] = narrow
                else:
                    far_out[:, span] = narrow[:early_rows]
                    late_out[:, span] = narrow[early_rows:]
                second = narrow.astype(jnp.float32)
                wave = psi_in[at, :, span].astype(jnp.float32)
                sigma_one = weight * wave + off_in[at, :, span].astype(jnp.float32)
                sums[0] += fold(wave * second)
                sums[1] += fold(own * sigma_one)
                sums[2] += fold(own * second)
        return tuple(sums)

    sums = list(lax.fori_loop(0, sectors // step, column, (zero,) * (2 if first else 3)))
    if first:
        far_weight = (parts[0] + parts[1]).astype(jnp.float32)
        sums[1] += weight_own[...] + (far_weight[0:8] + far_weight[16:24] + far_weight[32:40])
    stats_out[...] = jnp.zeros_like(stats_out)
    for at, value in enumerate(sums):
        stats_out[at : at + 1, :] = jnp.sum(value, axis=0, keepdims=True)
    if not first:
        stats_out[3:5, :] = stats_in[0:2, :]


def operate(first, plan, pieces, cols, pattern, right, left, extra):
    _, table, block, _ = right.shape
    width = pieces[0].shape[2]
    sectors = width // block
    links = table // sectors
    rows = jax.ShapeDtypeStruct((2, block, width), jnp.bfloat16)
    one = jax.ShapeDtypeStruct((block, width), jnp.bfloat16)
    some = jax.ShapeDtypeStruct((block // 2, width), jnp.bfloat16)
    stats = jax.ShapeDtypeStruct((8, LANES), jnp.float32)
    out_shape = (rows, rows, stats) if first else (one, some, some, stats)
    extra_specs = [ANY, ANY, VMEM] if first else [ANY, ANY, VMEM, VMEM, VMEM]
    inner = 2 * 2 * sectors * 2 * links * links * block * block * block
    outer = 2 * 2 * 2 * links * block * block * width
    return pl.pallas_call(
        functools.partial(operate_kernel, first, plan),
        out_shape=out_shape,
        in_specs=[SMEM, SMEM, SMEM, SMEM, VMEM, ANY, ANY] + [ANY if first else VMEM] * len(pieces) + extra_specs,
        out_specs=(VMEM,) * len(out_shape),
        scratch_shapes=[
            pltpu.VMEM((sectors, block, width), jnp.bfloat16),
            pltpu.VMEM((2, 2 * links * block, width), jnp.bfloat16),
            pltpu.VMEM((2, 2 * links, block, block), jnp.bfloat16),
            pltpu.VMEM((2, block, width), jnp.bfloat16),
            pltpu.VMEM((2, 48, LANES), jnp.bfloat16),
            pltpu.SemaphoreType.DMA((5 + len(plan),)),
        ],
        compiler_params=pltpu.CompilerParams(vmem_limit_bytes=PREPARE_LIMIT if first else OPERATE_LIMIT),
        cost_estimate=pl.CostEstimate(
            flops=inner + outer if first else 0,
            bytes_accessed=16 * 1024 * 1024 if first else 1024,
            transcendentals=0,
        ),
        name="operate_first" if first else "operate_second",
    )(*cols, pattern, right, *left, *pieces, *extra)


def arrange_kernel(own, near, far, out, found, sems):
    _, _, c = place()
    part = own.shape[0] // 2
    copies = [
        pltpu.make_async_copy(own, found.at[0], sems.at[0]),
        pltpu.make_async_copy(near.at[pl.ds(0, part)], found.at[1, pl.ds(c * part, part)], sems.at[1]),
        pltpu.make_async_copy(far.at[pl.ds(0, part)], found.at[1, pl.ds((1 - c) * part, part)], sems.at[2]),
    ]
    for copy in copies:
        copy.start()
    for copy in copies:
        copy.wait()

    def turn(at, carry):
        for term in range(2):
            out[term, at] = found[term, at].T
        return carry

    lax.fori_loop(0, found.shape[1], turn, 0, unroll=4)


def arrange(own, near, far):
    shape = (2, *own.shape)
    return pl.pallas_call(
        arrange_kernel,
        out_shape=jax.ShapeDtypeStruct(shape, own.dtype),
        in_specs=[ANY] * 3,
        out_specs=VMEM,
        scratch_shapes=[pltpu.VMEM(shape, own.dtype), pltpu.SemaphoreType.DMA((3,))],
        compiler_params=pltpu.CompilerParams(vmem_limit_bytes=VMEM_LIMIT),
        name="arrange",
    )(own, near, far)


def prepare_kernel(
    pattern, theta, hd, right, left, right_cols, left_cols, mix_a, mix_b, packed, own_out, waves, diag, spots, sems
):
    z, x, c = place()
    half = z // 2
    middle = in_middle(z)
    mine = 4 * z + 2 * c + x
    block, width = diag.shape
    sectors = width // block
    links = right.shape[0] // sectors
    part = right.shape[0] // 2
    root_a = jnp.where(middle, half, 1 - half)
    rows = pl.ds(0, width)
    sources = (
        (theta.at[half, x], waves.at[0]),
        (theta.at[1 - half, x], waves.at[1]),
        (hd.at[x], diag),
        (theta.at[root_a, jnp.where(middle, 0, x)], mix_a.at[:, rows]),
        (theta.at[1 - root_a, jnp.where(middle, x, 0)], mix_b.at[:, rows]),
        (right.at[pl.ds(c * part, part)], packed.at[pl.ds(0, part)]),
        (left.at[pl.ds((mine ^ 1) * links, links)], packed.at[pl.ds(part, links)]),
        (left.at[pl.ds((mine ^ 13) * links, links)], packed.at[pl.ds(part + links, links)]),
    )
    copies = [
        pltpu.make_async_copy(source, target, sems.at[at])
        for at, (source, target) in enumerate(sources)
    ]
    for copy in copies:
        copy.start()
    last = part + 2 * links
    spots[...] = jnp.zeros_like(spots)
    spots[0:links, 0:sectors] = right_cols[:, 0, :].astype(jnp.float32)
    spots[8 : 8 + links, 0:sectors] = left_cols[:, 0, :].astype(jnp.float32)
    packed[last] = jnp.zeros_like(packed[last])
    packed[last, 0:16, :] = spots[...].astype(jnp.bfloat16)
    for copy in copies[:3]:
        copy.wait()
    zero = jnp.zeros((8, LANES), jnp.float32)

    def column(q, sums):
        span = pl.ds(pl.multiple_of(q * block, block), block)
        weight = diag[:, span].astype(jnp.float32)
        weight = jnp.where(pattern[mine, q] != 0, weight, jnp.zeros_like(weight))
        found = []
        for root in range(2):
            wave = waves[root, :, span].astype(jnp.float32)
            found.append(sums[root] + fold(weight * wave * wave))
        return tuple(found)

    near, far = lax.fori_loop(0, sectors, column, (zero, zero), unroll=4)
    own_out[...] = near
    left_over = jnp.concatenate([far, zero], axis=0)
    parts = []
    for _ in range(3):
        piece = left_over.astype(jnp.bfloat16)
        parts.append(piece)
        left_over = left_over - piece.astype(jnp.float32)
    parts.append(jnp.zeros((block - 48, LANES), jnp.bfloat16))
    tail = jnp.concatenate(parts, axis=0)
    none = jnp.zeros_like(tail)
    mix_a[:, width:] = jnp.where(middle, none, tail)
    mix_b[:, width:] = jnp.where(middle, tail, none)
    for copy in copies[3:]:
        copy.wait()


def prepare(pattern, theta, hd, right, left, *cols):
    _, _, block, width = theta.shape
    table = right.shape[0]
    links = table * block // width
    kind = jnp.bfloat16
    mix = jax.ShapeDtypeStruct((block, width + LANES), kind)
    packed = jax.ShapeDtypeStruct((table // 2 + 2 * links + 1, block, block), kind)
    return pl.pallas_call(
        prepare_kernel,
        out_shape=(mix, mix, packed, jax.ShapeDtypeStruct((8, LANES), jnp.float32)),
        in_specs=[SMEM, ANY, ANY, ANY, ANY, VMEM, VMEM],
        out_specs=(VMEM,) * 4,
        scratch_shapes=[
            pltpu.VMEM((2, block, width), kind),
            pltpu.VMEM((block, width), kind),
            pltpu.VMEM((16, LANES), jnp.float32),
            pltpu.SemaphoreType.DMA((8,)),
        ],
        compiler_params=pltpu.CompilerParams(vmem_limit_bytes=PREPARE_LIMIT),
        name="prepare",
    )(pattern, theta, hd, right, left, *cols)


def total_of(rows):
    return jnp.sum(rows, axis=1, keepdims=True)


def update_kernel(psi_ref, off_ref, hd_own, hd_far, *refs):
    stats, (t_out, stats_out, psi, off, diag, sems) = refs[:4], refs[4:]
    z, x, c = place()
    copies = [
        pltpu.make_async_copy(hd_own.at[x], diag.at[0], sems.at[0]),
        pltpu.make_async_copy(hd_far, diag.at[1], sems.at[1]),
        pltpu.make_async_copy(psi_ref, psi, sems.at[2]),
        pltpu.make_async_copy(off_ref, off, sems.at[3]),
    ]
    for copy in copies:
        copy.start()
    whole = sum(ref[at, 0:2, :] for ref in stats for at in range(2))
    norm_sq, energy_sum = total_of(whole[0:1, :]), total_of(whole[1:2, :])
    energy = energy_sum / (norm_sq + 1e-06)
    mine = total_of(stats[0][0, 0:1, :])
    for copy in copies:
        copy.wait()
    _, block, width = psi.shape
    step = 16
    zero = jnp.zeros((8, LANES), jnp.float32)

    def chunk(n, total):
        span = pl.ds(pl.multiple_of(n * step, step), step)
        for at in range(2):
            wave = psi[at, span, :].astype(jnp.float32)
            weight = diag[at, span, :].astype(jnp.float32)
            sigma = weight * wave + off[at, span, :].astype(jnp.float32)
            shifted = weight - energy
            t = (sigma - energy * wave) * shifted / (shifted * shifted + 1.0)
            t_out[at, span, :] = t
            total = total + fold(wave * t)
        return total

    lanes = jnp.sum(lax.fori_loop(0, block // step, chunk, zero), axis=0, keepdims=True)
    correlation = total_of(lanes)
    local = jnp.where(mine > 0.0, correlation / jnp.where(mine > 0.0, mine, 1.0), 0.0)

    def within(n, total):
        span = pl.ds(pl.multiple_of(n * step, step), step)
        for at in range(2):
            rest = t_out[at, span, :] - local * psi[at, span, :].astype(jnp.float32)
            total = total + fold(rest * rest)
        return total

    spread = jnp.sum(lax.fori_loop(0, block // step, within, zero), axis=0, keepdims=True)
    stats_out[...] = jnp.zeros_like(stats_out)
    stats_out[0:1, :] = jnp.broadcast_to(correlation, (1, LANES))
    stats_out[1:2, :] = jnp.broadcast_to(total_of(spread), (1, LANES))
    stats_out[2:3, :] = jnp.broadcast_to(mine, (1, LANES))
    stats_out[3:4, :] = jnp.broadcast_to(local, (1, LANES))
    stats_out[4:5, :] = jnp.broadcast_to(norm_sq, (1, LANES))


def correct_kernel(psi, t, *refs):
    stats, outs = refs[:4], refs[4:]
    stats = [ref.at[at] for ref in stats for at in range(2)]
    norm_sq = stats[0][4:5, 0:1]
    factor = sum(ref[0:1, 0:1] for ref in stats) / (norm_sq + 1e-06)
    length_sq = jnp.zeros((1, 1), jnp.float32)
    for ref in stats:
        gap = factor - ref[3:4, 0:1]
        length_sq = length_sq + (ref[1:2, 0:1] + gap * gap * ref[2:3, 0:1])
    scale = jnp.sqrt(norm_sq / (length_sq + 1e-06))
    _, block, width = psi.shape
    step = 16

    def chunk(n, carry):
        span = pl.ds(pl.multiple_of(n * step, step), step)
        for at in range(2):
            wave = psi[at, span, :].astype(jnp.float32)
            outs[at][span, :] = ((t[at, span, :] - factor * wave) * scale).astype(jnp.bfloat16)
        return carry

    lax.fori_loop(0, block // step, chunk, 0)


def assemble_kernel(places, based, *refs):
    count = len(places)
    pieces, (out, sems) = refs[:count], refs[count + based :]
    z, x, c = place()
    half = z // 2
    copies = []
    for at, (root, flip, start) in enumerate(places):
        size = pieces[at].shape[0]
        target = out.at[half ^ root, x ^ flip, pl.ds(start, size)]
        copies.append(pltpu.make_async_copy(pieces[at], target, sems.at[at]))
    for copy in copies:
        copy.start()
    for copy in copies:
        copy.wait()


def assemble(block, pieces, places, base=None):
    width = pieces[0].shape[1]
    based = [] if base is None else [base]
    return pl.pallas_call(
        functools.partial(assemble_kernel, places, len(based)),
        out_shape=jax.ShapeDtypeStruct((2, 2, block, width), pieces[0].dtype),
        in_specs=[VMEM] * len(pieces) + [ANY] * len(based),
        out_specs=ANY,
        scratch_shapes=[pltpu.SemaphoreType.DMA((len(pieces),))],
        input_output_aliases={len(pieces): 0} if based else {},
        compiler_params=pltpu.CompilerParams(vmem_limit_bytes=VMEM_LIMIT),
        name="assemble",
    )(*pieces, *based)


def after(value, *others):
    return lax.optimization_barrier((value, *others))[0]


def shards(theta, hdiag, pattern, left_blocks, left_cols, right_blocks, right_cols):
    roots, row_count, width = theta.shape
    sectors = pattern.shape[0]
    block = width // sectors
    z, x, c = place()
    half = z // 2
    mine = 4 * z + 2 * c + x

    halves = theta.reshape(roots, 2, block, width)
    diag = hdiag.reshape(2, block, width)
    middle = in_middle(z)
    right = right_blocks.reshape(-1, block, block)
    left = left_blocks.reshape(-1, block, block)
    cols = (right_cols.transpose(2, 0, 1), left_cols.transpose(2, 0, 1))

    mix_a, mix_b, packed, weight_own = prepare(pattern, halves, diag, right, left, *cols)
    mix_a = lax.ppermute(mix_a, "blk", [(0, 2), (2, 3), (3, 1), (1, 0)])
    mix_b = lax.ppermute(mix_b, "blk", [(0, 1), (1, 3), (3, 2), (2, 0)])
    operators = across(packed, "ops", 1)

    def masked(row, value):
        line = lax.dynamic_index_in_dim(pattern, row, 0, keepdims=False).astype(jnp.bfloat16)
        return value * jnp.repeat(line, block)[None, :]

    own = [
        masked(row_of(0, 2 + at, 0), lax.dynamic_slice(halves, (half, at, 0, 0), (1, 1, block, width))[0, 0])
        for at in range(2)
    ]
    own = list(lax.optimization_barrier(tuple(own)))
    own_core = [across(value, "sub", 1) for value in own]

    mix_a, mix_b = after((mix_a, mix_b), *own_core)
    far = masked(row_of(2, 0, 0), jnp.where(middle, mix_a[:, :width], mix_b[:, :width]))
    far_z = across(far, "blk", 1)
    far_x = across(far, "ops", 1)
    late_a, late_b = after((mix_a, mix_b), far)
    near_a = masked(row_of(1, 2, 0), jnp.where(middle, late_b[:, :width], late_a[:, :width]))
    far_core = across(far, "sub", 1)
    near_a_core = across(near_a, "sub", 1)

    operators = after(operators, mix_b)
    operators_core = across(operators, "sub", 1)
    turned = arrange(right, operators, operators_core)
    cols_other = operators[-1, :16, :sectors].astype(jnp.int32)
    cols = (*cols, cols_other)
    next_b, far_z = after((own[1], far_z), far_core, near_a_core, turned, cols_other)
    near_b = across(next_b, "blk", 1)
    far_zx = across(far_z, "ops", 1)
    far_x_core = across(far_x, "sub", 1)
    far_z_core = across(far_z, "sub", 1)
    hd_far = lax.dynamic_index_in_dim(diag, x, 0, keepdims=False)
    hd_far = across(after(hd_far, far_z), "blk", 3)
    far_zx_core = across(far_zx, "sub", 1)
    near_b_core = across(near_b, "sub", 1)

    left = (left, operators)
    pieces = []
    plan = []
    for piece, offset in (
        (own[0], (0, 2, 0)),
        (own[1], (0, 3, 0)),
        (own_core[0], (0, 2, 1)),
        (own_core[1], (0, 3, 1)),
        (near_a, (1, 2, 0)),
        (near_b, (1, 3, 0)),
        (near_a_core, (1, 2, 1)),
        (near_b_core, (1, 3, 1)),
        (far, (2, 0, 0)),
        (far_core, (2, 0, 1)),
        (far_x, (2, 1, 0)),
        (far_x_core, (2, 1, 1)),
        (far_z, (3, 0, 0)),
        (far_z_core, (3, 0, 1)),
        (far_zx, (3, 1, 0)),
        (far_zx_core, (3, 1, 1)),
    ):
        pieces.append(piece[None])
        plan.append((offset + (0, block),))
    psi, off_one, stats_one = operate(
        True, tuple(plan), pieces, cols, pattern, turned, left, (mix_a, mix_b, weight_own)
    )

    found = share(stats_one)
    t, stats_two = pl.pallas_call(
        update_kernel,
        out_shape=(
            jax.ShapeDtypeStruct((2, block, width), jnp.float32),
            jax.ShapeDtypeStruct((8, LANES), jnp.float32),
        ),
        in_specs=[ANY] * 4 + [VMEM] * 4,
        out_specs=(VMEM, VMEM),
        scratch_shapes=[
            pltpu.VMEM((2, block, width), jnp.bfloat16),
            pltpu.VMEM((2, block, width), jnp.bfloat16),
            pltpu.VMEM((2, block, width), jnp.bfloat16),
            pltpu.SemaphoreType.DMA((4,)),
        ],
        compiler_params=pltpu.CompilerParams(vmem_limit_bytes=VMEM_LIMIT),
        name="update",
    )(psi, off_one, diag, hd_far, *found)
    found = share(stats_two)
    one = jax.ShapeDtypeStruct((block, width), jnp.bfloat16)
    changed_near, changed_far = pl.pallas_call(
        correct_kernel,
        out_shape=(one, one),
        in_specs=[VMEM, VMEM] + [VMEM] * 4,
        out_specs=(VMEM, VMEM),
        compiler_params=pltpu.CompilerParams(vmem_limit_bytes=VMEM_LIMIT),
        name="correct",
    )(psi, t, *found)

    near_z = across(changed_near, "blk", 1)
    far_x = across(changed_far, "ops", 1)
    near_core = across(changed_near, "sub", 1)
    far_core = across(changed_far, "sub", 1)
    other_middle = lax.ppermute(changed_far, "blk", [(1, 2), (2, 1)])
    near_z, far_x = after((near_z, far_x), other_middle)
    near_zx = across(near_z, "ops", 1)
    far_xz = across(far_x, "blk", 1)
    near_x = across(after(changed_near, near_z, far_x), "ops", 1)
    far_z = across(after(changed_far, near_z, far_x), "blk", 1)
    near_z_core = across(near_z, "sub", 1)
    far_x_core = across(far_x, "sub", 1)
    near_x_core = across(near_x, "sub", 1)
    far_z_core = across(far_z, "sub", 1)
    near_zx_core = across(near_zx, "sub", 1)
    far_xz_core = across(far_xz, "sub", 1)
    other_end = lax.ppermute(after(changed_far, near_z, far_x), "blk", [(0, 3), (3, 0)])
    pieces, plan = [], []
    for piece, offset in (
        (changed_near, (0, 0, 0)),
        (changed_far, (3, 0, 0)),
        (near_core, (0, 0, 1)),
        (far_core, (3, 0, 1)),
        (near_z, (1, 0, 0)),
        (far_z, (2, 0, 0)),
        (near_z_core, (1, 0, 1)),
        (far_z_core, (2, 0, 1)),
        (near_x, (0, 1, 0)),
        (far_x, (3, 1, 0)),
        (near_x_core, (0, 1, 1)),
        (far_x_core, (3, 1, 1)),
        (near_zx, (1, 1, 0)),
        (far_xz, (2, 1, 0)),
        (near_zx_core, (1, 1, 1)),
        (far_xz_core, (2, 1, 1)),
    ):
        pieces.append(piece[None])
        plan.append((offset + (0, block),))
    two_near, two_far, two_late, stats_three = operate(
        False, tuple(plan), pieces, cols, pattern, turned, left, (diag, hd_far, psi, off_one, stats_one)
    )

    far_in = across(two_far, "blk", 3)
    near_in = across(two_near, "ops", 1)
    late_in = across(after(two_late, far_in), "blk", 3)
    far_in_x = across(after(far_in, near_in), "ops", 1)
    sums = stats_three + across(stats_three, "sub", 1)
    other = jnp.where(middle, other_middle, after(other_end, two_near))
    other_x = across(other, "ops", 1)
    sums = after(sums, far_in)
    both = jnp.stack([sums + across(sums, "blk", 1), across(sums, "blk", 2) + across(sums, "blk", 3)])
    both = after(both, late_in)
    both = both + across(both, "ops", 1)
    other, other_x = after((other, other_x), late_in)
    late_in_x = across(late_in, "ops", 1)
    both = jnp.sum(jnp.where(half == 0, both, both[::-1])[:, :5], axis=2)
    scale = both[:, 3:4] + 1e-06
    subspace = jnp.concatenate([both[:, 4:5], both[:, 0:3]], axis=1) / scale
    places = ((0, 0, 0), (0, 1, 0), (1, 0, 0), (1, 1, 0))
    correction = assemble(block, (changed_near, near_x, other, other_x), places)
    places = ((0, 0, 0), (0, 1, 0), (1, 0, 0), (1, 0, block // 2), (1, 1, 0))
    sigma_two = assemble(block, (two_near, near_in, far_in, late_in, far_in_x), places)
    sigma_two = assemble(block, (late_in_x,), ((1, 1, block // 2),), sigma_two)
    return correction.reshape(theta.shape), sigma_two.reshape(theta.shape), subspace


def solution(mesh):
    in_specs = (
        P("groups", ("blk", "sub"), None),
        P(("groups", "blk", "sub"), None),
        P("groups", None),
        P(("groups", "ops"), None, None, None, None),
        P(("groups", "ops"), None, None),
        P(("groups", "ops"), None, None, None, None),
        P(("groups", "ops"), None, None),
    )
    out_specs = (
        P("groups", ("blk", "sub"), None),
        P("groups", ("blk", "sub"), None),
        P("groups", None),
    )
    body = shards if halves_fit(mesh) else general_shards
    return jax.shard_map(body, mesh=mesh, in_specs=in_specs, out_specs=out_specs, check_vma=False)
```
